32 devices in a mesh: row: 4 (over x, core), col: 8 (over z, y).
Axes of the slice: x: 2, y: 2, z: 4, core: 2. Of those that a mesh axis runs over, the one named last changes fastest.
Arguments:
- object_field: float32 [2, 2048, 4096], P(None, 'row', 'col'), may hold values from -5 to 5
- probe: float32 [2, 2, 256, 256], replicated, may hold values from -5 to 5
- amplitudes: float32 [256, 256, 256], P(('row', 'col')), may hold values from 0 to 2.5
- positions: int32 [256, 2], P(('row', 'col')), may hold values from 0 to 3840, as said below
- counts: int32 [32], P(('row', 'col')), may hold values from 1 to 8, as said below
Outputs:
- new_object: float32 [2, 2048, 4096], P(None, 'row', 'col')
- new_probe: float32 [2, 2, 256, 256], replicated
The draws below stay inside these ranges and needn't reach their ends.
Inputs may be any that keep to these rules, and one draw needn't show every extreme that they name: `positions`: each slot's patch lies inside the object, and its top-left pixel lies in the tile of the device that holds the slot. `counts`: one device holds exactly 8 live slots in every draw; the others fewer.
All inputs are finite; a program needn't handle non-finite values.
Results may differ from the reference program's by a relative error of at most 0.0003.
Values sent between devices are 32-bit elements; how exact they have to be, the bound alone decides.
No kernel may reach another device: no remote copies, remote signals or barrier semaphores. Data moves between devices by JAX's collectives and lax.ppermute only.
A program may use at most 256 MiB of HBM per device.

```python
import jax
import jax.numpy as jnp
from jax import lax

P_SIZE = 256
M = 2
TH = 512
TW = 512
CAP = 8
NY = 2048
NX = 4096
SLOTS = 256
N_ROW = 4
N_COL = 8


def draw_counts(key, part):
    key = jax.random.fold_in(key, 11)
    first, second = jax.random.split(key)
    devices_all = N_ROW * N_COL
    base = jax.random.randint(first, (devices_all,), max(1, CAP // 4), CAP // 2 + 1, dtype=jnp.int32)
    busiest = jax.random.randint(second, (), 0, devices_all, dtype=jnp.int32)
    return jnp.where(jnp.arange(devices_all, dtype=jnp.int32) == busiest, CAP, base).astype(jnp.int32)


def draw_positions(key, part):
    key = jax.random.fold_in(key, 23)
    first, second = jax.random.split(key)
    slot_ids = jnp.arange(SLOTS, dtype=jnp.int32)
    device = slot_ids // CAP
    tile_row = device // N_COL
    tile_col = device % N_COL
    rows = tile_row * TH + jax.random.randint(first, (SLOTS,), 0, TH, dtype=jnp.int32)
    cols = tile_col * TW + jax.random.randint(second, (SLOTS,), 0, TW, dtype=jnp.int32)
    rows = jnp.minimum(rows, NY - P_SIZE)
    cols = jnp.minimum(cols, NX - P_SIZE)
    return jnp.stack([rows, cols], axis=1).astype(jnp.int32)


def block_levels(stream_key, dims, cuts, least, largest):
    def one(dim, parts):
        steps = jax.random.uniform(jax.random.fold_in(jax.random.fold_in(stream_key, 6), dim), (parts,), jnp.float32, least / len(cuts), largest / len(cuts))
        return jnp.repeat(jnp.exp(steps), dims[dim] // parts).reshape((-1,) + (1,) * (len(dims) - dim - 1))

    level = one(*cuts[0])
    for cut in cuts[1:]:
        level = level * one(*cut)
    return level


def gaussian(rng, dims, scale, limit, pieces=(), kind=jnp.bfloat16):
    array = scale * jax.random.normal(rng, dims, jnp.float32)
    if pieces:
        array = array * block_levels(rng, dims, pieces, -0.22, 0.18)
    return jnp.clip(array, -limit, limit).astype(kind)


def setup_inputs(seed: int = 0) -> dict:
    seeds = jax.random.split(jax.random.key(seed), 6)
    object_field = gaussian(seeds[0], (2, NY, NX), 0.7, 5.0, ((1, 4), (2, 8)), jnp.float32)
    probe = gaussian(seeds[1], (M, 2, P_SIZE, P_SIZE), 0.7, 5.0, (), jnp.float32)
    amplitudes = jnp.clip(2.5 * jax.random.uniform(seeds[2], (SLOTS, P_SIZE, P_SIZE), jnp.float32) ** block_levels(seeds[2], (SLOTS, P_SIZE, P_SIZE), ((0, 32),), -0.2, 0.2), 0.0, 2.5)
    positions = draw_positions(jax.random.fold_in(seeds[5], 71), 0)
    counts = draw_counts(jax.random.fold_in(seeds[5], 71), 0)
    return {"object_field": object_field, "probe": probe, "amplitudes": amplitudes, "positions": positions, "counts": counts}


def pattern_terms(patch, probe, amplitude):
    patch_c = patch[0] + 1j * patch[1]
    probe_c = probe[:, 0] + 1j * probe[:, 1]
    exit_wave = probe_c * patch_c[None]
    far_field = jnp.fft.fft2(exit_wave, norm='ortho')
    intensity = lax.optimization_barrier(jnp.sum(jnp.real(far_field) ** 2 + jnp.imag(far_field) ** 2, axis=0))
    factor = amplitude / jnp.maximum(jnp.sqrt(intensity), 0.3) - 1.0
    back_wave = jnp.fft.ifft2(far_field * factor[None], norm='ortho')
    object_grad = lax.optimization_barrier(jnp.sum(jnp.conj(probe_c) * back_wave, axis=0))
    object_light = lax.optimization_barrier(jnp.sum(probe[:, 0] ** 2 + probe[:, 1] ** 2, axis=0))
    object_terms = jnp.stack([jnp.real(object_grad), jnp.imag(object_grad), object_light])
    probe_grad = jnp.conj(patch_c)[None] * back_wave
    probe_terms = jnp.stack([jnp.real(probe_grad), jnp.imag(probe_grad)], axis=1)
    probe_light = patch[0] ** 2 + patch[1] ** 2
    return (object_terms, probe_terms, probe_light)

def reference(object_field, probe, amplitudes, positions, counts):
    slot_ids = jnp.arange(SLOTS, dtype=jnp.int32)
    live = (slot_ids % CAP < counts[slot_ids // CAP]).astype(jnp.float32)
    zero_index = jnp.zeros((), jnp.int32)

    def visit(carry, inputs):
        grid, probe_sum, light_sum = carry
        amplitude, position, weight = inputs
        top = position[0].astype(jnp.int32)
        left = position[1].astype(jnp.int32)
        patch = lax.dynamic_slice(object_field, (zero_index, top, left), (2, P_SIZE, P_SIZE))
        object_terms, probe_terms, probe_light = pattern_terms(patch, probe, amplitude)
        current = lax.dynamic_slice(grid, (zero_index, top, left), (3, P_SIZE, P_SIZE))
        grid = lax.dynamic_update_slice(grid, current + weight * object_terms, (zero_index, top, left))
        return ((grid, probe_sum + weight * probe_terms, light_sum + weight * probe_light), None)
    start = (jnp.zeros((3, NY, NX), jnp.float32), jnp.zeros((M, 2, P_SIZE, P_SIZE), jnp.float32), jnp.zeros((P_SIZE, P_SIZE), jnp.float32))
    (grid, probe_sum, light_sum), _ = lax.scan(visit, start, (amplitudes, positions, live))
    new_object = object_field + grid[:2] / (grid[2] + 1.0)
    new_probe = probe + probe_sum / (light_sum + 1.0)
    return (new_object, new_probe)
```

```python
import functools
import math

import jax
import jax.numpy as jnp
import ml_dtypes
import numpy as np
from jax import lax
from jax.experimental import pallas as pl
from jax.experimental.pallas import tpu as pltpu
from jax.sharding import PartitionSpec as P

F32 = jnp.float32
BF16 = jnp.bfloat16
MIB = 1024 * 1024
FLOOR = 0.3


def split_np(table):
    high = table.astype(ml_dtypes.bfloat16)
    low = (table - high.astype(np.float64)).astype(ml_dtypes.bfloat16)
    return high, low


def dft_tables(length):
    half = length // 2
    q = np.arange(half)[:, None]
    n = np.arange(half)[None, :]
    forward = []
    for odd in range(2):
        phase = (n * (2 * q + odd)) % length
        angle = phase * (-2.0 * math.pi / length)
        re = np.cos(angle) / math.sqrt(length)
        im = np.sin(angle) / math.sqrt(length)
        forward.append(np.stack(split_np(np.block([[re, -im], [im, re]]))))
    forward = np.stack(forward)
    return forward, np.ascontiguousarray(forward.transpose(0, 1, 3, 2))


def order_tables(length):
    order = np.concatenate([np.arange(0, length, 2), np.arange(1, length, 2)])
    table = np.eye(length)[order]
    rows = np.concatenate([table] * 3, axis=1)
    return rows.astype(ml_dtypes.bfloat16), rows.T.astype(ml_dtypes.bfloat16)


def dot(a, b):
    return jnp.dot(a, b, preferred_element_type=F32)


def split(x):
    high = x.astype(BF16)
    return high, (x - high.astype(F32)).astype(BF16)


def roll_rows(x, shift):
    return pltpu.roll(x.reshape(x.shape[0] // 8, 8, x.shape[1]), shift, 1)


def split_three(x):
    high = x.astype(BF16)
    rest = x - high.astype(F32)
    middle = rest.astype(BF16)
    return high, middle, (rest - middle.astype(F32)).astype(BF16)


def add_shifted(template, grid, where_t, where_g, top, left, size):
    top_s = top & 7
    top_b = pl.multiple_of(top - top_s, 8)
    left_s = left & 127
    left_b = pl.multiple_of(left - left_s, 128)
    step = 24
    wrapped = lax.broadcasted_iota(jnp.int32, (step, 128), 1) < left_s
    wrapped_rows = lax.broadcasted_iota(jnp.int32, (step // 8, 8, 128), 1) < top_s
    zero = jnp.zeros((step, 128), F32)
    blocks = size // 128
    for at in range(0, size + 8, step):
        parts = []
        for j in range(blocks):
            x = roll_rows(template[where_t + (pl.ds(at, step + 8), pl.ds(128 * j, 128))], top_s)
            x = jnp.where(wrapped_rows, x[:-1], x[1:]).reshape(step, 128)
            parts.append(pltpu.roll(x, left_s, 1))
        for j in range(blocks + 1):
            before = parts[j - 1] if j > 0 else zero
            after = parts[j] if j < blocks else zero
            spot = where_g + (pl.ds(top_b + at, step), pl.ds(left_b + 128 * j, 128))
            grid[spot] += jnp.where(wrapped, before, after)


def take_shifted(field, where, top, left, at, step, size):
    top_s = top & 7
    top_b = pl.multiple_of(top - top_s, 8)
    left_s = left & 127
    left_b = pl.multiple_of(left - left_s, 128)
    back = (128 - left_s) & 127
    keep = lax.broadcasted_iota(jnp.int32, (step + 8, 128), 1) < 128 - left_s
    keep_rows = lax.broadcasted_iota(jnp.int32, (step // 8, 8, 128), 1) < 8 - top_s
    blocks = size // 128
    parts = [
        pltpu.roll(field[where + (pl.ds(top_b + at, step + 8), pl.ds(left_b + 128 * j, 128))], back, 1)
        for j in range(blocks + 1)
    ]
    pieces = []
    for j in range(blocks):
        x = roll_rows(jnp.where(keep, parts[j], parts[j + 1]), (8 - top_s) & 7)
        pieces.append(jnp.where(keep_rows, x[:-1], x[1:]).reshape(step, 128))
    return jnp.concatenate(pieces, axis=1)


def light_kernel(meta, probe, inverse_light, template, grid):
    size = probe.shape[2]
    tile_rows, tile_cols = inverse_light.shape
    template[0:8, :] = jnp.zeros((8, size), F32)
    template[8 + size :, :] = jnp.zeros((8, size), F32)
    for at in range(0, size, 32):
        rows = pl.ds(at, 32)
        total = jnp.zeros((32, size), F32)
        for m in range(probe.shape[0]):
            total += probe[m, 0, rows] * probe[m, 0, rows] + probe[m, 1, rows] * probe[m, 1, rows]
        template[pl.ds(8 + at, 32), :] = total

    @pl.loop(0, tile_rows // 32)
    def _(step):
        rows = pl.ds(pl.multiple_of(size + step * 32, 32), 32)
        grid[rows, size : size + tile_cols] = jnp.zeros((32, tile_cols), F32)

    slots = meta.shape[1] // 2
    for device in range(4):

        @pl.loop(0, meta[device, 2 * slots])
        def _(slot):
            top = meta[device, 2 * slot] + size
            left = meta[device, 2 * slot + 1] + size

            @pl.when((top > 0) & (left > 0))
            def _():
                add_shifted(template, grid, (), (), top, left, size)

    @pl.loop(0, tile_rows // 32)
    def _(step):
        rows = pl.ds(pl.multiple_of(size + step * 32, 32), 32)
        out_rows = pl.ds(pl.multiple_of(step * 32, 32), 32)
        inverse_light[out_rows, :] = 1.0 / (grid[rows, size : size + tile_cols] + 1.0)


def light(meta, probe, tile_shape):
    size = probe.shape[2]
    vmem = pl.BlockSpec(memory_space=pltpu.VMEM)
    return pl.pallas_call(
        light_kernel,
        out_shape=jax.ShapeDtypeStruct(tile_shape, F32),
        in_specs=[pl.BlockSpec(memory_space=pltpu.SMEM), vmem],
        out_specs=vmem,
        scratch_shapes=[
            pltpu.VMEM((size + 16, size), F32),
            pltpu.VMEM((tile_shape[0] + 2 * size, tile_shape[1] + 2 * size), F32),
        ],
        compiler_params=pltpu.CompilerParams(vmem_limit_bytes=16 * MIB),
        cost_estimate=pl.CostEstimate(flops=4_000_000_000, bytes_accessed=16_000_000, transcendentals=0),
        name="light",
    )(meta, probe)


def arrange_kernel(meta, amplitudes, order_rows, order_cols, out):
    @pl.loop(0, meta[0, meta.shape[1] - 1])
    def _(slot):
        x = dot(order_rows[...], jnp.concatenate(split_three(amplitudes[slot]), axis=0))
        out[slot] = dot(jnp.concatenate(split_three(x), axis=1), order_cols[...])


def arrange(meta, amplitudes):
    order_rows, order_cols = (jnp.asarray(table) for table in order_tables(amplitudes.shape[2]))
    vmem = pl.BlockSpec(memory_space=pltpu.VMEM)
    return pl.pallas_call(
        arrange_kernel,
        out_shape=jax.ShapeDtypeStruct(amplitudes.shape, F32),
        in_specs=[pl.BlockSpec(memory_space=pltpu.SMEM)] + [vmem] * 3,
        out_specs=vmem,
        compiler_params=pltpu.CompilerParams(vmem_limit_bytes=16 * MIB),
        cost_estimate=pl.CostEstimate(flops=2_000_000_000, bytes_accessed=8_000_000, transcendentals=0),
        name="arrange",
    )(meta, amplitudes, order_rows, order_cols)


def three_left(table, t):
    return jnp.concatenate([table[t, 0], table[t, 0], table[t, 1]], axis=1)


def three_right(table, v):
    return jnp.concatenate([table[v, 0], table[v, 0], table[v, 1]], axis=0)


def weave(first, second):
    total = max(len(first), len(second))
    done = [0, 0]
    for i in range(1, total + 1):
        for k, pieces in enumerate((first, second)):
            while done[k] * total < i * len(pieces):
                pieces[done[k]]()
                done[k] += 1


def slots_kernel(
    needs_rim, meta, probe, amplitudes, sources, forward_t, backward_t, init, outs, probe_out,
    ext, grid, amp, chosen, patch_f, patch_b, x_f, y_f, z_f, g_s, x_b, z_b, back, template, sems,
):
    size = probe.shape[2]
    half = size // 2
    modes = probe.shape[0]
    slots = amplitudes.shape[0]
    tile_rows, tile_cols = (n - size for n in ext.shape[1:])
    step = 32
    load_sems, amp_sems, out_sems = sems

    regions = (
        (pl.ds(0, tile_rows), pl.ds(0, tile_cols)),
        (pl.ds(tile_rows, size), pl.ds(0, tile_cols)),
        (pl.ds(0, size), pl.ds(tile_cols, size)),
        (pl.ds(size, tile_rows - size), pl.ds(tile_cols, size)),
        (pl.ds(tile_rows, size), pl.ds(tile_cols, size)),
    )
    loads = [
        pltpu.make_async_copy(source, ext.at[:, rows, cols], load_sems.at[i])
        for i, (source, (rows, cols)) in enumerate(zip(sources, regions))
    ]
    if needs_rim:
        loads.append(pltpu.make_async_copy(init[0], grid.at[:, :, pl.ds(0, tile_cols)], load_sems.at[5]))
        loads.append(pltpu.make_async_copy(init[1], probe_out, load_sems.at[6]))
    for load in loads:
        load.start()

    def amp_copy(slot):
        return pltpu.make_async_copy(amplitudes.at[slot], amp.at[slot], amp_sems.at[slot])

    def choose(slot, found):
        beyond = meta[0, 2 * slot + 1] + size > tile_cols
        wanted = beyond if needs_rim else jnp.logical_not(beyond)

        @pl.when(wanted)
        def _():
            chosen[found] = slot
            amp_copy(slot).start()

        return found + wanted.astype(jnp.int32)

    count = lax.fori_loop(0, meta[0, 2 * slots], choose, jnp.zeros((), jnp.int32))

    @pl.loop(0, (tile_rows + size) // step)
    def _(at):
        rows = pl.ds(pl.multiple_of(at * step, step), step)
        for c in range(2):
            if needs_rim:
                grid[c, rows, tile_cols:] = jnp.zeros((step, size), F32)
            else:
                grid[c, rows, :] = jnp.zeros((step, tile_cols + size), F32)

    if not needs_rim:

        @pl.loop(0, size // step)
        def _(at):
            rows = pl.ds(pl.multiple_of(at * step, step), step)
            for c in range(2 * modes + 1):
                probe_out[c, rows, :] = jnp.zeros((step, size), F32)

    for c in range(2):
        template[c, 0:8, :] = jnp.zeros((8, size), F32)
        template[c, 8 + size :, :] = jnp.zeros((8, size), F32)
    for load in loads:
        load.wait()

    def corner(slot):
        return meta[0, 2 * slot], meta[0, 2 * slot + 1]

    def forward(slot):
        top, left = corner(slot)

        def take(at):
            rows = pl.ds(at, step)
            total = jnp.zeros((step, size), F32)
            for c in range(2):
                piece = take_shifted(ext, (c,), top, left, at, step, size)
                patch_f[c, rows, :] = piece
                total += piece * piece
            probe_out[2 * modes, rows, :] += total

        def fold_rows(m, at):
            cols = pl.ds(m * size, size)
            parts = []
            for base in (at, half + at):
                rows = pl.ds(base, step)
                pr, pi = patch_f[0, rows, :], patch_f[1, rows, :]
                qr, qi = probe[m, 0, rows, :], probe[m, 1, rows, :]
                parts.append((qr * pr - qi * pi, qr * pi + qi * pr))
            for c in range(2):
                rows = pl.ds(c * half + at, step)
                for t, value in enumerate((parts[0][c] + parts[1][c], parts[0][c] - parts[1][c])):
                    x_f[t, 0, rows, cols], x_f[t, 1, rows, cols] = split(value)

        def dft_rows(m, t):
            cols = pl.ds(m * size, size)
            high = x_f[t, 0, :, cols]
            u = dot(three_left(forward_t, t), jnp.concatenate([high, x_f[t, 1, :, cols], high], axis=0))
            rows = pl.ds(m * size + t * half, half)
            for v, value in enumerate((u[:, :half] + u[:, half:], u[:, :half] - u[:, half:])):
                high, low = split(value)
                for c in range(2):
                    lanes = pl.ds(c * half, half)
                    y_f[v, 0, rows, lanes] = high[c * half : (c + 1) * half]
                    y_f[v, 1, rows, lanes] = low[c * half : (c + 1) * half]

        def dft_cols(m, v):
            rows = pl.ds(m * size, size)
            high = y_f[v, 0, rows, :]
            z_f[v, rows, :] = dot(
                jnp.concatenate([high, y_f[v, 1, rows, :], high], axis=1), three_right(backward_t, v)
            )

        def scale(v, at):
            if v == 0 and at == 0:
                amp_copy(slot).wait()
            waves = [z_f[v, pl.ds(m * size + at, step), :] for m in range(modes)]
            total = jnp.zeros((step, half), F32)
            for wave in waves:
                total += wave[:, :half] * wave[:, :half] + wave[:, half:] * wave[:, half:]
            measured = amp[slot, pl.ds(at, step), pl.ds(v * half, half)]
            factor = measured * lax.rsqrt(jnp.maximum(total, FLOOR * FLOOR)) - 1.0
            factor = jnp.concatenate([factor, factor], axis=1)
            for m in range(modes):
                rows = pl.ds(m * size + at, step)
                g_s[v, 0, rows, :], g_s[v, 1, rows, :] = split(waves[m] * factor)

        pieces = [(take, at) for at in range(0, size, step)]
        for m in range(modes):
            pieces += [(fold_rows, m, at) for at in range(0, half, step)]
            pieces += [(dft_rows, m, t) for t in range(2)]
            pieces += [(dft_cols, m, v) for v in range(2)]
        pieces += [(scale, v, at) for v in range(2) for at in range(0, size, step)]
        return [functools.partial(*piece) for piece in pieces]

    def backward(slot):
        top, left = corner(slot)

        def dft_cols(m, v):
            rows = pl.ds(m * size, size)
            high = g_s[v, 0, rows, :]
            z_b[v, rows, :] = dot(
                jnp.concatenate([high, g_s[v, 1, rows, :], high], axis=1), three_right(forward_t, v)
            )

        def unfold_cols(m, t, at):
            rows = pl.ds(m * size + t * half + at, step)
            even, odd = z_b[0, rows, :], z_b[1, rows, :]
            for v, value in enumerate((even + odd, even - odd)):
                high, low = split(value)
                cols = pl.ds(m * size + v * half, half)
                for c in range(2):
                    spot = pl.ds(c * half + at, step)
                    x_b[t, 0, spot, cols] = high[:, c * half : (c + 1) * half]
                    x_b[t, 1, spot, cols] = low[:, c * half : (c + 1) * half]

        def dft_rows(m, t):
            cols = pl.ds(m * size, size)
            high = x_b[t, 0, :, cols]
            back[m, t] = dot(three_left(backward_t, t), jnp.concatenate([high, x_b[t, 1, :, cols], high], axis=0))

        def gradients(at):
            waves = []
            for m in range(modes):
                pair = []
                for c in range(2):
                    rows = pl.ds(c * half + at, step)
                    even, odd = back[m, 0, rows, :], back[m, 1, rows, :]
                    pair.append((even + odd, even - odd))
                waves.append(pair)
            for h in range(2):
                rows = pl.ds(h * half + at, step)
                pr, pi = patch_b[0, rows, :], patch_b[1, rows, :]
                grad_r = jnp.zeros((step, size), F32)
                grad_i = jnp.zeros((step, size), F32)
                for m in range(modes):
                    br, bi = waves[m][0][h], waves[m][1][h]
                    qr, qi = probe[m, 0, rows, :], probe[m, 1, rows, :]
                    grad_r += qr * br + qi * bi
                    grad_i += qr * bi - qi * br
                    probe_out[2 * m, rows, :] += pr * br + pi * bi
                    probe_out[2 * m + 1, rows, :] += pr * bi - pi * br
                spot = pl.ds(8 + h * half + at, step)
                template[0, spot, :] = grad_r
                template[1, spot, :] = grad_i

        def add(c):
            add_shifted(template, grid, (c,), (c,), top, left, size)

        pieces = []
        for m in range(modes):
            pieces += [(dft_cols, m, v) for v in range(2)]
        for m in range(modes):
            pieces += [(unfold_cols, m, t, at) for t in range(2) for at in range(0, half, step)]
            pieces += [(dft_rows, m, t) for t in range(2)]
        pieces += [(gradients, at) for at in range(0, half, step)]
        pieces += [(add, c) for c in range(2)]
        return [functools.partial(*piece) for piece in pieces]

    def hand_over():
        for at in range(0, size, step):
            for c in range(2):
                patch_b[c, pl.ds(at, step), :] = patch_f[c, pl.ds(at, step), :]

    @pl.when(count > 0)
    def _():
        weave(forward(chosen[0]), [])
        hand_over()

        def visit(index, _):
            weave(backward(chosen[index]), forward(chosen[index + 1]))
            hand_over()
            return 0

        lax.fori_loop(0, count - 1, visit, 0)
        weave(backward(chosen[count - 1]), [])

    if needs_rim:
        parts = [
            grid.at[:, pl.ds(0, tile_rows), pl.ds(0, tile_cols)],
            grid.at[:, pl.ds(0, tile_rows), pl.ds(tile_cols, size)],
            grid.at[:, pl.ds(tile_rows, size), pl.ds(0, tile_cols)],
            grid.at[:, pl.ds(tile_rows, size), pl.ds(tile_cols, size)],
        ]
    else:
        parts = [grid.at[:, :, pl.ds(0, tile_cols)]]
    stores = [pltpu.make_async_copy(part, out, out_sems.at[i]) for i, (part, out) in enumerate(zip(parts, outs))]
    for store in stores:
        store.start()
    for store in stores:
        store.wait()


def visit_slots(meta, probe, amplitudes, sources, init):
    size = probe.shape[2]
    modes = probe.shape[0]
    slots = amplitudes.shape[0]
    rows, cols = sources[0].shape[1:]
    tables = [jnp.asarray(item) for item in dft_tables(size)]
    vmem = pl.BlockSpec(memory_space=pltpu.VMEM)
    anywhere = pl.BlockSpec(memory_space=pl.ANY)
    needs_rim = bool(init)
    if needs_rim:
        shapes = [(2, rows, cols), (2, rows, size), (2, size, cols), (2, size, size)]
    else:
        shapes = [(2, rows + size, cols)]
    splits = np.cumsum([1, 1, 1, len(sources), 1, 1, len(init), len(shapes), 1])

    def kernel(*refs):
        meta, probe, amplitudes, sources, forward_t, backward_t, init, outs, probe_out = (
            refs[a:b] for a, b in zip([0, *splits[:-1]], splits)
        )
        scratch = refs[splits[-1] :]
        slots_kernel(
            needs_rim, meta[0], probe[0], amplitudes[0], sources, forward_t[0], backward_t[0], init, outs,
            probe_out[0], *scratch[:-3], scratch[-3:],
        )

    return pl.pallas_call(
        kernel,
        out_shape=[jax.ShapeDtypeStruct(shape, F32) for shape in shapes]
        + [jax.ShapeDtypeStruct((2 * modes + 1, size, size), F32)],
        in_specs=[pl.BlockSpec(memory_space=pltpu.SMEM), vmem] + [anywhere] * (1 + len(sources))
        + [vmem] * 2 + [anywhere] * len(init),
        out_specs=[anywhere] * len(shapes) + [vmem],
        scratch_shapes=[
            pltpu.VMEM((2, rows + size, cols + size), F32),
            pltpu.VMEM((2, rows + size, cols + size), F32),
            pltpu.VMEM(amplitudes.shape, F32),
            pltpu.SMEM((slots,), jnp.int32),
            pltpu.VMEM((2, size, size), F32),
            pltpu.VMEM((2, size, size), F32),
            pltpu.VMEM((2, 2, size, modes * size), BF16),
            pltpu.VMEM((2, 2, modes * size, size), BF16),
            pltpu.VMEM((2, modes * size, size), F32),
            pltpu.VMEM((2, 2, modes * size, size), BF16),
            pltpu.VMEM((2, 2, size, modes * size), BF16),
            pltpu.VMEM((2, modes * size, size), F32),
            pltpu.VMEM((modes, 2, size, size), F32),
            pltpu.VMEM((2, size + 16, size), F32),
            pltpu.SemaphoreType.DMA((7,)),
            pltpu.SemaphoreType.DMA((slots,)),
            pltpu.SemaphoreType.DMA((4,)),
        ],
        compiler_params=pltpu.CompilerParams(vmem_limit_bytes=32 * MIB),
        cost_estimate=pl.CostEstimate(flops=12_000_000_000, bytes_accessed=16_000_000, transcendentals=0),
        name="slots_beyond" if needs_rim else "slots_inside",
    )(meta, probe, amplitudes, *sources, *tables, *init)


def finish_kernel(own, right, lower, corner, inverse_light, tile, out):
    size = right.shape[2]
    step = pl.program_id(0)
    scale = inverse_light[...]
    spill = jnp.where(step < size // own.shape[1], 1.0, 0.0)
    for c in range(2):
        near = own[c, :, :size] + right[c] + spill * (lower[c, :, :size] + corner[c])
        far = own[c, :, size:] + spill * lower[c, :, size:]
        out[c, :, :size] = tile[c, :, :size] + near * scale[:, :size]
        out[c, :, size:] = tile[c, :, size:] + far * scale[:, size:]


def finish(own, right, lower, corner, inverse_light, tile):
    rows, cols = tile.shape[1:]
    size = right.shape[2]
    block = 128
    last = size // block - 1
    whole = pl.BlockSpec((2, block, cols), lambda i: (0, i, 0))
    return pl.pallas_call(
        finish_kernel,
        grid=(rows // block,),
        out_shape=jax.ShapeDtypeStruct(tile.shape, F32),
        in_specs=[
            whole,
            pl.BlockSpec((2, block, size), lambda i: (0, i, 0)),
            pl.BlockSpec((2, block, cols), lambda i: (0, jnp.minimum(i, last), 0)),
            pl.BlockSpec((2, block, size), lambda i: (0, jnp.minimum(i, last), 0)),
            pl.BlockSpec((block, cols), lambda i: (i, 0)),
            whole,
        ],
        out_specs=whole,
        cost_estimate=pl.CostEstimate(flops=3_000_000, bytes_accessed=12_000_000, transcendentals=0),
        name="finish",
    )(own, right, lower, corner, inverse_light, tile)


def from_behind(array, axis, by):
    count = lax.axis_size(axis)
    pairs = [(i, i + by) for i in range(count) if 0 <= i + by < count]
    return lax.ppermute(array, axis, pairs)


def exchange(array, axis, bit):
    count = lax.axis_size(axis)
    return lax.ppermute(array, axis, [(i, i ^ bit) for i in range(count)])


def together(*arrays):
    return lax.optimization_barrier(arrays)


def body(object_field, probe, amplitudes, positions, counts):
    modes, _, size, _ = probe.shape
    tile_rows, tile_cols = object_field.shape[1:]
    slots = amplitudes.shape[0]
    origin = jnp.stack([lax.axis_index("row") * tile_rows, lax.axis_index("col") * tile_cols]).astype(jnp.int32)

    def relative(table):
        return jnp.concatenate([table[:, : 2 * slots] - jnp.tile(origin, slots)[None], table[:, 2 * slots :]], axis=1)

    meta = jnp.concatenate([positions.reshape(1, 2 * slots), counts.reshape(1, 1)], axis=1)
    mine = relative(meta)

    right_up = from_behind(object_field[:, :size, :size], "col", -1)
    lower = from_behind(object_field[:, :size, :], "row", -1)
    amplitudes = arrange(mine, amplitudes)
    right_up, amplitudes, rest = together(right_up, amplitudes, object_field[:, size:, :size])
    corner = from_behind(right_up, "row", -1)
    right_down = from_behind(rest, "col", -1)
    init = visit_slots(mine, probe, amplitudes, [object_field, lower], [])
    right_up, right_down, corner, *init = together(right_up, right_down, corner, *init)
    own, right_spill, lower_spill, corner_spill, sums = visit_slots(
        mine, probe, amplitudes, [object_field, lower, right_up, right_down, corner], list(init)
    )
    corner_spill = from_behind(corner_spill, "row", 1)
    right_spill = from_behind(right_spill, "col", 1)
    lower_spill = from_behind(lower_spill, "row", 1)

    share = sums
    start = jnp.zeros((), jnp.int32)
    bits = [1 << k for k in range(lax.axis_size("row").bit_length() - 1)]
    inverse_light = None
    for bit in bits:
        half = share.shape[1] // 2
        upper = (lax.axis_index("row") // bit) % 2
        keep = lax.dynamic_slice_in_dim(share, upper * half, half, axis=1)
        send = lax.dynamic_slice_in_dim(share, (1 - upper) * half, half, axis=1)
        got = exchange(send, "row", bit)
        if bit == bits[-1]:
            meta, keep = together(meta, keep)
            table = jnp.concatenate([meta, from_behind(meta, "col", 1)], axis=0)
            table = jnp.concatenate([table, from_behind(table, "row", 1)], axis=0)
            inverse_light = light(relative(table), probe, (tile_rows, tile_cols))
            got, inverse_light = together(got, inverse_light)
        share = keep + got
        start = start + upper * half
    parts = lax.axis_size("col")
    rows = share.shape[1] // parts
    share = share.reshape(2 * modes + 1, parts, rows, size).transpose(1, 0, 2, 3)
    share = lax.all_to_all(share, "col", 0, 0, tiled=True).sum(axis=0)
    old = lax.dynamic_slice_in_dim(
        probe.reshape(2 * modes, size, size), start + lax.axis_index("col") * rows, rows, axis=1
    )
    new = old + share[: 2 * modes] / (share[2 * modes :] + 1.0)
    new = jnp.broadcast_to(new[None], (parts,) + new.shape)
    new = lax.all_to_all(new, "col", 0, 0, tiled=True)
    new = new.transpose(1, 0, 2, 3).reshape(2 * modes, parts * rows, size)
    new, corner_spill, right_spill, lower_spill = together(new, corner_spill, right_spill, lower_spill)
    corner_spill = from_behind(corner_spill, "col", 1)
    for bit in reversed(bits):
        upper = (lax.axis_index("row") // bit) % 2 == 1
        other = exchange(new, "row", bit)
        if bit == bits[-1]:
            new_object = finish(own, right_spill, lower_spill, corner_spill, inverse_light, object_field)
            other, new_object = together(other, new_object)
        new = jnp.concatenate([jnp.where(upper, other, new), jnp.where(upper, new, other)], axis=1)
    return (new_object, new.reshape(modes, 2, size, size))


def solution(mesh):
    in_specs = (
        P(None, "row", "col"),
        P(),
        P(("row", "col"), None, None),
        P(("row", "col"), None),
        P(("row", "col")),
    )
    out_specs = (P(None, "row", "col"), P())
    return jax.shard_map(body, mesh=mesh, in_specs=in_specs, out_specs=out_specs, check_vma=False)
```

```python
import functools
import math

import jax
import jax.numpy as jnp
import ml_dtypes
import numpy as np
from jax import lax
from jax.experimental import pallas as pl
from jax.experimental.pallas import tpu as pltpu
from jax.sharding import PartitionSpec as P

F32 = jnp.float32
BF16 = jnp.bfloat16
MIB = 1024 * 1024
FLOOR = 0.3


def split_np(table):
    high = table.astype(ml_dtypes.bfloat16)
    low = (table - high.astype(np.float64)).astype(ml_dtypes.bfloat16)
    return high, low


def dft_tables(length):
    half = length // 2
    q = np.arange(half)[:, None]
    n = np.arange(half)[None, :]
    forward = []
    for odd in range(2):
        phase = (n * (2 * q + odd)) % length
        angle = phase * (-2.0 * math.pi / length)
        re = np.cos(angle) / math.sqrt(length)
        im = np.sin(angle) / math.sqrt(length)
        forward.append(np.stack(split_np(np.block([[re, -im], [im, re]]))))
    forward = np.stack(forward)
    return forward, np.ascontiguousarray(forward.transpose(0, 1, 3, 2))


def order_tables(length):
    order = np.concatenate([np.arange(0, length, 2), np.arange(1, length, 2)])
    table = np.eye(length)[order]
    rows = np.concatenate([table] * 3, axis=1)
    return rows.astype(ml_dtypes.bfloat16), rows.T.astype(ml_dtypes.bfloat16)


def dot(a, b):
    return jnp.dot(a, b, preferred_element_type=F32)


def split(x):
    high = x.astype(BF16)
    return high, (x - high.astype(F32)).astype(BF16)


def roll_rows(x, shift):
    return pltpu.roll(x.reshape(x.shape[0] // 8, 8, x.shape[1]), shift, 1)


def split_three(x):
    high = x.astype(BF16)
    rest = x - high.astype(F32)
    middle = rest.astype(BF16)
    return high, middle, (rest - middle.astype(F32)).astype(BF16)


def add_shifted(template, grid, where_t, where_g, top, left, size):
    top_s = top & 7
    top_b = pl.multiple_of(top - top_s, 8)
    left_s = left & 127
    left_b = pl.multiple_of(left - left_s, 128)
    step = 24
    wrapped = lax.broadcasted_iota(jnp.int32, (step, 128), 1) < left_s
    wrapped_rows = lax.broadcasted_iota(jnp.int32, (step // 8, 8, 128), 1) < top_s
    zero = jnp.zeros((step, 128), F32)
    blocks = size // 128
    for at in range(0, size + 8, step):
        parts = []
        for j in range(blocks):
            x = roll_rows(template[where_t + (pl.ds(at, step + 8), pl.ds(128 * j, 128))], top_s)
            x = jnp.where(wrapped_rows, x[:-1], x[1:]).reshape(step, 128)
            parts.append(pltpu.roll(x, left_s, 1))
        for j in range(blocks + 1):
            before = parts[j - 1] if j > 0 else zero
            after = parts[j] if j < blocks else zero
            spot = where_g + (pl.ds(top_b + at, step), pl.ds(left_b + 128 * j, 128))
            grid[spot] += jnp.where(wrapped, before, after)


def take_shifted(field, where, top, left, at, step, size):
    top_s = top & 7
    top_b = pl.multiple_of(top - top_s, 8)
    left_s = left & 127
    left_b = pl.multiple_of(left - left_s, 128)
    back = (128 - left_s) & 127
    keep = lax.broadcasted_iota(jnp.int32, (step + 8, 128), 1) < 128 - left_s
    keep_rows = lax.broadcasted_iota(jnp.int32, (step // 8, 8, 128), 1) < 8 - top_s
    blocks = size // 128
    parts = [
        pltpu.roll(field[where + (pl.ds(top_b + at, step + 8), pl.ds(left_b + 128 * j, 128))], back, 1)
        for j in range(blocks + 1)
    ]
    pieces = []
    for j in range(blocks):
        x = roll_rows(jnp.where(keep, parts[j], parts[j + 1]), (8 - top_s) & 7)
        pieces.append(jnp.where(keep_rows, x[:-1], x[1:]).reshape(step, 128))
    return jnp.concatenate(pieces, axis=1)


def light_kernel(meta, probe, inverse_light, template, grid):
    size = probe.shape[2]
    tile_rows, tile_cols = inverse_light.shape
    template[0:8, :] = jnp.zeros((8, size), F32)
    template[8 + size :, :] = jnp.zeros((8, size), F32)
    for at in range(0, size, 32):
        rows = pl.ds(at, 32)
        total = jnp.zeros((32, size), F32)
        for m in range(probe.shape[0]):
            total += probe[m, 0, rows] * probe[m, 0, rows] + probe[m, 1, rows] * probe[m, 1, rows]
        template[pl.ds(8 + at, 32), :] = total

    @pl.loop(0, tile_rows // 32)
    def _(step):
        rows = pl.ds(pl.multiple_of(size + step * 32, 32), 32)
        grid[rows, size : size + tile_cols] = jnp.zeros((32, tile_cols), F32)

    slots = meta.shape[1] // 2
    for device in range(4):

        @pl.loop(0, meta[device, 2 * slots])
        def _(slot):
            top = meta[device, 2 * slot] + size
            left = meta[device, 2 * slot + 1] + size

            @pl.when((top > 0) & (left > 0))
            def _():
                add_shifted(template, grid, (), (), top, left, size)

    @pl.loop(0, tile_rows // 32)
    def _(step):
        rows = pl.ds(pl.multiple_of(size + step * 32, 32), 32)
        out_rows = pl.ds(pl.multiple_of(step * 32, 32), 32)
        inverse_light[out_rows, :] = 1.0 / (grid[rows, size : size + tile_cols] + 1.0)


def light(meta, probe, tile_shape):
    size = probe.shape[2]
    vmem = pl.BlockSpec(memory_space=pltpu.VMEM)
    return pl.pallas_call(
        light_kernel,
        out_shape=jax.ShapeDtypeStruct(tile_shape, F32),
        in_specs=[pl.BlockSpec(memory_space=pltpu.SMEM), vmem],
        out_specs=vmem,
        scratch_shapes=[
            pltpu.VMEM((size + 16, size), F32),
            pltpu.VMEM((tile_shape[0] + 2 * size, tile_shape[1] + 2 * size), F32),
        ],
        compiler_params=pltpu.CompilerParams(vmem_limit_bytes=8 * MIB),
        cost_estimate=pl.CostEstimate(flops=4_000_000_000, bytes_accessed=16_000_000, transcendentals=0),
        name="light",
    )(meta, probe)


def arrange_kernel(meta, amplitudes, order_rows, order_cols, out):
    @pl.loop(0, meta[0, 2 * amplitudes.shape[0]])
    def _(slot):
        x = dot(order_rows[...], jnp.concatenate(split_three(amplitudes[slot]), axis=0))
        out[slot] = dot(jnp.concatenate(split_three(x), axis=1), order_cols[...])


def arrange(meta, amplitudes):
    order_rows, order_cols = (jnp.asarray(table) for table in order_tables(amplitudes.shape[2]))
    vmem = pl.BlockSpec(memory_space=pltpu.VMEM)
    return pl.pallas_call(
        arrange_kernel,
        out_shape=jax.ShapeDtypeStruct(amplitudes.shape, F32),
        in_specs=[pl.BlockSpec(memory_space=pltpu.SMEM)] + [vmem] * 3,
        out_specs=vmem,
        compiler_params=pltpu.CompilerParams(vmem_limit_bytes=8 * MIB),
        cost_estimate=pl.CostEstimate(flops=2_000_000_000, bytes_accessed=8_000_000, transcendentals=0),
        name="arrange",
    )(meta, amplitudes, order_rows, order_cols)


def three_left(table, t):
    return jnp.concatenate([table[t, 0], table[t, 0], table[t, 1]], axis=1)


def three_right(table, v):
    return jnp.concatenate([table[v, 0], table[v, 0], table[v, 1]], axis=0)


def weave(first, second):
    total = max(len(first), len(second))
    done = [0, 0]
    for i in range(1, total + 1):
        for k, pieces in enumerate((first, second)):
            while done[k] * total < i * len(pieces):
                pieces[done[k]]()
                done[k] += 1


def slots_kernel(
    needs_rim, meta, probe, amplitudes, sources, forward_t, backward_t, init, outs, probe_out,
    ext, grid, chosen, patch_f, patch_b, x_f, y_f, z_f, g_s, x_b, z_b, back, template, sems,
):
    size = probe.shape[2]
    half = size // 2
    modes = probe.shape[0]
    slots = amplitudes.shape[0]
    tile_rows, tile_cols = (n - size for n in ext.shape[1:])
    step = 32
    load_sems, out_sems = sems

    regions = (
        (pl.ds(0, tile_rows), pl.ds(0, tile_cols)),
        (pl.ds(tile_rows, size), pl.ds(0, tile_cols)),
        (pl.ds(0, size), pl.ds(tile_cols, size)),
        (pl.ds(size, tile_rows - size), pl.ds(tile_cols, size)),
        (pl.ds(tile_rows, size), pl.ds(tile_cols, size)),
    )
    loads = [
        pltpu.make_async_copy(source, ext.at[:, rows, cols], load_sems.at[i])
        for i, (source, (rows, cols)) in enumerate(zip(sources, regions))
    ]
    if needs_rim:
        loads.append(pltpu.make_async_copy(init[0], grid.at[:, :, pl.ds(0, tile_cols)], load_sems.at[5]))
        loads.append(pltpu.make_async_copy(init[1], probe_out, load_sems.at[6]))
    for load in loads:
        load.start()

    def choose(slot, found):
        beyond = meta[0, 2 * slot + 1] + size > tile_cols
        wanted = beyond if needs_rim else jnp.logical_not(beyond)

        @pl.when(wanted)
        def _():
            chosen[found] = slot

        return found + wanted.astype(jnp.int32)

    count = lax.fori_loop(0, meta[0, 2 * slots], choose, jnp.zeros((), jnp.int32))

    @pl.loop(0, (tile_rows + size) // step)
    def _(at):
        rows = pl.ds(pl.multiple_of(at * step, step), step)
        for c in range(2):
            if needs_rim:
                grid[c, rows, tile_cols:] = jnp.zeros((step, size), F32)
            else:
                grid[c, rows, :] = jnp.zeros((step, tile_cols + size), F32)

    if not needs_rim:

        @pl.loop(0, size // step)
        def _(at):
            rows = pl.ds(pl.multiple_of(at * step, step), step)
            for c in range(2 * modes + 1):
                probe_out[c, rows, :] = jnp.zeros((step, size), F32)

    for c in range(2):
        template[c, 0:8, :] = jnp.zeros((8, size), F32)
        template[c, 8 + size :, :] = jnp.zeros((8, size), F32)
    for load in loads:
        load.wait()

    def corner(slot):
        return meta[0, 2 * slot], meta[0, 2 * slot + 1]

    def forward(slot):
        top, left = corner(slot)

        def take(at):
            rows = pl.ds(at, step)
            total = jnp.zeros((step, size), F32)
            for c in range(2):
                piece = take_shifted(ext, (c,), top, left, at, step, size)
                patch_f[c, rows, :] = piece
                total += piece * piece
            probe_out[2 * modes, rows, :] += total

        def fold_rows(m, at):
            cols = pl.ds(m * size, size)
            parts = []
            for base in (at, half + at):
                rows = pl.ds(base, step)
                pr, pi = patch_f[0, rows, :], patch_f[1, rows, :]
                qr, qi = probe[m, 0, rows, :], probe[m, 1, rows, :]
                parts.append((qr * pr - qi * pi, qr * pi + qi * pr))
            for c in range(2):
                rows = pl.ds(c * half + at, step)
                for t, value in enumerate((parts[0][c] + parts[1][c], parts[0][c] - parts[1][c])):
                    x_f[t, 0, rows, cols], x_f[t, 1, rows, cols] = split(value)

        def dft_rows(m, t):
            cols = pl.ds(m * size, size)
            high = x_f[t, 0, :, cols]
            u = dot(three_left(forward_t, t), jnp.concatenate([high, x_f[t, 1, :, cols], high], axis=0))
            rows = pl.ds(m * size + t * half, half)
            for v, value in enumerate((u[:, :half] + u[:, half:], u[:, :half] - u[:, half:])):
                high, low = split(value)
                for c in range(2):
                    lanes = pl.ds(c * half, half)
                    y_f[v, 0, rows, lanes] = high[c * half : (c + 1) * half]
                    y_f[v, 1, rows, lanes] = low[c * half : (c + 1) * half]

        def dft_cols(m, v):
            rows = pl.ds(m * size, size)
            high = y_f[v, 0, rows, :]
            z_f[v, rows, :] = dot(
                jnp.concatenate([high, y_f[v, 1, rows, :], high], axis=1), three_right(backward_t, v)
            )

        def scale(v, at):
            waves = [z_f[v, pl.ds(m * size + at, step), :] for m in range(modes)]
            total = jnp.zeros((step, half), F32)
            for wave in waves:
                total += wave[:, :half] * wave[:, :half] + wave[:, half:] * wave[:, half:]
            measured = amplitudes[slot, pl.ds(at, step), pl.ds(v * half, half)]
            factor = measured * lax.rsqrt(jnp.maximum(total, FLOOR * FLOOR)) - 1.0
            factor = jnp.concatenate([factor, factor], axis=1)
            for m in range(modes):
                rows = pl.ds(m * size + at, step)
                g_s[v, 0, rows, :], g_s[v, 1, rows, :] = split(waves[m] * factor)

        pieces = [(take, at) for at in range(0, size, step)]
        for m in range(modes):
            pieces += [(fold_rows, m, at) for at in range(0, half, step)]
            pieces += [(dft_rows, m, t) for t in range(2)]
            pieces += [(dft_cols, m, v) for v in range(2)]
        pieces += [(scale, v, at) for v in range(2) for at in range(0, size, step)]
        return [functools.partial(*piece) for piece in pieces]

    def backward(slot):
        top, left = corner(slot)

        def dft_cols(m, v):
            rows = pl.ds(m * size, size)
            high = g_s[v, 0, rows, :]
            z_b[v, rows, :] = dot(
                jnp.concatenate([high, g_s[v, 1, rows, :], high], axis=1), three_right(forward_t, v)
            )

        def unfold_cols(m, t, at):
            rows = pl.ds(m * size + t * half + at, step)
            even, odd = z_b[0, rows, :], z_b[1, rows, :]
            for v, value in enumerate((even + odd, even - odd)):
                high, low = split(value)
                cols = pl.ds(m * size + v * half, half)
                for c in range(2):
                    spot = pl.ds(c * half + at, step)
                    x_b[t, 0, spot, cols] = high[:, c * half : (c + 1) * half]
                    x_b[t, 1, spot, cols] = low[:, c * half : (c + 1) * half]

        def dft_rows(m, t):
            cols = pl.ds(m * size, size)
            high = x_b[t, 0, :, cols]
            back[m, t] = dot(three_left(backward_t, t), jnp.concatenate([high, x_b[t, 1, :, cols], high], axis=0))

        def gradients(at):
            waves = []
            for m in range(modes):
                pair = []
                for c in range(2):
                    rows = pl.ds(c * half + at, step)
                    even, odd = back[m, 0, rows, :], back[m, 1, rows, :]
                    pair.append((even + odd, even - odd))
                waves.append(pair)
            for h in range(2):
                rows = pl.ds(h * half + at, step)
                pr, pi = patch_b[0, rows, :], patch_b[1, rows, :]
                grad_r = jnp.zeros((step, size), F32)
                grad_i = jnp.zeros((step, size), F32)
                for m in range(modes):
                    br, bi = waves[m][0][h], waves[m][1][h]
                    qr, qi = probe[m, 0, rows, :], probe[m, 1, rows, :]
                    grad_r += qr * br + qi * bi
                    grad_i += qr * bi - qi * br
                    probe_out[2 * m, rows, :] += pr * br + pi * bi
                    probe_out[2 * m + 1, rows, :] += pr * bi - pi * br
                spot = pl.ds(8 + h * half + at, step)
                template[0, spot, :] = grad_r
                template[1, spot, :] = grad_i

        def add(c):
            add_shifted(template, grid, (c,), (c,), top, left, size)

        pieces = []
        for m in range(modes):
            pieces += [(dft_cols, m, v) for v in range(2)]
        for m in range(modes):
            pieces += [(unfold_cols, m, t, at) for t in range(2) for at in range(0, half, step)]
            pieces += [(dft_rows, m, t) for t in range(2)]
        pieces += [(gradients, at) for at in range(0, half, step)]
        pieces += [(add, c) for c in range(2)]
        return [functools.partial(*piece) for piece in pieces]

    def hand_over():
        for at in range(0, size, step):
            for c in range(2):
                patch_b[c, pl.ds(at, step), :] = patch_f[c, pl.ds(at, step), :]

    @pl.when(count > 0)
    def _():
        weave(forward(chosen[0]), [])
        hand_over()

        def visit(index, _):
            weave(backward(chosen[index]), forward(chosen[index + 1]))
            hand_over()
            return 0

        lax.fori_loop(0, count - 1, visit, 0)
        weave(backward(chosen[count - 1]), [])

    if needs_rim:
        parts = [
            grid.at[:, pl.ds(0, tile_rows), pl.ds(0, tile_cols)],
            grid.at[:, :, pl.ds(tile_cols, size)],
            grid.at[:, pl.ds(tile_rows, size), pl.ds(0, tile_cols)],
            probe_out.at[:, pl.ds(pl.multiple_of(meta[0, 2 * slots + 1] * half, half), half)],
        ]
    else:
        parts = [grid.at[:, :, pl.ds(0, tile_cols)]]
    stores = [pltpu.make_async_copy(part, out, out_sems.at[i]) for i, (part, out) in enumerate(zip(parts, outs))]
    for store in stores:
        store.start()
    for store in stores:
        store.wait()


def visit_slots(meta, probe, amplitudes, sources, init):
    size = probe.shape[2]
    modes = probe.shape[0]
    slots = amplitudes.shape[0]
    rows, cols = sources[0].shape[1:]
    tables = [jnp.asarray(item) for item in dft_tables(size)]
    vmem = pl.BlockSpec(memory_space=pltpu.VMEM)
    anywhere = pl.BlockSpec(memory_space=pl.ANY)
    needs_rim = bool(init)
    if needs_rim:
        shapes = [(2, rows, cols), (2, rows + size, size), (2, size, cols), (2 * modes + 1, size // 2, size)]
    else:
        shapes = [(2, rows + size, cols)]
    splits = np.cumsum([1, 1, 1, len(sources), 1, 1, len(init), len(shapes), 1])

    def kernel(*refs):
        meta, probe, amplitudes, sources, forward_t, backward_t, init, outs, probe_out = (
            refs[a:b] for a, b in zip([0, *splits[:-1]], splits)
        )
        scratch = refs[splits[-1] :]
        slots_kernel(
            needs_rim, meta[0], probe[0], amplitudes[0], sources, forward_t[0], backward_t[0], init, outs,
            probe_out[0], *scratch[:-2], scratch[-2:],
        )

    return pl.pallas_call(
        kernel,
        out_shape=[jax.ShapeDtypeStruct(shape, F32) for shape in shapes]
        + [jax.ShapeDtypeStruct((2 * modes + 1, size, size), F32)],
        in_specs=[pl.BlockSpec(memory_space=pltpu.SMEM), vmem, vmem] + [anywhere] * len(sources)
        + [vmem] * 2 + [anywhere] * len(init),
        out_specs=[anywhere] * len(shapes) + [vmem],
        scratch_shapes=[
            pltpu.VMEM((2, rows + size, cols + size), F32),
            pltpu.VMEM((2, rows + size, cols + size), F32),
            pltpu.SMEM((slots,), jnp.int32),
            pltpu.VMEM((2, size, size), F32),
            pltpu.VMEM((2, size, size), F32),
            pltpu.VMEM((2, 2, size, modes * size), BF16),
            pltpu.VMEM((2, 2, modes * size, size), BF16),
            pltpu.VMEM((2, modes * size, size), F32),
            pltpu.VMEM((2, 2, modes * size, size), BF16),
            pltpu.VMEM((2, 2, size, modes * size), BF16),
            pltpu.VMEM((2, modes * size, size), F32),
            pltpu.VMEM((modes, 2, size, size), F32),
            pltpu.VMEM((2, size + 16, size), F32),
            pltpu.SemaphoreType.DMA((7,)),
            pltpu.SemaphoreType.DMA((4,)),
        ],
        compiler_params=pltpu.CompilerParams(vmem_limit_bytes=28 * MIB),
        cost_estimate=pl.CostEstimate(flops=12_000_000_000, bytes_accessed=16_000_000, transcendentals=0),
        name="slots_beyond" if needs_rim else "slots_inside",
    )(meta, probe, amplitudes, *sources, *tables, *init)


def finish_kernel(own, right, lower, corner, inverse_light, tile, out):
    size = right.shape[2]
    step = pl.program_id(0)
    scale = inverse_light[...]
    spill = jnp.where(step < size // own.shape[1], 1.0, 0.0)
    for c in range(2):
        near = own[c, :, :size] + right[c] + spill * (lower[c, :, :size] + corner[c])
        far = own[c, :, size:] + spill * lower[c, :, size:]
        out[c, :, :size] = tile[c, :, :size] + near * scale[:, :size]
        out[c, :, size:] = tile[c, :, size:] + far * scale[:, size:]


def finish(own, right, lower, corner, inverse_light, tile):
    rows, cols = tile.shape[1:]
    size = right.shape[2]
    block = 128
    last = size // block - 1
    whole = pl.BlockSpec((2, block, cols), lambda i: (0, i, 0))
    return pl.pallas_call(
        finish_kernel,
        grid=(rows // block,),
        out_shape=jax.ShapeDtypeStruct(tile.shape, F32),
        in_specs=[
            whole,
            pl.BlockSpec((2, block, size), lambda i: (0, i, 0)),
            pl.BlockSpec((2, block, cols), lambda i: (0, jnp.minimum(i, last), 0)),
            pl.BlockSpec((2, block, size), lambda i: (0, jnp.minimum(i, last), 0)),
            pl.BlockSpec((block, cols), lambda i: (i, 0)),
            whole,
        ],
        out_specs=whole,
        compiler_params=pltpu.CompilerParams(vmem_limit_bytes=8 * MIB),
        cost_estimate=pl.CostEstimate(flops=3_000_000, bytes_accessed=12_000_000, transcendentals=0),
        name="finish",
    )(own, right, lower, corner, inverse_light, tile)


def from_behind(array, axis, by):
    count = lax.axis_size(axis)
    pairs = [(i, i + by) for i in range(count) if 0 <= i + by < count]
    return lax.ppermute(array, axis, pairs)


def exchange(array, axis, bit):
    count = lax.axis_size(axis)
    return lax.ppermute(array, axis, [(i, i ^ bit) for i in range(count)])


def together(*arrays):
    return lax.optimization_barrier(arrays)


def cut(tile, size):
    rows, cols = tile.shape[1:]
    regions = ((0, size, size), (0, size, cols), (size, rows - size, size))

    def kernel(tile, *refs):
        sems = refs[-1]
        copies = [
            pltpu.make_async_copy(tile.at[:, pl.ds(at, height), pl.ds(0, width)], out, sems.at[i])
            for i, ((at, height, width), out) in enumerate(zip(regions, refs[:-1]))
        ]
        for copy in copies:
            copy.start()
        for copy in copies:
            copy.wait()

    anywhere = pl.BlockSpec(memory_space=pl.ANY)
    return pl.pallas_call(
        kernel,
        out_shape=[jax.ShapeDtypeStruct((2, height, width), F32) for _, height, width in regions],
        in_specs=[anywhere],
        out_specs=[anywhere] * len(regions),
        scratch_shapes=[pltpu.SemaphoreType.DMA((len(regions),))],
        compiler_params=pltpu.CompilerParams(vmem_limit_bytes=MIB),
        cost_estimate=pl.CostEstimate(flops=0, bytes_accessed=4_000_000, transcendentals=0),
        name="cut",
    )(tile)


def join(upper, mine, other):
    half = mine.shape[1]

    def kernel(upper, mine, other, out, sems):
        copies = [
            pltpu.make_async_copy(source, out.at[:, pl.ds(pl.multiple_of(at * half, half), half)], sems.at[i])
            for i, (source, at) in enumerate(((mine, upper[0]), (other, 1 - upper[0])))
        ]
        for copy in copies:
            copy.start()
        for copy in copies:
            copy.wait()

    anywhere = pl.BlockSpec(memory_space=pl.ANY)
    return pl.pallas_call(
        kernel,
        out_shape=jax.ShapeDtypeStruct((mine.shape[0], 2 * half) + mine.shape[2:], F32),
        in_specs=[pl.BlockSpec(memory_space=pltpu.SMEM), anywhere, anywhere],
        out_specs=anywhere,
        scratch_shapes=[pltpu.SemaphoreType.DMA((2,))],
        compiler_params=pltpu.CompilerParams(vmem_limit_bytes=MIB),
        cost_estimate=pl.CostEstimate(flops=0, bytes_accessed=2_000_000, transcendentals=0),
        name="join",
    )(upper.reshape(1), mine, other)


def body(object_field, probe, amplitudes, positions, counts):
    modes, _, size, _ = probe.shape
    tile_rows, tile_cols = object_field.shape[1:]
    slots = amplitudes.shape[0]
    origin = jnp.stack([lax.axis_index("row") * tile_rows, lax.axis_index("col") * tile_cols]).astype(jnp.int32)
    bits = [1 << k for k in range(lax.axis_size("row").bit_length() - 1)]
    uppers = [(lax.axis_index("row") & bit) // bit for bit in bits]

    def relative(table):
        return jnp.concatenate([table[:, : 2 * slots] - jnp.tile(origin, slots)[None], table[:, 2 * slots :]], axis=1)

    right_up, lower, rest = cut(object_field, size)
    right_up = from_behind(right_up, "col", -1)
    lower = from_behind(lower, "row", -1)

    meta = jnp.concatenate([positions.reshape(1, 2 * slots), counts.reshape(1, 1)], axis=1)
    mine = jnp.concatenate([relative(meta), (1 - uppers[0]).astype(jnp.int32).reshape(1, 1)], axis=1)
    amplitudes = arrange(mine, amplitudes)
    amplitudes, rest = together(amplitudes, rest)
    right_down = from_behind(rest, "col", -1)
    table = jnp.concatenate([meta, from_behind(meta, "col", 1)], axis=0)
    table = relative(jnp.concatenate([table, from_behind(table, "row", 1)], axis=0))
    right_up, amplitudes, lower, table = together(right_up, amplitudes, lower, table)
    corner = from_behind(right_up, "row", -1)
    init = visit_slots(mine, probe, amplitudes, [object_field, lower], [])
    right_up, right_down, corner, *init = together(right_up, right_down, corner, *init)
    own, right_spill, lower_spill, send, share = visit_slots(
        mine, probe, amplitudes, [object_field, lower, right_up, right_down, corner], list(init)
    )

    start = jnp.zeros((), jnp.int32)
    got = None
    for bit, upper in zip(bits, uppers):
        half = share.shape[1] // 2
        if got is not None:
            send = lax.dynamic_slice_in_dim(share, (1 - upper) * half, half, axis=1)
        got = exchange(send, "row", bit)
        if bit == bits[0]:
            right_spill = from_behind(right_spill, "col", 1)
            lower_spill = from_behind(lower_spill, "row", 1)
        if bit == bits[-1]:
            table, send = together(table, send)
            inverse_light = light(table, probe, (tile_rows, tile_cols))
            got, inverse_light = together(got, inverse_light)
        share = lax.dynamic_slice_in_dim(share, upper * half, half, axis=1) + got
        start = start + upper * half
    parts = lax.axis_size("col")
    rows = share.shape[1] // parts
    share, right_spill, lower_spill = together(share, right_spill, lower_spill)
    corner_spill = from_behind(right_spill[:, tile_rows:], "row", 1)
    share = share.reshape(2 * modes + 1, parts, rows, size).transpose(1, 0, 2, 3)
    share = lax.all_to_all(share, "col", 0, 0, tiled=True).sum(axis=0)
    old = lax.dynamic_slice_in_dim(
        probe.reshape(2 * modes, size, size), start + lax.axis_index("col") * rows, rows, axis=1
    )
    new = old + share[: 2 * modes] / (share[2 * modes :] + 1.0)
    new = jnp.broadcast_to(new[None], (parts,) + new.shape)
    new = lax.all_to_all(new, "col", 0, 0, tiled=True)
    new = new.transpose(1, 0, 2, 3).reshape(2 * modes, parts * rows, size)
    new, corner_spill = together(new, corner_spill)
    for bit, upper in reversed(list(zip(bits, uppers))):
        other = exchange(new, "row", bit)
        if bit == bits[-1]:
            new_object = finish(own, right_spill, lower_spill, corner_spill, inverse_light, object_field)
            other, new_object = together(other, new_object)
        new = join(upper, new, other)
    return (new_object, new.reshape(modes, 2, size, size))


def solution(mesh):
    in_specs = (
        P(None, "row", "col"),
        P(),
        P(("row", "col"), None, None),
        P(("row", "col"), None),
        P(("row", "col")),
    )
    out_specs = (P(None, "row", "col"), P())
    return jax.shard_map(body, mesh=mesh, in_specs=in_specs, out_specs=out_specs, check_vma=False)
```

```python
import functools
import math

import jax
import jax.numpy as jnp
import ml_dtypes
import numpy as np
from jax import lax
from jax.experimental import pallas as pl
from jax.experimental.pallas import tpu as pltpu
from jax.sharding import PartitionSpec as P

F32 = jnp.float32
BF16 = jnp.bfloat16
MIB = 1024 * 1024
LONG = pl.CostEstimate(flops=30_000_000_000, bytes_accessed=4_000_000, transcendentals=0)
SHORT = pl.CostEstimate(flops=0, bytes_accessed=1_000_000, transcendentals=0)
FLOOR = 0.3


def split_np(table):
    high = table.astype(ml_dtypes.bfloat16)
    low = (table - high.astype(np.float64)).astype(ml_dtypes.bfloat16)
    return high, low


def dft_tables(length):
    half = length // 2
    q = np.arange(half)[:, None]
    n = np.arange(half)[None, :]
    forward = []
    for odd in range(2):
        phase = (n * (2 * q + odd)) % length
        angle = phase * (-2.0 * math.pi / length)
        re = np.cos(angle) / math.sqrt(length)
        im = np.sin(angle) / math.sqrt(length)
        forward.append(np.stack(split_np(np.block([[re, -im], [im, re]]))))
    forward = np.stack(forward)
    return forward, np.ascontiguousarray(forward.transpose(0, 1, 3, 2))


def in_hbm(array):
    return pltpu.with_memory_space_constraint(array, pltpu.HBM)


def dot(a, b):
    return jnp.dot(a, b, preferred_element_type=F32)


def split(x):
    high = x.astype(BF16)
    return high, (x - high.astype(F32)).astype(BF16)


def roll_rows(x, shift):
    return pltpu.roll(x.reshape(x.shape[0] // 8, 8, x.shape[1]), shift, 1)


def roll_rows(x, shift):
    return pltpu.roll(x.reshape(x.shape[0] // 8, 8, x.shape[1]), shift, 1)


def roll_rows(x, shift):
    return pltpu.roll(x.reshape(x.shape[0] // 8, 8, x.shape[1]), shift, 1)


def roll_rows(x, shift):
    return pltpu.roll(x.reshape(x.shape[0] // 8, 8, x.shape[1]), shift, 1)


def split_three(x):
    high = x.astype(BF16)
    rest = x - high.astype(F32)
    middle = rest.astype(BF16)
    return high, middle, (rest - middle.astype(F32)).astype(BF16)


def add_shifted(template, grid, where_t, where_g, top, left, size):
    top_s = top & 7
    top_b = pl.multiple_of(top - top_s, 8)
    left_s = left & 127
    left_b = pl.multiple_of(left - left_s, 128)
    step = 24
    wrapped = lax.broadcasted_iota(jnp.int32, (step, 128), 1) < left_s
    wrapped_rows = lax.broadcasted_iota(jnp.int32, (step // 8, 8, 128), 1) < top_s
    zero = jnp.zeros((step, 128), F32)
    blocks = size // 128
    for at in range(0, size + 8, step):
        parts = []
        for j in range(blocks):
            x = roll_rows(template[where_t + (pl.ds(at, step + 8), pl.ds(128 * j, 128))], top_s)
            x = jnp.where(wrapped_rows, x[:-1], x[1:]).reshape(step, 128)
            parts.append(pltpu.roll(x, left_s, 1))
        for j in range(blocks + 1):
            before = parts[j - 1] if j > 0 else zero
            after = parts[j] if j < blocks else zero
            spot = where_g + (pl.ds(top_b + at, step), pl.ds(left_b + 128 * j, 128))
            grid[spot] += jnp.where(wrapped, before, after)


def take_shifted(field, where, top, left, at, step, size):
    top_s = top & 7
    top_b = pl.multiple_of(top - top_s, 8)
    left_s = left & 127
    left_b = pl.multiple_of(left - left_s, 128)
    back = (128 - left_s) & 127
    keep = lax.broadcasted_iota(jnp.int32, (step + 8, 128), 1) < 128 - left_s
    keep_rows = lax.broadcasted_iota(jnp.int32, (step // 8, 8, 128), 1) < 8 - top_s
    blocks = size // 128
    parts = [
        pltpu.roll(field[where + (pl.ds(top_b + at, step + 8), pl.ds(left_b + 128 * j, 128))], back, 1)
        for j in range(blocks + 1)
    ]
    pieces = []
    for j in range(blocks):
        x = roll_rows(jnp.where(keep, parts[j], parts[j + 1]), (8 - top_s) & 7)
        pieces.append(jnp.where(keep_rows, x[:-1], x[1:]).reshape(step, 128))
    return jnp.concatenate(pieces, axis=1)


def light_kernel(meta, probe, inverse_light, template, grid):
    size = probe.shape[2]
    tile_rows, tile_cols = inverse_light.shape
    template[0:8, :] = jnp.zeros((8, size), F32)
    template[8 + size :, :] = jnp.zeros((8, size), F32)
    for at in range(0, size, 32):
        rows = pl.ds(at, 32)
        total = jnp.zeros((32, size), F32)
        for m in range(probe.shape[0]):
            total += probe[m, 0, rows] * probe[m, 0, rows] + probe[m, 1, rows] * probe[m, 1, rows]
        template[pl.ds(8 + at, 32), :] = total

    @pl.loop(0, tile_rows // 32)
    def _(step):
        rows = pl.ds(pl.multiple_of(size + step * 32, 32), 32)
        grid[rows, size : size + tile_cols] = jnp.zeros((32, tile_cols), F32)

    slots = meta.shape[1] // 2
    for device in range(4):

        @pl.loop(0, meta[device, 2 * slots])
        def _(slot):
            top = meta[device, 2 * slot] + size
            left = meta[device, 2 * slot + 1] + size

            @pl.when((top > 0) & (left > 0))
            def _():
                add_shifted(template, grid, (), (), top, left, size)

    @pl.loop(0, tile_rows // 32)
    def _(step):
        rows = pl.ds(pl.multiple_of(size + step * 32, 32), 32)
        out_rows = pl.ds(pl.multiple_of(step * 32, 32), 32)
        inverse_light[out_rows, :] = 1.0 / (grid[rows, size : size + tile_cols] + 1.0)


def light(meta, probe, tile_shape):
    size = probe.shape[2]
    vmem = pl.BlockSpec(memory_space=pltpu.VMEM)
    return pl.pallas_call(
        light_kernel,
        out_shape=jax.ShapeDtypeStruct(tile_shape, F32),
        in_specs=[pl.BlockSpec(memory_space=pltpu.SMEM), vmem],
        out_specs=vmem,
        scratch_shapes=[
            pltpu.VMEM((size + 16, size), F32),
            pltpu.VMEM((tile_shape[0] + 2 * size, tile_shape[1] + 2 * size), F32),
        ],
        compiler_params=pltpu.CompilerParams(vmem_limit_bytes=8 * MIB),
        cost_estimate=pl.CostEstimate(flops=4_000_000_000, bytes_accessed=1_000_000, transcendentals=0),
        name="light",
    )(meta, probe)


def arrange_kernel(meta, amplitudes, out, given, moved, in_sems, out_sems):
    slots, size, _ = amplitudes.shape
    count = meta[0, 2 * slots]

    def load(slot):
        return pltpu.make_async_copy(amplitudes.at[slot], given.at[slot], in_sems.at[slot])

    def store(slot):
        return pltpu.make_async_copy(moved.at[slot], out.at[slot], out_sems.at[slot])

    @pl.loop(0, count)
    def _(slot):
        load(slot).start()

    first = lax.broadcasted_iota(jnp.int32, (size, size), 0)
    second = lax.broadcasted_iota(jnp.int32, (size, size), 1)
    half = size // 2

    def source(index):
        return jnp.where(index < half, 2 * index, 2 * index - (size - 1))

    rows = (source(first) == second).astype(F32).astype(BF16)
    cols = (source(second) == first).astype(F32).astype(BF16)
    rows = jnp.concatenate([rows, rows], axis=1)
    cols = jnp.concatenate([cols, cols], axis=0)

    @pl.loop(0, count)
    def _(slot):
        load(slot).wait()
        x = dot(rows, jnp.concatenate(split(given[slot]), axis=0))
        moved[slot] = dot(jnp.concatenate(split(x), axis=1), cols)
        store(slot).start()

    @pl.loop(0, count)
    def _(slot):
        store(slot).wait()


def arrange(meta, amplitudes):
    slots = amplitudes.shape[0]
    hbm = pl.BlockSpec(memory_space=pltpu.HBM)
    return pl.pallas_call(
        arrange_kernel,
        out_shape=pltpu.HBM(amplitudes.shape, F32),
        in_specs=[pl.BlockSpec(memory_space=pltpu.SMEM), hbm],
        out_specs=hbm,
        scratch_shapes=[
            pltpu.VMEM(amplitudes.shape, F32),
            pltpu.VMEM(amplitudes.shape, F32),
            pltpu.SemaphoreType.DMA((slots,)),
            pltpu.SemaphoreType.DMA((slots,)),
        ],
        compiler_params=pltpu.CompilerParams(vmem_limit_bytes=8 * MIB),
        cost_estimate=LONG,
        name="arrange",
    )(meta, in_hbm(amplitudes))


def three_left(table, t):
    return jnp.concatenate([table[t, 0], table[t, 0], table[t, 1]], axis=1)


def three_right(table, v):
    return jnp.concatenate([table[v, 0], table[v, 0], table[v, 1]], axis=0)


def weave(first, second):
    total = max(len(first), len(second))
    done = [0, 0]
    for i in range(1, total + 1):
        for k, pieces in enumerate((first, second)):
            while done[k] * total < i * len(pieces):
                pieces[done[k]]()
                done[k] += 1


def slots_kernel(
    needs_rim, meta, probe, amplitudes, sources, forward_h, backward_h, init, note, outs, probe_out,
    ext, grid, amp, forward_t, backward_t, chosen, patch_f, patch_b, x_f, y_f, z_f, g_s, x_b, z_b, back, template, sums, sems,
):
    size = probe.shape[2]
    half = size // 2
    modes = probe.shape[0]
    slots = amplitudes.shape[0]
    tile_rows, tile_cols = (n - size for n in ext.shape[1:])
    step = 32
    fine = 16
    load_sems, amp_sems, out_sems = sems
    sums_out = probe_out
    if not needs_rim:
        probe_out = sums

    regions = (
        (pl.ds(0, tile_rows), pl.ds(0, tile_cols)),
        (pl.ds(tile_rows, size), pl.ds(0, tile_cols)),
        (pl.ds(0, size), pl.ds(tile_cols, size)),
        (pl.ds(size, tile_rows - size), pl.ds(tile_cols, size)),
        (pl.ds(tile_rows, size), pl.ds(tile_cols, size)),
    )
    loads = [
        pltpu.make_async_copy(source, ext.at[:, rows, cols], load_sems.at[i])
        for i, (source, (rows, cols)) in enumerate(zip(sources, regions))
    ]
    loads.append(pltpu.make_async_copy(forward_h, forward_t, load_sems.at[7]))
    loads.append(pltpu.make_async_copy(backward_h, backward_t, load_sems.at[8]))
    if needs_rim:
        loads.append(pltpu.make_async_copy(init[0], grid.at[:, :, pl.ds(0, tile_cols)], load_sems.at[5]))
        loads.append(pltpu.make_async_copy(init[1], probe_out, load_sems.at[6]))
    for load in loads:
        load.start()

    def amp_copy(slot):
        return pltpu.make_async_copy(amplitudes.at[slot], amp.at[slot], amp_sems.at[slot])

    def choose(slot, found):
        beyond = meta[0, 2 * slot + 1] + size > tile_cols
        wanted = beyond if needs_rim else jnp.logical_not(beyond)

        @pl.when(wanted)
        def _():
            chosen[found] = slot
            amp_copy(slot).start()

        return found + wanted.astype(jnp.int32)

    count = lax.fori_loop(0, meta[0, 2 * slots], choose, jnp.zeros((), jnp.int32))

    @pl.loop(0, (tile_rows + size) // step)
    def _(at):
        rows = pl.ds(pl.multiple_of(at * step, step), step)
        for c in range(2):
            if needs_rim:
                grid[c, rows, tile_cols:] = jnp.zeros((step, size), F32)
            else:
                grid[c, rows, :] = jnp.zeros((step, tile_cols + size), F32)

    if not needs_rim:

        @pl.loop(0, size // step)
        def _(at):
            rows = pl.ds(pl.multiple_of(at * step, step), step)
            for c in range(2 * modes + 1):
                probe_out[c, rows, :] = jnp.zeros((step, size), F32)

    for c in range(2):
        template[c, 0:8, :] = jnp.zeros((8, size), F32)
        template[c, 8 + size :, :] = jnp.zeros((8, size), F32)
    for load in loads:
        load.wait()

    def corner(slot):
        return meta[0, 2 * slot], meta[0, 2 * slot + 1]

    def forward(slot):
        top, left = corner(slot)

        def take(at):
            rows = pl.ds(at, step)
            total = jnp.zeros((step, size), F32)
            for c in range(2):
                piece = take_shifted(ext, (c,), top, left, at, step, size)
                patch_f[c, rows, :] = piece
                total += piece * piece
            probe_out[2 * modes, rows, :] += total

        def fold_rows(m, at):
            cols = pl.ds(m * size, size)
            parts = []
            for base in (at, half + at):
                rows = pl.ds(base, fine)
                pr, pi = patch_f[0, rows, :], patch_f[1, rows, :]
                qr, qi = probe[m, 0, rows, :], probe[m, 1, rows, :]
                parts.append((qr * pr - qi * pi, qr * pi + qi * pr))
            for c in range(2):
                rows = pl.ds(c * half + at, fine)
                for t, value in enumerate((parts[0][c] + parts[1][c], parts[0][c] - parts[1][c])):
                    x_f[t, 0, rows, cols], x_f[t, 1, rows, cols] = split(value)

        def dft_rows(m, t):
            cols = pl.ds(m * size, size)
            high = x_f[t, 0, :, cols]
            u = dot(three_left(forward_t, t), jnp.concatenate([high, x_f[t, 1, :, cols], high], axis=0))
            rows = pl.ds(m * size + t * half, half)
            for v, value in enumerate((u[:, :half] + u[:, half:], u[:, :half] - u[:, half:])):
                high, low = split(value)
                for c in range(2):
                    lanes = pl.ds(c * half, half)
                    y_f[v, 0, rows, lanes] = high[c * half : (c + 1) * half]
                    y_f[v, 1, rows, lanes] = low[c * half : (c + 1) * half]

        def dft_cols(m, v):
            rows = pl.ds(m * size, size)
            high = y_f[v, 0, rows, :]
            z_f[v, rows, :] = dot(
                jnp.concatenate([high, y_f[v, 1, rows, :], high], axis=1), three_right(backward_t, v)
            )

        def scale(v, at):
            if v == 0 and at == 0:
                amp_copy(slot).wait()
            waves = [z_f[v, pl.ds(m * size + at, fine), :] for m in range(modes)]
            total = jnp.zeros((fine, half), F32)
            for wave in waves:
                total += wave[:, :half] * wave[:, :half] + wave[:, half:] * wave[:, half:]
            measured = amp[slot, pl.ds(at, fine), pl.ds(v * half, half)]
            factor = measured * lax.rsqrt(jnp.maximum(total, FLOOR * FLOOR)) - 1.0
            factor = jnp.concatenate([factor, factor], axis=1)
            for m in range(modes):
                rows = pl.ds(m * size + at, fine)
                g_s[v, 0, rows, :], g_s[v, 1, rows, :] = split(waves[m] * factor)

        pieces = [(take, at) for at in range(0, size, step)]
        for m in range(modes):
            pieces += [(fold_rows, m, at) for at in range(0, half, fine)]
            pieces += [(dft_rows, m, t) for t in range(2)]
            pieces += [(dft_cols, m, v) for v in range(2)]
        pieces += [(scale, v, at) for v in range(2) for at in range(0, size, fine)]
        return [functools.partial(*piece) for piece in pieces]

    def backward(slot):
        top, left = corner(slot)

        def dft_cols(m, v):
            rows = pl.ds(m * size, size)
            high = g_s[v, 0, rows, :]
            z_b[v, rows, :] = dot(
                jnp.concatenate([high, g_s[v, 1, rows, :], high], axis=1), three_right(forward_t, v)
            )

        def unfold_cols(m, t, at):
            rows = pl.ds(m * size + t * half + at, step)
            even, odd = z_b[0, rows, :], z_b[1, rows, :]
            for v, value in enumerate((even + odd, even - odd)):
                high, low = split(value)
                cols = pl.ds(m * size + v * half, half)
                for c in range(2):
                    spot = pl.ds(c * half + at, step)
                    x_b[t, 0, spot, cols] = high[:, c * half : (c + 1) * half]
                    x_b[t, 1, spot, cols] = low[:, c * half : (c + 1) * half]

        def dft_rows(m, t):
            cols = pl.ds(m * size, size)
            high = x_b[t, 0, :, cols]
            back[m, t] = dot(three_left(backward_t, t), jnp.concatenate([high, x_b[t, 1, :, cols], high], axis=0))

        def gradients(at):
            waves = []
            for m in range(modes):
                pair = []
                for c in range(2):
                    rows = pl.ds(c * half + at, fine)
                    even, odd = back[m, 0, rows, :], back[m, 1, rows, :]
                    pair.append((even + odd, even - odd))
                waves.append(pair)
            for h in range(2):
                rows = pl.ds(h * half + at, fine)
                pr, pi = patch_b[0, rows, :], patch_b[1, rows, :]
                grad_r = jnp.zeros((fine, size), F32)
                grad_i = jnp.zeros((fine, size), F32)
                for m in range(modes):
                    br, bi = waves[m][0][h], waves[m][1][h]
                    qr, qi = probe[m, 0, rows, :], probe[m, 1, rows, :]
                    grad_r += qr * br + qi * bi
                    grad_i += qr * bi - qi * br
                    probe_out[2 * m, rows, :] += pr * br + pi * bi
                    probe_out[2 * m + 1, rows, :] += pr * bi - pi * br
                spot = pl.ds(8 + h * half + at, fine)
                template[0, spot, :] = grad_r
                template[1, spot, :] = grad_i

        def add(c):
            add_shifted(template, grid, (c,), (c,), top, left, size)

        pieces = []
        for m in range(modes):
            pieces += [(dft_cols, m, v) for v in range(2)]
        for m in range(modes):
            pieces += [(unfold_cols, m, t, at) for t in range(2) for at in range(0, half, step)]
            pieces += [(dft_rows, m, t) for t in range(2)]
        pieces += [(gradients, at) for at in range(0, half, fine)]
        pieces += [(add, c) for c in range(2)]
        return [functools.partial(*piece) for piece in pieces]

    def hand_over():
        for at in range(0, size, step):
            for c in range(2):
                patch_b[c, pl.ds(at, step), :] = patch_f[c, pl.ds(at, step), :]

    @pl.when(count > 0)
    def _():
        weave(forward(chosen[0]), [])
        hand_over()

        def visit(index, _):
            weave(backward(chosen[index]), forward(chosen[index + 1]))
            hand_over()
            return 0

        lax.fori_loop(0, count - 1, visit, 0)
        weave(backward(chosen[count - 1]), [])

    if needs_rim:
        top, bottom, rest = pl.ds(0, size), pl.ds(size, tile_rows - size), pl.ds(tile_cols, size)
        note_rows = pl.ds(size, 8)
        parts = [
            grid.at[:, pl.ds(0, tile_rows), pl.ds(0, tile_cols)],
            grid.at[:, bottom, rest],
            grid.at[:, top, rest],
            grid.at[:, pl.ds(tile_rows, size), :],
            note[0],
            note[0],
        ]
        outs = [
            outs[0],
            outs[1],
            outs[2].at[:, top],
            outs[3].at[:, top],
            outs[2].at[0, note_rows],
            outs[3].at[0, note_rows, pl.ds(0, size)],
        ]
    else:
        parts = [grid.at[:, :, pl.ds(0, tile_cols)], sums]
        outs = [*outs, sums_out]
    stores = [pltpu.make_async_copy(part, out, out_sems.at[i]) for i, (part, out) in enumerate(zip(parts, outs))]
    for store in stores:
        store.start()
    for store in stores:
        store.wait()


def visit_slots(meta, probe, amplitudes, sources, init, note=()):
    size = probe.shape[2]
    modes = probe.shape[0]
    slots = amplitudes.shape[0]
    rows, cols = sources[0].shape[1:]
    tables = [jnp.asarray(item) for item in dft_tables(size)]
    vmem = pl.BlockSpec(memory_space=pltpu.VMEM)
    anywhere = pl.BlockSpec(memory_space=pl.ANY)
    hbm = pl.BlockSpec(memory_space=pltpu.HBM)
    needs_rim = bool(init)
    if needs_rim:
        shapes = [(2, rows, cols), (2, rows - size, size), (2, size + 8, size), (2, size + 8, cols + size)]
    else:
        shapes = [(2, rows + size, cols)]
    splits = np.cumsum([1, 1, 1, len(sources), 1, 1, len(init), len(note), len(shapes), 1])

    def kernel(*refs):
        meta, probe, amplitudes, sources, forward_t, backward_t, init, note, outs, probe_out = (
            refs[a:b] for a, b in zip([0, *splits[:-1]], splits)
        )
        scratch = refs[splits[-1] :]
        slots_kernel(
            needs_rim, meta[0], probe[0], amplitudes[0], sources, forward_t[0], backward_t[0], init, note, outs,
            probe_out[0], *scratch[:-3], scratch[-3:],
        )

    return pl.pallas_call(
        kernel,
        out_shape=[pltpu.HBM(shapes[0], F32)]
        + [jax.ShapeDtypeStruct(shape, F32) for shape in shapes[1:]]
        + [(jax.ShapeDtypeStruct if needs_rim else pltpu.HBM)((2 * modes + 1, size, size), F32)],
        in_specs=[pl.BlockSpec(memory_space=pltpu.SMEM), vmem, hbm, hbm] + [anywhere] * (len(sources) - 1)
        + [hbm] * (2 + len(init)) + [anywhere] * len(note),
        out_specs=[hbm] + [anywhere] * (len(shapes) - 1) + [vmem if needs_rim else hbm],
        scratch_shapes=[
            pltpu.VMEM((2, rows + size, cols + size), F32),
            pltpu.VMEM((2, rows + size, cols + size), F32),
            pltpu.VMEM(amplitudes.shape, F32),
            pltpu.VMEM(tables[0].shape, BF16),
            pltpu.VMEM(tables[1].shape, BF16),
            pltpu.SMEM((slots,), jnp.int32),
            pltpu.VMEM((2, size, size), F32),
            pltpu.VMEM((2, size, size), F32),
            pltpu.VMEM((2, 2, size, modes * size), BF16),
            pltpu.VMEM((2, 2, modes * size, size), BF16),
            pltpu.VMEM((2, modes * size, size), F32),
            pltpu.VMEM((2, 2, modes * size, size), BF16),
            pltpu.VMEM((2, 2, size, modes * size), BF16),
            pltpu.VMEM((2, modes * size, size), F32),
            pltpu.VMEM((modes, 2, size, size), F32),
            pltpu.VMEM((2, size + 16, size), F32),
            pltpu.VMEM((8, 128) if needs_rim else (2 * modes + 1, size, size), F32),
            pltpu.SemaphoreType.DMA((9,)),
            pltpu.SemaphoreType.DMA((slots,)),
            pltpu.SemaphoreType.DMA((6,)),
        ],
        compiler_params=pltpu.CompilerParams(vmem_limit_bytes=28 * MIB),
        cost_estimate=pl.CostEstimate(flops=12_000_000_000, bytes_accessed=16_000_000, transcendentals=0),
        name="slots_beyond" if needs_rim else "slots_inside",
    )(meta, probe, in_hbm(amplitudes), in_hbm(sources[0]), *sources[1:], *map(in_hbm, tables), *map(in_hbm, init), *note)


def finish_kernel(
    own, top, bottom, lower, scale, tile, out, own_s, right_s, lower_s, scale_s, tile_s, in_sems, out_sems
):
    size = right_s.shape[2]
    block = 128
    blocks = own_s.shape[1] // block

    def copies(i):
        rows = pl.ds(i * block, block)
        pairs = [
            (own.at[:, rows], own_s.at[:, rows]),
            (scale.at[rows], scale_s.at[rows]),
            (tile.at[:, rows], tile_s.at[:, rows]),
        ]
        if i < size // block:
            pairs.append((top.at[:, rows], right_s.at[:, rows]))
            pairs.append((lower.at[:, rows, pl.ds(0, lower_s.shape[2])], lower_s.at[:, rows]))
        else:
            pairs.append((bottom.at[:, pl.ds(i * block - size, block)], right_s.at[:, rows]))
        return [pltpu.make_async_copy(a, b, in_sems.at[i, k]) for k, (a, b) in enumerate(pairs)]

    loads = [copies(i) for i in range(blocks)]
    for load in loads:
        for copy in load:
            copy.start()
    stores = []
    for i in range(blocks):
        for copy in loads[i]:
            copy.wait()
        rows = pl.ds(i * block, block)
        for at in range(i * block, (i + 1) * block, 32):
            part = pl.ds(at, 32)
            for c in range(2):
                near, far = own_s[c, part, :size] + right_s[c, part, :], own_s[c, part, size:]
                if i < size // block:
                    near, far = near + lower_s[c, part, :size], far + lower_s[c, part, size:]
                own_s[c, part, :size] = tile_s[c, part, :size] + near * scale_s[part, :size]
                own_s[c, part, size:] = tile_s[c, part, size:] + far * scale_s[part, size:]
        stores.append(pltpu.make_async_copy(own_s.at[:, rows], out.at[:, rows], out_sems.at[i]))
        stores[-1].start()
    for store in stores:
        store.wait()


def finish(own, top, bottom, lower, inverse_light, tile):
    rows, cols = tile.shape[1:]
    size = top.shape[2]
    anywhere = pl.BlockSpec(memory_space=pl.ANY)
    hbm = pl.BlockSpec(memory_space=pltpu.HBM)
    return pl.pallas_call(
        finish_kernel,
        out_shape=jax.ShapeDtypeStruct(tile.shape, F32),
        in_specs=[hbm] + [anywhere] * 4 + [hbm],
        out_specs=hbm,
        scratch_shapes=[
            pltpu.VMEM(tile.shape, F32),
            pltpu.VMEM((2, rows, size), F32),
            pltpu.VMEM((2, size, cols), F32),
            pltpu.VMEM((rows, cols), F32),
            pltpu.VMEM(tile.shape, F32),
            pltpu.SemaphoreType.DMA((rows // 128, 5)),
            pltpu.SemaphoreType.DMA((rows // 128,)),
        ],
        compiler_params=pltpu.CompilerParams(vmem_limit_bytes=10 * MIB),
        cost_estimate=pl.CostEstimate(flops=3_000_000, bytes_accessed=12_000_000, transcendentals=0),
        name="finish",
    )(in_hbm(own), top, bottom, lower, inverse_light, in_hbm(tile))


def from_behind(array, axis, by):
    count = lax.axis_size(axis)
    pairs = [(i, i + by) for i in range(count) if 0 <= i + by < count]
    return lax.ppermute(array, axis, pairs)


def exchange(array, axis, bit):
    count = lax.axis_size(axis)
    return lax.ppermute(array, axis, [(i, i ^ bit) for i in range(count)])


def together(*arrays):
    return lax.optimization_barrier(arrays)


def cut(tile, regions, cost, name):
    def kernel(tile, *refs):
        sems = refs[-1]
        copies = [
            pltpu.make_async_copy(tile.at[:, pl.ds(at, height), pl.ds(0, width)], out, sems.at[i])
            for i, ((at, height, width), out) in enumerate(zip(regions, refs[:-1]))
        ]
        for copy in copies:
            copy.start()
        for copy in copies:
            copy.wait()

    return pl.pallas_call(
        kernel,
        out_shape=[jax.ShapeDtypeStruct((2, height, width), F32) for _, height, width in regions],
        in_specs=[pl.BlockSpec(memory_space=pltpu.HBM)],
        out_specs=[pl.BlockSpec(memory_space=pltpu.VMEM)] * len(regions),
        scratch_shapes=[pltpu.SemaphoreType.DMA((len(regions),))],
        compiler_params=pltpu.CompilerParams(vmem_limit_bytes=4 * MIB),
        cost_estimate=cost,
        name=name,
    )(in_hbm(tile))


def pick(share, index):
    half = share.shape[1] // 2

    def kernel(index, share, out, sem):
        rows = pl.ds(pl.multiple_of(index[0] * half, half), half)
        copy = pltpu.make_async_copy(share.at[:, rows], out, sem.at[0])
        copy.start()
        copy.wait()

    anywhere = pl.BlockSpec(memory_space=pl.ANY)
    return pl.pallas_call(
        kernel,
        out_shape=jax.ShapeDtypeStruct((share.shape[0], half, share.shape[2]), F32),
        in_specs=[pl.BlockSpec(memory_space=pltpu.SMEM), anywhere],
        out_specs=anywhere,
        scratch_shapes=[pltpu.SemaphoreType.DMA((1,))],
        compiler_params=pltpu.CompilerParams(vmem_limit_bytes=MIB),
        cost_estimate=LONG,
        name="pick",
    )(index.reshape(1), share)


def fold(mine, index, got, upper):
    count, half, width = got.shape
    quarter = half // 2

    def kernel(place, mine, got, send, keep):
        for k, out in ((1 - place[1], send), (place[1], keep)):
            for c in range(count):
                out[c] = (
                    mine[c, pl.ds(pl.multiple_of(place[0] * half + k * quarter, quarter), quarter), :]
                    + got[c, pl.ds(pl.multiple_of(k * quarter, quarter), quarter), :]
                )

    vmem = pl.BlockSpec(memory_space=pltpu.VMEM)
    shape = jax.ShapeDtypeStruct((count, quarter, width), F32)
    return pl.pallas_call(
        kernel,
        out_shape=[shape, shape],
        in_specs=[pl.BlockSpec(memory_space=pltpu.SMEM), vmem, vmem],
        out_specs=[vmem, vmem],
        compiler_params=pltpu.CompilerParams(vmem_limit_bytes=6 * MIB),
        cost_estimate=SHORT,
        name="fold",
    )(jnp.stack([index, upper]), mine, got)


def merge(right, lower):
    _, height, size = right.shape
    rows = height - 8
    cols = lower.shape[2] - size

    def kernel(right, lower, out, corner, sems):
        copies = [
            pltpu.make_async_copy(lower.at[:, pl.ds(0, rows), pl.ds(cols, size)], corner, sems.at[0]),
            pltpu.make_async_copy(lower.at[0, pl.ds(rows, 8), pl.ds(0, size)], out.at[1, pl.ds(rows, 8)], sems.at[1]),
        ]
        for copy in copies:
            copy.start()
        out[0, rows:, :] = right[0, rows:, :]
        for copy in copies:
            copy.wait()
        for c in range(2):
            out[c, :rows, :] = right[c, :rows, :] + corner[c]

    vmem = pl.BlockSpec(memory_space=pltpu.VMEM)
    return pl.pallas_call(
        kernel,
        out_shape=jax.ShapeDtypeStruct(right.shape, F32),
        in_specs=[vmem, pl.BlockSpec(memory_space=pl.ANY)],
        out_specs=vmem,
        scratch_shapes=[pltpu.VMEM((2, rows, size), F32), pltpu.SemaphoreType.DMA((2,))],
        compiler_params=pltpu.CompilerParams(vmem_limit_bytes=4 * MIB),
        cost_estimate=SHORT,
        name="merge",
    )(right, lower)


def join(upper, mine, other):
    half = mine.shape[1]

    def kernel(upper, mine, other, out, sems):
        copies = [
            pltpu.make_async_copy(source, out.at[:, pl.ds(pl.multiple_of(at * half, half), half)], sems.at[i])
            for i, (source, at) in enumerate(((mine, upper[0]), (other, 1 - upper[0])))
        ]
        for copy in copies:
            copy.start()
        for copy in copies:
            copy.wait()

    anywhere = pl.BlockSpec(memory_space=pl.ANY)
    return pl.pallas_call(
        kernel,
        out_shape=jax.ShapeDtypeStruct((mine.shape[0], 2 * half) + mine.shape[2:], F32),
        in_specs=[pl.BlockSpec(memory_space=pltpu.SMEM), anywhere, anywhere],
        out_specs=anywhere,
        scratch_shapes=[pltpu.SemaphoreType.DMA((2,))],
        compiler_params=pltpu.CompilerParams(vmem_limit_bytes=MIB),
        cost_estimate=pl.CostEstimate(flops=0, bytes_accessed=2_000_000, transcendentals=0),
        name="join",
    )(upper.reshape(1), mine, other)


def body(object_field, probe, amplitudes, positions, counts):
    modes, _, size, _ = probe.shape
    tile_rows, tile_cols = object_field.shape[1:]
    slots = amplitudes.shape[0]
    origin = jnp.stack([lax.axis_index("row") * tile_rows, lax.axis_index("col") * tile_cols]).astype(jnp.int32)
    bits = [1 << k for k in range(lax.axis_size("row").bit_length() - 1)]
    uppers = [(lax.axis_index("row") & bit) // bit for bit in bits]

    def relative(table):
        return jnp.concatenate([table[:, : 2 * slots] - jnp.tile(origin, slots)[None], table[:, 2 * slots :]], axis=1)

    right_up, right_down = cut(
        object_field, ((0, size, size), (size, tile_rows - size, size)), SHORT, "cut_right"
    )
    right_up, right_down, after_right = together(right_up, right_down, object_field)
    right_up = from_behind(right_up, "col", -1)
    right_down = from_behind(right_down, "col", -1)
    (lower,) = cut(after_right, ((0, size, tile_cols),), LONG, "cut_lower")
    meta = jnp.concatenate([positions.reshape(1, 2 * slots), counts.reshape(1, 1)], axis=1)
    lower = from_behind(lower, "row", -1)

    mine = relative(meta)
    note = jnp.pad(meta.astype(F32), ((0, 7), (0, size - meta.shape[1])))
    amplitudes = arrange(mine, amplitudes)
    right_up, amplitudes = together(right_up, amplitudes)
    corner = from_behind(right_up, "row", -1)
    amplitudes, lower = together(amplitudes, lower)
    init = visit_slots(mine, probe, amplitudes, [object_field, lower], [])
    right_up, right_down, corner, *init = together(right_up, right_down, corner, *init)
    own, bottom_spill, top_spill, lower_spill, share = visit_slots(
        mine, probe, amplitudes, [object_field, lower, right_up, right_down, corner], list(init), [note]
    )

    bottom_spill = from_behind(bottom_spill, "col", 1)
    lower_spill = from_behind(lower_spill, "row", 1)
    start = jnp.zeros((), jnp.int32)
    index = uppers[0]
    send = pick(share, 1 - index)
    for k, (bit, upper) in enumerate(zip(bits, uppers)):
        got = exchange(send, "row", bit)
        start = start + upper * (size >> (k + 1))
        if k + 1 < len(bits):
            send, share = fold(share, index, got, uppers[k + 1])
            index = jnp.zeros((), jnp.int32)
    share = share + got
    share, bottom_spill, lower_spill = together(share, bottom_spill, lower_spill)
    top_spill = from_behind(merge(top_spill, lower_spill), "col", 1)
    parts = lax.axis_size("col")
    rows = share.shape[1] // parts
    share = share.reshape(2 * modes + 1, parts, rows, size).transpose(1, 0, 2, 3)
    share = lax.all_to_all(share, "col", 0, 0, tiled=True).sum(axis=0)
    old = lax.dynamic_slice_in_dim(
        probe.reshape(2 * modes, size, size), start + lax.axis_index("col") * rows, rows, axis=1
    )
    new = old + share[: 2 * modes] / (share[2 * modes :] + 1.0)
    new, top_spill = together(new, top_spill)
    new = jnp.broadcast_to(new[None], (parts,) + new.shape)
    new = lax.all_to_all(new, "col", 0, 0, tiled=True)
    new = new.transpose(1, 0, 2, 3).reshape(2 * modes, parts * rows, size)
    width = 2 * slots + 1
    notes = [top_spill[:1, size], lower_spill[:1, size], top_spill[1:, size]]
    table = jnp.concatenate([meta] + [item[:, :width].astype(jnp.int32) for item in notes], axis=0)
    inverse_light = light(relative(table), probe, (tile_rows, tile_cols))
    for bit, upper in reversed(list(zip(bits, uppers))):
        other = exchange(new, "row", bit)
        if bit == bits[-1]:
            new_object = finish(own, top_spill, bottom_spill, lower_spill, inverse_light, object_field)
            other, new_object = together(other, new_object)
        new = join(upper, new, other)
    return (new_object, new.reshape(modes, 2, size, size))


def solution(mesh):
    in_specs = (
        P(None, "row", "col"),
        P(),
        P(("row", "col"), None, None),
        P(("row", "col"), None),
        P(("row", "col")),
    )
    out_specs = (P(None, "row", "col"), P())
    return jax.shard_map(body, mesh=mesh, in_specs=in_specs, out_specs=out_specs, check_vma=False)
```

```python
import functools
import math

import jax
import jax.numpy as jnp
import ml_dtypes
import numpy as np
from jax import lax
from jax.experimental import pallas as pl
from jax.experimental.pallas import tpu as pltpu
from jax.sharding import PartitionSpec as P

F32 = jnp.float32
BF16 = jnp.bfloat16
MIB = 1024 * 1024
LONG = pl.CostEstimate(flops=30_000_000_000, bytes_accessed=4_000_000, transcendentals=0)
SHORT = pl.CostEstimate(flops=0, bytes_accessed=1_000_000, transcendentals=0)
FLOOR = 0.3


def split_np(table):
    high = table.astype(ml_dtypes.bfloat16)
    low = (table - high.astype(np.float64)).astype(ml_dtypes.bfloat16)
    return high, low


def dft_tables(length):
    half = length // 2
    q = np.arange(half)[:, None]
    n = np.arange(half)[None, :]
    forward = []
    for odd in range(2):
        phase = (n * (2 * q + odd)) % length
        angle = phase * (-2.0 * math.pi / length)
        re = np.cos(angle) / math.sqrt(length)
        im = np.sin(angle) / math.sqrt(length)
        forward.append(np.stack(split_np(np.block([[re, -im], [im, re]]))))
    forward = np.stack(forward)
    return forward, np.ascontiguousarray(forward.transpose(0, 1, 3, 2))


def in_hbm(array):
    return pltpu.with_memory_space_constraint(array, pltpu.HBM)


def dot(a, b):
    return jnp.dot(a, b, preferred_element_type=F32)


def split(x):
    high = x.astype(BF16)
    return high, (x - high.astype(F32)).astype(BF16)


def roll_rows(x, shift):
    return pltpu.roll(x.reshape(x.shape[0] // 8, 8, x.shape[1]), shift, 1)


def roll_rows(x, shift):
    return pltpu.roll(x.reshape(x.shape[0] // 8, 8, x.shape[1]), shift, 1)


def roll_rows(x, shift):
    return pltpu.roll(x.reshape(x.shape[0] // 8, 8, x.shape[1]), shift, 1)


def roll_rows(x, shift):
    return pltpu.roll(x.reshape(x.shape[0] // 8, 8, x.shape[1]), shift, 1)


def split_three(x):
    high = x.astype(BF16)
    rest = x - high.astype(F32)
    middle = rest.astype(BF16)
    return high, middle, (rest - middle.astype(F32)).astype(BF16)


def add_shifted(template, grid, where_t, where_g, top, left, size):
    top_s = top & 7
    top_b = pl.multiple_of(top - top_s, 8)
    left_s = left & 127
    left_b = pl.multiple_of(left - left_s, 128)
    step = 24
    wrapped = lax.broadcasted_iota(jnp.int32, (step, 128), 1) < left_s
    wrapped_rows = lax.broadcasted_iota(jnp.int32, (step // 8, 8, 128), 1) < top_s
    zero = jnp.zeros((step, 128), F32)
    blocks = size // 128
    for at in range(0, size + 8, step):
        parts = []
        for j in range(blocks):
            x = roll_rows(template[where_t + (pl.ds(at, step + 8), pl.ds(128 * j, 128))], top_s)
            x = jnp.where(wrapped_rows, x[:-1], x[1:]).reshape(step, 128)
            parts.append(pltpu.roll(x, left_s, 1))
        for j in range(blocks + 1):
            before = parts[j - 1] if j > 0 else zero
            after = parts[j] if j < blocks else zero
            spot = where_g + (pl.ds(top_b + at, step), pl.ds(left_b + 128 * j, 128))
            grid[spot] += jnp.where(wrapped, before, after)


def take_shifted(field, where, top, left, at, step, size):
    top_s = top & 7
    top_b = pl.multiple_of(top - top_s, 8)
    left_s = left & 127
    left_b = pl.multiple_of(left - left_s, 128)
    back = (128 - left_s) & 127
    keep = lax.broadcasted_iota(jnp.int32, (step + 8, 128), 1) < 128 - left_s
    keep_rows = lax.broadcasted_iota(jnp.int32, (step // 8, 8, 128), 1) < 8 - top_s
    blocks = size // 128
    parts = [
        pltpu.roll(field[where + (pl.ds(top_b + at, step + 8), pl.ds(left_b + 128 * j, 128))], back, 1)
        for j in range(blocks + 1)
    ]
    pieces = []
    for j in range(blocks):
        x = roll_rows(jnp.where(keep, parts[j], parts[j + 1]), (8 - top_s) & 7)
        pieces.append(jnp.where(keep_rows, x[:-1], x[1:]).reshape(step, 128))
    return jnp.concatenate(pieces, axis=1)


def light_kernel(meta, probe_h, inverse_light, probe, template, grid, sem):
    size = probe.shape[2]
    tile_rows, tile_cols = inverse_light.shape
    copy = pltpu.make_async_copy(probe_h, probe, sem.at[0])
    copy.start()
    template[0:8, :] = jnp.zeros((8, size), F32)
    template[8 + size :, :] = jnp.zeros((8, size), F32)
    copy.wait()
    for at in range(0, size, 32):
        rows = pl.ds(at, 32)
        total = jnp.zeros((32, size), F32)
        for m in range(probe.shape[0]):
            total += probe[m, 0, rows] * probe[m, 0, rows] + probe[m, 1, rows] * probe[m, 1, rows]
        template[pl.ds(8 + at, 32), :] = total

    @pl.loop(0, tile_rows // 32)
    def _(step):
        rows = pl.ds(pl.multiple_of(size + step * 32, 32), 32)
        grid[rows, size : size + tile_cols] = jnp.zeros((32, tile_cols), F32)

    slots = meta.shape[1] // 2
    for device in range(4):

        @pl.loop(0, meta[device, 2 * slots])
        def _(slot):
            top = meta[device, 2 * slot] + size
            left = meta[device, 2 * slot + 1] + size

            @pl.when((top > 0) & (left > 0))
            def _():
                add_shifted(template, grid, (), (), top, left, size)

    @pl.loop(0, tile_rows // 32)
    def _(step):
        rows = pl.ds(pl.multiple_of(size + step * 32, 32), 32)
        out_rows = pl.ds(pl.multiple_of(step * 32, 32), 32)
        inverse_light[out_rows, :] = 1.0 / (grid[rows, size : size + tile_cols] + 1.0)


def light(meta, probe, tile_shape):
    size = probe.shape[2]
    vmem = pl.BlockSpec(memory_space=pltpu.VMEM)
    return pl.pallas_call(
        light_kernel,
        out_shape=jax.ShapeDtypeStruct(tile_shape, F32),
        in_specs=[pl.BlockSpec(memory_space=pltpu.SMEM), pl.BlockSpec(memory_space=pltpu.HBM)],
        out_specs=vmem,
        scratch_shapes=[
            pltpu.VMEM(probe.shape, F32),
            pltpu.VMEM((size + 16, size), F32),
            pltpu.VMEM((tile_shape[0] + 2 * size, tile_shape[1] + 2 * size), F32),
            pltpu.SemaphoreType.DMA((1,)),
        ],
        compiler_params=pltpu.CompilerParams(vmem_limit_bytes=8 * MIB),
        cost_estimate=pl.CostEstimate(flops=4_000_000_000, bytes_accessed=1_000_000, transcendentals=0),
        name="light",
    )(meta, in_hbm(probe))


def arrange_kernel(meta, amplitudes, out, given, moved, in_sems, out_sems):
    slots, size, _ = amplitudes.shape
    count = meta[0, 2 * slots]

    def load(slot):
        return pltpu.make_async_copy(amplitudes.at[slot], given.at[slot], in_sems.at[slot])

    def store(slot):
        return pltpu.make_async_copy(moved.at[slot], out.at[slot], out_sems.at[slot])

    @pl.loop(0, count)
    def _(slot):
        load(slot).start()

    first = lax.broadcasted_iota(jnp.int32, (size, size), 0)
    second = lax.broadcasted_iota(jnp.int32, (size, size), 1)
    half = size // 2

    def source(index):
        return jnp.where(index < half, 2 * index, 2 * index - (size - 1))

    rows = (source(first) == second).astype(F32).astype(BF16)
    cols = (source(second) == first).astype(F32).astype(BF16)
    rows = jnp.concatenate([rows, rows], axis=1)
    cols = jnp.concatenate([cols, cols], axis=0)

    @pl.loop(0, count)
    def _(slot):
        load(slot).wait()
        x = dot(rows, jnp.concatenate(split(given[slot]), axis=0))
        moved[slot] = dot(jnp.concatenate(split(x), axis=1), cols)
        store(slot).start()

    @pl.loop(0, count)
    def _(slot):
        store(slot).wait()


def arrange(meta, amplitudes):
    slots = amplitudes.shape[0]
    hbm = pl.BlockSpec(memory_space=pltpu.HBM)
    return pl.pallas_call(
        arrange_kernel,
        out_shape=pltpu.HBM(amplitudes.shape, F32),
        in_specs=[pl.BlockSpec(memory_space=pltpu.SMEM), hbm],
        out_specs=hbm,
        scratch_shapes=[
            pltpu.VMEM(amplitudes.shape, F32),
            pltpu.VMEM(amplitudes.shape, F32),
            pltpu.SemaphoreType.DMA((slots,)),
            pltpu.SemaphoreType.DMA((slots,)),
        ],
        compiler_params=pltpu.CompilerParams(vmem_limit_bytes=8 * MIB),
        cost_estimate=LONG,
        name="arrange",
    )(meta, in_hbm(amplitudes))


def three_left(table, t):
    return jnp.concatenate([table[t, 0], table[t, 0], table[t, 1]], axis=1)


def three_right(table, v):
    return jnp.concatenate([table[v, 0], table[v, 0], table[v, 1]], axis=0)


def weave(first, second):
    total = max(len(first), len(second))
    done = [0, 0]
    for i in range(1, total + 1):
        for k, pieces in enumerate((first, second)):
            while done[k] * total < i * len(pieces):
                pieces[done[k]]()
                done[k] += 1


def slots_kernel(
    needs_rim, meta, probe, amplitudes, sources, forward_h, backward_h, init, note, outs, probe_out,
    ext, grid, amp, forward_t, backward_t, chosen, patch_f, patch_b, x_f, y_f, z_f, g_s, x_b, z_b, back, template, sums, sems,
):
    size = probe.shape[2]
    half = size // 2
    modes = probe.shape[0]
    slots = amplitudes.shape[0]
    tile_rows, tile_cols = (n - size for n in ext.shape[1:])
    step = 32
    fine = 16
    load_sems, amp_sems, out_sems = sems
    sums_out = probe_out
    if not needs_rim:
        probe_out = sums

    regions = (
        (pl.ds(0, tile_rows), pl.ds(0, tile_cols)),
        (pl.ds(tile_rows, size), pl.ds(0, tile_cols)),
        (pl.ds(0, size), pl.ds(tile_cols, size)),
        (pl.ds(size, tile_rows - size), pl.ds(tile_cols, size)),
        (pl.ds(tile_rows, size), pl.ds(tile_cols, size)),
    )
    loads = [
        pltpu.make_async_copy(source, ext.at[:, rows, cols], load_sems.at[i])
        for i, (source, (rows, cols)) in enumerate(zip(sources, regions))
    ]
    loads.append(pltpu.make_async_copy(forward_h, forward_t, load_sems.at[7]))
    loads.append(pltpu.make_async_copy(backward_h, backward_t, load_sems.at[8]))
    late = []
    if needs_rim:
        loads.append(pltpu.make_async_copy(init[1], probe_out, load_sems.at[6]))
        below = grid.at[:, pl.ds(tile_rows, size), pl.ds(0, tile_cols)]
        late.append(pltpu.make_async_copy(init[0], below, load_sems.at[5]))
    for load in loads + late:
        load.start()

    def amp_copy(slot):
        return pltpu.make_async_copy(amplitudes.at[slot], amp.at[slot], amp_sems.at[slot])

    def choose(slot, found):
        beyond = meta[0, 2 * slot + 1] + size > tile_cols
        wanted = beyond if needs_rim else jnp.logical_not(beyond)

        @pl.when(wanted)
        def _():
            chosen[found] = slot
            amp_copy(slot).start()

        return found + wanted.astype(jnp.int32)

    count = lax.fori_loop(0, meta[0, 2 * slots], choose, jnp.zeros((), jnp.int32))

    @pl.loop(0, tile_rows // step)
    def _(at):
        rows = pl.ds(pl.multiple_of(at * step, step), step)
        for c in range(2):
            grid[c, rows, :] = jnp.zeros((step, tile_cols + size), F32)

    @pl.loop(tile_rows // step, (tile_rows + size) // step)
    def _(at):
        rows = pl.ds(pl.multiple_of(at * step, step), step)
        for c in range(2):
            if needs_rim:
                grid[c, rows, tile_cols:] = jnp.zeros((step, size), F32)
            else:
                grid[c, rows, :] = jnp.zeros((step, tile_cols + size), F32)

    if not needs_rim:

        @pl.loop(0, size // step)
        def _(at):
            rows = pl.ds(pl.multiple_of(at * step, step), step)
            for c in range(2 * modes + 1):
                probe_out[c, rows, :] = jnp.zeros((step, size), F32)

    for c in range(2):
        template[c, 0:8, :] = jnp.zeros((8, size), F32)
        template[c, 8 + size :, :] = jnp.zeros((8, size), F32)
    for load in loads:
        load.wait()

    def corner(slot):
        return meta[0, 2 * slot], meta[0, 2 * slot + 1]

    def forward(slot):
        top, left = corner(slot)

        def take(at):
            rows = pl.ds(at, step)
            total = jnp.zeros((step, size), F32)
            for c in range(2):
                piece = take_shifted(ext, (c,), top, left, at, step, size)
                patch_f[c, rows, :] = piece
                total += piece * piece
            probe_out[2 * modes, rows, :] += total

        def fold_rows(m, at):
            cols = pl.ds(m * size, size)
            parts = []
            for base in (at, half + at):
                rows = pl.ds(base, fine)
                pr, pi = patch_f[0, rows, :], patch_f[1, rows, :]
                qr, qi = probe[m, 0, rows, :], probe[m, 1, rows, :]
                parts.append((qr * pr - qi * pi, qr * pi + qi * pr))
            for c in range(2):
                rows = pl.ds(c * half + at, fine)
                for t, value in enumerate((parts[0][c] + parts[1][c], parts[0][c] - parts[1][c])):
                    x_f[t, 0, rows, cols], x_f[t, 1, rows, cols] = split(value)

        def dft_rows(m, t):
            cols = pl.ds(m * size, size)
            high = x_f[t, 0, :, cols]
            u = dot(three_left(forward_t, t), jnp.concatenate([high, x_f[t, 1, :, cols], high], axis=0))
            rows = pl.ds(m * size + t * half, half)
            for v, value in enumerate((u[:, :half] + u[:, half:], u[:, :half] - u[:, half:])):
                high, low = split(value)
                for c in range(2):
                    lanes = pl.ds(c * half, half)
                    y_f[v, 0, rows, lanes] = high[c * half : (c + 1) * half]
                    y_f[v, 1, rows, lanes] = low[c * half : (c + 1) * half]

        def dft_cols(m, v):
            rows = pl.ds(m * size, size)
            high = y_f[v, 0, rows, :]
            z_f[v, rows, :] = dot(
                jnp.concatenate([high, y_f[v, 1, rows, :], high], axis=1), three_right(backward_t, v)
            )

        def scale(v, at):
            if v == 0 and at == 0:
                amp_copy(slot).wait()
            waves = [z_f[v, pl.ds(m * size + at, fine), :] for m in range(modes)]
            total = jnp.zeros((fine, half), F32)
            for wave in waves:
                total += wave[:, :half] * wave[:, :half] + wave[:, half:] * wave[:, half:]
            measured = amp[slot, pl.ds(at, fine), pl.ds(v * half, half)]
            factor = measured * lax.rsqrt(jnp.maximum(total, FLOOR * FLOOR)) - 1.0
            factor = jnp.concatenate([factor, factor], axis=1)
            for m in range(modes):
                rows = pl.ds(m * size + at, fine)
                g_s[v, 0, rows, :], g_s[v, 1, rows, :] = split(waves[m] * factor)

        pieces = [(take, at) for at in range(0, size, step)]
        for m in range(modes):
            pieces += [(fold_rows, m, at) for at in range(0, half, fine)]
            pieces += [(dft_rows, m, t) for t in range(2)]
            pieces += [(dft_cols, m, v) for v in range(2)]
        pieces += [(scale, v, at) for v in range(2) for at in range(0, size, fine)]
        return [functools.partial(*piece) for piece in pieces]

    def backward(slot):
        top, left = corner(slot)

        def dft_cols(m, v):
            rows = pl.ds(m * size, size)
            high = g_s[v, 0, rows, :]
            z_b[v, rows, :] = dot(
                jnp.concatenate([high, g_s[v, 1, rows, :], high], axis=1), three_right(forward_t, v)
            )

        def unfold_cols(m, t, at):
            rows = pl.ds(m * size + t * half + at, step)
            even, odd = z_b[0, rows, :], z_b[1, rows, :]
            for v, value in enumerate((even + odd, even - odd)):
                high, low = split(value)
                cols = pl.ds(m * size + v * half, half)
                for c in range(2):
                    spot = pl.ds(c * half + at, step)
                    x_b[t, 0, spot, cols] = high[:, c * half : (c + 1) * half]
                    x_b[t, 1, spot, cols] = low[:, c * half : (c + 1) * half]

        def dft_rows(m, t):
            cols = pl.ds(m * size, size)
            high = x_b[t, 0, :, cols]
            back[m, t] = dot(three_left(backward_t, t), jnp.concatenate([high, x_b[t, 1, :, cols], high], axis=0))

        def gradients(at):
            waves = []
            for m in range(modes):
                pair = []
                for c in range(2):
                    rows = pl.ds(c * half + at, fine)
                    even, odd = back[m, 0, rows, :], back[m, 1, rows, :]
                    pair.append((even + odd, even - odd))
                waves.append(pair)
            for h in range(2):
                rows = pl.ds(h * half + at, fine)
                pr, pi = patch_b[0, rows, :], patch_b[1, rows, :]
                grad_r = jnp.zeros((fine, size), F32)
                grad_i = jnp.zeros((fine, size), F32)
                for m in range(modes):
                    br, bi = waves[m][0][h], waves[m][1][h]
                    qr, qi = probe[m, 0, rows, :], probe[m, 1, rows, :]
                    grad_r += qr * br + qi * bi
                    grad_i += qr * bi - qi * br
                    probe_out[2 * m, rows, :] += pr * br + pi * bi
                    probe_out[2 * m + 1, rows, :] += pr * bi - pi * br
                spot = pl.ds(8 + h * half + at, fine)
                template[0, spot, :] = grad_r
                template[1, spot, :] = grad_i

        def add(c):
            add_shifted(template, grid, (c,), (c,), top, left, size)

        pieces = []
        for m in range(modes):
            pieces += [(dft_cols, m, v) for v in range(2)]
        for m in range(modes):
            pieces += [(unfold_cols, m, t, at) for t in range(2) for at in range(0, half, step)]
            pieces += [(dft_rows, m, t) for t in range(2)]
        pieces += [(gradients, at) for at in range(0, half, fine)]
        pieces += [(add, c) for c in range(2)]
        return [functools.partial(*piece) for piece in pieces]

    def hand_over():
        for at in range(0, size, step):
            for c in range(2):
                patch_b[c, pl.ds(at, step), :] = patch_f[c, pl.ds(at, step), :]

    @pl.when(count > 0)
    def _():
        weave(forward(chosen[0]), [])
        hand_over()
        for load in late:
            load.wait()

        def visit(index, _):
            weave(backward(chosen[index]), forward(chosen[index + 1]))
            hand_over()
            return 0

        lax.fori_loop(0, count - 1, visit, 0)
        weave(backward(chosen[count - 1]), [])

    @pl.when(count == 0)
    def _():
        for load in late:
            load.wait()

    if needs_rim:
        top, bottom, rest = pl.ds(0, size), pl.ds(size, tile_rows - size), pl.ds(tile_cols, size)
        note_rows = pl.ds(size, 8)
        parts = [
            grid.at[:, pl.ds(0, tile_rows), pl.ds(0, tile_cols)],
            grid.at[:, bottom, rest],
            grid.at[:, top, rest],
            grid.at[:, pl.ds(tile_rows, size), :],
            note[0],
            note[0],
        ]
        outs = [
            outs[0],
            outs[1],
            outs[2].at[:, top],
            outs[3].at[:, top],
            outs[2].at[0, note_rows],
            outs[3].at[0, note_rows, pl.ds(0, size)],
        ]
    else:
        parts = [
            grid.at[:, pl.ds(0, tile_rows), pl.ds(0, tile_cols)],
            grid.at[:, pl.ds(tile_rows, size), pl.ds(0, tile_cols)],
            sums,
        ]
        outs = [*outs, sums_out]
    stores = [pltpu.make_async_copy(part, out, out_sems.at[i]) for i, (part, out) in enumerate(zip(parts, outs))]
    for store in stores:
        store.start()
    for store in stores:
        store.wait()


def visit_slots(meta, probe, amplitudes, sources, init, note=()):
    size = probe.shape[2]
    modes = probe.shape[0]
    slots = amplitudes.shape[0]
    rows, cols = sources[0].shape[1:]
    tables = [jnp.asarray(item) for item in dft_tables(size)]
    vmem = pl.BlockSpec(memory_space=pltpu.VMEM)
    anywhere = pl.BlockSpec(memory_space=pl.ANY)
    hbm = pl.BlockSpec(memory_space=pltpu.HBM)
    needs_rim = bool(init)
    if needs_rim:
        shapes = [(2, rows, cols), (2, rows - size, size), (2, size + 8, size), (2, size + 8, cols + size)]
    else:
        shapes = [(2, rows, cols), (2, size, cols)]
    splits = np.cumsum([1, 1, 1, len(sources), 1, 1, len(init), len(note), len(shapes), 1])

    def kernel(*refs):
        meta, probe, amplitudes, sources, forward_t, backward_t, init, note, outs, probe_out = (
            refs[a:b] for a, b in zip([0, *splits[:-1]], splits)
        )
        scratch = refs[splits[-1] :]
        slots_kernel(
            needs_rim, meta[0], probe[0], amplitudes[0], sources, forward_t[0], backward_t[0], init, note, outs,
            probe_out[0], *scratch[:-3], scratch[-3:],
        )

    return pl.pallas_call(
        kernel,
        out_shape=[pltpu.HBM(shapes[0], F32)]
        + [(jax.ShapeDtypeStruct if needs_rim else pltpu.HBM)(shape, F32) for shape in shapes[1:]]
        + [(jax.ShapeDtypeStruct if needs_rim else pltpu.HBM)((2 * modes + 1, size, size), F32)],
        in_specs=[pl.BlockSpec(memory_space=pltpu.SMEM), vmem, hbm, hbm] + [anywhere] * (len(sources) - 1)
        + [hbm] * (2 + len(init)) + [anywhere] * len(note),
        out_specs=[hbm] + [anywhere if needs_rim else hbm] * (len(shapes) - 1) + [vmem if needs_rim else hbm],
        scratch_shapes=[
            pltpu.VMEM((2, rows + size, cols + size), F32),
            pltpu.VMEM((2, rows + size, cols + size), F32),
            pltpu.VMEM(amplitudes.shape, F32),
            pltpu.VMEM(tables[0].shape, BF16),
            pltpu.VMEM(tables[1].shape, BF16),
            pltpu.SMEM((slots,), jnp.int32),
            pltpu.VMEM((2, size, size), F32),
            pltpu.VMEM((2, size, size), F32),
            pltpu.VMEM((2, 2, size, modes * size), BF16),
            pltpu.VMEM((2, 2, modes * size, size), BF16),
            pltpu.VMEM((2, modes * size, size), F32),
            pltpu.VMEM((2, 2, modes * size, size), BF16),
            pltpu.VMEM((2, 2, size, modes * size), BF16),
            pltpu.VMEM((2, modes * size, size), F32),
            pltpu.VMEM((modes, 2, size, size), F32),
            pltpu.VMEM((2, size + 16, size), F32),
            pltpu.VMEM((8, 128) if needs_rim else (2 * modes + 1, size, size), F32),
            pltpu.SemaphoreType.DMA((9,)),
            pltpu.SemaphoreType.DMA((slots,)),
            pltpu.SemaphoreType.DMA((6,)),
        ],
        compiler_params=pltpu.CompilerParams(vmem_limit_bytes=26 * MIB),
        cost_estimate=pl.CostEstimate(flops=12_000_000_000, bytes_accessed=16_000_000, transcendentals=0),
        name="slots_beyond" if needs_rim else "slots_inside",
    )(
        meta, probe, *map(in_hbm, [amplitudes, sources[0]]), *sources[1:], *map(in_hbm, [*tables, *init]), *note
    )


def finish_kernel(
    own, first, top, bottom, lower, scale, tile, out, own_s, first_s, right_s, lower_s, scale_s, tile_s, in_sems, out_sems
):
    size = right_s.shape[2]
    block = 128
    blocks = own_s.shape[1] // block

    def copies(i):
        rows = pl.ds(i * block, block)
        pairs = [
            (own.at[:, rows], own_s.at[:, rows]),
            (first.at[:, rows], first_s.at[:, rows]),
            (scale.at[rows], scale_s.at[rows]),
            (tile.at[:, rows], tile_s.at[:, rows]),
        ]
        if i < size // block:
            pairs.append((top.at[:, rows], right_s.at[:, rows]))
            pairs.append((lower.at[:, rows, pl.ds(0, lower_s.shape[2])], lower_s.at[:, rows]))
        else:
            pairs.append((bottom.at[:, pl.ds(i * block - size, block)], right_s.at[:, rows]))
        return [pltpu.make_async_copy(a, b, in_sems.at[i, k]) for k, (a, b) in enumerate(pairs)]

    loads = [copies(i) for i in range(blocks)]
    for load in loads:
        for copy in load:
            copy.start()
    stores = []
    for i in range(blocks):
        for copy in loads[i]:
            copy.wait()
        rows = pl.ds(i * block, block)
        for at in range(i * block, (i + 1) * block, 32):
            part = pl.ds(at, 32)
            for c in range(2):
                near = own_s[c, part, :size] + first_s[c, part, :size] + right_s[c, part, :]
                far = own_s[c, part, size:] + first_s[c, part, size:]
                if i < size // block:
                    near, far = near + lower_s[c, part, :size], far + lower_s[c, part, size:]
                own_s[c, part, :size] = tile_s[c, part, :size] + near * scale_s[part, :size]
                own_s[c, part, size:] = tile_s[c, part, size:] + far * scale_s[part, size:]
        stores.append(pltpu.make_async_copy(own_s.at[:, rows], out.at[:, rows], out_sems.at[i]))
        stores[-1].start()
    for store in stores:
        store.wait()


def finish(own, first, top, bottom, lower, inverse_light, tile):
    rows, cols = tile.shape[1:]
    size = top.shape[2]
    hbm = pl.BlockSpec(memory_space=pltpu.HBM)
    return pl.pallas_call(
        finish_kernel,
        out_shape=jax.ShapeDtypeStruct(tile.shape, F32),
        in_specs=[hbm] * 2 + [pl.BlockSpec(memory_space=pl.ANY)] * 4 + [hbm],
        out_specs=hbm,
        scratch_shapes=[
            pltpu.VMEM(tile.shape, F32),
            pltpu.VMEM(tile.shape, F32),
            pltpu.VMEM((2, rows, size), F32),
            pltpu.VMEM((2, size, cols), F32),
            pltpu.VMEM((rows, cols), F32),
            pltpu.VMEM(tile.shape, F32),
            pltpu.SemaphoreType.DMA((rows // 128, 6)),
            pltpu.SemaphoreType.DMA((rows // 128,)),
        ],
        compiler_params=pltpu.CompilerParams(vmem_limit_bytes=12 * MIB),
        cost_estimate=pl.CostEstimate(flops=3_000_000, bytes_accessed=12_000_000, transcendentals=0),
        name="finish",
    )(in_hbm(own), in_hbm(first), top, bottom, lower, inverse_light, in_hbm(tile))


def from_behind(array, axis, by):
    count = lax.axis_size(axis)
    pairs = [(i, i + by) for i in range(count) if 0 <= i + by < count]
    return lax.ppermute(array, axis, pairs)


def exchange(array, axis, bit):
    count = lax.axis_size(axis)
    return lax.ppermute(array, axis, [(i, i ^ bit) for i in range(count)])


def together(*arrays):
    return lax.optimization_barrier(arrays)


def cut(tile, regions, cost, name):
    def kernel(tile, *refs):
        sems = refs[-1]
        copies = [
            pltpu.make_async_copy(tile.at[:, pl.ds(at, height), pl.ds(0, width)], out, sems.at[i])
            for i, ((at, height, width), out) in enumerate(zip(regions, refs[:-1]))
        ]
        for copy in copies:
            copy.start()
        for copy in copies:
            copy.wait()

    return pl.pallas_call(
        kernel,
        out_shape=[jax.ShapeDtypeStruct((2, height, width), F32) for _, height, width in regions],
        in_specs=[pl.BlockSpec(memory_space=pltpu.HBM)],
        out_specs=[pl.BlockSpec(memory_space=pltpu.VMEM)] * len(regions),
        scratch_shapes=[pltpu.SemaphoreType.DMA((len(regions),))],
        compiler_params=pltpu.CompilerParams(vmem_limit_bytes=4 * MIB),
        cost_estimate=cost,
        name=name,
    )(in_hbm(tile))


def pick(share, index):
    half = share.shape[1] // 2

    def kernel(index, share, out, sem):
        rows = pl.ds(pl.multiple_of(index[0] * half, half), half)
        copy = pltpu.make_async_copy(share.at[:, rows], out, sem.at[0])
        copy.start()
        copy.wait()

    anywhere = pl.BlockSpec(memory_space=pl.ANY)
    return pl.pallas_call(
        kernel,
        out_shape=jax.ShapeDtypeStruct((share.shape[0], half, share.shape[2]), F32),
        in_specs=[pl.BlockSpec(memory_space=pltpu.SMEM), anywhere],
        out_specs=anywhere,
        scratch_shapes=[pltpu.SemaphoreType.DMA((1,))],
        compiler_params=pltpu.CompilerParams(vmem_limit_bytes=MIB),
        cost_estimate=LONG,
        name="pick",
    )(index.reshape(1), share)


def fold(mine, index, got, upper):
    count, half, width = got.shape
    quarter = half // 2

    def kernel(place, mine, got, send, keep):
        for k, out in ((1 - place[1], send), (place[1], keep)):
            for c in range(count):
                out[c] = (
                    mine[c, pl.ds(pl.multiple_of(place[0] * half + k * quarter, quarter), quarter), :]
                    + got[c, pl.ds(pl.multiple_of(k * quarter, quarter), quarter), :]
                )

    vmem = pl.BlockSpec(memory_space=pltpu.VMEM)
    shape = jax.ShapeDtypeStruct((count, quarter, width), F32)
    return pl.pallas_call(
        kernel,
        out_shape=[shape, shape],
        in_specs=[pl.BlockSpec(memory_space=pltpu.SMEM), vmem, vmem],
        out_specs=[vmem, vmem],
        compiler_params=pltpu.CompilerParams(vmem_limit_bytes=6 * MIB),
        cost_estimate=SHORT,
        name="fold",
    )(jnp.stack([index, upper]), mine, got)


def merge(right, lower):
    _, height, size = right.shape
    rows = height - 8
    cols = lower.shape[2] - size

    def kernel(right, lower, out, corner, sems):
        copies = [
            pltpu.make_async_copy(lower.at[:, pl.ds(0, rows), pl.ds(cols, size)], corner, sems.at[0]),
            pltpu.make_async_copy(lower.at[0, pl.ds(rows, 8), pl.ds(0, size)], out.at[1, pl.ds(rows, 8)], sems.at[1]),
        ]
        for copy in copies:
            copy.start()
        out[0, rows:, :] = right[0, rows:, :]
        for copy in copies:
            copy.wait()
        for c in range(2):
            out[c, :rows, :] = right[c, :rows, :] + corner[c]

    vmem = pl.BlockSpec(memory_space=pltpu.VMEM)
    return pl.pallas_call(
        kernel,
        out_shape=jax.ShapeDtypeStruct(right.shape, F32),
        in_specs=[vmem, pl.BlockSpec(memory_space=pl.ANY)],
        out_specs=vmem,
        scratch_shapes=[pltpu.VMEM((2, rows, size), F32), pltpu.SemaphoreType.DMA((2,))],
        compiler_params=pltpu.CompilerParams(vmem_limit_bytes=4 * MIB),
        cost_estimate=SHORT,
        name="merge",
    )(right, lower)


def deal(me, terms, parts, rows):
    aligned = rows % 8 == 0
    if not aligned:
        count, _, width = terms[0].shape
        terms = [sum(terms).reshape(count, parts, rows, width).transpose(1, 0, 2, 3)]
    count, width = terms[0].shape[0 if aligned else 1], terms[0].shape[-1]

    def kernel(me, *refs):
        terms, outs = refs[:-parts], refs[-parts:]
        for k, out in enumerate(outs):
            j = me[0] ^ k
            for c in range(count):
                if aligned:
                    spot = pl.ds(pl.multiple_of(j * rows, rows), rows)
                    out[c] = sum(term[c, spot, :] for term in terms)
                else:
                    out[c] = terms[0][j, c]

    vmem = pl.BlockSpec(memory_space=pltpu.VMEM)
    return pl.pallas_call(
        kernel,
        out_shape=[jax.ShapeDtypeStruct((count, rows, width), F32)] * parts,
        in_specs=[pl.BlockSpec(memory_space=pltpu.SMEM)] + [vmem] * len(terms),
        out_specs=[vmem] * parts,
        compiler_params=pltpu.CompilerParams(vmem_limit_bytes=4 * MIB),
        cost_estimate=SHORT,
        name="deal",
    )(me.reshape(1), *terms)


def collect(me, pieces):
    count, rows, width = pieces[0].shape
    parts = len(pieces)
    aligned = rows % 8 == 0
    shape = (count, parts * rows, width) if aligned else (parts, count, rows, width)

    def kernel(me, *refs):
        pieces, out = refs[:-1], refs[-1]
        for k, piece in enumerate(pieces):
            j = me[0] ^ k
            for c in range(count):
                if aligned:
                    out[c, pl.ds(pl.multiple_of(j * rows, rows), rows), :] = piece[c]
                else:
                    out[j, c] = piece[c]

    vmem = pl.BlockSpec(memory_space=pltpu.VMEM)
    out = pl.pallas_call(
        kernel,
        out_shape=jax.ShapeDtypeStruct(shape, F32),
        in_specs=[pl.BlockSpec(memory_space=pltpu.SMEM)] + [vmem] * parts,
        out_specs=vmem,
        compiler_params=pltpu.CompilerParams(vmem_limit_bytes=4 * MIB),
        cost_estimate=SHORT,
        name="collect",
    )(me.reshape(1), *pieces)
    if not aligned:
        out = out.transpose(1, 0, 2, 3).reshape(count, parts * rows, width)
    return out


def join(upper, mine, other):
    half = mine.shape[1]

    def kernel(upper, mine, other, out, sems):
        copies = [
            pltpu.make_async_copy(source, out.at[:, pl.ds(pl.multiple_of(at * half, half), half)], sems.at[i])
            for i, (source, at) in enumerate(((mine, upper[0]), (other, 1 - upper[0])))
        ]
        for copy in copies:
            copy.start()
        for copy in copies:
            copy.wait()

    anywhere = pl.BlockSpec(memory_space=pl.ANY)
    return pl.pallas_call(
        kernel,
        out_shape=jax.ShapeDtypeStruct((mine.shape[0], 2 * half) + mine.shape[2:], F32),
        in_specs=[pl.BlockSpec(memory_space=pltpu.SMEM), anywhere, anywhere],
        out_specs=anywhere,
        scratch_shapes=[pltpu.SemaphoreType.DMA((2,))],
        compiler_params=pltpu.CompilerParams(vmem_limit_bytes=MIB),
        cost_estimate=pl.CostEstimate(flops=0, bytes_accessed=2_000_000, transcendentals=0),
        name="join",
    )(upper.reshape(1), mine, other)


def body(object_field, probe, amplitudes, positions, counts):
    modes, _, size, _ = probe.shape
    tile_rows, tile_cols = object_field.shape[1:]
    slots = amplitudes.shape[0]
    origin = jnp.stack([lax.axis_index("row") * tile_rows, lax.axis_index("col") * tile_cols]).astype(jnp.int32)
    bits = [1 << k for k in range(lax.axis_size("row").bit_length() - 1)]
    uppers = [(lax.axis_index("row") & bit) // bit for bit in bits]

    def relative(table):
        return jnp.concatenate([table[:, : 2 * slots] - jnp.tile(origin, slots)[None], table[:, 2 * slots :]], axis=1)

    right_up, right_down = cut(
        object_field, ((0, size, size), (size, tile_rows - size, size)), SHORT, "cut_right"
    )
    right_up, right_down, after_right = together(right_up, right_down, object_field)
    right_up = from_behind(right_up, "col", -1)
    right_down = from_behind(right_down, "col", -1)
    (lower,) = cut(after_right, ((0, size, tile_cols),), LONG, "cut_lower")
    meta = jnp.concatenate([positions.reshape(1, 2 * slots), counts.reshape(1, 1)], axis=1)
    lower = from_behind(lower, "row", -1)

    mine = relative(meta)
    note = jnp.pad(meta.astype(F32), ((0, 7), (0, size - meta.shape[1])))
    amplitudes = arrange(mine, amplitudes)
    right_up, amplitudes = together(right_up, amplitudes)
    corner = from_behind(right_up, "row", -1)
    amplitudes, lower = together(amplitudes, lower)
    init = visit_slots(mine, probe, amplitudes, [object_field, lower], [])
    right_up, right_down, corner, *init = together(right_up, right_down, corner, *init)
    own, bottom_spill, top_spill, lower_spill, share = visit_slots(
        mine, probe, amplitudes, [object_field, lower, right_up, right_down, corner], list(init[1:]), [note]
    )

    bottom_spill = from_behind(bottom_spill, "col", 1)
    lower_spill = from_behind(lower_spill, "row", 1)
    start = jnp.zeros((), jnp.int32)
    index = uppers[0]
    send = pick(share, 1 - index)
    for k, (bit, upper) in enumerate(zip(bits, uppers)):
        got = exchange(send, "row", bit)
        start = start + upper * (size >> (k + 1))
        if k + 1 < len(bits):
            send, share = fold(share, index, got, uppers[k + 1])
            index = jnp.zeros((), jnp.int32)
    parts = lax.axis_size("col")
    rows = share.shape[1] // parts
    me = lax.axis_index("col")
    got, bottom_spill = together(got, bottom_spill)
    own_part, *pieces = deal(me, [share, got], parts, rows)
    share = own_part + sum(exchange(piece, "col", k + 1) for k, piece in enumerate(pieces))
    old = lax.dynamic_slice_in_dim(probe.reshape(2 * modes, size, size), start + me * rows, rows, axis=1)
    new = old + share[: 2 * modes] / (share[2 * modes :] + 1.0)
    new, lower_spill = together(new, lower_spill)
    top_spill = from_behind(merge(top_spill, lower_spill), "col", 1)
    new = collect(me, [new] + [exchange(new, "col", k) for k in range(1, parts)])
    new, top_spill = together(new, top_spill)
    width = 2 * slots + 1
    notes = [top_spill[:1, size], lower_spill[:1, size], top_spill[1:, size]]
    table = jnp.concatenate([meta] + [item[:, :width].astype(jnp.int32) for item in notes], axis=0)
    inverse_light = light(relative(table), probe, (tile_rows, tile_cols))
    for bit, upper in reversed(list(zip(bits, uppers))):
        other = exchange(new, "row", bit)
        if bit == bits[-1]:
            new_object = finish(own, init[0], top_spill, bottom_spill, lower_spill, inverse_light, object_field)
            other, new_object = together(other, new_object)
        new = join(upper, new, other)
    return (new_object, new.reshape(modes, 2, size, size))


def solution(mesh):
    in_specs = (
        P(None, "row", "col"),
        P(),
        P(("row", "col"), None, None),
        P(("row", "col"), None),
        P(("row", "col")),
    )
    out_specs = (P(None, "row", "col"), P())
    return jax.shard_map(body, mesh=mesh, in_specs=in_specs, out_specs=out_specs, check_vma=False)
```

```python
import functools
import math

import jax
import jax.numpy as jnp
import ml_dtypes
import numpy as np
from jax import lax
from jax.experimental import pallas as pl
from jax.experimental.pallas import tpu as pltpu
from jax.sharding import PartitionSpec as P

F32 = jnp.float32
BF16 = jnp.bfloat16
MIB = 1024 * 1024
LONG = pl.CostEstimate(flops=30_000_000_000, bytes_accessed=4_000_000, transcendentals=0)
SHORT = pl.CostEstimate(flops=0, bytes_accessed=1_000_000, transcendentals=0)
FLOOR = 0.3


def split_np(table):
    high = table.astype(ml_dtypes.bfloat16)
    low = (table - high.astype(np.float64)).astype(ml_dtypes.bfloat16)
    return high, low


def dft_tables(length):
    half = length // 2
    q = np.arange(half)[:, None]
    n = np.arange(half)[None, :]
    forward = []
    for odd in range(2):
        phase = (n * (2 * q + odd)) % length
        angle = phase * (-2.0 * math.pi / length)
        re = np.cos(angle) / math.sqrt(length)
        im = np.sin(angle) / math.sqrt(length)
        forward.append(np.stack(split_np(np.block([[re, -im], [im, re]]))))
    forward = np.stack(forward)
    return forward, np.ascontiguousarray(forward.transpose(0, 1, 3, 2))


def in_hbm(array):
    return pltpu.with_memory_space_constraint(array, pltpu.HBM)


def dot(a, b):
    return jnp.dot(a, b, preferred_element_type=F32)


def split(x):
    high = x.astype(BF16)
    return high, (x - high.astype(F32)).astype(BF16)


def roll_rows(x, shift):
    return pltpu.roll(x.reshape(x.shape[0] // 8, 8, x.shape[1]), shift, 1)


def roll_rows(x, shift):
    return pltpu.roll(x.reshape(x.shape[0] // 8, 8, x.shape[1]), shift, 1)


def roll_rows(x, shift):
    return pltpu.roll(x.reshape(x.shape[0] // 8, 8, x.shape[1]), shift, 1)


def roll_rows(x, shift):
    return pltpu.roll(x.reshape(x.shape[0] // 8, 8, x.shape[1]), shift, 1)


def split_three(x):
    high = x.astype(BF16)
    rest = x - high.astype(F32)
    middle = rest.astype(BF16)
    return high, middle, (rest - middle.astype(F32)).astype(BF16)


def add_shifted(template, grid, where_t, where_g, top, left, size):
    top_s = top & 7
    top_b = pl.multiple_of(top - top_s, 8)
    left_s = left & 127
    left_b = pl.multiple_of(left - left_s, 128)
    step = 24
    wrapped = lax.broadcasted_iota(jnp.int32, (step, 128), 1) < left_s
    wrapped_rows = lax.broadcasted_iota(jnp.int32, (step // 8, 8, 128), 1) < top_s
    zero = jnp.zeros((step, 128), F32)
    blocks = size // 128
    for at in range(0, size + 8, step):
        parts = []
        for j in range(blocks):
            x = roll_rows(template[where_t + (pl.ds(at, step + 8), pl.ds(128 * j, 128))], top_s)
            x = jnp.where(wrapped_rows, x[:-1], x[1:]).reshape(step, 128)
            parts.append(pltpu.roll(x, left_s, 1))
        for j in range(blocks + 1):
            before = parts[j - 1] if j > 0 else zero
            after = parts[j] if j < blocks else zero
            spot = where_g + (pl.ds(top_b + at, step), pl.ds(left_b + 128 * j, 128))
            grid[spot] += jnp.where(wrapped, before, after)


def take_shifted(field, where, top, left, at, step, size):
    top_s = top & 7
    top_b = pl.multiple_of(top - top_s, 8)
    left_s = left & 127
    left_b = pl.multiple_of(left - left_s, 128)
    back = (128 - left_s) & 127
    keep = lax.broadcasted_iota(jnp.int32, (step + 8, 128), 1) < 128 - left_s
    keep_rows = lax.broadcasted_iota(jnp.int32, (step // 8, 8, 128), 1) < 8 - top_s
    blocks = size // 128
    parts = [
        pltpu.roll(field[where + (pl.ds(top_b + at, step + 8), pl.ds(left_b + 128 * j, 128))], back, 1)
        for j in range(blocks + 1)
    ]
    pieces = []
    for j in range(blocks):
        x = roll_rows(jnp.where(keep, parts[j], parts[j + 1]), (8 - top_s) & 7)
        pieces.append(jnp.where(keep_rows, x[:-1], x[1:]).reshape(step, 128))
    return jnp.concatenate(pieces, axis=1)


def light_kernel(meta, probe_h, inverse_light, probe, template, grid, sem):
    size = probe.shape[2]
    tile_rows, tile_cols = inverse_light.shape
    copy = pltpu.make_async_copy(probe_h, probe, sem.at[0])
    copy.start()
    template[0:8, :] = jnp.zeros((8, size), F32)
    template[8 + size :, :] = jnp.zeros((8, size), F32)
    copy.wait()
    for at in range(0, size, 32):
        rows = pl.ds(at, 32)
        total = jnp.zeros((32, size), F32)
        for m in range(probe.shape[0]):
            total += probe[m, 0, rows] * probe[m, 0, rows] + probe[m, 1, rows] * probe[m, 1, rows]
        template[pl.ds(8 + at, 32), :] = total

    @pl.loop(0, tile_rows // 32)
    def _(step):
        rows = pl.ds(pl.multiple_of(size + step * 32, 32), 32)
        grid[rows, size : size + tile_cols] = jnp.zeros((32, tile_cols), F32)

    slots = meta.shape[1] // 2
    for device in range(4):

        @pl.loop(0, meta[device, 2 * slots])
        def _(slot):
            top = meta[device, 2 * slot] + size
            left = meta[device, 2 * slot + 1] + size

            @pl.when((top > 0) & (left > 0))
            def _():
                add_shifted(template, grid, (), (), top, left, size)

    @pl.loop(0, tile_rows // 32)
    def _(step):
        rows = pl.ds(pl.multiple_of(size + step * 32, 32), 32)
        out_rows = pl.ds(pl.multiple_of(step * 32, 32), 32)
        inverse_light[out_rows, :] = 1.0 / (grid[rows, size : size + tile_cols] + 1.0)


def light(meta, probe, tile_shape):
    size = probe.shape[2]
    vmem = pl.BlockSpec(memory_space=pltpu.VMEM)
    return pl.pallas_call(
        light_kernel,
        out_shape=jax.ShapeDtypeStruct(tile_shape, F32),
        in_specs=[pl.BlockSpec(memory_space=pltpu.SMEM), pl.BlockSpec(memory_space=pltpu.HBM)],
        out_specs=vmem,
        scratch_shapes=[
            pltpu.VMEM(probe.shape, F32),
            pltpu.VMEM((size + 16, size), F32),
            pltpu.VMEM((tile_shape[0] + 2 * size, tile_shape[1] + 2 * size), F32),
            pltpu.SemaphoreType.DMA((1,)),
        ],
        compiler_params=pltpu.CompilerParams(vmem_limit_bytes=8 * MIB),
        cost_estimate=pl.CostEstimate(flops=4_000_000_000, bytes_accessed=1_000_000, transcendentals=0),
        name="light",
    )(meta, in_hbm(probe))


def arrange_kernel(meta, amplitudes, out, given, moved, in_sems, out_sems):
    slots, size, _ = amplitudes.shape
    count = meta[0, 2 * slots]

    def load(slot):
        return pltpu.make_async_copy(amplitudes.at[slot], given.at[slot], in_sems.at[slot])

    def store(slot):
        return pltpu.make_async_copy(moved.at[slot], out.at[slot], out_sems.at[slot])

    @pl.loop(0, count)
    def _(slot):
        load(slot).start()

    first = lax.broadcasted_iota(jnp.int32, (size, size), 0)
    second = lax.broadcasted_iota(jnp.int32, (size, size), 1)
    half = size // 2

    def source(index):
        return jnp.where(index < half, 2 * index, 2 * index - (size - 1))

    rows = (source(first) == second).astype(F32).astype(BF16)
    cols = (source(second) == first).astype(F32).astype(BF16)
    rows = jnp.concatenate([rows, rows], axis=1)
    cols = jnp.concatenate([cols, cols], axis=0)

    @pl.loop(0, count)
    def _(slot):
        load(slot).wait()
        x = dot(rows, jnp.concatenate(split(given[slot]), axis=0))
        moved[slot] = dot(jnp.concatenate(split(x), axis=1), cols)
        store(slot).start()

    @pl.loop(0, count)
    def _(slot):
        store(slot).wait()


def arrange(meta, amplitudes):
    slots = amplitudes.shape[0]
    hbm = pl.BlockSpec(memory_space=pltpu.HBM)
    return pl.pallas_call(
        arrange_kernel,
        out_shape=pltpu.HBM(amplitudes.shape, F32),
        in_specs=[pl.BlockSpec(memory_space=pltpu.SMEM), hbm],
        out_specs=hbm,
        scratch_shapes=[
            pltpu.VMEM(amplitudes.shape, F32),
            pltpu.VMEM(amplitudes.shape, F32),
            pltpu.SemaphoreType.DMA((slots,)),
            pltpu.SemaphoreType.DMA((slots,)),
        ],
        compiler_params=pltpu.CompilerParams(vmem_limit_bytes=8 * MIB),
        cost_estimate=LONG,
        name="arrange",
    )(meta, in_hbm(amplitudes))


def three_left(table, t):
    return jnp.concatenate([table[t, 0], table[t, 0], table[t, 1]], axis=1)


def three_right(table, v):
    return jnp.concatenate([table[v, 0], table[v, 0], table[v, 1]], axis=0)


def weave(first, second):
    total = max(len(first), len(second))
    done = [0, 0]
    for i in range(1, total + 1):
        for k, pieces in enumerate((first, second)):
            while done[k] * total < i * len(pieces):
                pieces[done[k]]()
                done[k] += 1


def slots_kernel(
    needs_rim, meta, probe, amplitudes, sources, forward_h, backward_h, init, note, outs, probe_out,
    ext, grid, amp, forward_t, backward_t, chosen, patch_f, patch_b, x_f, y_f, z_f, g_s, x_b, z_b, back, template, sums, sems,
):
    size = probe.shape[2]
    half = size // 2
    modes = probe.shape[0]
    slots = amplitudes.shape[0]
    tile_rows, tile_cols = (n - size for n in ext.shape[1:])
    step = 32
    fine = 16
    load_sems, amp_sems, out_sems = sems
    sums_out = probe_out
    if not needs_rim:
        probe_out = sums

    regions = (
        (pl.ds(0, tile_rows), pl.ds(0, tile_cols)),
        (pl.ds(tile_rows, size), pl.ds(0, tile_cols)),
        (pl.ds(0, size), pl.ds(tile_cols, size)),
        (pl.ds(size, tile_rows - size), pl.ds(tile_cols, size)),
        (pl.ds(tile_rows, size), pl.ds(tile_cols, size)),
    )
    loads = [
        pltpu.make_async_copy(source, ext.at[:, rows, cols], load_sems.at[i])
        for i, (source, (rows, cols)) in enumerate(zip(sources, regions))
    ]
    loads.append(pltpu.make_async_copy(forward_h, forward_t, load_sems.at[7]))
    loads.append(pltpu.make_async_copy(backward_h, backward_t, load_sems.at[8]))
    late = []
    if needs_rim:
        late.append(pltpu.make_async_copy(init[1], probe_out, load_sems.at[6]))
        below = grid.at[:, pl.ds(tile_rows, size), pl.ds(0, tile_cols)]
        late.append(pltpu.make_async_copy(init[0], below, load_sems.at[5]))
    for load in loads + late:
        load.start()

    def amp_copy(slot):
        return pltpu.make_async_copy(amplitudes.at[slot], amp.at[slot], amp_sems.at[slot])

    def choose(slot, found):
        beyond = meta[0, 2 * slot + 1] + size > tile_cols
        wanted = beyond if needs_rim else jnp.logical_not(beyond)

        @pl.when(wanted)
        def _():
            chosen[found] = slot
            amp_copy(slot).start()

        return found + wanted.astype(jnp.int32)

    count = lax.fori_loop(0, meta[0, 2 * slots], choose, jnp.zeros((), jnp.int32))

    @pl.loop(0, tile_rows // step)
    def _(at):
        rows = pl.ds(pl.multiple_of(at * step, step), step)
        for c in range(2):
            grid[c, rows, :] = jnp.zeros((step, tile_cols + size), F32)

    @pl.loop(tile_rows // step, (tile_rows + size) // step)
    def _(at):
        rows = pl.ds(pl.multiple_of(at * step, step), step)
        for c in range(2):
            if needs_rim:
                grid[c, rows, tile_cols:] = jnp.zeros((step, size), F32)
            else:
                grid[c, rows, :] = jnp.zeros((step, tile_cols + size), F32)

    if not needs_rim:

        @pl.loop(0, size // step)
        def _(at):
            rows = pl.ds(pl.multiple_of(at * step, step), step)
            for c in range(2 * modes + 1):
                probe_out[c, rows, :] = jnp.zeros((step, size), F32)

    for c in range(2):
        template[c, 0:8, :] = jnp.zeros((8, size), F32)
        template[c, 8 + size :, :] = jnp.zeros((8, size), F32)
    for load in loads:
        load.wait()

    def corner(slot):
        return meta[0, 2 * slot], meta[0, 2 * slot + 1]

    def forward(slot):
        top, left = corner(slot)

        def take(at):
            for c in range(2):
                patch_f[c, pl.ds(at, step), :] = take_shifted(ext, (c,), top, left, at, step, size)

        def fold_rows(m, at):
            cols = pl.ds(m * size, size)
            parts = []
            for base in (at, half + at):
                rows = pl.ds(base, fine)
                pr, pi = patch_f[0, rows, :], patch_f[1, rows, :]
                qr, qi = probe[m, 0, rows, :], probe[m, 1, rows, :]
                parts.append((qr * pr - qi * pi, qr * pi + qi * pr))
            for c in range(2):
                rows = pl.ds(c * half + at, fine)
                for t, value in enumerate((parts[0][c] + parts[1][c], parts[0][c] - parts[1][c])):
                    x_f[t, 0, rows, cols], x_f[t, 1, rows, cols] = split(value)

        def dft_rows(m, t):
            cols = pl.ds(m * size, size)
            high = x_f[t, 0, :, cols]
            u = dot(three_left(forward_t, t), jnp.concatenate([high, x_f[t, 1, :, cols], high], axis=0))
            rows = pl.ds(m * size + t * half, half)
            for v, value in enumerate((u[:, :half] + u[:, half:], u[:, :half] - u[:, half:])):
                high, low = split(value)
                for c in range(2):
                    lanes = pl.ds(c * half, half)
                    y_f[v, 0, rows, lanes] = high[c * half : (c + 1) * half]
                    y_f[v, 1, rows, lanes] = low[c * half : (c + 1) * half]

        def dft_cols(v):
            high = y_f[v, 0]
            z_f[v] = dot(jnp.concatenate([high, y_f[v, 1], high], axis=1), three_right(backward_t, v))

        def scale(v, at):
            if v == 0 and at == 0:
                amp_copy(slot).wait()
            waves = [z_f[v, pl.ds(m * size + at, fine), :] for m in range(modes)]
            total = jnp.zeros((fine, half), F32)
            for wave in waves:
                total += wave[:, :half] * wave[:, :half] + wave[:, half:] * wave[:, half:]
            measured = amp[slot, pl.ds(at, fine), pl.ds(v * half, half)]
            factor = measured * lax.rsqrt(jnp.maximum(total, FLOOR * FLOOR)) - 1.0
            factor = jnp.concatenate([factor, factor], axis=1)
            for m in range(modes):
                rows = pl.ds(m * size + at, fine)
                g_s[v, 0, rows, :], g_s[v, 1, rows, :] = split(waves[m] * factor)

        pieces = [(take, at) for at in range(0, size, step)]
        for m in range(modes):
            pieces += [(fold_rows, m, at) for at in range(0, half, fine)]
            pieces += [(dft_rows, m, t) for t in range(2)]
        pieces += [(dft_cols, v) for v in range(2)]
        pieces += [(scale, v, at) for v in range(2) for at in range(0, size, fine)]
        return [functools.partial(*piece) for piece in pieces]

    def backward(slot):
        top, left = corner(slot)

        def dft_cols(v):
            high = g_s[v, 0]
            z_b[v] = dot(jnp.concatenate([high, g_s[v, 1], high], axis=1), three_right(forward_t, v))

        def unfold_cols(m, t, at):
            rows = pl.ds(m * size + t * half + at, step)
            even, odd = z_b[0, rows, :], z_b[1, rows, :]
            for v, value in enumerate((even + odd, even - odd)):
                high, low = split(value)
                cols = pl.ds(m * size + v * half, half)
                for c in range(2):
                    spot = pl.ds(c * half + at, step)
                    x_b[t, 0, spot, cols] = high[:, c * half : (c + 1) * half]
                    x_b[t, 1, spot, cols] = low[:, c * half : (c + 1) * half]

        def dft_rows(m, t):
            cols = pl.ds(m * size, size)
            high = x_b[t, 0, :, cols]
            back[m, t] = dot(three_left(backward_t, t), jnp.concatenate([high, x_b[t, 1, :, cols], high], axis=0))

        def gradients(at):
            waves = []
            for m in range(modes):
                pair = []
                for c in range(2):
                    rows = pl.ds(c * half + at, fine)
                    even, odd = back[m, 0, rows, :], back[m, 1, rows, :]
                    pair.append((even + odd, even - odd))
                waves.append(pair)
            for h in range(2):
                rows = pl.ds(h * half + at, fine)
                pr, pi = patch_b[0, rows, :], patch_b[1, rows, :]
                grad_r = jnp.zeros((fine, size), F32)
                grad_i = jnp.zeros((fine, size), F32)
                for m in range(modes):
                    br, bi = waves[m][0][h], waves[m][1][h]
                    qr, qi = probe[m, 0, rows, :], probe[m, 1, rows, :]
                    grad_r += qr * br + qi * bi
                    grad_i += qr * bi - qi * br
                    probe_out[2 * m, rows, :] += pr * br + pi * bi
                    probe_out[2 * m + 1, rows, :] += pr * bi - pi * br
                probe_out[2 * modes, rows, :] += pr * pr + pi * pi
                spot = pl.ds(8 + h * half + at, fine)
                template[0, spot, :] = grad_r
                template[1, spot, :] = grad_i

        def add(c):
            add_shifted(template, grid, (c,), (c,), top, left, size)

        pieces = [(dft_cols, v) for v in range(2)]
        for m in range(modes):
            pieces += [(unfold_cols, m, t, at) for t in range(2) for at in range(0, half, step)]
            pieces += [(dft_rows, m, t) for t in range(2)]
        pieces += [(gradients, at) for at in range(0, half, fine)]
        pieces += [(add, c) for c in range(2)]
        return [functools.partial(*piece) for piece in pieces]

    def hand_over():
        for at in range(0, size, step):
            for c in range(2):
                patch_b[c, pl.ds(at, step), :] = patch_f[c, pl.ds(at, step), :]

    @pl.when(count > 0)
    def _():
        weave(forward(chosen[0]), [])
        hand_over()
        for load in late:
            load.wait()

        def visit(index, _):
            weave(backward(chosen[index]), forward(chosen[index + 1]))
            hand_over()
            return 0

        lax.fori_loop(0, count - 1, visit, 0)
        weave(backward(chosen[count - 1]), [])

    @pl.when(count == 0)
    def _():
        for load in late:
            load.wait()

    if needs_rim:
        top, bottom, rest = pl.ds(0, size), pl.ds(size, tile_rows - size), pl.ds(tile_cols, size)
        note_rows = pl.ds(size, 8)
        parts = [
            grid.at[:, pl.ds(0, tile_rows), pl.ds(0, tile_cols)],
            grid.at[:, bottom, rest],
            grid.at[:, top, rest],
            grid.at[:, pl.ds(tile_rows, size), :],
            note[0],
            note[0],
            probe_out.at[:, pl.ds(pl.multiple_of(meta[0, 2 * slots + 1] * half, half), half)],
        ]
        outs = [
            outs[0],
            outs[1],
            outs[2].at[:, top],
            outs[3].at[:, top],
            outs[2].at[0, note_rows],
            outs[3].at[0, note_rows, pl.ds(0, size)],
            outs[4],
        ]
    else:
        parts = [
            grid.at[:, pl.ds(0, tile_rows), pl.ds(0, tile_cols)],
            grid.at[:, pl.ds(tile_rows, size), pl.ds(0, tile_cols)],
            sums,
        ]
        outs = [*outs, sums_out]
    stores = [pltpu.make_async_copy(part, out, out_sems.at[i]) for i, (part, out) in enumerate(zip(parts, outs))]
    for store in stores:
        store.start()
    for store in stores:
        store.wait()


def visit_slots(meta, probe, amplitudes, sources, init, note=()):
    size = probe.shape[2]
    modes = probe.shape[0]
    slots = amplitudes.shape[0]
    rows, cols = sources[0].shape[1:]
    tables = [jnp.asarray(item) for item in dft_tables(size)]
    vmem = pl.BlockSpec(memory_space=pltpu.VMEM)
    anywhere = pl.BlockSpec(memory_space=pl.ANY)
    hbm = pl.BlockSpec(memory_space=pltpu.HBM)
    needs_rim = bool(init)
    if needs_rim:
        shapes = [
            (2, rows, cols),
            (2, rows - size, size),
            (2, size + 8, size),
            (2, size + 8, cols + size),
            (2 * modes + 1, size // 2, size),
        ]
    else:
        shapes = [(2, rows, cols), (2, size, cols)]
    splits = np.cumsum([1, 1, 1, len(sources), 1, 1, len(init), len(note), len(shapes), 1])

    def kernel(*refs):
        meta, probe, amplitudes, sources, forward_t, backward_t, init, note, outs, probe_out = (
            refs[a:b] for a, b in zip([0, *splits[:-1]], splits)
        )
        scratch = refs[splits[-1] :]
        slots_kernel(
            needs_rim, meta[0], probe[0], amplitudes[0], sources, forward_t[0], backward_t[0], init, note, outs,
            probe_out[0], *scratch[:-3], scratch[-3:],
        )

    return pl.pallas_call(
        kernel,
        out_shape=[pltpu.HBM(shapes[0], F32)]
        + [(jax.ShapeDtypeStruct if needs_rim else pltpu.HBM)(shape, F32) for shape in shapes[1:]]
        + [(jax.ShapeDtypeStruct if needs_rim else pltpu.HBM)((2 * modes + 1, size, size), F32)],
        in_specs=[pl.BlockSpec(memory_space=pltpu.SMEM), vmem, hbm, hbm] + [anywhere] * (len(sources) - 1)
        + [hbm] * (2 + len(init)) + [anywhere] * len(note),
        out_specs=[hbm] + [anywhere if needs_rim else hbm] * (len(shapes) - 1) + [vmem if needs_rim else hbm],
        scratch_shapes=[
            pltpu.VMEM((2, rows + size, cols + size), F32),
            pltpu.VMEM((2, rows + size, cols + size), F32),
            pltpu.VMEM(amplitudes.shape, F32),
            pltpu.VMEM(tables[0].shape, BF16),
            pltpu.VMEM(tables[1].shape, BF16),
            pltpu.SMEM((slots,), jnp.int32),
            pltpu.VMEM((2, size, size), F32),
            pltpu.VMEM((2, size, size), F32),
            pltpu.VMEM((2, 2, size, modes * size), BF16),
            pltpu.VMEM((2, 2, modes * size, size), BF16),
            pltpu.VMEM((2, modes * size, size), F32),
            pltpu.VMEM((2, 2, modes * size, size), BF16),
            pltpu.VMEM((2, 2, size, modes * size), BF16),
            pltpu.VMEM((2, modes * size, size), F32),
            pltpu.VMEM((modes, 2, size, size), F32),
            pltpu.VMEM((2, size + 16, size), F32),
            pltpu.VMEM((8, 128) if needs_rim else (2 * modes + 1, size, size), F32),
            pltpu.SemaphoreType.DMA((9,)),
            pltpu.SemaphoreType.DMA((slots,)),
            pltpu.SemaphoreType.DMA((7,)),
        ],
        compiler_params=pltpu.CompilerParams(vmem_limit_bytes=26 * MIB),
        cost_estimate=pl.CostEstimate(flops=12_000_000_000, bytes_accessed=16_000_000, transcendentals=0),
        name="slots_beyond" if needs_rim else "slots_inside",
    )(
        meta, probe, *map(in_hbm, [amplitudes, sources[0]]), *sources[1:], *map(in_hbm, [*tables, *init]), *note
    )


def finish_kernel(
    own, first, top, bottom, lower, scale, tile, out, own_s, first_s, right_s, lower_s, scale_s, tile_s, in_sems, out_sems
):
    size = right_s.shape[2]
    block = 128
    blocks = own_s.shape[1] // block

    def copies(i):
        rows = pl.ds(i * block, block)
        pairs = [
            (own.at[:, rows], own_s.at[:, rows]),
            (first.at[:, rows], first_s.at[:, rows]),
            (scale.at[rows], scale_s.at[rows]),
            (tile.at[:, rows], tile_s.at[:, rows]),
        ]
        if i < size // block:
            pairs.append((top.at[:, rows], right_s.at[:, rows]))
            pairs.append((lower.at[:, rows, pl.ds(0, lower_s.shape[2])], lower_s.at[:, rows]))
        else:
            pairs.append((bottom.at[:, pl.ds(i * block - size, block)], right_s.at[:, rows]))
        return [pltpu.make_async_copy(a, b, in_sems.at[i, k]) for k, (a, b) in enumerate(pairs)]

    loads = [copies(i) for i in range(blocks)]
    for load in loads:
        for copy in load:
            copy.start()
    stores = []
    for i in range(blocks):
        for copy in loads[i]:
            copy.wait()
        rows = pl.ds(i * block, block)
        for at in range(i * block, (i + 1) * block, 32):
            part = pl.ds(at, 32)
            for c in range(2):
                near = own_s[c, part, :size] + first_s[c, part, :size] + right_s[c, part, :]
                far = own_s[c, part, size:] + first_s[c, part, size:]
                if i < size // block:
                    near, far = near + lower_s[c, part, :size], far + lower_s[c, part, size:]
                own_s[c, part, :size] = tile_s[c, part, :size] + near * scale_s[part, :size]
                own_s[c, part, size:] = tile_s[c, part, size:] + far * scale_s[part, size:]
        stores.append(pltpu.make_async_copy(own_s.at[:, rows], out.at[:, rows], out_sems.at[i]))
        stores[-1].start()
    for store in stores:
        store.wait()


def finish(own, first, top, bottom, lower, inverse_light, tile):
    rows, cols = tile.shape[1:]
    size = top.shape[2]
    hbm = pl.BlockSpec(memory_space=pltpu.HBM)
    return pl.pallas_call(
        finish_kernel,
        out_shape=jax.ShapeDtypeStruct(tile.shape, F32),
        in_specs=[hbm] * 2 + [pl.BlockSpec(memory_space=pl.ANY)] * 4 + [hbm],
        out_specs=hbm,
        scratch_shapes=[
            pltpu.VMEM(tile.shape, F32),
            pltpu.VMEM(tile.shape, F32),
            pltpu.VMEM((2, rows, size), F32),
            pltpu.VMEM((2, size, cols), F32),
            pltpu.VMEM((rows, cols), F32),
            pltpu.VMEM(tile.shape, F32),
            pltpu.SemaphoreType.DMA((rows // 128, 6)),
            pltpu.SemaphoreType.DMA((rows // 128,)),
        ],
        compiler_params=pltpu.CompilerParams(vmem_limit_bytes=12 * MIB),
        cost_estimate=pl.CostEstimate(flops=3_000_000, bytes_accessed=12_000_000, transcendentals=0),
        name="finish",
    )(in_hbm(own), in_hbm(first), top, bottom, lower, inverse_light, in_hbm(tile))


def from_behind(array, axis, by):
    count = lax.axis_size(axis)
    pairs = [(i, i + by) for i in range(count) if 0 <= i + by < count]
    return lax.ppermute(array, axis, pairs)


def exchange(array, axis, bit):
    count = lax.axis_size(axis)
    return lax.ppermute(array, axis, [(i, i ^ bit) for i in range(count)])


def together(*arrays):
    return lax.optimization_barrier(arrays)


def cut(tile, regions, cost, name):
    def kernel(tile, *refs):
        sems = refs[-1]
        copies = [
            pltpu.make_async_copy(tile.at[:, pl.ds(at, height), pl.ds(0, width)], out, sems.at[i])
            for i, ((at, height, width), out) in enumerate(zip(regions, refs[:-1]))
        ]
        for copy in copies:
            copy.start()
        for copy in copies:
            copy.wait()

    return pl.pallas_call(
        kernel,
        out_shape=[jax.ShapeDtypeStruct((2, height, width), F32) for _, height, width in regions],
        in_specs=[pl.BlockSpec(memory_space=pltpu.HBM)],
        out_specs=[pl.BlockSpec(memory_space=pltpu.VMEM)] * len(regions),
        scratch_shapes=[pltpu.SemaphoreType.DMA((len(regions),))],
        compiler_params=pltpu.CompilerParams(vmem_limit_bytes=4 * MIB),
        cost_estimate=cost,
        name=name,
    )(in_hbm(tile))


def fold(mine, index, got, upper):
    count, half, width = got.shape
    quarter = half // 2

    def kernel(place, mine, got, send, keep):
        for k, out in ((1 - place[1], send), (place[1], keep)):
            for c in range(count):
                out[c] = (
                    mine[c, pl.ds(pl.multiple_of(place[0] * half + k * quarter, quarter), quarter), :]
                    + got[c, pl.ds(pl.multiple_of(k * quarter, quarter), quarter), :]
                )

    vmem = pl.BlockSpec(memory_space=pltpu.VMEM)
    shape = jax.ShapeDtypeStruct((count, quarter, width), F32)
    return pl.pallas_call(
        kernel,
        out_shape=[shape, shape],
        in_specs=[pl.BlockSpec(memory_space=pltpu.SMEM), vmem, vmem],
        out_specs=[vmem, vmem],
        compiler_params=pltpu.CompilerParams(vmem_limit_bytes=6 * MIB),
        cost_estimate=SHORT,
        name="fold",
    )(jnp.stack([index, upper]), mine, got)


def merge(right, lower):
    _, height, size = right.shape
    rows = height - 8
    cols = lower.shape[2] - size

    def kernel(right, lower, out, corner, sems):
        copies = [
            pltpu.make_async_copy(lower.at[:, pl.ds(0, rows), pl.ds(cols, size)], corner, sems.at[0]),
            pltpu.make_async_copy(lower.at[0, pl.ds(rows, 8), pl.ds(0, size)], out.at[1, pl.ds(rows, 8)], sems.at[1]),
        ]
        for copy in copies:
            copy.start()
        out[0, rows:, :] = right[0, rows:, :]
        for copy in copies:
            copy.wait()
        for c in range(2):
            out[c, :rows, :] = right[c, :rows, :] + corner[c]

    vmem = pl.BlockSpec(memory_space=pltpu.VMEM)
    return pl.pallas_call(
        kernel,
        out_shape=jax.ShapeDtypeStruct(right.shape, F32),
        in_specs=[vmem, pl.BlockSpec(memory_space=pl.ANY)],
        out_specs=vmem,
        scratch_shapes=[pltpu.VMEM((2, rows, size), F32), pltpu.SemaphoreType.DMA((2,))],
        compiler_params=pltpu.CompilerParams(vmem_limit_bytes=4 * MIB),
        cost_estimate=SHORT,
        name="merge",
    )(right, lower)


def deal(me, terms, parts, rows):
    aligned = rows % 8 == 0
    if not aligned:
        count, _, width = terms[0].shape
        terms = [sum(terms).reshape(count, parts, rows, width).transpose(1, 0, 2, 3)]
    count, width = terms[0].shape[0 if aligned else 1], terms[0].shape[-1]

    def kernel(me, *refs):
        terms, outs = refs[:-parts], refs[-parts:]
        for k, out in enumerate(outs):
            j = me[0] ^ k
            for c in range(count):
                if aligned:
                    spot = pl.ds(pl.multiple_of(j * rows, rows), rows)
                    out[c] = sum(term[c, spot, :] for term in terms)
                else:
                    out[c] = terms[0][j, c]

    vmem = pl.BlockSpec(memory_space=pltpu.VMEM)
    return pl.pallas_call(
        kernel,
        out_shape=[jax.ShapeDtypeStruct((count, rows, width), F32)] * parts,
        in_specs=[pl.BlockSpec(memory_space=pltpu.SMEM)] + [vmem] * len(terms),
        out_specs=[vmem] * parts,
        compiler_params=pltpu.CompilerParams(vmem_limit_bytes=4 * MIB),
        cost_estimate=SHORT,
        name="deal",
    )(me.reshape(1), *terms)


def collect(me, pieces):
    count, rows, width = pieces[0].shape
    parts = len(pieces)
    aligned = rows % 8 == 0
    shape = (count, parts * rows, width) if aligned else (parts, count, rows, width)

    def kernel(me, *refs):
        pieces, out = refs[:-1], refs[-1]
        for k, piece in enumerate(pieces):
            j = me[0] ^ k
            for c in range(count):
                if aligned:
                    out[c, pl.ds(pl.multiple_of(j * rows, rows), rows), :] = piece[c]
                else:
                    out[j, c] = piece[c]

    vmem = pl.BlockSpec(memory_space=pltpu.VMEM)
    out = pl.pallas_call(
        kernel,
        out_shape=jax.ShapeDtypeStruct(shape, F32),
        in_specs=[pl.BlockSpec(memory_space=pltpu.SMEM)] + [vmem] * parts,
        out_specs=vmem,
        compiler_params=pltpu.CompilerParams(vmem_limit_bytes=4 * MIB),
        cost_estimate=SHORT,
        name="collect",
    )(me.reshape(1), *pieces)
    if not aligned:
        out = out.transpose(1, 0, 2, 3).reshape(count, parts * rows, width)
    return out


def join(upper, mine, other):
    half = mine.shape[1]

    def kernel(upper, mine, other, out, sems):
        copies = [
            pltpu.make_async_copy(source, out.at[:, pl.ds(pl.multiple_of(at * half, half), half)], sems.at[i])
            for i, (source, at) in enumerate(((mine, upper[0]), (other, 1 - upper[0])))
        ]
        for copy in copies:
            copy.start()
        for copy in copies:
            copy.wait()

    anywhere = pl.BlockSpec(memory_space=pl.ANY)
    return pl.pallas_call(
        kernel,
        out_shape=jax.ShapeDtypeStruct((mine.shape[0], 2 * half) + mine.shape[2:], F32),
        in_specs=[pl.BlockSpec(memory_space=pltpu.SMEM), anywhere, anywhere],
        out_specs=anywhere,
        scratch_shapes=[pltpu.SemaphoreType.DMA((2,))],
        compiler_params=pltpu.CompilerParams(vmem_limit_bytes=MIB),
        cost_estimate=pl.CostEstimate(flops=0, bytes_accessed=2_000_000, transcendentals=0),
        name="join",
    )(upper.reshape(1), mine, other)


def body(object_field, probe, amplitudes, positions, counts):
    modes, _, size, _ = probe.shape
    tile_rows, tile_cols = object_field.shape[1:]
    slots = amplitudes.shape[0]
    origin = jnp.stack([lax.axis_index("row") * tile_rows, lax.axis_index("col") * tile_cols]).astype(jnp.int32)
    bits = [1 << k for k in range(lax.axis_size("row").bit_length() - 1)]
    uppers = [(lax.axis_index("row") & bit) // bit for bit in bits]

    def relative(table):
        return jnp.concatenate([table[:, : 2 * slots] - jnp.tile(origin, slots)[None], table[:, 2 * slots :]], axis=1)

    right_up, right_down = cut(
        object_field, ((0, size, size), (size, tile_rows - size, size)), SHORT, "cut_right"
    )
    right_up, right_down, after_right = together(right_up, right_down, object_field)
    right_up = from_behind(right_up, "col", -1)
    right_down = from_behind(right_down, "col", -1)
    (lower,) = cut(after_right, ((0, size, tile_cols),), LONG, "cut_lower")
    meta = jnp.concatenate([positions.reshape(1, 2 * slots), counts.reshape(1, 1)], axis=1)
    lower = from_behind(lower, "row", -1)

    mine = jnp.concatenate([relative(meta), (1 - uppers[0]).astype(jnp.int32).reshape(1, 1)], axis=1)
    note = jnp.pad(meta.astype(F32), ((0, 7), (0, size - meta.shape[1])))
    amplitudes = arrange(mine, amplitudes)
    right_up, amplitudes = together(right_up, amplitudes)
    corner = from_behind(right_up, "row", -1)
    amplitudes, lower = together(amplitudes, lower)
    init = visit_slots(mine, probe, amplitudes, [object_field, lower], [])
    right_up, right_down, corner, *init = together(right_up, right_down, corner, *init)
    own, bottom_spill, top_spill, lower_spill, send, share = visit_slots(
        mine, probe, amplitudes, [object_field, lower, right_up, right_down, corner], list(init[1:]), [note]
    )

    start = jnp.zeros((), jnp.int32)
    index = uppers[0]
    for k, (bit, upper) in enumerate(zip(bits, uppers)):
        got = exchange(send, "row", bit)
        start = start + upper * (size >> (k + 1))
        if k + 1 < len(bits):
            send, share = fold(share, index, got, uppers[k + 1])
            index = jnp.zeros((), jnp.int32)
        if k == 0:
            bottom_spill = from_behind(bottom_spill, "col", 1)
            send, share, lower_spill = together(send, share, lower_spill)
            lower_spill = from_behind(lower_spill, "row", 1)
    parts = lax.axis_size("col")
    rows = share.shape[1] // parts
    me = lax.axis_index("col")
    got, bottom_spill = together(got, bottom_spill)
    own_part, *pieces = deal(me, [share, got], parts, rows)
    share = own_part + sum(exchange(piece, "col", k + 1) for k, piece in enumerate(pieces))
    old = lax.dynamic_slice_in_dim(probe.reshape(2 * modes, size, size), start + me * rows, rows, axis=1)
    new = old + share[: 2 * modes] / (share[2 * modes :] + 1.0)
    new, lower_spill = together(new, lower_spill)
    top_spill = from_behind(merge(top_spill, lower_spill), "col", 1)
    new = collect(me, [new] + [exchange(new, "col", k) for k in range(1, parts)])
    new, top_spill = together(new, top_spill)
    width = 2 * slots + 1
    notes = [top_spill[:1, size], lower_spill[:1, size], top_spill[1:, size]]
    table = jnp.concatenate([meta] + [item[:, :width].astype(jnp.int32) for item in notes], axis=0)
    inverse_light = light(relative(table), probe, (tile_rows, tile_cols))
    for bit, upper in reversed(list(zip(bits, uppers))):
        if bit == bits[0]:
            new, own = together(new, own)
            new_object = finish(own, init[0], top_spill, bottom_spill, lower_spill, inverse_light, object_field)
        other = exchange(new, "row", bit)
        if bit == bits[-1]:
            other, inverse_light = together(other, inverse_light)
        if bit == bits[0]:
            other, new_object = together(other, new_object)
        new = join(upper, new, other)
    return (new_object, new.reshape(modes, 2, size, size))


def solution(mesh):
    in_specs = (
        P(None, "row", "col"),
        P(),
        P(("row", "col"), None, None),
        P(("row", "col"), None),
        P(("row", "col")),
    )
    out_specs = (P(None, "row", "col"), P())
    return jax.shard_map(body, mesh=mesh, in_specs=in_specs, out_specs=out_specs, check_vma=False)
```

```python
import functools
import math

import jax
import jax.numpy as jnp
import ml_dtypes
import numpy as np
from jax import lax
from jax.experimental import pallas as pl
from jax.experimental.pallas import tpu as pltpu
from jax.sharding import PartitionSpec as P

F32 = jnp.float32
BF16 = jnp.bfloat16
MIB = 1024 * 1024
LONG = pl.CostEstimate(flops=30_000_000_000, bytes_accessed=4_000_000, transcendentals=0)
SHORT = pl.CostEstimate(flops=0, bytes_accessed=1_000_000, transcendentals=0)
FLOOR = 0.3


def split_np(table):
    high = table.astype(ml_dtypes.bfloat16)
    low = (table - high.astype(np.float64)).astype(ml_dtypes.bfloat16)
    return high, low


def dft_tables(length):
    half = length // 2
    q = np.arange(half)[:, None]
    n = np.arange(half)[None, :]
    forward = []
    for odd in range(2):
        phase = (n * (2 * q + odd)) % length
        angle = phase * (-2.0 * math.pi / length)
        re = np.cos(angle) / math.sqrt(length)
        im = np.sin(angle) / math.sqrt(length)
        forward.append(np.stack(split_np(np.block([[re, -im], [im, re]]))))
    forward = np.stack(forward)
    return forward, np.ascontiguousarray(forward.transpose(0, 1, 3, 2))


def in_hbm(array):
    return pltpu.with_memory_space_constraint(array, pltpu.HBM)


def dot(a, b):
    return jnp.dot(a, b, preferred_element_type=F32)


def split(x):
    high = x.astype(BF16)
    return high, (x - high.astype(F32)).astype(BF16)


def roll_rows(x, shift):
    return pltpu.roll(x.reshape(x.shape[0] // 8, 8, x.shape[1]), shift, 1)


def roll_rows(x, shift):
    return pltpu.roll(x.reshape(x.shape[0] // 8, 8, x.shape[1]), shift, 1)


def roll_rows(x, shift):
    return pltpu.roll(x.reshape(x.shape[0] // 8, 8, x.shape[1]), shift, 1)


def roll_rows(x, shift):
    return pltpu.roll(x.reshape(x.shape[0] // 8, 8, x.shape[1]), shift, 1)


def split_three(x):
    high = x.astype(BF16)
    rest = x - high.astype(F32)
    middle = rest.astype(BF16)
    return high, middle, (rest - middle.astype(F32)).astype(BF16)


def add_shifted(template, grid, where_t, where_g, top, left, size):
    top_s = top & 7
    top_b = pl.multiple_of(top - top_s, 8)
    left_s = left & 127
    left_b = pl.multiple_of(left - left_s, 128)
    step = 24
    wrapped = lax.broadcasted_iota(jnp.int32, (step, 128), 1) < left_s
    wrapped_rows = lax.broadcasted_iota(jnp.int32, (step // 8, 8, 128), 1) < top_s
    zero = jnp.zeros((step, 128), F32)
    blocks = size // 128
    for at in range(0, size + 8, step):
        parts = []
        for j in range(blocks):
            x = roll_rows(template[where_t + (pl.ds(at, step + 8), pl.ds(128 * j, 128))], top_s)
            x = jnp.where(wrapped_rows, x[:-1], x[1:]).reshape(step, 128)
            parts.append(pltpu.roll(x, left_s, 1))
        for j in range(blocks + 1):
            before = parts[j - 1] if j > 0 else zero
            after = parts[j] if j < blocks else zero
            spot = where_g + (pl.ds(top_b + at, step), pl.ds(left_b + 128 * j, 128))
            grid[spot] += jnp.where(wrapped, before, after)


def take_shifted(field, where, top, left, at, step, size):
    top_s = top & 7
    top_b = pl.multiple_of(top - top_s, 8)
    left_s = left & 127
    left_b = pl.multiple_of(left - left_s, 128)
    back = (128 - left_s) & 127
    keep = lax.broadcasted_iota(jnp.int32, (step + 8, 128), 1) < 128 - left_s
    keep_rows = lax.broadcasted_iota(jnp.int32, (step // 8, 8, 128), 1) < 8 - top_s
    blocks = size // 128
    parts = [
        pltpu.roll(field[where + (pl.ds(top_b + at, step + 8), pl.ds(left_b + 128 * j, 128))], back, 1)
        for j in range(blocks + 1)
    ]
    pieces = []
    for j in range(blocks):
        x = roll_rows(jnp.where(keep, parts[j], parts[j + 1]), (8 - top_s) & 7)
        pieces.append(jnp.where(keep_rows, x[:-1], x[1:]).reshape(step, 128))
    return jnp.concatenate(pieces, axis=1)


def light_kernel(slots, origin, meta, probe_h, top, corner, inverse_light, probe, template, grid, notes, sems):
    size = probe.shape[2]
    tile_rows, tile_cols = inverse_light.shape
    rows = pl.ds(top.shape[1] - 8, 8)
    cols = pl.ds(0, 128)
    copies = [
        pltpu.make_async_copy(top.at[0, rows, cols], notes.at[0], sems.at[0]),
        pltpu.make_async_copy(corner.at[0, rows, cols], notes.at[1], sems.at[1]),
        pltpu.make_async_copy(top.at[1, rows, cols], notes.at[2], sems.at[2]),
    ]
    copy = pltpu.make_async_copy(probe_h, probe, sems.at[3])
    copy.start()
    for item in copies:
        item.start()
    template[0:8, :] = jnp.zeros((8, size), F32)
    template[8 + size :, :] = jnp.zeros((8, size), F32)
    copy.wait()
    for at in range(0, size, 32):
        rows = pl.ds(at, 32)
        total = jnp.zeros((32, size), F32)
        for m in range(probe.shape[0]):
            total += probe[m, 0, rows] * probe[m, 0, rows] + probe[m, 1, rows] * probe[m, 1, rows]
        template[pl.ds(8 + at, 32), :] = total

    @pl.loop(0, tile_rows // 32)
    def _(step):
        rows = pl.ds(pl.multiple_of(size + step * 32, 32), 32)
        grid[rows, size : size + tile_cols] = jnp.zeros((32, tile_cols), F32)

    def add(top, left):
        @pl.when((top > 0) & (left > 0))
        def _():
            add_shifted(template, grid, (), (), top, left, size)

    @pl.loop(0, meta[0, 2 * slots])
    def _(slot):
        add(meta[0, 2 * slot] + size, meta[0, 2 * slot + 1] + size)

    for item in copies:
        item.wait()
    for device in range(3):

        @pl.loop(0, notes[device, 0, 2 * slots].astype(jnp.int32))
        def _(slot):
            top = notes[device, 0, 2 * slot].astype(jnp.int32) - meta[0, origin]
            left = notes[device, 0, 2 * slot + 1].astype(jnp.int32) - meta[0, origin + 1]
            add(top + size, left + size)

    @pl.loop(0, tile_rows // 32)
    def _(step):
        rows = pl.ds(pl.multiple_of(size + step * 32, 32), 32)
        out_rows = pl.ds(pl.multiple_of(step * 32, 32), 32)
        inverse_light[out_rows, :] = 1.0 / (grid[rows, size : size + tile_cols] + 1.0)


def light(meta, slots, origin, probe, top, corner, tile_shape):
    size = probe.shape[2]
    hbm = pl.BlockSpec(memory_space=pltpu.HBM)
    anywhere = pl.BlockSpec(memory_space=pl.ANY)
    return pl.pallas_call(
        functools.partial(light_kernel, slots, origin),
        out_shape=jax.ShapeDtypeStruct(tile_shape, F32),
        in_specs=[pl.BlockSpec(memory_space=pltpu.SMEM), hbm, anywhere, anywhere],
        out_specs=pl.BlockSpec(memory_space=pltpu.VMEM),
        scratch_shapes=[
            pltpu.VMEM(probe.shape, F32),
            pltpu.VMEM((size + 16, size), F32),
            pltpu.VMEM((tile_shape[0] + 2 * size, tile_shape[1] + 2 * size), F32),
            pltpu.SMEM((3, 8, 128), F32),
            pltpu.SemaphoreType.DMA((4,)),
        ],
        compiler_params=pltpu.CompilerParams(vmem_limit_bytes=8 * MIB),
        cost_estimate=pl.CostEstimate(flops=4_000_000_000, bytes_accessed=1_000_000, transcendentals=0),
        name="light",
    )(meta, in_hbm(probe), top, corner)


def arrange_kernel(meta, amplitudes, out, given, moved, in_sems, out_sems):
    slots, size, _ = amplitudes.shape
    count = meta[0, 2 * slots]

    def load(slot):
        return pltpu.make_async_copy(amplitudes.at[slot], given.at[slot], in_sems.at[slot])

    def store(slot):
        return pltpu.make_async_copy(moved.at[slot], out.at[slot], out_sems.at[slot])

    @pl.loop(0, count)
    def _(slot):
        load(slot).start()

    first = lax.broadcasted_iota(jnp.int32, (size, size), 0)
    second = lax.broadcasted_iota(jnp.int32, (size, size), 1)
    half = size // 2

    def source(index):
        return jnp.where(index < half, 2 * index, 2 * index - (size - 1))

    rows = (source(first) == second).astype(F32).astype(BF16)
    cols = (source(second) == first).astype(F32).astype(BF16)
    rows = jnp.concatenate([rows, rows], axis=1)
    cols = jnp.concatenate([cols, cols], axis=0)

    @pl.loop(0, count)
    def _(slot):
        load(slot).wait()
        x = dot(rows, jnp.concatenate(split(given[slot]), axis=0))
        moved[slot] = dot(jnp.concatenate(split(x), axis=1), cols)
        store(slot).start()

    @pl.loop(0, count)
    def _(slot):
        store(slot).wait()


def arrange(meta, amplitudes):
    slots = amplitudes.shape[0]
    hbm = pl.BlockSpec(memory_space=pltpu.HBM)
    return pl.pallas_call(
        arrange_kernel,
        out_shape=pltpu.HBM(amplitudes.shape, F32),
        in_specs=[pl.BlockSpec(memory_space=pltpu.SMEM), hbm],
        out_specs=hbm,
        scratch_shapes=[
            pltpu.VMEM(amplitudes.shape, F32),
            pltpu.VMEM(amplitudes.shape, F32),
            pltpu.SemaphoreType.DMA((slots,)),
            pltpu.SemaphoreType.DMA((slots,)),
        ],
        compiler_params=pltpu.CompilerParams(vmem_limit_bytes=8 * MIB),
        cost_estimate=LONG,
        name="arrange",
    )(meta, in_hbm(amplitudes))


def three_left(table, t):
    return jnp.concatenate([table[t, 0], table[t, 0], table[t, 1]], axis=1)


def three_right(table, v):
    return jnp.concatenate([table[v, 0], table[v, 0], table[v, 1]], axis=0)


def weave(first, second):
    total = max(len(first), len(second))
    done = [0, 0]
    for i in range(1, total + 1):
        for k, pieces in enumerate((first, second)):
            while done[k] * total < i * len(pieces):
                pieces[done[k]]()
                done[k] += 1


def slots_kernel(
    needs_rim, meta, probe, amplitudes, sources, forward_h, backward_h, init, note, outs, probe_out,
    ext, grid, amp, forward_t, backward_t, chosen, patch_f, patch_b, x_f, y_f, z_f, g_s, x_b, z_b, back, template, sums, sems,
):
    size = probe.shape[2]
    half = size // 2
    modes = probe.shape[0]
    slots = amplitudes.shape[0]
    tile_rows, tile_cols = (n - size for n in ext.shape[1:])
    step = 32
    fine = 16
    load_sems, amp_sems, out_sems = sems
    sums_out = probe_out
    if not needs_rim:
        probe_out = sums

    regions = (
        (pl.ds(0, tile_rows), pl.ds(0, tile_cols)),
        (pl.ds(tile_rows, size), pl.ds(0, tile_cols)),
        (pl.ds(0, size), pl.ds(tile_cols, size)),
        (pl.ds(size, tile_rows - size), pl.ds(tile_cols, size)),
        (pl.ds(tile_rows, size), pl.ds(tile_cols, size)),
    )
    loads = [
        pltpu.make_async_copy(source, ext.at[:, rows, cols], load_sems.at[i])
        for i, (source, (rows, cols)) in enumerate(zip(sources, regions))
    ]
    loads.append(pltpu.make_async_copy(forward_h, forward_t, load_sems.at[7]))
    loads.append(pltpu.make_async_copy(backward_h, backward_t, load_sems.at[8]))
    late = []
    if needs_rim:
        late.append(pltpu.make_async_copy(init[1], probe_out, load_sems.at[6]))
        below = grid.at[:, pl.ds(tile_rows, size), pl.ds(0, tile_cols)]
        late.append(pltpu.make_async_copy(init[0], below, load_sems.at[5]))
    for load in loads + late:
        load.start()

    def amp_copy(slot):
        return pltpu.make_async_copy(amplitudes.at[slot], amp.at[slot], amp_sems.at[slot])

    def choose(slot, found):
        beyond = meta[0, 2 * slot + 1] + size > tile_cols
        wanted = beyond if needs_rim else jnp.logical_not(beyond)

        @pl.when(wanted)
        def _():
            chosen[found] = slot
            amp_copy(slot).start()

        return found + wanted.astype(jnp.int32)

    count = lax.fori_loop(0, meta[0, 2 * slots], choose, jnp.zeros((), jnp.int32))

    @pl.loop(0, tile_rows // step)
    def _(at):
        rows = pl.ds(pl.multiple_of(at * step, step), step)
        for c in range(2):
            grid[c, rows, :] = jnp.zeros((step, tile_cols + size), F32)

    @pl.loop(tile_rows // step, (tile_rows + size) // step)
    def _(at):
        rows = pl.ds(pl.multiple_of(at * step, step), step)
        for c in range(2):
            if needs_rim:
                grid[c, rows, tile_cols:] = jnp.zeros((step, size), F32)
            else:
                grid[c, rows, :] = jnp.zeros((step, tile_cols + size), F32)

    if not needs_rim:

        @pl.loop(0, size // step)
        def _(at):
            rows = pl.ds(pl.multiple_of(at * step, step), step)
            for c in range(2 * modes + 1):
                probe_out[c, rows, :] = jnp.zeros((step, size), F32)

    for c in range(2):
        template[c, 0:8, :] = jnp.zeros((8, size), F32)
        template[c, 8 + size :, :] = jnp.zeros((8, size), F32)
    for load in loads:
        load.wait()

    def corner(slot):
        return meta[0, 2 * slot], meta[0, 2 * slot + 1]

    def forward(slot):
        top, left = corner(slot)

        def take(at):
            for c in range(2):
                patch_f[c, pl.ds(at, step), :] = take_shifted(ext, (c,), top, left, at, step, size)

        def fold_rows(m, at):
            cols = pl.ds(m * size, size)
            parts = []
            for base in (at, half + at):
                rows = pl.ds(base, fine)
                pr, pi = patch_f[0, rows, :], patch_f[1, rows, :]
                qr, qi = probe[m, 0, rows, :], probe[m, 1, rows, :]
                parts.append((qr * pr - qi * pi, qr * pi + qi * pr))
            for c in range(2):
                rows = pl.ds(c * half + at, fine)
                for t, value in enumerate((parts[0][c] + parts[1][c], parts[0][c] - parts[1][c])):
                    x_f[t, 0, rows, cols], x_f[t, 1, rows, cols] = split(value)

        def dft_rows(m, t):
            cols = pl.ds(m * size, size)
            high = x_f[t, 0, :, cols]
            u = dot(three_left(forward_t, t), jnp.concatenate([high, x_f[t, 1, :, cols], high], axis=0))
            rows = pl.ds(m * size + t * half, half)
            for v, value in enumerate((u[:, :half] + u[:, half:], u[:, :half] - u[:, half:])):
                high, low = split(value)
                for c in range(2):
                    lanes = pl.ds(c * half, half)
                    y_f[v, 0, rows, lanes] = high[c * half : (c + 1) * half]
                    y_f[v, 1, rows, lanes] = low[c * half : (c + 1) * half]

        def dft_cols(v):
            high = y_f[v, 0]
            z_f[v] = dot(jnp.concatenate([high, y_f[v, 1], high], axis=1), three_right(backward_t, v))

        def scale(v, at):
            if v == 0 and at == 0:
                amp_copy(slot).wait()
            waves = [z_f[v, pl.ds(m * size + at, fine), :] for m in range(modes)]
            total = jnp.zeros((fine, half), F32)
            for wave in waves:
                total += wave[:, :half] * wave[:, :half] + wave[:, half:] * wave[:, half:]
            measured = amp[slot, pl.ds(at, fine), pl.ds(v * half, half)]
            factor = measured * lax.rsqrt(jnp.maximum(total, FLOOR * FLOOR)) - 1.0
            factor = jnp.concatenate([factor, factor], axis=1)
            for m in range(modes):
                rows = pl.ds(m * size + at, fine)
                g_s[v, 0, rows, :], g_s[v, 1, rows, :] = split(waves[m] * factor)

        pieces = [(take, at) for at in range(0, size, step)]
        for m in range(modes):
            pieces += [(fold_rows, m, at) for at in range(0, half, fine)]
            pieces += [(dft_rows, m, t) for t in range(2)]
        pieces += [(dft_cols, v) for v in range(2)]
        pieces += [(scale, v, at) for v in range(2) for at in range(0, size, fine)]
        return [functools.partial(*piece) for piece in pieces]

    def backward(slot):
        top, left = corner(slot)

        def dft_cols(v):
            high = g_s[v, 0]
            z_b[v] = dot(jnp.concatenate([high, g_s[v, 1], high], axis=1), three_right(forward_t, v))

        def unfold_cols(m, t, at):
            rows = pl.ds(m * size + t * half + at, step)
            even, odd = z_b[0, rows, :], z_b[1, rows, :]
            for v, value in enumerate((even + odd, even - odd)):
                high, low = split(value)
                cols = pl.ds(m * size + v * half, half)
                for c in range(2):
                    spot = pl.ds(c * half + at, step)
                    x_b[t, 0, spot, cols] = high[:, c * half : (c + 1) * half]
                    x_b[t, 1, spot, cols] = low[:, c * half : (c + 1) * half]

        def dft_rows(m, t):
            cols = pl.ds(m * size, size)
            high = x_b[t, 0, :, cols]
            back[m, t] = dot(three_left(backward_t, t), jnp.concatenate([high, x_b[t, 1, :, cols], high], axis=0))

        def gradients(at):
            waves = []
            for m in range(modes):
                pair = []
                for c in range(2):
                    rows = pl.ds(c * half + at, fine)
                    even, odd = back[m, 0, rows, :], back[m, 1, rows, :]
                    pair.append((even + odd, even - odd))
                waves.append(pair)
            for h in range(2):
                rows = pl.ds(h * half + at, fine)
                pr, pi = patch_b[0, rows, :], patch_b[1, rows, :]
                grad_r = jnp.zeros((fine, size), F32)
                grad_i = jnp.zeros((fine, size), F32)
                for m in range(modes):
                    br, bi = waves[m][0][h], waves[m][1][h]
                    qr, qi = probe[m, 0, rows, :], probe[m, 1, rows, :]
                    grad_r += qr * br + qi * bi
                    grad_i += qr * bi - qi * br
                    probe_out[2 * m, rows, :] += pr * br + pi * bi
                    probe_out[2 * m + 1, rows, :] += pr * bi - pi * br
                probe_out[2 * modes, rows, :] += pr * pr + pi * pi
                spot = pl.ds(8 + h * half + at, fine)
                template[0, spot, :] = grad_r
                template[1, spot, :] = grad_i

        def add(c):
            add_shifted(template, grid, (c,), (c,), top, left, size)

        pieces = [(dft_cols, v) for v in range(2)]
        for m in range(modes):
            pieces += [(unfold_cols, m, t, at) for t in range(2) for at in range(0, half, step)]
            pieces += [(dft_rows, m, t) for t in range(2)]
        pieces += [(gradients, at) for at in range(0, half, fine)]
        pieces += [(add, c) for c in range(2)]
        return [functools.partial(*piece) for piece in pieces]

    def hand_over():
        for at in range(0, size, step):
            for c in range(2):
                patch_b[c, pl.ds(at, step), :] = patch_f[c, pl.ds(at, step), :]

    @pl.when(count > 0)
    def _():
        weave(forward(chosen[0]), [])
        hand_over()
        for load in late:
            load.wait()

        def visit(index, _):
            weave(backward(chosen[index]), forward(chosen[index + 1]))
            hand_over()
            return 0

        lax.fori_loop(0, count - 1, visit, 0)
        weave(backward(chosen[count - 1]), [])

    @pl.when(count == 0)
    def _():
        for load in late:
            load.wait()

    if needs_rim:
        top, bottom, rest = pl.ds(0, size), pl.ds(size, tile_rows - size), pl.ds(tile_cols, size)
        note_rows = pl.ds(size, 8)
        parts = [
            grid.at[:, pl.ds(0, tile_rows), pl.ds(0, tile_cols)],
            grid.at[:, bottom, rest],
            grid.at[:, top, rest],
            grid.at[:, pl.ds(tile_rows, size), rest],
            grid.at[:, pl.ds(tile_rows, size), pl.ds(0, tile_cols)],
            note[0],
            note[0],
            probe_out.at[:, pl.ds(pl.multiple_of(meta[0, 2 * slots + 1] * half, half), half)],
        ]
        outs = [
            outs[0],
            outs[1],
            outs[2].at[:, top],
            outs[3].at[:, top],
            outs[4],
            outs[2].at[0, note_rows],
            outs[3].at[0, note_rows],
            outs[5],
        ]
    else:
        parts = [
            grid.at[:, pl.ds(0, tile_rows), pl.ds(0, tile_cols)],
            grid.at[:, pl.ds(tile_rows, size), pl.ds(0, tile_cols)],
            sums,
        ]
        outs = [*outs, sums_out]
    stores = [pltpu.make_async_copy(part, out, out_sems.at[i]) for i, (part, out) in enumerate(zip(parts, outs))]
    for store in stores:
        store.start()
    for store in stores:
        store.wait()


def visit_slots(meta, probe, amplitudes, sources, init, note=()):
    size = probe.shape[2]
    modes = probe.shape[0]
    slots = amplitudes.shape[0]
    rows, cols = sources[0].shape[1:]
    tables = [jnp.asarray(item) for item in dft_tables(size)]
    vmem = pl.BlockSpec(memory_space=pltpu.VMEM)
    anywhere = pl.BlockSpec(memory_space=pl.ANY)
    hbm = pl.BlockSpec(memory_space=pltpu.HBM)
    needs_rim = bool(init)
    if needs_rim:
        shapes = [
            (2, rows, cols),
            (2, rows - size, size),
            (2, size + 8, size),
            (2, size + 8, size),
            (2, size, cols),
            (2 * modes + 1, size // 2, size),
        ]
    else:
        shapes = [(2, rows, cols), (2, size, cols)]
    splits = np.cumsum([1, 1, 1, len(sources), 1, 1, len(init), len(note), len(shapes), 1])

    def kernel(*refs):
        meta, probe, amplitudes, sources, forward_t, backward_t, init, note, outs, probe_out = (
            refs[a:b] for a, b in zip([0, *splits[:-1]], splits)
        )
        scratch = refs[splits[-1] :]
        slots_kernel(
            needs_rim, meta[0], probe[0], amplitudes[0], sources, forward_t[0], backward_t[0], init, note, outs,
            probe_out[0], *scratch[:-3], scratch[-3:],
        )

    return pl.pallas_call(
        kernel,
        out_shape=[pltpu.HBM(shapes[0], F32)]
        + [(jax.ShapeDtypeStruct if needs_rim else pltpu.HBM)(shape, F32) for shape in shapes[1:]]
        + [(jax.ShapeDtypeStruct if needs_rim else pltpu.HBM)((2 * modes + 1, size, size), F32)],
        in_specs=[pl.BlockSpec(memory_space=pltpu.SMEM), vmem, hbm, hbm] + [anywhere] * (len(sources) - 1)
        + [hbm] * (2 + len(init)) + [anywhere] * len(note),
        out_specs=[hbm] + [anywhere if needs_rim else hbm] * (len(shapes) - 1) + [vmem if needs_rim else hbm],
        scratch_shapes=[
            pltpu.VMEM((2, rows + size, cols + size), F32),
            pltpu.VMEM((2, rows + size, cols + size), F32),
            pltpu.VMEM(amplitudes.shape, F32),
            pltpu.VMEM(tables[0].shape, BF16),
            pltpu.VMEM(tables[1].shape, BF16),
            pltpu.SMEM((slots,), jnp.int32),
            pltpu.VMEM((2, size, size), F32),
            pltpu.VMEM((2, size, size), F32),
            pltpu.VMEM((2, 2, size, modes * size), BF16),
            pltpu.VMEM((2, 2, modes * size, size), BF16),
            pltpu.VMEM((2, modes * size, size), F32),
            pltpu.VMEM((2, 2, modes * size, size), BF16),
            pltpu.VMEM((2, 2, size, modes * size), BF16),
            pltpu.VMEM((2, modes * size, size), F32),
            pltpu.VMEM((modes, 2, size, size), F32),
            pltpu.VMEM((2, size + 16, size), F32),
            pltpu.VMEM((8, 128) if needs_rim else (2 * modes + 1, size, size), F32),
            pltpu.SemaphoreType.DMA((9,)),
            pltpu.SemaphoreType.DMA((slots,)),
            pltpu.SemaphoreType.DMA((8,)),
        ],
        compiler_params=pltpu.CompilerParams(vmem_limit_bytes=26 * MIB),
        cost_estimate=pl.CostEstimate(flops=12_000_000_000, bytes_accessed=16_000_000, transcendentals=0),
        name="slots_beyond" if needs_rim else "slots_inside",
    )(
        meta, probe, *map(in_hbm, [amplitudes, sources[0]]), *sources[1:], *map(in_hbm, [*tables, *init]), *note
    )


def finish_kernel(
    own, first, top, bottom, lower, scale, tile, out, own_s, first_s, right_s, lower_s, scale_s, tile_s, in_sems, out_sems
):
    size = right_s.shape[2]
    block = 128
    blocks = own_s.shape[1] // block

    def copies(i):
        rows = pl.ds(i * block, block)
        pairs = [
            (own.at[:, rows], own_s.at[:, rows]),
            (first.at[:, rows], first_s.at[:, rows]),
            (scale.at[rows], scale_s.at[rows]),
            (tile.at[:, rows], tile_s.at[:, rows]),
        ]
        if i < size // block:
            pairs.append((top.at[:, rows], right_s.at[:, rows]))
            pairs.append((lower.at[:, rows], lower_s.at[:, rows]))
        else:
            pairs.append((bottom.at[:, pl.ds(i * block - size, block)], right_s.at[:, rows]))
        return [pltpu.make_async_copy(a, b, in_sems.at[i, k]) for k, (a, b) in enumerate(pairs)]

    loads = [copies(i) for i in range(blocks)]
    for load in loads:
        for copy in load:
            copy.start()
    stores = []
    for i in range(blocks):
        for copy in loads[i]:
            copy.wait()
        rows = pl.ds(i * block, block)
        for at in range(i * block, (i + 1) * block, 32):
            part = pl.ds(at, 32)
            for c in range(2):
                near = own_s[c, part, :size] + first_s[c, part, :size] + right_s[c, part, :]
                far = own_s[c, part, size:] + first_s[c, part, size:]
                if i < size // block:
                    near, far = near + lower_s[c, part, :size], far + lower_s[c, part, size:]
                own_s[c, part, :size] = tile_s[c, part, :size] + near * scale_s[part, :size]
                own_s[c, part, size:] = tile_s[c, part, size:] + far * scale_s[part, size:]
        stores.append(pltpu.make_async_copy(own_s.at[:, rows], out.at[:, rows], out_sems.at[i]))
        stores[-1].start()
    for store in stores:
        store.wait()


def finish(own, first, top, bottom, lower, inverse_light, tile):
    rows, cols = tile.shape[1:]
    size = top.shape[2]
    hbm = pl.BlockSpec(memory_space=pltpu.HBM)
    return pl.pallas_call(
        finish_kernel,
        out_shape=jax.ShapeDtypeStruct(tile.shape, F32),
        in_specs=[hbm] * 2 + [pl.BlockSpec(memory_space=pl.ANY)] * 4 + [hbm],
        out_specs=hbm,
        scratch_shapes=[
            pltpu.VMEM(tile.shape, F32),
            pltpu.VMEM(tile.shape, F32),
            pltpu.VMEM((2, rows, size), F32),
            pltpu.VMEM((2, size, cols), F32),
            pltpu.VMEM((rows, cols), F32),
            pltpu.VMEM(tile.shape, F32),
            pltpu.SemaphoreType.DMA((rows // 128, 6)),
            pltpu.SemaphoreType.DMA((rows // 128,)),
        ],
        compiler_params=pltpu.CompilerParams(vmem_limit_bytes=12 * MIB),
        cost_estimate=pl.CostEstimate(flops=3_000_000, bytes_accessed=12_000_000, transcendentals=0),
        name="finish",
    )(in_hbm(own), in_hbm(first), top, bottom, lower, inverse_light, in_hbm(tile))


def from_behind(array, axis, by):
    count = lax.axis_size(axis)
    pairs = [(i, i + by) for i in range(count) if 0 <= i + by < count]
    return lax.ppermute(array, axis, pairs)


def exchange(array, axis, bit):
    count = lax.axis_size(axis)
    return lax.ppermute(array, axis, [(i, i ^ bit) for i in range(count)])


def together(*arrays):
    return lax.optimization_barrier(arrays)


def cut(tile, regions, cost, name):
    def kernel(tile, *refs):
        sems = refs[-1]
        copies = [
            pltpu.make_async_copy(tile.at[:, pl.ds(at, height), pl.ds(0, width)], out, sems.at[i])
            for i, ((at, height, width), out) in enumerate(zip(regions, refs[:-1]))
        ]
        for copy in copies:
            copy.start()
        for copy in copies:
            copy.wait()

    return pl.pallas_call(
        kernel,
        out_shape=[jax.ShapeDtypeStruct((2, height, width), F32) for _, height, width in regions],
        in_specs=[pl.BlockSpec(memory_space=pltpu.HBM)],
        out_specs=[pl.BlockSpec(memory_space=pltpu.VMEM)] * len(regions),
        scratch_shapes=[pltpu.SemaphoreType.DMA((len(regions),))],
        compiler_params=pltpu.CompilerParams(vmem_limit_bytes=4 * MIB),
        cost_estimate=cost,
        name=name,
    )(in_hbm(tile))


def fold(places, index, mine, got, upper):
    count, half, width = got.shape
    quarter = half // 2

    def kernel(places, mine, got, send, keep):
        base = 0 if index is None else places[0, index] * half
        for k, out in ((1 - places[0, upper], send), (places[0, upper], keep)):
            for c in range(count):
                out[c] = (
                    mine[c, pl.ds(pl.multiple_of(base + k * quarter, quarter), quarter), :]
                    + got[c, pl.ds(pl.multiple_of(k * quarter, quarter), quarter), :]
                )

    vmem = pl.BlockSpec(memory_space=pltpu.VMEM)
    shape = jax.ShapeDtypeStruct((count, quarter, width), F32)
    return pl.pallas_call(
        kernel,
        out_shape=[shape, shape],
        in_specs=[pl.BlockSpec(memory_space=pltpu.SMEM), vmem, vmem],
        out_specs=[vmem, vmem],
        compiler_params=pltpu.CompilerParams(vmem_limit_bytes=6 * MIB),
        cost_estimate=SHORT,
        name="fold",
    )(places, mine, got)


def merge(right, corner):
    rows = right.shape[1] - 8

    def kernel(right, corner, out):
        for c in range(2):
            out[c, :rows, :] = right[c, :rows, :] + corner[c, :rows, :]
        out[0, rows:, :] = right[0, rows:, :]
        out[1, rows:, :] = corner[0, rows:, :]

    vmem = pl.BlockSpec(memory_space=pltpu.VMEM)
    return pl.pallas_call(
        kernel,
        out_shape=jax.ShapeDtypeStruct(right.shape, F32),
        in_specs=[vmem, vmem],
        out_specs=vmem,
        compiler_params=pltpu.CompilerParams(vmem_limit_bytes=4 * MIB),
        cost_estimate=SHORT,
        name="merge",
    )(right, corner)


def deal(places, me, terms, parts, rows):
    aligned = rows % 8 == 0
    if not aligned:
        count, _, width = terms[0].shape
        terms = [sum(terms).reshape(count, parts, rows, width).transpose(1, 0, 2, 3)]
    count, width = terms[0].shape[0 if aligned else 1], terms[0].shape[-1]

    def kernel(places, *refs):
        terms, outs = refs[:-parts], refs[-parts:]
        for k, out in enumerate(outs):
            j = places[0, me] ^ k
            for c in range(count):
                if aligned:
                    spot = pl.ds(pl.multiple_of(j * rows, rows), rows)
                    out[c] = sum(term[c, spot, :] for term in terms)
                else:
                    out[c] = terms[0][j, c]

    vmem = pl.BlockSpec(memory_space=pltpu.VMEM)
    return pl.pallas_call(
        kernel,
        out_shape=[jax.ShapeDtypeStruct((count, rows, width), F32)] * parts,
        in_specs=[pl.BlockSpec(memory_space=pltpu.SMEM)] + [vmem] * len(terms),
        out_specs=[vmem] * parts,
        compiler_params=pltpu.CompilerParams(vmem_limit_bytes=4 * MIB),
        cost_estimate=SHORT,
        name="deal",
    )(places, *terms)


def settle(places, start, probe, pieces):
    count, rows, width = pieces[0].shape
    if rows % 8:
        share = sum(pieces)
        old = lax.dynamic_slice_in_dim(probe, places[0, start], rows, axis=1)
        return old + share[:-1] / (share[-1:] + 1.0)

    def kernel(places, probe, *refs):
        pieces, (out, old, sem) = refs[:-3], refs[-3:]
        spot = pl.ds(pl.multiple_of(places[0, start], 8), rows)
        copy = pltpu.make_async_copy(probe.at[:, spot], old, sem.at[0])
        copy.start()
        share = sum(piece[...] for piece in pieces)
        copy.wait()
        out[...] = old[...] + share[:-1] / (share[-1:] + 1.0)

    vmem = pl.BlockSpec(memory_space=pltpu.VMEM)
    return pl.pallas_call(
        kernel,
        out_shape=jax.ShapeDtypeStruct((count - 1, rows, width), F32),
        in_specs=[pl.BlockSpec(memory_space=pltpu.SMEM), pl.BlockSpec(memory_space=pltpu.HBM)] + [vmem] * len(pieces),
        out_specs=vmem,
        scratch_shapes=[pltpu.VMEM((count - 1, rows, width), F32), pltpu.SemaphoreType.DMA((1,))],
        compiler_params=pltpu.CompilerParams(vmem_limit_bytes=4 * MIB),
        cost_estimate=SHORT,
        name="settle",
    )(places, in_hbm(probe), *pieces)


def collect(places, me, pieces):
    count, rows, width = pieces[0].shape
    parts = len(pieces)
    aligned = rows % 8 == 0
    shape = (count, parts * rows, width) if aligned else (parts, count, rows, width)

    def kernel(places, *refs):
        pieces, out = refs[:-1], refs[-1]
        for k, piece in enumerate(pieces):
            j = places[0, me] ^ k
            for c in range(count):
                if aligned:
                    out[c, pl.ds(pl.multiple_of(j * rows, rows), rows), :] = piece[c]
                else:
                    out[j, c] = piece[c]

    vmem = pl.BlockSpec(memory_space=pltpu.VMEM)
    out = pl.pallas_call(
        kernel,
        out_shape=jax.ShapeDtypeStruct(shape, F32),
        in_specs=[pl.BlockSpec(memory_space=pltpu.SMEM)] + [vmem] * parts,
        out_specs=vmem,
        compiler_params=pltpu.CompilerParams(vmem_limit_bytes=4 * MIB),
        cost_estimate=SHORT,
        name="collect",
    )(places, *pieces)
    if not aligned:
        out = out.transpose(1, 0, 2, 3).reshape(count, parts * rows, width)
    return out


def join(places, upper, mine, other):
    half = mine.shape[1]

    def kernel(places, mine, other, out, sems):
        copies = [
            pltpu.make_async_copy(source, out.at[:, pl.ds(pl.multiple_of(at * half, half), half)], sems.at[i])
            for i, (source, at) in enumerate(((mine, places[0, upper]), (other, 1 - places[0, upper])))
        ]
        for copy in copies:
            copy.start()
        for copy in copies:
            copy.wait()

    anywhere = pl.BlockSpec(memory_space=pl.ANY)
    return pl.pallas_call(
        kernel,
        out_shape=jax.ShapeDtypeStruct((mine.shape[0], 2 * half) + mine.shape[2:], F32),
        in_specs=[pl.BlockSpec(memory_space=pltpu.SMEM), anywhere, anywhere],
        out_specs=anywhere,
        scratch_shapes=[pltpu.SemaphoreType.DMA((2,))],
        compiler_params=pltpu.CompilerParams(vmem_limit_bytes=MIB),
        cost_estimate=pl.CostEstimate(flops=0, bytes_accessed=2_000_000, transcendentals=0),
        name="join",
    )(places, mine, other)


def body(object_field, probe, amplitudes, positions, counts):
    modes, _, size, _ = probe.shape
    tile_rows, tile_cols = object_field.shape[1:]
    slots = amplitudes.shape[0]
    origin = jnp.stack([lax.axis_index("row") * tile_rows, lax.axis_index("col") * tile_cols]).astype(jnp.int32)
    bits = [1 << k for k in range(lax.axis_size("row").bit_length() - 1)]
    uppers = [(lax.axis_index("row") & bit) // bit for bit in bits]

    def relative(table):
        return jnp.concatenate([table[:, : 2 * slots] - jnp.tile(origin, slots)[None], table[:, 2 * slots :]], axis=1)

    right_up, right_down = cut(
        object_field, ((0, size, size), (size, tile_rows - size, size)), SHORT, "cut_right"
    )
    right_up, right_down, after_right = together(right_up, right_down, object_field)
    right_up = from_behind(right_up, "col", -1)
    right_down = from_behind(right_down, "col", -1)
    (lower,) = cut(after_right, ((0, size, tile_cols),), LONG, "cut_lower")
    meta = jnp.concatenate([positions.reshape(1, 2 * slots), counts.reshape(1, 1)], axis=1)
    lower = from_behind(lower, "row", -1)

    parts = lax.axis_size("col")
    rows = (size >> len(bits)) // parts
    me = lax.axis_index("col")
    start = sum(upper * (size >> (k + 1)) for k, upper in enumerate(uppers)) + me * rows
    bit_at = 2 * slots + 2
    me_at = bit_at + len(bits)
    start_at, origin_at = me_at + 1, me_at + 2
    extra = [1 - uppers[0], *uppers, me, start, origin[0], origin[1]]
    mine = jnp.concatenate([relative(meta), jnp.stack([item.astype(jnp.int32) for item in extra])[None]], axis=1)
    note = jnp.pad(meta.astype(F32), ((0, 7), (0, size - meta.shape[1])))
    mine, note = together(mine, note)
    amplitudes = arrange(mine, amplitudes)
    right_up, amplitudes = together(right_up, amplitudes)
    corner = from_behind(right_up, "row", -1)
    amplitudes, lower = together(amplitudes, lower)
    init = visit_slots(mine, probe, amplitudes, [object_field, lower], [])
    right_up, right_down, corner, *init = together(right_up, right_down, corner, *init)
    own, bottom_spill, top_spill, corner_spill, lower_spill, send, share = visit_slots(
        mine, probe, amplitudes, [object_field, lower, right_up, right_down, corner], list(init[1:]), [note]
    )

    index = bit_at
    for k, bit in enumerate(bits):
        got = exchange(send, "row", bit)
        if k == 0:
            bottom_spill = from_behind(bottom_spill, "col", 1)
            corner_spill = from_behind(corner_spill, "row", 1)
        if k + 1 < len(bits):
            send, share = fold(mine, index, share, got, bit_at + k + 1)
            index = None
    got, bottom_spill, corner_spill, lower_spill = together(got, bottom_spill, corner_spill, lower_spill)
    lower_spill = from_behind(lower_spill, "row", 1)
    top_spill = from_behind(merge(top_spill, corner_spill), "col", 1)
    own_part, *pieces = deal(mine, me_at, [share, got], parts, rows)
    pieces = [exchange(piece, "col", k + 1) for k, piece in enumerate(pieces)]
    new = settle(mine, start_at, probe.reshape(2 * modes, size, size), [own_part, *pieces])
    new = collect(mine, me_at, [new] + [exchange(new, "col", k) for k in range(1, parts)])
    new, top_spill = together(new, top_spill)
    inverse_light = light(mine, slots, origin_at, probe, top_spill, corner_spill, (tile_rows, tile_cols))
    for k, bit in reversed(list(enumerate(bits))):
        if k == 0:
            new, own = together(new, own)
            new_object = finish(own, init[0], top_spill, bottom_spill, lower_spill, inverse_light, object_field)
        other = exchange(new, "row", bit)
        if k + 1 == len(bits):
            other, inverse_light = together(other, inverse_light)
        if k == 0:
            other, new_object = together(other, new_object)
        new = join(mine, bit_at + k, new, other)
    return (new_object, new.reshape(modes, 2, size, size))


def solution(mesh):
    in_specs = (
        P(None, "row", "col"),
        P(),
        P(("row", "col"), None, None),
        P(("row", "col"), None),
        P(("row", "col")),
    )
    out_specs = (P(None, "row", "col"), P())
    return jax.shard_map(body, mesh=mesh, in_specs=in_specs, out_specs=out_specs, check_vma=False)
```

```python
import functools
import math

import jax
import jax.numpy as jnp
import ml_dtypes
import numpy as np
from jax import lax
from jax.experimental import pallas as pl
from jax.experimental.pallas import tpu as pltpu
from jax.sharding import PartitionSpec as P

F32 = jnp.float32
BF16 = jnp.bfloat16
MIB = 1024 * 1024
LONG = pl.CostEstimate(flops=30_000_000_000, bytes_accessed=4_000_000, transcendentals=0)
SHORT = pl.CostEstimate(flops=0, bytes_accessed=1_000_000, transcendentals=0)
FLOOR = 0.3


def split_np(table):
    high = table.astype(ml_dtypes.bfloat16)
    low = (table - high.astype(np.float64)).astype(ml_dtypes.bfloat16)
    return high, low


def dft_tables(length):
    half = length // 2
    q = np.arange(half)[:, None]
    n = np.arange(half)[None, :]
    forward = []
    for odd in range(2):
        phase = (n * (2 * q + odd)) % length
        angle = phase * (-2.0 * math.pi / length)
        re = np.cos(angle) / math.sqrt(length)
        im = np.sin(angle) / math.sqrt(length)
        forward.append(np.stack(split_np(np.block([[re, -im], [im, re]]))))
    forward = np.stack(forward)
    return forward, np.ascontiguousarray(forward.transpose(0, 1, 3, 2))


def in_hbm(array):
    return pltpu.with_memory_space_constraint(array, pltpu.HBM)


def dot(a, b):
    return jnp.dot(a, b, preferred_element_type=F32)


def split(x):
    high = x.astype(BF16)
    return high, (x - high.astype(F32)).astype(BF16)


def roll_rows(x, shift):
    return pltpu.roll(x.reshape(x.shape[0] // 8, 8, x.shape[1]), shift, 1)


def roll_rows(x, shift):
    return pltpu.roll(x.reshape(x.shape[0] // 8, 8, x.shape[1]), shift, 1)


def roll_rows(x, shift):
    return pltpu.roll(x.reshape(x.shape[0] // 8, 8, x.shape[1]), shift, 1)


def roll_rows(x, shift):
    return pltpu.roll(x.reshape(x.shape[0] // 8, 8, x.shape[1]), shift, 1)


def split_three(x):
    high = x.astype(BF16)
    rest = x - high.astype(F32)
    middle = rest.astype(BF16)
    return high, middle, (rest - middle.astype(F32)).astype(BF16)


def add_shifted(template, grid, where_t, where_g, top, left, size):
    top_s = top & 7
    top_b = pl.multiple_of(top - top_s, 8)
    left_s = left & 127
    left_b = pl.multiple_of(left - left_s, 128)
    step = 24
    wrapped = lax.broadcasted_iota(jnp.int32, (step, 128), 1) < left_s
    wrapped_rows = lax.broadcasted_iota(jnp.int32, (step // 8, 8, 128), 1) < top_s
    zero = jnp.zeros((step, 128), F32)
    blocks = size // 128
    for at in range(0, size + 8, step):
        parts = []
        for j in range(blocks):
            x = roll_rows(template[where_t + (pl.ds(at, step + 8), pl.ds(128 * j, 128))], top_s)
            x = jnp.where(wrapped_rows, x[:-1], x[1:]).reshape(step, 128)
            parts.append(pltpu.roll(x, left_s, 1))
        for j in range(blocks + 1):
            before = parts[j - 1] if j > 0 else zero
            after = parts[j] if j < blocks else zero
            spot = where_g + (pl.ds(top_b + at, step), pl.ds(left_b + 128 * j, 128))
            grid[spot] += jnp.where(wrapped, before, after)


def take_shifted(field, where, top, left, at, step, size):
    top_s = top & 7
    top_b = pl.multiple_of(top - top_s, 8)
    left_s = left & 127
    left_b = pl.multiple_of(left - left_s, 128)
    back = (128 - left_s) & 127
    keep = lax.broadcasted_iota(jnp.int32, (step + 8, 128), 1) < 128 - left_s
    keep_rows = lax.broadcasted_iota(jnp.int32, (step // 8, 8, 128), 1) < 8 - top_s
    blocks = size // 128
    parts = [
        pltpu.roll(field[where + (pl.ds(top_b + at, step + 8), pl.ds(left_b + 128 * j, 128))], back, 1)
        for j in range(blocks + 1)
    ]
    pieces = []
    for j in range(blocks):
        x = roll_rows(jnp.where(keep, parts[j], parts[j + 1]), (8 - top_s) & 7)
        pieces.append(jnp.where(keep_rows, x[:-1], x[1:]).reshape(step, 128))
    return jnp.concatenate(pieces, axis=1)


def light_kernel(slots, origin, meta, probe_h, top, corner, inverse_light, probe, template, grid, notes, sems):
    size = probe.shape[2]
    tile_rows, tile_cols = inverse_light.shape
    rows = pl.ds(top.shape[1] - 8, 8)
    cols = pl.ds(0, 128)
    copies = [
        pltpu.make_async_copy(top.at[0, rows, cols], notes.at[0], sems.at[0]),
        pltpu.make_async_copy(corner.at[0, pl.ds(corner.shape[1] - 8, 8), cols], notes.at[1], sems.at[1]),
        pltpu.make_async_copy(top.at[1, rows, cols], notes.at[2], sems.at[2]),
    ]
    copy = pltpu.make_async_copy(probe_h, probe, sems.at[3])
    copy.start()
    for item in copies:
        item.start()
    template[0:8, :] = jnp.zeros((8, size), F32)
    template[8 + size :, :] = jnp.zeros((8, size), F32)
    copy.wait()
    for at in range(0, size, 32):
        rows = pl.ds(at, 32)
        total = jnp.zeros((32, size), F32)
        for m in range(probe.shape[0]):
            total += probe[m, 0, rows] * probe[m, 0, rows] + probe[m, 1, rows] * probe[m, 1, rows]
        template[pl.ds(8 + at, 32), :] = total

    @pl.loop(0, tile_rows // 32)
    def _(step):
        rows = pl.ds(pl.multiple_of(size + step * 32, 32), 32)
        grid[rows, size : size + tile_cols] = jnp.zeros((32, tile_cols), F32)

    def add(top, left):
        @pl.when((top > 0) & (left > 0))
        def _():
            add_shifted(template, grid, (), (), top, left, size)

    @pl.loop(0, meta[0, 2 * slots])
    def _(slot):
        add(meta[0, 2 * slot] + size, meta[0, 2 * slot + 1] + size)

    for item in copies:
        item.wait()
    for device in range(3):

        @pl.loop(0, notes[device, 0, 2 * slots].astype(jnp.int32))
        def _(slot):
            top = notes[device, 0, 2 * slot].astype(jnp.int32) - meta[0, origin]
            left = notes[device, 0, 2 * slot + 1].astype(jnp.int32) - meta[0, origin + 1]
            add(top + size, left + size)

    @pl.loop(0, tile_rows // 32)
    def _(step):
        rows = pl.ds(pl.multiple_of(size + step * 32, 32), 32)
        out_rows = pl.ds(pl.multiple_of(step * 32, 32), 32)
        inverse_light[out_rows, :] = 1.0 / (grid[rows, size : size + tile_cols] + 1.0)


def light(meta, slots, origin, probe, top, corner, tile_shape):
    size = probe.shape[2]
    hbm = pl.BlockSpec(memory_space=pltpu.HBM)
    anywhere = pl.BlockSpec(memory_space=pl.ANY)
    return pl.pallas_call(
        functools.partial(light_kernel, slots, origin),
        out_shape=jax.ShapeDtypeStruct(tile_shape, F32),
        in_specs=[pl.BlockSpec(memory_space=pltpu.SMEM), hbm, anywhere, anywhere],
        out_specs=pl.BlockSpec(memory_space=pltpu.VMEM),
        scratch_shapes=[
            pltpu.VMEM(probe.shape, F32),
            pltpu.VMEM((size + 16, size), F32),
            pltpu.VMEM((tile_shape[0] + 2 * size, tile_shape[1] + 2 * size), F32),
            pltpu.SMEM((3, 8, 128), F32),
            pltpu.SemaphoreType.DMA((4,)),
        ],
        compiler_params=pltpu.CompilerParams(vmem_limit_bytes=8 * MIB),
        cost_estimate=pl.CostEstimate(flops=4_000_000_000, bytes_accessed=1_000_000, transcendentals=0),
        name="light",
    )(meta, in_hbm(probe), top, corner)


def arrange_kernel(meta, amplitudes, out, given, moved, in_sems, out_sems):
    slots, size, _ = amplitudes.shape
    count = meta[0, 2 * slots]

    def load(slot):
        return pltpu.make_async_copy(amplitudes.at[slot], given.at[slot], in_sems.at[slot])

    def store(slot):
        return pltpu.make_async_copy(moved.at[slot], out.at[slot], out_sems.at[slot])

    @pl.loop(0, count)
    def _(slot):
        load(slot).start()

    first = lax.broadcasted_iota(jnp.int32, (size, size), 0)
    second = lax.broadcasted_iota(jnp.int32, (size, size), 1)
    half = size // 2

    def source(index):
        return jnp.where(index < half, 2 * index, 2 * index - (size - 1))

    rows = (source(first) == second).astype(F32).astype(BF16)
    cols = (source(second) == first).astype(F32).astype(BF16)
    rows = jnp.concatenate([rows, rows], axis=1)
    cols = jnp.concatenate([cols, cols], axis=0)

    @pl.loop(0, count)
    def _(slot):
        load(slot).wait()
        x = dot(rows, jnp.concatenate(split(given[slot]), axis=0))
        moved[slot] = dot(jnp.concatenate(split(x), axis=1), cols)
        store(slot).start()

    @pl.loop(0, count)
    def _(slot):
        store(slot).wait()


def arrange(meta, amplitudes):
    slots = amplitudes.shape[0]
    hbm = pl.BlockSpec(memory_space=pltpu.HBM)
    return pl.pallas_call(
        arrange_kernel,
        out_shape=pltpu.HBM(amplitudes.shape, F32),
        in_specs=[pl.BlockSpec(memory_space=pltpu.SMEM), hbm],
        out_specs=hbm,
        scratch_shapes=[
            pltpu.VMEM(amplitudes.shape, F32),
            pltpu.VMEM(amplitudes.shape, F32),
            pltpu.SemaphoreType.DMA((slots,)),
            pltpu.SemaphoreType.DMA((slots,)),
        ],
        compiler_params=pltpu.CompilerParams(vmem_limit_bytes=8 * MIB),
        cost_estimate=LONG,
        name="arrange",
    )(meta, in_hbm(amplitudes))


def three_left(table, t):
    return jnp.concatenate([table[t, 0], table[t, 0], table[t, 1]], axis=1)


def three_right(table, v):
    return jnp.concatenate([table[v, 0], table[v, 0], table[v, 1]], axis=0)


def weave(first, second):
    total = max(len(first), len(second))
    done = [0, 0]
    for i in range(1, total + 1):
        for k, pieces in enumerate((first, second)):
            while done[k] * total < i * len(pieces):
                pieces[done[k]]()
                done[k] += 1


def slots_kernel(
    needs_rim, meta, probe, amplitudes, sources, tables, note, state, outs,
    amp, chosen, patch_f, patch_b, x_f, y_f, z_f, g_s, x_b, z_b, back, template, load_sems, amp_sems, out_sems,
):
    ext, grid, probe_out, forward_t, backward_t = state
    size = probe.shape[2]
    half = size // 2
    modes = probe.shape[0]
    slots = amplitudes.shape[0]
    tile_rows, tile_cols = (n - size for n in ext.shape[1:])
    step = 32
    fine = 16

    body_rows, rim_rows = pl.ds(0, tile_rows), pl.ds(tile_rows, size)
    body_cols, rim_cols = pl.ds(0, tile_cols), pl.ds(tile_cols, size)
    if needs_rim:
        places = [
            ext.at[:, pl.ds(0, size), rim_cols],
            ext.at[:, pl.ds(size, tile_rows - size), rim_cols],
            ext.at[:, rim_rows, rim_cols],
        ]
    else:
        places = [ext.at[:, body_rows, body_cols], ext.at[:, rim_rows, body_cols], forward_t, backward_t]
    loads = [
        pltpu.make_async_copy(source, place, load_sems.at[i])
        for i, (source, place) in enumerate(zip([*sources, *tables], places))
    ]
    for load in loads:
        load.start()

    def amp_copy(slot):
        return pltpu.make_async_copy(amplitudes.at[slot], amp.at[slot], amp_sems.at[slot])

    def choose(slot, found):
        beyond = meta[0, 2 * slot + 1] + size > tile_cols
        wanted = beyond if needs_rim else jnp.logical_not(beyond)

        @pl.when(wanted)
        def _():
            chosen[found] = slot
            amp_copy(slot).start()

        return found + wanted.astype(jnp.int32)

    count = lax.fori_loop(0, meta[0, 2 * slots], choose, jnp.zeros((), jnp.int32))

    if not needs_rim:

        @pl.loop(0, (tile_rows + size) // step)
        def _(at):
            rows = pl.ds(pl.multiple_of(at * step, step), step)
            for c in range(2):
                grid[c, rows, :] = jnp.zeros((step, tile_cols + size), F32)

        @pl.loop(0, size // step)
        def _(at):
            rows = pl.ds(pl.multiple_of(at * step, step), step)
            for c in range(2 * modes + 1):
                probe_out[c, rows, :] = jnp.zeros((step, size), F32)

    for c in range(2):
        template[c, 0:8, :] = jnp.zeros((8, size), F32)
        template[c, 8 + size :, :] = jnp.zeros((8, size), F32)
    for load in loads:
        load.wait()

    def corner(slot):
        return meta[0, 2 * slot], meta[0, 2 * slot + 1]

    def forward(slot):
        top, left = corner(slot)

        def take(at):
            for c in range(2):
                patch_f[c, pl.ds(at, step), :] = take_shifted(ext, (c,), top, left, at, step, size)

        def fold_rows(m, at):
            cols = pl.ds(m * size, size)
            parts = []
            for base in (at, half + at):
                rows = pl.ds(base, fine)
                pr, pi = patch_f[0, rows, :], patch_f[1, rows, :]
                qr, qi = probe[m, 0, rows, :], probe[m, 1, rows, :]
                parts.append((qr * pr - qi * pi, qr * pi + qi * pr))
            for c in range(2):
                rows = pl.ds(c * half + at, fine)
                for t, value in enumerate((parts[0][c] + parts[1][c], parts[0][c] - parts[1][c])):
                    x_f[t, 0, rows, cols], x_f[t, 1, rows, cols] = split(value)

        def dft_rows(m, t):
            cols = pl.ds(m * size, size)
            high = x_f[t, 0, :, cols]
            u = dot(three_left(forward_t, t), jnp.concatenate([high, x_f[t, 1, :, cols], high], axis=0))
            rows = pl.ds(m * size + t * half, half)
            for v, value in enumerate((u[:, :half] + u[:, half:], u[:, :half] - u[:, half:])):
                high, low = split(value)
                for c in range(2):
                    lanes = pl.ds(c * half, half)
                    y_f[v, 0, rows, lanes] = high[c * half : (c + 1) * half]
                    y_f[v, 1, rows, lanes] = low[c * half : (c + 1) * half]

        def dft_cols(v):
            high = y_f[v, 0]
            z_f[v] = dot(jnp.concatenate([high, y_f[v, 1], high], axis=1), three_right(backward_t, v))

        def scale(v, at):
            if v == 0 and at == 0:
                amp_copy(slot).wait()
            waves = [z_f[v, pl.ds(m * size + at, fine), :] for m in range(modes)]
            total = jnp.zeros((fine, half), F32)
            for wave in waves:
                total += wave[:, :half] * wave[:, :half] + wave[:, half:] * wave[:, half:]
            measured = amp[slot, pl.ds(at, fine), pl.ds(v * half, half)]
            factor = measured * lax.rsqrt(jnp.maximum(total, FLOOR * FLOOR)) - 1.0
            factor = jnp.concatenate([factor, factor], axis=1)
            for m in range(modes):
                rows = pl.ds(m * size + at, fine)
                g_s[v, 0, rows, :], g_s[v, 1, rows, :] = split(waves[m] * factor)

        pieces = [(take, at) for at in range(0, size, step)]
        for m in range(modes):
            pieces += [(fold_rows, m, at) for at in range(0, half, fine)]
            pieces += [(dft_rows, m, t) for t in range(2)]
        pieces += [(dft_cols, v) for v in range(2)]
        pieces += [(scale, v, at) for v in range(2) for at in range(0, size, fine)]
        return [functools.partial(*piece) for piece in pieces]

    def backward(slot):
        top, left = corner(slot)

        def dft_cols(v):
            high = g_s[v, 0]
            z_b[v] = dot(jnp.concatenate([high, g_s[v, 1], high], axis=1), three_right(forward_t, v))

        def unfold_cols(m, t, at):
            rows = pl.ds(m * size + t * half + at, step)
            even, odd = z_b[0, rows, :], z_b[1, rows, :]
            for v, value in enumerate((even + odd, even - odd)):
                high, low = split(value)
                cols = pl.ds(m * size + v * half, half)
                for c in range(2):
                    spot = pl.ds(c * half + at, step)
                    x_b[t, 0, spot, cols] = high[:, c * half : (c + 1) * half]
                    x_b[t, 1, spot, cols] = low[:, c * half : (c + 1) * half]

        def dft_rows(m, t):
            cols = pl.ds(m * size, size)
            high = x_b[t, 0, :, cols]
            back[m, t] = dot(three_left(backward_t, t), jnp.concatenate([high, x_b[t, 1, :, cols], high], axis=0))

        def gradients(at):
            waves = []
            for m in range(modes):
                pair = []
                for c in range(2):
                    rows = pl.ds(c * half + at, fine)
                    even, odd = back[m, 0, rows, :], back[m, 1, rows, :]
                    pair.append((even + odd, even - odd))
                waves.append(pair)
            for h in range(2):
                rows = pl.ds(h * half + at, fine)
                pr, pi = patch_b[0, rows, :], patch_b[1, rows, :]
                grad_r = jnp.zeros((fine, size), F32)
                grad_i = jnp.zeros((fine, size), F32)
                for m in range(modes):
                    br, bi = waves[m][0][h], waves[m][1][h]
                    qr, qi = probe[m, 0, rows, :], probe[m, 1, rows, :]
                    grad_r += qr * br + qi * bi
                    grad_i += qr * bi - qi * br
                    probe_out[2 * m, rows, :] += pr * br + pi * bi
                    probe_out[2 * m + 1, rows, :] += pr * bi - pi * br
                probe_out[2 * modes, rows, :] += pr * pr + pi * pi
                spot = pl.ds(8 + h * half + at, fine)
                template[0, spot, :] = grad_r
                template[1, spot, :] = grad_i

        def add(c):
            add_shifted(template, grid, (c,), (c,), top, left, size)

        pieces = [(dft_cols, v) for v in range(2)]
        for m in range(modes):
            pieces += [(unfold_cols, m, t, at) for t in range(2) for at in range(0, half, step)]
            pieces += [(dft_rows, m, t) for t in range(2)]
        pieces += [(gradients, at) for at in range(0, half, fine)]
        pieces += [(add, c) for c in range(2)]
        return [functools.partial(*piece) for piece in pieces]

    def hand_over():
        for at in range(0, size, step):
            for c in range(2):
                patch_b[c, pl.ds(at, step), :] = patch_f[c, pl.ds(at, step), :]

    @pl.when(count > 0)
    def _():
        weave(forward(chosen[0]), [])
        hand_over()

        def visit(index, _):
            weave(backward(chosen[index]), forward(chosen[index + 1]))
            hand_over()
            return 0

        lax.fori_loop(0, count - 1, visit, 0)
        weave(backward(chosen[count - 1]), [])

    if needs_rim:
        note_rows = pl.ds(size, 8)
        parts = [
            (grid.at[:, body_rows, body_cols], outs[0]),
            (grid.at[:, body_rows, rim_cols], outs[1].at[:, body_rows]),
            (note, outs[1].at[0, pl.ds(tile_rows, 8)]),
            (grid.at[:, rim_rows, rim_cols], outs[2].at[:, pl.ds(0, size)]),
            (note, outs[2].at[0, note_rows]),
            (grid.at[:, rim_rows, body_cols], outs[3]),
            (probe_out.at[:, pl.ds(pl.multiple_of(meta[0, 2 * slots + 1] * half, half), half)], outs[4]),
        ]
        stores = [pltpu.make_async_copy(part, out, out_sems.at[i]) for i, (part, out) in enumerate(parts)]
        for store in stores:
            store.start()
        for store in stores:
            store.wait()


def scratch_for(size, modes, slots):
    return [
        pltpu.VMEM((slots, size, size), F32),
        pltpu.SMEM((slots,), jnp.int32),
        pltpu.VMEM((2, size, size), F32),
        pltpu.VMEM((2, size, size), F32),
        pltpu.VMEM((2, 2, size, modes * size), BF16),
        pltpu.VMEM((2, 2, modes * size, size), BF16),
        pltpu.VMEM((2, modes * size, size), F32),
        pltpu.VMEM((2, 2, modes * size, size), BF16),
        pltpu.VMEM((2, 2, size, modes * size), BF16),
        pltpu.VMEM((2, modes * size, size), F32),
        pltpu.VMEM((modes, 2, size, size), F32),
        pltpu.VMEM((2, size + 16, size), F32),
        pltpu.SemaphoreType.DMA((4,)),
        pltpu.SemaphoreType.DMA((slots,)),
        pltpu.SemaphoreType.DMA((7,)),
    ]


SLOTS_COST = pl.CostEstimate(flops=12_000_000_000, bytes_accessed=16_000_000, transcendentals=0)


def visit_inside(meta, probe, amplitudes, tile, lower):
    size, modes, slots = probe.shape[2], probe.shape[0], amplitudes.shape[0]
    rows, cols = tile.shape[1:]
    tables = [jnp.asarray(item) for item in dft_tables(size)]
    vmem = pl.BlockSpec(memory_space=pltpu.VMEM)
    hbm = pl.BlockSpec(memory_space=pltpu.HBM)
    field = pltpu.VMEM((2, rows + size, cols + size), F32)

    def kernel(meta, probe, amplitudes, tile, lower, forward_h, backward_h, *refs):
        state, scratch = refs[:5], refs[5:]
        slots_kernel(
            False, meta, probe, amplitudes, [tile, lower], [forward_h, backward_h], None, state, None, *scratch
        )

    return pl.pallas_call(
        kernel,
        out_shape=[field, field, pltpu.VMEM((2 * modes + 1, size, size), F32)]
        + [pltpu.VMEM(item.shape, BF16) for item in tables],
        in_specs=[pl.BlockSpec(memory_space=pltpu.SMEM), vmem, hbm, hbm, pl.BlockSpec(memory_space=pl.ANY), hbm, hbm],
        out_specs=[vmem] * 5,
        scratch_shapes=scratch_for(size, modes, slots),
        compiler_params=pltpu.CompilerParams(vmem_limit_bytes=28 * MIB),
        cost_estimate=SLOTS_COST,
        name="slots_inside",
    )(meta, probe, in_hbm(amplitudes), in_hbm(tile), lower, *map(in_hbm, tables))


def visit_beyond(meta, probe, amplitudes, rims, note, state):
    size, modes, slots = probe.shape[2], probe.shape[0], amplitudes.shape[0]
    rows, cols = (n - size for n in state[0].shape[1:])
    vmem = pl.BlockSpec(memory_space=pltpu.VMEM)
    hbm = pl.BlockSpec(memory_space=pltpu.HBM)
    anywhere = pl.BlockSpec(memory_space=pl.ANY)
    shapes = [(2, rows + 8, size), (2, size + 8, size), (2, size, cols), (2 * modes + 1, size // 2, size)]

    def kernel(meta, probe, amplitudes, *refs):
        rims, note, refs = refs[:3], refs[3], refs[9:]
        state, outs, scratch = refs[:5], refs[5:10], refs[10:]
        slots_kernel(True, meta, probe, amplitudes, rims, [], note, state, outs, *scratch)

    out = pl.pallas_call(
        kernel,
        out_shape=[pltpu.VMEM(item.shape, item.dtype) for item in state]
        + [pltpu.HBM((2, rows, cols), F32)]
        + [jax.ShapeDtypeStruct(shape, F32) for shape in shapes],
        in_specs=[pl.BlockSpec(memory_space=pltpu.SMEM), vmem, hbm] + [anywhere] * 4 + [vmem] * 5,
        out_specs=[vmem] * 5 + [hbm] + [anywhere] * 4,
        input_output_aliases={7 + i: i for i in range(5)},
        scratch_shapes=scratch_for(size, modes, slots),
        compiler_params=pltpu.CompilerParams(vmem_limit_bytes=28 * MIB),
        cost_estimate=SLOTS_COST,
        name="slots_beyond",
    )(meta, probe, in_hbm(amplitudes), *rims, note, *state)
    return (*out[5:], out[2])


def finish_kernel(
    own, right, lower, scale, tile, out, own_s, right_s, lower_s, scale_s, tile_s, in_sems, out_sems
):
    size = right_s.shape[2]
    block = 128
    blocks = own_s.shape[1] // block

    def copies(i):
        rows = pl.ds(i * block, block)
        pairs = [
            (own.at[:, rows], own_s.at[:, rows]),
            (right.at[:, rows], right_s.at[:, rows]),
            (scale.at[rows], scale_s.at[rows]),
            (tile.at[:, rows], tile_s.at[:, rows]),
        ]
        if i < size // block:
            pairs.append((lower.at[:, rows], lower_s.at[:, rows]))
        return [pltpu.make_async_copy(a, b, in_sems.at[i, k]) for k, (a, b) in enumerate(pairs)]

    loads = [copies(i) for i in range(blocks)]
    for load in loads:
        for copy in load:
            copy.start()
    stores = []
    for i in range(blocks):
        for copy in loads[i]:
            copy.wait()
        rows = pl.ds(i * block, block)
        for at in range(i * block, (i + 1) * block, 32):
            part = pl.ds(at, 32)
            for c in range(2):
                near, far = own_s[c, part, :size] + right_s[c, part, :], own_s[c, part, size:]
                if i < size // block:
                    near, far = near + lower_s[c, part, :size], far + lower_s[c, part, size:]
                own_s[c, part, :size] = tile_s[c, part, :size] + near * scale_s[part, :size]
                own_s[c, part, size:] = tile_s[c, part, size:] + far * scale_s[part, size:]
        stores.append(pltpu.make_async_copy(own_s.at[:, rows], out.at[:, rows], out_sems.at[i]))
        stores[-1].start()
    for store in stores:
        store.wait()


def finish(own, right, lower, inverse_light, tile):
    rows, cols = tile.shape[1:]
    size = right.shape[2]
    hbm = pl.BlockSpec(memory_space=pltpu.HBM)
    return pl.pallas_call(
        finish_kernel,
        out_shape=jax.ShapeDtypeStruct(tile.shape, F32),
        in_specs=[hbm] + [pl.BlockSpec(memory_space=pl.ANY)] * 3 + [hbm],
        out_specs=hbm,
        scratch_shapes=[
            pltpu.VMEM(tile.shape, F32),
            pltpu.VMEM((2, rows, size), F32),
            pltpu.VMEM((2, size, cols), F32),
            pltpu.VMEM((rows, cols), F32),
            pltpu.VMEM(tile.shape, F32),
            pltpu.SemaphoreType.DMA((rows // 128, 5)),
            pltpu.SemaphoreType.DMA((rows // 128,)),
        ],
        compiler_params=pltpu.CompilerParams(vmem_limit_bytes=12 * MIB),
        cost_estimate=pl.CostEstimate(flops=3_000_000, bytes_accessed=12_000_000, transcendentals=0),
        name="finish",
    )(in_hbm(own), right, lower, inverse_light, in_hbm(tile))


def from_behind(array, axis, by):
    count = lax.axis_size(axis)
    pairs = [(i, i + by) for i in range(count) if 0 <= i + by < count]
    return lax.ppermute(array, axis, pairs)


def exchange(array, axis, bit):
    count = lax.axis_size(axis)
    return lax.ppermute(array, axis, [(i, i ^ bit) for i in range(count)])


def together(*arrays):
    return lax.optimization_barrier(arrays)


def cut(tile, regions, cost, name):
    def kernel(tile, *refs):
        sems = refs[-1]
        copies = [
            pltpu.make_async_copy(tile.at[:, pl.ds(at, height), pl.ds(0, width)], out, sems.at[i])
            for i, ((at, height, width), out) in enumerate(zip(regions, refs[:-1]))
        ]
        for copy in copies:
            copy.start()
        for copy in copies:
            copy.wait()

    return pl.pallas_call(
        kernel,
        out_shape=[jax.ShapeDtypeStruct((2, height, width), F32) for _, height, width in regions],
        in_specs=[pl.BlockSpec(memory_space=pltpu.HBM)],
        out_specs=[pl.BlockSpec(memory_space=pltpu.VMEM)] * len(regions),
        scratch_shapes=[pltpu.SemaphoreType.DMA((len(regions),))],
        compiler_params=pltpu.CompilerParams(vmem_limit_bytes=4 * MIB),
        cost_estimate=cost,
        name=name,
    )(in_hbm(tile))


def fold(places, index, mine, got, upper):
    count, half, width = got.shape
    quarter = half // 2

    def kernel(places, mine, got, send, keep):
        base = 0 if index is None else places[0, index] * half
        for k, out in ((1 - places[0, upper], send), (places[0, upper], keep)):
            for c in range(count):
                out[c] = (
                    mine[c, pl.ds(pl.multiple_of(base + k * quarter, quarter), quarter), :]
                    + got[c, pl.ds(pl.multiple_of(k * quarter, quarter), quarter), :]
                )

    vmem = pl.BlockSpec(memory_space=pltpu.VMEM)
    shape = jax.ShapeDtypeStruct((count, quarter, width), F32)
    return pl.pallas_call(
        kernel,
        out_shape=[shape, shape],
        in_specs=[pl.BlockSpec(memory_space=pltpu.SMEM), vmem, vmem],
        out_specs=[vmem, vmem],
        compiler_params=pltpu.CompilerParams(vmem_limit_bytes=6 * MIB),
        cost_estimate=SHORT,
        name="fold",
    )(places, mine, got)


def merge(right, corner):
    rows, size = right.shape[1] - 8, right.shape[2]

    def kernel(right, corner, out):
        for c in range(2):
            out[c, :size, :] = right[c, :size, :] + corner[c, :size, :]
            out[c, size:rows, :] = right[c, size:rows, :]
        out[0, rows:, :] = right[0, rows:, :]
        out[1, rows:, :] = corner[0, size:, :]

    vmem = pl.BlockSpec(memory_space=pltpu.VMEM)
    return pl.pallas_call(
        kernel,
        out_shape=jax.ShapeDtypeStruct(right.shape, F32),
        in_specs=[vmem, vmem],
        out_specs=vmem,
        compiler_params=pltpu.CompilerParams(vmem_limit_bytes=4 * MIB),
        cost_estimate=SHORT,
        name="merge",
    )(right, corner)


def deal(terms, parts, rows):
    count, _, width = terms[0].shape
    if rows % 8:
        return sum(terms).reshape(count, parts, rows, width).transpose(1, 0, 2, 3)

    def kernel(*refs):
        terms, out = refs[:-1], refs[-1]
        for j in range(parts):
            for c in range(count):
                out[j, c] = sum(term[c, j * rows : (j + 1) * rows, :] for term in terms)

    vmem = pl.BlockSpec(memory_space=pltpu.VMEM)
    return pl.pallas_call(
        kernel,
        out_shape=jax.ShapeDtypeStruct((parts, count, rows, width), F32),
        in_specs=[vmem] * len(terms),
        out_specs=vmem,
        compiler_params=pltpu.CompilerParams(vmem_limit_bytes=4 * MIB),
        cost_estimate=SHORT,
        name="deal",
    )(*terms)


def settle(places, start, probe, pieces):
    parts, count, rows, width = pieces.shape
    shape = (parts, count - 1, rows, width)
    if rows % 8:
        share = pieces.sum(axis=0)
        old = lax.dynamic_slice_in_dim(probe, places[0, start], rows, axis=1)
        return jnp.broadcast_to((old + share[:-1] / (share[-1:] + 1.0))[None], shape)

    def kernel(places, probe, pieces, out, old, sem):
        spot = pl.ds(pl.multiple_of(places[0, start], 8), rows)
        copy = pltpu.make_async_copy(probe.at[:, spot], old, sem.at[0])
        copy.start()
        share = sum(pieces[j] for j in range(parts))
        copy.wait()
        new = old[...] + share[:-1] / (share[-1:] + 1.0)
        for j in range(parts):
            out[j] = new

    vmem = pl.BlockSpec(memory_space=pltpu.VMEM)
    return pl.pallas_call(
        kernel,
        out_shape=jax.ShapeDtypeStruct(shape, F32),
        in_specs=[pl.BlockSpec(memory_space=pltpu.SMEM), pl.BlockSpec(memory_space=pltpu.HBM), vmem],
        out_specs=vmem,
        scratch_shapes=[pltpu.VMEM(shape[1:], F32), pltpu.SemaphoreType.DMA((1,))],
        compiler_params=pltpu.CompilerParams(vmem_limit_bytes=4 * MIB),
        cost_estimate=SHORT,
        name="settle",
    )(places, in_hbm(probe), pieces)


def collect(pieces):
    parts, count, rows, width = pieces.shape
    if rows % 8:
        return pieces.transpose(1, 0, 2, 3).reshape(count, parts * rows, width)

    def kernel(pieces, out):
        for j in range(parts):
            for c in range(count):
                out[c, j * rows : (j + 1) * rows, :] = pieces[j, c]

    vmem = pl.BlockSpec(memory_space=pltpu.VMEM)
    return pl.pallas_call(
        kernel,
        out_shape=jax.ShapeDtypeStruct((count, parts * rows, width), F32),
        in_specs=[vmem],
        out_specs=vmem,
        compiler_params=pltpu.CompilerParams(vmem_limit_bytes=4 * MIB),
        cost_estimate=SHORT,
        name="collect",
    )(pieces)


def join(places, upper, mine, other):
    half = mine.shape[1]

    def kernel(places, mine, other, out, sems):
        copies = [
            pltpu.make_async_copy(source, out.at[:, pl.ds(pl.multiple_of(at * half, half), half)], sems.at[i])
            for i, (source, at) in enumerate(((mine, places[0, upper]), (other, 1 - places[0, upper])))
        ]
        for copy in copies:
            copy.start()
        for copy in copies:
            copy.wait()

    anywhere = pl.BlockSpec(memory_space=pl.ANY)
    return pl.pallas_call(
        kernel,
        out_shape=jax.ShapeDtypeStruct((mine.shape[0], 2 * half) + mine.shape[2:], F32),
        in_specs=[pl.BlockSpec(memory_space=pltpu.SMEM), anywhere, anywhere],
        out_specs=anywhere,
        scratch_shapes=[pltpu.SemaphoreType.DMA((2,))],
        compiler_params=pltpu.CompilerParams(vmem_limit_bytes=MIB),
        cost_estimate=pl.CostEstimate(flops=0, bytes_accessed=2_000_000, transcendentals=0),
        name="join",
    )(places, mine, other)


def body(object_field, probe, amplitudes, positions, counts):
    modes, _, size, _ = probe.shape
    tile_rows, tile_cols = object_field.shape[1:]
    slots = amplitudes.shape[0]
    origin = jnp.stack([lax.axis_index("row") * tile_rows, lax.axis_index("col") * tile_cols]).astype(jnp.int32)
    bits = [1 << k for k in range(lax.axis_size("row").bit_length() - 1)]
    uppers = [(lax.axis_index("row") & bit) // bit for bit in bits]

    def relative(table):
        return jnp.concatenate([table[:, : 2 * slots] - jnp.tile(origin, slots)[None], table[:, 2 * slots :]], axis=1)

    right_up, right_down = cut(
        object_field, ((0, size, size), (size, tile_rows - size, size)), SHORT, "cut_right"
    )
    right_up, right_down, after_right = together(right_up, right_down, object_field)
    right_up = from_behind(right_up, "col", -1)
    right_down = from_behind(right_down, "col", -1)
    (lower,) = cut(after_right, ((0, size, tile_cols),), LONG, "cut_lower")
    meta = jnp.concatenate([positions.reshape(1, 2 * slots), counts.reshape(1, 1)], axis=1)
    lower = from_behind(lower, "row", -1)

    parts = lax.axis_size("col")
    rows = (size >> len(bits)) // parts
    me = lax.axis_index("col")
    start = sum(upper * (size >> (k + 1)) for k, upper in enumerate(uppers)) + me * rows
    bit_at = 2 * slots + 2
    me_at = bit_at + len(bits)
    start_at, origin_at = me_at + 1, me_at + 2
    extra = [1 - uppers[0], *uppers, me, start, origin[0], origin[1]]
    mine = jnp.concatenate([relative(meta), jnp.stack([item.astype(jnp.int32) for item in extra])[None]], axis=1)
    note = jnp.pad(meta.astype(F32), ((0, 7), (0, size - meta.shape[1])))
    mine, note = together(mine, note)
    amplitudes = arrange(mine, amplitudes)
    right_up, amplitudes = together(right_up, amplitudes)
    corner = from_behind(right_up, "row", -1)
    amplitudes, lower = together(amplitudes, lower)
    state = visit_inside(mine, probe, amplitudes, object_field, lower)
    right_up, right_down, corner, *state = together(right_up, right_down, corner, *state)
    own, right_spill, corner_spill, lower_spill, send, share = visit_beyond(
        mine, probe, amplitudes, [right_up, right_down, corner], note, state
    )

    index = bit_at
    for k, bit in enumerate(bits):
        got = exchange(send, "row", bit)
        if k == 0:
            corner_spill = from_behind(corner_spill, "row", 1)
        if k + 1 < len(bits):
            send, share = fold(mine, index, share, got, bit_at + k + 1)
            index = None
    got, corner_spill, lower_spill = together(got, corner_spill, lower_spill)
    lower_spill = from_behind(lower_spill, "row", 1)
    right_spill = from_behind(merge(right_spill, corner_spill), "col", 1)
    pieces = lax.all_to_all(deal([share, got], parts, rows), "col", 0, 0, tiled=True)
    new = settle(mine, start_at, probe.reshape(2 * modes, size, size), pieces)
    new = collect(lax.all_to_all(new, "col", 0, 0, tiled=True))
    new, right_spill = together(new, right_spill)
    inverse_light = light(mine, slots, origin_at, probe, right_spill, corner_spill, (tile_rows, tile_cols))
    for k, bit in reversed(list(enumerate(bits))):
        if k == 0:
            new, own = together(new, own)
            new_object = finish(own, right_spill, lower_spill, inverse_light, object_field)
        other = exchange(new, "row", bit)
        if k + 1 == len(bits):
            other, inverse_light = together(other, inverse_light)
        if k == 0:
            other, new_object = together(other, new_object)
        new = join(mine, bit_at + k, new, other)
    return (new_object, new.reshape(modes, 2, size, size))


def solution(mesh):
    in_specs = (
        P(None, "row", "col"),
        P(),
        P(("row", "col"), None, None),
        P(("row", "col"), None),
        P(("row", "col")),
    )
    out_specs = (P(None, "row", "col"), P())
    return jax.shard_map(body, mesh=mesh, in_specs=in_specs, out_specs=out_specs, check_vma=False)
```

```python
import functools
import math

import jax
import jax.numpy as jnp
import ml_dtypes
import numpy as np
from jax import lax
from jax.experimental import pallas as pl
from jax.experimental.pallas import tpu as pltpu
from jax.sharding import PartitionSpec as P

F32 = jnp.float32
BF16 = jnp.bfloat16
MIB = 1024 * 1024
LONG = pl.CostEstimate(flops=30_000_000_000, bytes_accessed=4_000_000, transcendentals=0)
SHORT = pl.CostEstimate(flops=0, bytes_accessed=1_000_000, transcendentals=0)
FLOOR = 0.3


def split_np(table):
    high = table.astype(ml_dtypes.bfloat16)
    low = (table - high.astype(np.float64)).astype(ml_dtypes.bfloat16)
    return high, low


def dft_tables(length):
    half = length // 2
    q = np.arange(half)[:, None]
    n = np.arange(half)[None, :]
    forward = []
    for odd in range(2):
        phase = (n * (2 * q + odd)) % length
        angle = phase * (-2.0 * math.pi / length)
        re = np.cos(angle) / math.sqrt(length)
        im = np.sin(angle) / math.sqrt(length)
        forward.append(np.stack(split_np(np.block([[re, -im], [im, re]]))))
    forward = np.stack(forward)
    return forward, np.ascontiguousarray(forward.transpose(0, 1, 3, 2))


def in_hbm(array):
    return pltpu.with_memory_space_constraint(array, pltpu.HBM)


def dot(a, b):
    return jnp.dot(a, b, preferred_element_type=F32)


def split(x):
    high = x.astype(BF16)
    return high, (x - high.astype(F32)).astype(BF16)


def roll_rows(x, shift):
    return pltpu.roll(x.reshape(x.shape[0] // 8, 8, x.shape[1]), shift, 1)


def roll_rows(x, shift):
    return pltpu.roll(x.reshape(x.shape[0] // 8, 8, x.shape[1]), shift, 1)


def roll_rows(x, shift):
    return pltpu.roll(x.reshape(x.shape[0] // 8, 8, x.shape[1]), shift, 1)


def roll_rows(x, shift):
    return pltpu.roll(x.reshape(x.shape[0] // 8, 8, x.shape[1]), shift, 1)


def split_three(x):
    high = x.astype(BF16)
    rest = x - high.astype(F32)
    middle = rest.astype(BF16)
    return high, middle, (rest - middle.astype(F32)).astype(BF16)


def add_shifted(template, grid, where_t, where_g, top, left, size):
    top_s = top & 7
    top_b = pl.multiple_of(top - top_s, 8)
    left_s = left & 127
    left_b = pl.multiple_of(left - left_s, 128)
    step = 24
    wrapped = lax.broadcasted_iota(jnp.int32, (step, 128), 1) < left_s
    wrapped_rows = lax.broadcasted_iota(jnp.int32, (step // 8, 8, 128), 1) < top_s
    zero = jnp.zeros((step, 128), F32)
    blocks = size // 128
    for at in range(0, size + 8, step):
        parts = []
        for j in range(blocks):
            x = roll_rows(template[where_t + (pl.ds(at, step + 8), pl.ds(128 * j, 128))], top_s)
            x = jnp.where(wrapped_rows, x[:-1], x[1:]).reshape(step, 128)
            parts.append(pltpu.roll(x, left_s, 1))
        for j in range(blocks + 1):
            before = parts[j - 1] if j > 0 else zero
            after = parts[j] if j < blocks else zero
            spot = where_g + (pl.ds(top_b + at, step), pl.ds(left_b + 128 * j, 128))
            grid[spot] += jnp.where(wrapped, before, after)


def take_shifted(field, where, top, left, at, step, size):
    top_s = top & 7
    top_b = pl.multiple_of(top - top_s, 8)
    left_s = left & 127
    left_b = pl.multiple_of(left - left_s, 128)
    back = (128 - left_s) & 127
    keep = lax.broadcasted_iota(jnp.int32, (step + 8, 128), 1) < 128 - left_s
    keep_rows = lax.broadcasted_iota(jnp.int32, (step // 8, 8, 128), 1) < 8 - top_s
    blocks = size // 128
    parts = [
        pltpu.roll(field[where + (pl.ds(top_b + at, step + 8), pl.ds(left_b + 128 * j, 128))], back, 1)
        for j in range(blocks + 1)
    ]
    pieces = []
    for j in range(blocks):
        x = roll_rows(jnp.where(keep, parts[j], parts[j + 1]), (8 - top_s) & 7)
        pieces.append(jnp.where(keep_rows, x[:-1], x[1:]).reshape(step, 128))
    return jnp.concatenate(pieces, axis=1)


def light_kernel(slots, origin, meta, probe_h, bottom, corner, lower, inverse_light, probe, template, grid, notes, sems):
    size = probe.shape[2]
    tile_rows, tile_cols = inverse_light.shape
    copies = [
        pltpu.make_async_copy(spill.at[0, pl.ds(spill.shape[1] - 8, 8), pl.ds(0, 128)], notes.at[i], sems.at[i])
        for i, spill in enumerate((bottom, corner, lower))
    ]
    copy = pltpu.make_async_copy(probe_h, probe, sems.at[3])
    copy.start()
    for item in copies:
        item.start()
    template[0:8, :] = jnp.zeros((8, size), F32)
    template[8 + size :, :] = jnp.zeros((8, size), F32)
    copy.wait()
    for at in range(0, size, 32):
        rows = pl.ds(at, 32)
        total = jnp.zeros((32, size), F32)
        for m in range(probe.shape[0]):
            total += probe[m, 0, rows] * probe[m, 0, rows] + probe[m, 1, rows] * probe[m, 1, rows]
        template[pl.ds(8 + at, 32), :] = total

    @pl.loop(0, tile_rows // 32)
    def _(step):
        rows = pl.ds(pl.multiple_of(size + step * 32, 32), 32)
        grid[rows, size : size + tile_cols] = jnp.zeros((32, tile_cols), F32)

    def add(top, left):
        @pl.when((top > 0) & (left > 0))
        def _():
            add_shifted(template, grid, (), (), top, left, size)

    @pl.loop(0, meta[0, 2 * slots])
    def _(slot):
        add(meta[0, 2 * slot] + size, meta[0, 2 * slot + 1] + size)

    for item in copies:
        item.wait()
    for device in range(3):

        @pl.loop(0, notes[device, 0, 2 * slots].astype(jnp.int32))
        def _(slot):
            top = notes[device, 0, 2 * slot].astype(jnp.int32) - meta[0, origin]
            left = notes[device, 0, 2 * slot + 1].astype(jnp.int32) - meta[0, origin + 1]
            add(top + size, left + size)

    @pl.loop(0, tile_rows // 32)
    def _(step):
        rows = pl.ds(pl.multiple_of(size + step * 32, 32), 32)
        out_rows = pl.ds(pl.multiple_of(step * 32, 32), 32)
        inverse_light[out_rows, :] = 1.0 / (grid[rows, size : size + tile_cols] + 1.0)


def light(meta, slots, origin, probe, bottom, corner, lower, tile_shape):
    size = probe.shape[2]
    hbm = pl.BlockSpec(memory_space=pltpu.HBM)
    anywhere = pl.BlockSpec(memory_space=pl.ANY)
    return pl.pallas_call(
        functools.partial(light_kernel, slots, origin),
        out_shape=jax.ShapeDtypeStruct(tile_shape, F32),
        in_specs=[pl.BlockSpec(memory_space=pltpu.SMEM), hbm] + [anywhere] * 3,
        out_specs=pl.BlockSpec(memory_space=pltpu.VMEM),
        scratch_shapes=[
            pltpu.VMEM(probe.shape, F32),
            pltpu.VMEM((size + 16, size), F32),
            pltpu.VMEM((tile_shape[0] + 2 * size, tile_shape[1] + 2 * size), F32),
            pltpu.SMEM((3, 8, 128), F32),
            pltpu.SemaphoreType.DMA((4,)),
        ],
        compiler_params=pltpu.CompilerParams(vmem_limit_bytes=8 * MIB),
        cost_estimate=pl.CostEstimate(flops=4_000_000_000, bytes_accessed=1_000_000, transcendentals=0),
        name="light",
    )(meta, in_hbm(probe), bottom, corner, lower)


def arrange_kernel(meta, amplitudes, out, given, moved, in_sems, out_sems):
    slots, size, _ = amplitudes.shape
    count = meta[0, 2 * slots]

    def load(slot):
        return pltpu.make_async_copy(amplitudes.at[slot], given.at[slot], in_sems.at[slot])

    def store(slot):
        return pltpu.make_async_copy(moved.at[slot], out.at[slot], out_sems.at[slot])

    @pl.loop(0, count)
    def _(slot):
        load(slot).start()

    first = lax.broadcasted_iota(jnp.int32, (size, size), 0)
    second = lax.broadcasted_iota(jnp.int32, (size, size), 1)
    half = size // 2

    def source(index):
        return jnp.where(index < half, 2 * index, 2 * index - (size - 1))

    rows = (source(first) == second).astype(F32).astype(BF16)
    cols = (source(second) == first).astype(F32).astype(BF16)
    rows = jnp.concatenate([rows, rows], axis=1)
    cols = jnp.concatenate([cols, cols], axis=0)

    @pl.loop(0, count)
    def _(slot):
        load(slot).wait()
        x = dot(rows, jnp.concatenate(split(given[slot]), axis=0))
        moved[slot] = dot(jnp.concatenate(split(x), axis=1), cols)
        store(slot).start()

    @pl.loop(0, count)
    def _(slot):
        store(slot).wait()


def arrange(meta, amplitudes):
    slots = amplitudes.shape[0]
    hbm = pl.BlockSpec(memory_space=pltpu.HBM)
    return pl.pallas_call(
        arrange_kernel,
        out_shape=pltpu.HBM(amplitudes.shape, F32),
        in_specs=[pl.BlockSpec(memory_space=pltpu.SMEM), hbm],
        out_specs=hbm,
        scratch_shapes=[
            pltpu.VMEM(amplitudes.shape, F32),
            pltpu.VMEM(amplitudes.shape, F32),
            pltpu.SemaphoreType.DMA((slots,)),
            pltpu.SemaphoreType.DMA((slots,)),
        ],
        compiler_params=pltpu.CompilerParams(vmem_limit_bytes=8 * MIB),
        cost_estimate=LONG,
        name="arrange",
    )(meta, in_hbm(amplitudes))


def three_left(table, t):
    return jnp.concatenate([table[t, 0], table[t, 0], table[t, 1]], axis=1)


def three_right(table, v):
    return jnp.concatenate([table[v, 0], table[v, 0], table[v, 1]], axis=0)


def weave(first, second):
    total = max(len(first), len(second))
    done = [0, 0]
    for i in range(1, total + 1):
        for k, pieces in enumerate((first, second)):
            while done[k] * total < i * len(pieces):
                pieces[done[k]]()
                done[k] += 1


def slots_kernel(
    needs_rim, meta, probe, amplitudes, sources, tables, note, state, outs,
    amp, forward_t, backward_t, chosen, patch_f, patch_b, x_f, y_f, z_f, g_s, x_b, z_b, back, template,
    load_sems, amp_sems, out_sems,
):
    ext, grid, probe_out = state
    size = probe.shape[2]
    half = size // 2
    modes = probe.shape[0]
    slots = amplitudes.shape[0]
    tile_rows, tile_cols = (n - size for n in ext.shape[1:])
    step = 32
    fine = 16

    body_rows, rim_rows = pl.ds(0, tile_rows), pl.ds(tile_rows, size)
    body_cols, rim_cols = pl.ds(0, tile_cols), pl.ds(tile_cols, size)
    if needs_rim:
        places = [
            ext.at[:, pl.ds(0, size), rim_cols],
            ext.at[:, pl.ds(size, tile_rows - size), rim_cols],
            ext.at[:, rim_rows, rim_cols],
        ]
    else:
        places = [ext.at[:, body_rows, body_cols], ext.at[:, rim_rows, body_cols]]
    places += [forward_t, backward_t]
    loads = [
        pltpu.make_async_copy(source, place, load_sems.at[i])
        for i, (source, place) in enumerate(zip([*sources, *tables], places))
    ]
    for load in loads:
        load.start()

    def amp_copy(slot):
        return pltpu.make_async_copy(amplitudes.at[slot], amp.at[slot], amp_sems.at[slot])

    def choose(slot, found):
        beyond = meta[0, 2 * slot + 1] + size > tile_cols
        wanted = beyond if needs_rim else jnp.logical_not(beyond)

        @pl.when(wanted)
        def _():
            chosen[found] = slot
            amp_copy(slot).start()

        return found + wanted.astype(jnp.int32)

    count = lax.fori_loop(0, meta[0, 2 * slots], choose, jnp.zeros((), jnp.int32))

    if not needs_rim:

        @pl.loop(0, (tile_rows + size) // step)
        def _(at):
            rows = pl.ds(pl.multiple_of(at * step, step), step)
            for c in range(2):
                grid[c, rows, :] = jnp.zeros((step, tile_cols + size), F32)

        @pl.loop(0, size // step)
        def _(at):
            rows = pl.ds(pl.multiple_of(at * step, step), step)
            for c in range(2 * modes + 1):
                probe_out[c, rows, :] = jnp.zeros((step, size), F32)

    for c in range(2):
        template[c, 0:8, :] = jnp.zeros((8, size), F32)
        template[c, 8 + size :, :] = jnp.zeros((8, size), F32)
    for load in loads:
        load.wait()

    def corner(slot):
        return meta[0, 2 * slot], meta[0, 2 * slot + 1]

    def forward(slot):
        top, left = corner(slot)

        def take(at):
            for c in range(2):
                patch_f[c, pl.ds(at, step), :] = take_shifted(ext, (c,), top, left, at, step, size)

        def fold_rows(m, at):
            cols = pl.ds(m * size, size)
            parts = []
            for base in (at, half + at):
                rows = pl.ds(base, fine)
                pr, pi = patch_f[0, rows, :], patch_f[1, rows, :]
                qr, qi = probe[m, 0, rows, :], probe[m, 1, rows, :]
                parts.append((qr * pr - qi * pi, qr * pi + qi * pr))
            for c in range(2):
                rows = pl.ds(c * half + at, fine)
                for t, value in enumerate((parts[0][c] + parts[1][c], parts[0][c] - parts[1][c])):
                    x_f[t, 0, rows, cols], x_f[t, 1, rows, cols] = split(value)

        def dft_rows(m, t):
            cols = pl.ds(m * size, size)
            high = x_f[t, 0, :, cols]
            u = dot(three_left(forward_t, t), jnp.concatenate([high, x_f[t, 1, :, cols], high], axis=0))
            rows = pl.ds(m * size + t * half, half)
            for v, value in enumerate((u[:, :half] + u[:, half:], u[:, :half] - u[:, half:])):
                high, low = split(value)
                for c in range(2):
                    lanes = pl.ds(c * half, half)
                    y_f[v, 0, rows, lanes] = high[c * half : (c + 1) * half]
                    y_f[v, 1, rows, lanes] = low[c * half : (c + 1) * half]

        def dft_cols(v):
            high = y_f[v, 0]
            z_f[v] = dot(jnp.concatenate([high, y_f[v, 1], high], axis=1), three_right(backward_t, v))

        def scale(v, at):
            if v == 0 and at == 0:
                amp_copy(slot).wait()
            waves = [z_f[v, pl.ds(m * size + at, fine), :] for m in range(modes)]
            total = jnp.zeros((fine, half), F32)
            for wave in waves:
                total += wave[:, :half] * wave[:, :half] + wave[:, half:] * wave[:, half:]
            measured = amp[slot, pl.ds(at, fine), pl.ds(v * half, half)]
            factor = measured * lax.rsqrt(jnp.maximum(total, FLOOR * FLOOR)) - 1.0
            factor = jnp.concatenate([factor, factor], axis=1)
            for m in range(modes):
                rows = pl.ds(m * size + at, fine)
                g_s[v, 0, rows, :], g_s[v, 1, rows, :] = split(waves[m] * factor)

        pieces = [(take, at) for at in range(0, size, step)]
        for m in range(modes):
            pieces += [(fold_rows, m, at) for at in range(0, half, fine)]
            pieces += [(dft_rows, m, t) for t in range(2)]
        pieces += [(dft_cols, v) for v in range(2)]
        pieces += [(scale, v, at) for v in range(2) for at in range(0, size, fine)]
        return [functools.partial(*piece) for piece in pieces]

    def backward(slot):
        top, left = corner(slot)

        def dft_cols(v):
            high = g_s[v, 0]
            z_b[v] = dot(jnp.concatenate([high, g_s[v, 1], high], axis=1), three_right(forward_t, v))

        def unfold_cols(m, t, at):
            rows = pl.ds(m * size + t * half + at, step)
            even, odd = z_b[0, rows, :], z_b[1, rows, :]
            for v, value in enumerate((even + odd, even - odd)):
                high, low = split(value)
                cols = pl.ds(m * size + v * half, half)
                for c in range(2):
                    spot = pl.ds(c * half + at, step)
                    x_b[t, 0, spot, cols] = high[:, c * half : (c + 1) * half]
                    x_b[t, 1, spot, cols] = low[:, c * half : (c + 1) * half]

        def dft_rows(m, t):
            cols = pl.ds(m * size, size)
            high = x_b[t, 0, :, cols]
            back[m, t] = dot(three_left(backward_t, t), jnp.concatenate([high, x_b[t, 1, :, cols], high], axis=0))

        def gradients(at):
            waves = []
            for m in range(modes):
                pair = []
                for c in range(2):
                    rows = pl.ds(c * half + at, fine)
                    even, odd = back[m, 0, rows, :], back[m, 1, rows, :]
                    pair.append((even + odd, even - odd))
                waves.append(pair)
            for h in range(2):
                rows = pl.ds(h * half + at, fine)
                pr, pi = patch_b[0, rows, :], patch_b[1, rows, :]
                grad_r = jnp.zeros((fine, size), F32)
                grad_i = jnp.zeros((fine, size), F32)
                for m in range(modes):
                    br, bi = waves[m][0][h], waves[m][1][h]
                    qr, qi = probe[m, 0, rows, :], probe[m, 1, rows, :]
                    grad_r += qr * br + qi * bi
                    grad_i += qr * bi - qi * br
                    probe_out[2 * m, rows, :] += pr * br + pi * bi
                    probe_out[2 * m + 1, rows, :] += pr * bi - pi * br
                probe_out[2 * modes, rows, :] += pr * pr + pi * pi
                spot = pl.ds(8 + h * half + at, fine)
                template[0, spot, :] = grad_r
                template[1, spot, :] = grad_i

        def add(c):
            add_shifted(template, grid, (c,), (c,), top, left, size)

        pieces = [(dft_cols, v) for v in range(2)]
        for m in range(modes):
            pieces += [(unfold_cols, m, t, at) for t in range(2) for at in range(0, half, step)]
            pieces += [(dft_rows, m, t) for t in range(2)]
        pieces += [(gradients, at) for at in range(0, half, fine)]
        pieces += [(add, c) for c in range(2)]
        return [functools.partial(*piece) for piece in pieces]

    def hand_over():
        for at in range(0, size, step):
            for c in range(2):
                patch_b[c, pl.ds(at, step), :] = patch_f[c, pl.ds(at, step), :]

    @pl.when(count > 0)
    def _():
        weave(forward(chosen[0]), [])
        hand_over()

        def visit(index, _):
            weave(backward(chosen[index]), forward(chosen[index + 1]))
            hand_over()
            return 0

        lax.fori_loop(0, count - 1, visit, 0)
        weave(backward(chosen[count - 1]), [])

    if needs_rim:
        top, bottom = pl.ds(0, size), pl.ds(size, tile_rows - size)
        parts = [
            (grid.at[:, body_rows, body_cols], outs[0]),
            (grid.at[:, bottom, rim_cols], outs[1].at[:, pl.ds(0, tile_rows - size)]),
            (note, outs[1].at[0, pl.ds(tile_rows - size, 8)]),
            (grid.at[:, top, rim_cols], outs[2]),
            (grid.at[:, rim_rows, rim_cols], outs[3].at[:, top]),
            (note, outs[3].at[0, pl.ds(size, 8)]),
            (grid.at[:, rim_rows, body_cols], outs[4].at[:, top]),
            (probe_out.at[:, pl.ds(pl.multiple_of(meta[0, 2 * slots + 1] * half, half), half)], outs[5]),
        ]
        stores = [pltpu.make_async_copy(part, out, out_sems.at[i]) for i, (part, out) in enumerate(parts)]
        for store in stores:
            store.start()
        for store in stores:
            store.wait()


def scratch_for(size, modes, slots):
    return [
        pltpu.VMEM((slots, size, size), F32),
        pltpu.VMEM((2, 2, size, size), BF16),
        pltpu.VMEM((2, 2, size, size), BF16),
        pltpu.SMEM((slots,), jnp.int32),
        pltpu.VMEM((2, size, size), F32),
        pltpu.VMEM((2, size, size), F32),
        pltpu.VMEM((2, 2, size, modes * size), BF16),
        pltpu.VMEM((2, 2, modes * size, size), BF16),
        pltpu.VMEM((2, modes * size, size), F32),
        pltpu.VMEM((2, 2, modes * size, size), BF16),
        pltpu.VMEM((2, 2, size, modes * size), BF16),
        pltpu.VMEM((2, modes * size, size), F32),
        pltpu.VMEM((modes, 2, size, size), F32),
        pltpu.VMEM((2, size + 16, size), F32),
        pltpu.SemaphoreType.DMA((5,)),
        pltpu.SemaphoreType.DMA((slots,)),
        pltpu.SemaphoreType.DMA((8,)),
    ]


SLOTS_COST = pl.CostEstimate(flops=12_000_000_000, bytes_accessed=16_000_000, transcendentals=0)


def visit_inside(meta, probe, amplitudes, tile, lower):
    size, modes, slots = probe.shape[2], probe.shape[0], amplitudes.shape[0]
    rows, cols = tile.shape[1:]
    tables = [jnp.asarray(item) for item in dft_tables(size)]
    vmem = pl.BlockSpec(memory_space=pltpu.VMEM)
    hbm = pl.BlockSpec(memory_space=pltpu.HBM)
    field = pltpu.VMEM((2, rows + size, cols + size), F32)

    def kernel(meta, probe, amplitudes, tile, lower, forward_h, backward_h, *refs):
        state, scratch = refs[:3], refs[3:]
        slots_kernel(
            False, meta, probe, amplitudes, [tile, lower], [forward_h, backward_h], None, state, None, *scratch
        )

    return pl.pallas_call(
        kernel,
        out_shape=[field, field, pltpu.VMEM((2 * modes + 1, size, size), F32)],
        in_specs=[pl.BlockSpec(memory_space=pltpu.SMEM), vmem, hbm, hbm, pl.BlockSpec(memory_space=pl.ANY), hbm, hbm],
        out_specs=[vmem] * 3,
        scratch_shapes=scratch_for(size, modes, slots),
        compiler_params=pltpu.CompilerParams(vmem_limit_bytes=28 * MIB),
        cost_estimate=SLOTS_COST,
        name="slots_inside",
    )(meta, probe, in_hbm(amplitudes), in_hbm(tile), lower, *map(in_hbm, tables))


def visit_beyond(meta, probe, amplitudes, rims, note, state):
    size, modes, slots = probe.shape[2], probe.shape[0], amplitudes.shape[0]
    rows, cols = (n - size for n in state[0].shape[1:])
    tables = [jnp.asarray(item) for item in dft_tables(size)]
    vmem = pl.BlockSpec(memory_space=pltpu.VMEM)
    hbm = pl.BlockSpec(memory_space=pltpu.HBM)
    anywhere = pl.BlockSpec(memory_space=pl.ANY)
    shapes = [
        (2, rows - size + 8, size),
        (2, size, size),
        (2, size + 8, size),
        (2, size + 8, cols),
        (2 * modes + 1, size // 2, size),
    ]

    def kernel(meta, probe, amplitudes, forward_h, backward_h, *refs):
        rims, note, refs = refs[:3], refs[3], refs[7:]
        state, outs, scratch = refs[:3], refs[3:9], refs[9:]
        slots_kernel(True, meta, probe, amplitudes, rims, [forward_h, backward_h], note, state, outs, *scratch)

    out = pl.pallas_call(
        kernel,
        out_shape=[pltpu.VMEM(item.shape, item.dtype) for item in state]
        + [pltpu.HBM((2, rows, cols), F32)]
        + [jax.ShapeDtypeStruct(shape, F32) for shape in shapes],
        in_specs=[pl.BlockSpec(memory_space=pltpu.SMEM), vmem] + [hbm] * 3 + [anywhere] * 4 + [vmem] * 3,
        out_specs=[vmem] * 3 + [hbm] + [anywhere] * 5,
        input_output_aliases={9 + i: i for i in range(3)},
        scratch_shapes=scratch_for(size, modes, slots),
        compiler_params=pltpu.CompilerParams(vmem_limit_bytes=28 * MIB),
        cost_estimate=SLOTS_COST,
        name="slots_beyond",
    )(meta, probe, *map(in_hbm, [amplitudes, *tables]), *rims, note, *state)
    return (*out[3:], out[2])


def finish_kernel(
    own, top, bottom, lower, scale, tile, out, own_s, right_s, lower_s, scale_s, tile_s, in_sems, out_sems
):
    size = right_s.shape[2]
    block = 128
    blocks = own_s.shape[1] // block

    def copies(i):
        rows = pl.ds(i * block, block)
        pairs = [
            (own.at[:, rows], own_s.at[:, rows]),
            (scale.at[rows], scale_s.at[rows]),
            (tile.at[:, rows], tile_s.at[:, rows]),
        ]
        if i < size // block:
            pairs.append((top.at[:, rows], right_s.at[:, rows]))
            pairs.append((lower.at[:, rows], lower_s.at[:, rows]))
        else:
            pairs.append((bottom.at[:, pl.ds(i * block - size, block)], right_s.at[:, rows]))
        return [pltpu.make_async_copy(a, b, in_sems.at[i, k]) for k, (a, b) in enumerate(pairs)]

    loads = [copies(i) for i in range(blocks)]
    for load in loads:
        for copy in load:
            copy.start()
    stores = []
    for i in range(blocks):
        for copy in loads[i]:
            copy.wait()
        rows = pl.ds(i * block, block)
        for at in range(i * block, (i + 1) * block, 32):
            part = pl.ds(at, 32)
            for c in range(2):
                near, far = own_s[c, part, :size] + right_s[c, part, :], own_s[c, part, size:]
                if i < size // block:
                    near, far = near + lower_s[c, part, :size], far + lower_s[c, part, size:]
                own_s[c, part, :size] = tile_s[c, part, :size] + near * scale_s[part, :size]
                own_s[c, part, size:] = tile_s[c, part, size:] + far * scale_s[part, size:]
        stores.append(pltpu.make_async_copy(own_s.at[:, rows], out.at[:, rows], out_sems.at[i]))
        stores[-1].start()
    for store in stores:
        store.wait()


def finish(own, top, bottom, lower, inverse_light, tile):
    rows, cols = tile.shape[1:]
    size = top.shape[2]
    hbm = pl.BlockSpec(memory_space=pltpu.HBM)
    return pl.pallas_call(
        finish_kernel,
        out_shape=jax.ShapeDtypeStruct(tile.shape, F32),
        in_specs=[hbm] + [pl.BlockSpec(memory_space=pl.ANY)] * 4 + [hbm],
        out_specs=hbm,
        scratch_shapes=[
            pltpu.VMEM(tile.shape, F32),
            pltpu.VMEM((2, rows, size), F32),
            pltpu.VMEM((2, size, cols), F32),
            pltpu.VMEM((rows, cols), F32),
            pltpu.VMEM(tile.shape, F32),
            pltpu.SemaphoreType.DMA((rows // 128, 5)),
            pltpu.SemaphoreType.DMA((rows // 128,)),
        ],
        compiler_params=pltpu.CompilerParams(vmem_limit_bytes=12 * MIB),
        cost_estimate=pl.CostEstimate(flops=3_000_000, bytes_accessed=12_000_000, transcendentals=0),
        name="finish",
    )(in_hbm(own), top, bottom, lower, inverse_light, in_hbm(tile))


def from_behind(array, axis, by):
    count = lax.axis_size(axis)
    pairs = [(i, i + by) for i in range(count) if 0 <= i + by < count]
    return lax.ppermute(array, axis, pairs)


def exchange(array, axis, bit):
    count = lax.axis_size(axis)
    return lax.ppermute(array, axis, [(i, i ^ bit) for i in range(count)])


def together(*arrays):
    return lax.optimization_barrier(arrays)


def cut(tile, regions, cost, name):
    def kernel(tile, *refs):
        sems = refs[-1]
        copies = [
            pltpu.make_async_copy(tile.at[:, pl.ds(at, height), pl.ds(0, width)], out, sems.at[i])
            for i, ((at, height, width), out) in enumerate(zip(regions, refs[:-1]))
        ]
        for copy in copies:
            copy.start()
        for copy in copies:
            copy.wait()

    return pl.pallas_call(
        kernel,
        out_shape=[jax.ShapeDtypeStruct((2, height, width), F32) for _, height, width in regions],
        in_specs=[pl.BlockSpec(memory_space=pltpu.HBM)],
        out_specs=[pl.BlockSpec(memory_space=pltpu.VMEM)] * len(regions),
        scratch_shapes=[pltpu.SemaphoreType.DMA((len(regions),))],
        compiler_params=pltpu.CompilerParams(vmem_limit_bytes=4 * MIB),
        cost_estimate=cost,
        name=name,
    )(in_hbm(tile))


def fold(places, index, mine, got, upper):
    count, half, width = got.shape
    quarter = half // 2

    def kernel(places, mine, got, send, keep):
        base = 0 if index is None else places[0, index] * half
        for k, out in ((1 - places[0, upper], send), (places[0, upper], keep)):
            for c in range(count):
                out[c] = (
                    mine[c, pl.ds(pl.multiple_of(base + k * quarter, quarter), quarter), :]
                    + got[c, pl.ds(pl.multiple_of(k * quarter, quarter), quarter), :]
                )

    vmem = pl.BlockSpec(memory_space=pltpu.VMEM)
    shape = jax.ShapeDtypeStruct((count, quarter, width), F32)
    return pl.pallas_call(
        kernel,
        out_shape=[shape, shape],
        in_specs=[pl.BlockSpec(memory_space=pltpu.SMEM), vmem, vmem],
        out_specs=[vmem, vmem],
        compiler_params=pltpu.CompilerParams(vmem_limit_bytes=6 * MIB),
        cost_estimate=SHORT,
        name="fold",
    )(places, mine, got)


def merge(top, corner):
    size = top.shape[1]

    def kernel(top, corner, out):
        for c in range(2):
            out[c] = top[c] + corner[c, :size, :]

    vmem = pl.BlockSpec(memory_space=pltpu.VMEM)
    return pl.pallas_call(
        kernel,
        out_shape=jax.ShapeDtypeStruct(top.shape, F32),
        in_specs=[vmem, vmem],
        out_specs=vmem,
        compiler_params=pltpu.CompilerParams(vmem_limit_bytes=4 * MIB),
        cost_estimate=SHORT,
        name="merge",
    )(top, corner)


def annotate(lower, bottom):
    size = bottom.shape[2]

    def kernel(lower, bottom, out, sem):
        source = bottom.at[0, pl.ds(bottom.shape[1] - 8, 8)]
        copy = pltpu.make_async_copy(source, out.at[0, pl.ds(out.shape[1] - 8, 8), pl.ds(0, size)], sem.at[0])
        copy.start()
        copy.wait()

    anywhere = pl.BlockSpec(memory_space=pl.ANY)
    return pl.pallas_call(
        kernel,
        out_shape=jax.ShapeDtypeStruct(lower.shape, F32),
        in_specs=[anywhere, anywhere],
        out_specs=anywhere,
        input_output_aliases={0: 0},
        scratch_shapes=[pltpu.SemaphoreType.DMA((1,))],
        compiler_params=pltpu.CompilerParams(vmem_limit_bytes=MIB),
        cost_estimate=SHORT,
        name="annotate",
    )(lower, bottom)


def deal(terms, parts, rows):
    count, _, width = terms[0].shape
    if rows % 8:
        return sum(terms).reshape(count, parts, rows, width).transpose(1, 0, 2, 3)

    def kernel(*refs):
        terms, out = refs[:-1], refs[-1]
        for j in range(parts):
            for c in range(count):
                out[j, c] = sum(term[c, j * rows : (j + 1) * rows, :] for term in terms)

    vmem = pl.BlockSpec(memory_space=pltpu.VMEM)
    return pl.pallas_call(
        kernel,
        out_shape=jax.ShapeDtypeStruct((parts, count, rows, width), F32),
        in_specs=[vmem] * len(terms),
        out_specs=vmem,
        compiler_params=pltpu.CompilerParams(vmem_limit_bytes=4 * MIB),
        cost_estimate=SHORT,
        name="deal",
    )(*terms)


def settle(places, start, probe, pieces):
    parts, count, rows, width = pieces.shape
    shape = (parts, count - 1, rows, width)
    if rows % 8:
        share = pieces.sum(axis=0)
        old = lax.dynamic_slice_in_dim(probe, places[0, start], rows, axis=1)
        return jnp.broadcast_to((old + share[:-1] / (share[-1:] + 1.0))[None], shape)

    def kernel(places, probe, pieces, out, old, sem):
        spot = pl.ds(pl.multiple_of(places[0, start], 8), rows)
        copy = pltpu.make_async_copy(probe.at[:, spot], old, sem.at[0])
        copy.start()
        share = sum(pieces[j] for j in range(parts))
        copy.wait()
        new = old[...] + share[:-1] / (share[-1:] + 1.0)
        for j in range(parts):
            out[j] = new

    vmem = pl.BlockSpec(memory_space=pltpu.VMEM)
    return pl.pallas_call(
        kernel,
        out_shape=jax.ShapeDtypeStruct(shape, F32),
        in_specs=[pl.BlockSpec(memory_space=pltpu.SMEM), pl.BlockSpec(memory_space=pltpu.HBM), vmem],
        out_specs=vmem,
        scratch_shapes=[pltpu.VMEM(shape[1:], F32), pltpu.SemaphoreType.DMA((1,))],
        compiler_params=pltpu.CompilerParams(vmem_limit_bytes=4 * MIB),
        cost_estimate=SHORT,
        name="settle",
    )(places, in_hbm(probe), pieces)


def collect(pieces):
    parts, count, rows, width = pieces.shape
    if rows % 8:
        return pieces.transpose(1, 0, 2, 3).reshape(count, parts * rows, width)

    def kernel(pieces, out):
        for j in range(parts):
            for c in range(count):
                out[c, j * rows : (j + 1) * rows, :] = pieces[j, c]

    vmem = pl.BlockSpec(memory_space=pltpu.VMEM)
    return pl.pallas_call(
        kernel,
        out_shape=jax.ShapeDtypeStruct((count, parts * rows, width), F32),
        in_specs=[vmem],
        out_specs=vmem,
        compiler_params=pltpu.CompilerParams(vmem_limit_bytes=4 * MIB),
        cost_estimate=SHORT,
        name="collect",
    )(pieces)


def join(places, upper, mine, other):
    half = mine.shape[1]

    def kernel(places, mine, other, out, sems):
        copies = [
            pltpu.make_async_copy(source, out.at[:, pl.ds(pl.multiple_of(at * half, half), half)], sems.at[i])
            for i, (source, at) in enumerate(((mine, places[0, upper]), (other, 1 - places[0, upper])))
        ]
        for copy in copies:
            copy.start()
        for copy in copies:
            copy.wait()

    anywhere = pl.BlockSpec(memory_space=pl.ANY)
    return pl.pallas_call(
        kernel,
        out_shape=jax.ShapeDtypeStruct((mine.shape[0], 2 * half) + mine.shape[2:], F32),
        in_specs=[pl.BlockSpec(memory_space=pltpu.SMEM), anywhere, anywhere],
        out_specs=anywhere,
        scratch_shapes=[pltpu.SemaphoreType.DMA((2,))],
        compiler_params=pltpu.CompilerParams(vmem_limit_bytes=MIB),
        cost_estimate=pl.CostEstimate(flops=0, bytes_accessed=2_000_000, transcendentals=0),
        name="join",
    )(places, mine, other)


def body(object_field, probe, amplitudes, positions, counts):
    modes, _, size, _ = probe.shape
    tile_rows, tile_cols = object_field.shape[1:]
    slots = amplitudes.shape[0]
    origin = jnp.stack([lax.axis_index("row") * tile_rows, lax.axis_index("col") * tile_cols]).astype(jnp.int32)
    bits = [1 << k for k in range(lax.axis_size("row").bit_length() - 1)]
    uppers = [(lax.axis_index("row") & bit) // bit for bit in bits]

    def relative(table):
        return jnp.concatenate([table[:, : 2 * slots] - jnp.tile(origin, slots)[None], table[:, 2 * slots :]], axis=1)

    right_up, right_down = cut(
        object_field, ((0, size, size), (size, tile_rows - size, size)), SHORT, "cut_right"
    )
    right_up, right_down, after_right = together(right_up, right_down, object_field)
    right_up = from_behind(right_up, "col", -1)
    right_down = from_behind(right_down, "col", -1)
    (lower,) = cut(after_right, ((0, size, tile_cols),), LONG, "cut_lower")
    meta = jnp.concatenate([positions.reshape(1, 2 * slots), counts.reshape(1, 1)], axis=1)
    lower = from_behind(lower, "row", -1)

    parts = lax.axis_size("col")
    rows = (size >> len(bits)) // parts
    me = lax.axis_index("col")
    start = sum(upper * (size >> (k + 1)) for k, upper in enumerate(uppers)) + me * rows
    bit_at = 2 * slots + 2
    me_at = bit_at + len(bits)
    start_at, origin_at = me_at + 1, me_at + 2
    extra = [1 - uppers[0], *uppers, me, start, origin[0], origin[1]]
    mine = jnp.concatenate([relative(meta), jnp.stack([item.astype(jnp.int32) for item in extra])[None]], axis=1)
    note = jnp.pad(meta.astype(F32), ((0, 7), (0, size - meta.shape[1])))
    mine, note = together(mine, note)
    amplitudes = arrange(mine, amplitudes)
    right_up, amplitudes = together(right_up, amplitudes)
    corner = from_behind(right_up, "row", -1)
    amplitudes, lower = together(amplitudes, lower)
    state = visit_inside(mine, probe, amplitudes, object_field, lower)
    right_up, right_down, corner, *state = together(right_up, right_down, corner, *state)
    own, bottom_spill, top_spill, corner_spill, lower_spill, send, share = visit_beyond(
        mine, probe, amplitudes, [right_up, right_down, corner], note, state
    )

    index = bit_at
    for k, bit in enumerate(bits):
        got = exchange(send, "row", bit)
        if k == 0:
            bottom_spill = from_behind(bottom_spill, "col", 1)
        if k + 1 < len(bits):
            send, share = fold(mine, index, share, got, bit_at + k + 1)
            index = None
    got, bottom_spill, lower_spill = together(got, bottom_spill, lower_spill)
    lower_spill = from_behind(annotate(lower_spill, bottom_spill), "row", 1)
    pieces = lax.all_to_all(deal([share, got], parts, rows), "col", 0, 0, tiled=True)
    new = settle(mine, start_at, probe.reshape(2 * modes, size, size), pieces)
    new, lower_spill, corner_spill = together(new, lower_spill, corner_spill)
    corner_spill = from_behind(corner_spill, "row", 1)
    inverse_light = light(
        mine, slots, origin_at, probe, bottom_spill, corner_spill, lower_spill, (tile_rows, tile_cols)
    )
    new = collect(lax.all_to_all(new, "col", 0, 0, tiled=True))
    new, corner_spill = together(new, corner_spill)
    top_spill = from_behind(merge(top_spill, corner_spill), "col", 1)
    for k, bit in reversed(list(enumerate(bits))):
        if k == 0:
            new, own = together(new, own)
            new_object = finish(own, top_spill, bottom_spill, lower_spill, inverse_light, object_field)
        other = exchange(new, "row", bit)
        if k + 1 == len(bits):
            other, inverse_light = together(other, inverse_light)
        if k == 0:
            other, new_object = together(other, new_object)
        new = join(mine, bit_at + k, new, other)
    return (new_object, new.reshape(modes, 2, size, size))


def solution(mesh):
    in_specs = (
        P(None, "row", "col"),
        P(),
        P(("row", "col"), None, None),
        P(("row", "col"), None),
        P(("row", "col")),
    )
    out_specs = (P(None, "row", "col"), P())
    return jax.shard_map(body, mesh=mesh, in_specs=in_specs, out_specs=out_specs, check_vma=False)
```

```python
import functools
import math

import jax
import jax.numpy as jnp
import ml_dtypes
import numpy as np
from jax import lax
from jax.experimental import pallas as pl
from jax.experimental.pallas import tpu as pltpu
from jax.sharding import PartitionSpec as P

F32 = jnp.float32
BF16 = jnp.bfloat16
MIB = 1024 * 1024
LONG = pl.CostEstimate(flops=30_000_000_000, bytes_accessed=4_000_000, transcendentals=0)
SHORT = pl.CostEstimate(flops=0, bytes_accessed=1_000_000, transcendentals=0)
FLOOR = 0.3


def split_np(table):
    high = table.astype(ml_dtypes.bfloat16)
    low = (table - high.astype(np.float64)).astype(ml_dtypes.bfloat16)
    return high, low


def dft_tables(length):
    half = length // 2
    q = np.arange(half)[:, None]
    n = np.arange(half)[None, :]
    forward = []
    for odd in range(2):
        phase = (n * (2 * q + odd)) % length
        angle = phase * (-2.0 * math.pi / length)
        re = np.cos(angle) / math.sqrt(length)
        im = np.sin(angle) / math.sqrt(length)
        forward.append(np.stack(split_np(np.block([[re, -im], [im, re]]))))
    forward = np.stack(forward)
    return forward, np.ascontiguousarray(forward.transpose(0, 1, 3, 2))


def in_hbm(array):
    return pltpu.with_memory_space_constraint(array, pltpu.HBM)


def dot(a, b):
    return jnp.dot(a, b, preferred_element_type=F32)


def split(x):
    high = x.astype(BF16)
    return high, (x - high.astype(F32)).astype(BF16)


def roll_rows(x, shift):
    return pltpu.roll(x.reshape(x.shape[0] // 8, 8, x.shape[1]), shift, 1)


def roll_rows(x, shift):
    return pltpu.roll(x.reshape(x.shape[0] // 8, 8, x.shape[1]), shift, 1)


def roll_rows(x, shift):
    return pltpu.roll(x.reshape(x.shape[0] // 8, 8, x.shape[1]), shift, 1)


def roll_rows(x, shift):
    return pltpu.roll(x.reshape(x.shape[0] // 8, 8, x.shape[1]), shift, 1)


def split_three(x):
    high = x.astype(BF16)
    rest = x - high.astype(F32)
    middle = rest.astype(BF16)
    return high, middle, (rest - middle.astype(F32)).astype(BF16)


def add_shifted(template, grid, where_t, where_g, top, left, size):
    top_s = top & 7
    top_b = pl.multiple_of(top - top_s, 8)
    left_s = left & 127
    left_b = pl.multiple_of(left - left_s, 128)
    step = 24
    wrapped = lax.broadcasted_iota(jnp.int32, (step, 128), 1) < left_s
    wrapped_rows = lax.broadcasted_iota(jnp.int32, (step // 8, 8, 128), 1) < top_s
    zero = jnp.zeros((step, 128), F32)
    blocks = size // 128
    for at in range(0, size + 8, step):
        parts = []
        for j in range(blocks):
            x = roll_rows(template[where_t + (pl.ds(at, step + 8), pl.ds(128 * j, 128))], top_s)
            x = jnp.where(wrapped_rows, x[:-1], x[1:]).reshape(step, 128)
            parts.append(pltpu.roll(x, left_s, 1))
        for j in range(blocks + 1):
            before = parts[j - 1] if j > 0 else zero
            after = parts[j] if j < blocks else zero
            spot = where_g + (pl.ds(top_b + at, step), pl.ds(left_b + 128 * j, 128))
            grid[spot] += jnp.where(wrapped, before, after)


def take_shifted(field, where, top, left, at, step, size):
    top_s = top & 7
    top_b = pl.multiple_of(top - top_s, 8)
    left_s = left & 127
    left_b = pl.multiple_of(left - left_s, 128)
    back = (128 - left_s) & 127
    keep = lax.broadcasted_iota(jnp.int32, (step + 8, 128), 1) < 128 - left_s
    keep_rows = lax.broadcasted_iota(jnp.int32, (step // 8, 8, 128), 1) < 8 - top_s
    blocks = size // 128
    parts = [
        pltpu.roll(field[where + (pl.ds(top_b + at, step + 8), pl.ds(left_b + 128 * j, 128))], back, 1)
        for j in range(blocks + 1)
    ]
    pieces = []
    for j in range(blocks):
        x = roll_rows(jnp.where(keep, parts[j], parts[j + 1]), (8 - top_s) & 7)
        pieces.append(jnp.where(keep_rows, x[:-1], x[1:]).reshape(step, 128))
    return jnp.concatenate(pieces, axis=1)


def light_kernel(slots, origin, meta, probe_h, bottom, corner, lower, inverse_light, probe, template, grid, notes, sems):
    size = probe.shape[2]
    tile_rows, tile_cols = inverse_light.shape
    copies = [
        pltpu.make_async_copy(spill.at[0, pl.ds(spill.shape[1] - 8, 8), pl.ds(0, 128)], notes.at[i], sems.at[i])
        for i, spill in enumerate((bottom, corner, lower))
    ]
    copy = pltpu.make_async_copy(probe_h, probe, sems.at[3])
    copy.start()
    for item in copies:
        item.start()
    template[0:8, :] = jnp.zeros((8, size), F32)
    template[8 + size :, :] = jnp.zeros((8, size), F32)
    copy.wait()
    for at in range(0, size, 32):
        rows = pl.ds(at, 32)
        total = jnp.zeros((32, size), F32)
        for m in range(probe.shape[0]):
            total += probe[m, 0, rows] * probe[m, 0, rows] + probe[m, 1, rows] * probe[m, 1, rows]
        template[pl.ds(8 + at, 32), :] = total

    @pl.loop(0, tile_rows // 32)
    def _(step):
        rows = pl.ds(pl.multiple_of(size + step * 32, 32), 32)
        grid[rows, size : size + tile_cols] = jnp.zeros((32, tile_cols), F32)

    def add(top, left):
        @pl.when((top > 0) & (left > 0))
        def _():
            add_shifted(template, grid, (), (), top, left, size)

    @pl.loop(0, meta[0, 2 * slots])
    def _(slot):
        add(meta[0, 2 * slot] + size, meta[0, 2 * slot + 1] + size)

    for item in copies:
        item.wait()
    for device in range(3):

        @pl.loop(0, notes[device, 0, 2 * slots].astype(jnp.int32))
        def _(slot):
            top = notes[device, 0, 2 * slot].astype(jnp.int32) - meta[0, origin]
            left = notes[device, 0, 2 * slot + 1].astype(jnp.int32) - meta[0, origin + 1]
            add(top + size, left + size)

    @pl.loop(0, tile_rows // 32)
    def _(step):
        rows = pl.ds(pl.multiple_of(size + step * 32, 32), 32)
        out_rows = pl.ds(pl.multiple_of(step * 32, 32), 32)
        inverse_light[out_rows, :] = 1.0 / (grid[rows, size : size + tile_cols] + 1.0)


def light(meta, slots, origin, probe, bottom, corner, lower, tile_shape):
    size = probe.shape[2]
    hbm = pl.BlockSpec(memory_space=pltpu.HBM)
    anywhere = pl.BlockSpec(memory_space=pl.ANY)
    return pl.pallas_call(
        functools.partial(light_kernel, slots, origin),
        out_shape=jax.ShapeDtypeStruct(tile_shape, F32),
        in_specs=[pl.BlockSpec(memory_space=pltpu.SMEM), hbm] + [anywhere] * 3,
        out_specs=pl.BlockSpec(memory_space=pltpu.VMEM),
        scratch_shapes=[
            pltpu.VMEM(probe.shape, F32),
            pltpu.VMEM((size + 16, size), F32),
            pltpu.VMEM((tile_shape[0] + 2 * size, tile_shape[1] + 2 * size), F32),
            pltpu.SMEM((3, 8, 128), F32),
            pltpu.SemaphoreType.DMA((4,)),
        ],
        compiler_params=pltpu.CompilerParams(vmem_limit_bytes=8 * MIB),
        cost_estimate=pl.CostEstimate(flops=4_000_000_000, bytes_accessed=1_000_000, transcendentals=0),
        name="light",
    )(meta, in_hbm(probe), bottom, corner, lower)


def arrange_kernel(meta, amplitudes, out, given, moved, in_sems, out_sems):
    slots, size, _ = amplitudes.shape
    count = meta[0, 2 * slots]

    def load(slot):
        return pltpu.make_async_copy(amplitudes.at[slot], given.at[slot], in_sems.at[slot])

    def store(slot):
        return pltpu.make_async_copy(moved.at[slot], out.at[slot], out_sems.at[slot])

    @pl.loop(0, count)
    def _(slot):
        load(slot).start()

    first = lax.broadcasted_iota(jnp.int32, (size, size), 0)
    second = lax.broadcasted_iota(jnp.int32, (size, size), 1)
    half = size // 2

    def source(index):
        return jnp.where(index < half, 2 * index, 2 * index - (size - 1))

    rows = (source(first) == second).astype(F32).astype(BF16)
    cols = (source(second) == first).astype(F32).astype(BF16)
    rows = jnp.concatenate([rows, rows], axis=1)
    cols = jnp.concatenate([cols, cols], axis=0)

    def each(pair, act):
        act(2 * pair)

        @pl.when(2 * pair + 1 < count)
        def _():
            act(2 * pair + 1)

    @pl.loop(0, (count + 1) // 2)
    def _(pair):
        each(pair, lambda slot: load(slot).wait())
        x = [dot(rows, jnp.concatenate(split(given[2 * pair + k]), axis=0)) for k in range(2)]
        for k in range(2):
            moved[2 * pair + k] = dot(jnp.concatenate(split(x[k]), axis=1), cols)
        each(pair, lambda slot: store(slot).start())

    @pl.loop(0, count)
    def _(slot):
        store(slot).wait()


def arrange(meta, amplitudes):
    slots = amplitudes.shape[0]
    hbm = pl.BlockSpec(memory_space=pltpu.HBM)
    return pl.pallas_call(
        arrange_kernel,
        out_shape=pltpu.HBM(amplitudes.shape, F32),
        in_specs=[pl.BlockSpec(memory_space=pltpu.SMEM), hbm],
        out_specs=hbm,
        scratch_shapes=[
            pltpu.VMEM(amplitudes.shape, F32),
            pltpu.VMEM(amplitudes.shape, F32),
            pltpu.SemaphoreType.DMA((slots,)),
            pltpu.SemaphoreType.DMA((slots,)),
        ],
        compiler_params=pltpu.CompilerParams(vmem_limit_bytes=8 * MIB),
        cost_estimate=LONG,
        name="arrange",
    )(meta, in_hbm(amplitudes))


def three_left(table, t):
    return jnp.concatenate([table[t, 0], table[t, 0], table[t, 1]], axis=1)


def three_right(table, v):
    return jnp.concatenate([table[v, 0], table[v, 0], table[v, 1]], axis=0)


def weave(first, second):
    total = max(len(first), len(second))
    done = [0, 0]
    for i in range(1, total + 1):
        for k, pieces in enumerate((first, second)):
            while done[k] * total < i * len(pieces):
                pieces[done[k]]()
                done[k] += 1


def slots_kernel(
    needs_rim, meta, probe, amplitudes, sources, tables, note, state, outs,
    amp, forward_t, backward_t, chosen, patch_f, patch_b, x_f, y_f, z_f, g_s, x_b, z_b, back, template,
    load_sems, amp_sems, out_sems,
):
    ext, grid, probe_out = state
    size = probe.shape[2]
    half = size // 2
    modes = probe.shape[0]
    slots = amplitudes.shape[0]
    tile_rows, tile_cols = (n - size for n in ext.shape[1:])
    step = 32
    fine = 16

    body_rows, rim_rows = pl.ds(0, tile_rows), pl.ds(tile_rows, size)
    body_cols, rim_cols = pl.ds(0, tile_cols), pl.ds(tile_cols, size)
    if needs_rim:
        places = [
            ext.at[:, pl.ds(0, size), rim_cols],
            ext.at[:, pl.ds(size, tile_rows - size), rim_cols],
            ext.at[:, rim_rows, rim_cols],
        ]
    else:
        places = [ext.at[:, body_rows, body_cols], ext.at[:, rim_rows, body_cols]]
    places += [forward_t, backward_t]
    loads = [
        pltpu.make_async_copy(source, place, load_sems.at[i])
        for i, (source, place) in enumerate(zip([*sources, *tables], places))
    ]
    for load in loads:
        load.start()

    def amp_copy(slot):
        return pltpu.make_async_copy(amplitudes.at[slot], amp.at[slot], amp_sems.at[slot])

    def choose(slot, found):
        beyond = meta[0, 2 * slot + 1] + size > tile_cols
        wanted = beyond if needs_rim else jnp.logical_not(beyond)

        @pl.when(wanted)
        def _():
            chosen[found] = slot
            amp_copy(slot).start()

        return found + wanted.astype(jnp.int32)

    count = lax.fori_loop(0, meta[0, 2 * slots], choose, jnp.zeros((), jnp.int32))

    if not needs_rim:

        @pl.loop(0, (tile_rows + size) // step)
        def _(at):
            rows = pl.ds(pl.multiple_of(at * step, step), step)
            for c in range(2):
                grid[c, rows, :] = jnp.zeros((step, tile_cols + size), F32)

        @pl.loop(0, size // step)
        def _(at):
            rows = pl.ds(pl.multiple_of(at * step, step), step)
            for c in range(2 * modes + 1):
                probe_out[c, rows, :] = jnp.zeros((step, size), F32)

    for c in range(2):
        template[c, 0:8, :] = jnp.zeros((8, size), F32)
        template[c, 8 + size :, :] = jnp.zeros((8, size), F32)
    for load in loads:
        load.wait()

    def corner(slot):
        return meta[0, 2 * slot], meta[0, 2 * slot + 1]

    def forward(slot):
        top, left = corner(slot)

        def take(at):
            for c in range(2):
                patch_f[c, pl.ds(at, step), :] = take_shifted(ext, (c,), top, left, at, step, size)

        def fold_rows(m, at):
            cols = pl.ds(m * size, size)
            parts = []
            for base in (at, half + at):
                rows = pl.ds(base, fine)
                pr, pi = patch_f[0, rows, :], patch_f[1, rows, :]
                qr, qi = probe[m, 0, rows, :], probe[m, 1, rows, :]
                parts.append((qr * pr - qi * pi, qr * pi + qi * pr))
            for c in range(2):
                rows = pl.ds(c * half + at, fine)
                for t, value in enumerate((parts[0][c] + parts[1][c], parts[0][c] - parts[1][c])):
                    x_f[t, 0, rows, cols], x_f[t, 1, rows, cols] = split(value)

        def dft_rows(m, t):
            cols = pl.ds(m * size, size)
            high = x_f[t, 0, :, cols]
            u = dot(three_left(forward_t, t), jnp.concatenate([high, x_f[t, 1, :, cols], high], axis=0))
            rows = pl.ds(m * size + t * half, half)
            for v, value in enumerate((u[:, :half] + u[:, half:], u[:, :half] - u[:, half:])):
                high, low = split(value)
                for c in range(2):
                    lanes = pl.ds(c * half, half)
                    y_f[v, 0, rows, lanes] = high[c * half : (c + 1) * half]
                    y_f[v, 1, rows, lanes] = low[c * half : (c + 1) * half]

        def dft_cols(v):
            high = y_f[v, 0]
            z_f[v] = dot(jnp.concatenate([high, y_f[v, 1], high], axis=1), three_right(backward_t, v))

        def scale(v, at):
            if v == 0 and at == 0:
                amp_copy(slot).wait()
            waves = [z_f[v, pl.ds(m * size + at, fine), :] for m in range(modes)]
            total = jnp.zeros((fine, half), F32)
            for wave in waves:
                total += wave[:, :half] * wave[:, :half] + wave[:, half:] * wave[:, half:]
            measured = amp[slot, pl.ds(at, fine), pl.ds(v * half, half)]
            factor = measured * lax.rsqrt(jnp.maximum(total, FLOOR * FLOOR)) - 1.0
            factor = jnp.concatenate([factor, factor], axis=1)
            for m in range(modes):
                rows = pl.ds(m * size + at, fine)
                g_s[v, 0, rows, :], g_s[v, 1, rows, :] = split(waves[m] * factor)

        pieces = [(take, at) for at in range(0, size, step)]
        for m in range(modes):
            pieces += [(fold_rows, m, at) for at in range(0, half, fine)]
            pieces += [(dft_rows, m, t) for t in range(2)]
        pieces += [(dft_cols, v) for v in range(2)]
        pieces += [(scale, v, at) for v in range(2) for at in range(0, size, fine)]
        return [functools.partial(*piece) for piece in pieces]

    def backward(slot):
        top, left = corner(slot)

        def dft_cols(v):
            high = g_s[v, 0]
            z_b[v] = dot(jnp.concatenate([high, g_s[v, 1], high], axis=1), three_right(forward_t, v))

        def unfold_cols(m, t, at):
            rows = pl.ds(m * size + t * half + at, step)
            even, odd = z_b[0, rows, :], z_b[1, rows, :]
            for v, value in enumerate((even + odd, even - odd)):
                high, low = split(value)
                cols = pl.ds(m * size + v * half, half)
                for c in range(2):
                    spot = pl.ds(c * half + at, step)
                    x_b[t, 0, spot, cols] = high[:, c * half : (c + 1) * half]
                    x_b[t, 1, spot, cols] = low[:, c * half : (c + 1) * half]

        def dft_rows(m, t):
            cols = pl.ds(m * size, size)
            high = x_b[t, 0, :, cols]
            back[m, t] = dot(three_left(backward_t, t), jnp.concatenate([high, x_b[t, 1, :, cols], high], axis=0))

        def gradients(at):
            waves = []
            for m in range(modes):
                pair = []
                for c in range(2):
                    rows = pl.ds(c * half + at, fine)
                    even, odd = back[m, 0, rows, :], back[m, 1, rows, :]
                    pair.append((even + odd, even - odd))
                waves.append(pair)
            for h in range(2):
                rows = pl.ds(h * half + at, fine)
                pr, pi = patch_b[0, rows, :], patch_b[1, rows, :]
                grad_r = jnp.zeros((fine, size), F32)
                grad_i = jnp.zeros((fine, size), F32)
                for m in range(modes):
                    br, bi = waves[m][0][h], waves[m][1][h]
                    qr, qi = probe[m, 0, rows, :], probe[m, 1, rows, :]
                    grad_r += qr * br + qi * bi
                    grad_i += qr * bi - qi * br
                    probe_out[2 * m, rows, :] += pr * br + pi * bi
                    probe_out[2 * m + 1, rows, :] += pr * bi - pi * br
                probe_out[2 * modes, rows, :] += pr * pr + pi * pi
                spot = pl.ds(8 + h * half + at, fine)
                template[0, spot, :] = grad_r
                template[1, spot, :] = grad_i

        def add(c):
            add_shifted(template, grid, (c,), (c,), top, left, size)

        pieces = [(dft_cols, v) for v in range(2)]
        for m in range(modes):
            pieces += [(unfold_cols, m, t, at) for t in range(2) for at in range(0, half, step)]
            pieces += [(dft_rows, m, t) for t in range(2)]
        pieces += [(gradients, at) for at in range(0, half, fine)]
        pieces += [(add, c) for c in range(2)]
        return [functools.partial(*piece) for piece in pieces]

    def hand_over():
        for at in range(0, size, step):
            for c in range(2):
                patch_b[c, pl.ds(at, step), :] = patch_f[c, pl.ds(at, step), :]

    @pl.when(count > 0)
    def _():
        weave(forward(chosen[0]), [])
        hand_over()

        def visit(index, _):
            weave(backward(chosen[index]), forward(chosen[index + 1]))
            hand_over()
            return 0

        lax.fori_loop(0, count - 1, visit, 0)
        weave(backward(chosen[count - 1]), [])

    if needs_rim:
        top, bottom = pl.ds(0, size), pl.ds(size, tile_rows - size)
        parts = [
            (grid.at[:, body_rows, body_cols], outs[0]),
            (grid.at[:, bottom, rim_cols], outs[1].at[:, pl.ds(0, tile_rows - size)]),
            (note, outs[1].at[0, pl.ds(tile_rows - size, 8)]),
            (grid.at[:, top, rim_cols], outs[2]),
            (grid.at[:, rim_rows, rim_cols], outs[3].at[:, top]),
            (note, outs[3].at[0, pl.ds(size, 8)]),
            (grid.at[:, rim_rows, body_cols], outs[4].at[:, top]),
            (probe_out.at[:, pl.ds(pl.multiple_of(meta[0, 2 * slots + 1] * half, half), half)], outs[5]),
        ]
        stores = [pltpu.make_async_copy(part, out, out_sems.at[i]) for i, (part, out) in enumerate(parts)]
        for store in stores:
            store.start()
        for store in stores:
            store.wait()


def scratch_for(size, modes, slots):
    return [
        pltpu.VMEM((slots, size, size), F32),
        pltpu.VMEM((2, 2, size, size), BF16),
        pltpu.VMEM((2, 2, size, size), BF16),
        pltpu.SMEM((slots,), jnp.int32),
        pltpu.VMEM((2, size, size), F32),
        pltpu.VMEM((2, size, size), F32),
        pltpu.VMEM((2, 2, size, modes * size), BF16),
        pltpu.VMEM((2, 2, modes * size, size), BF16),
        pltpu.VMEM((2, modes * size, size), F32),
        pltpu.VMEM((2, 2, modes * size, size), BF16),
        pltpu.VMEM((2, 2, size, modes * size), BF16),
        pltpu.VMEM((2, modes * size, size), F32),
        pltpu.VMEM((modes, 2, size, size), F32),
        pltpu.VMEM((2, size + 16, size), F32),
        pltpu.SemaphoreType.DMA((5,)),
        pltpu.SemaphoreType.DMA((slots,)),
        pltpu.SemaphoreType.DMA((8,)),
    ]


SLOTS_COST = pl.CostEstimate(flops=12_000_000_000, bytes_accessed=16_000_000, transcendentals=0)


def visit_inside(meta, probe, amplitudes, tile, lower):
    size, modes, slots = probe.shape[2], probe.shape[0], amplitudes.shape[0]
    rows, cols = tile.shape[1:]
    tables = [jnp.asarray(item) for item in dft_tables(size)]
    vmem = pl.BlockSpec(memory_space=pltpu.VMEM)
    hbm = pl.BlockSpec(memory_space=pltpu.HBM)
    field = pltpu.VMEM((2, rows + size, cols + size), F32)

    def kernel(meta, probe, amplitudes, tile, lower, forward_h, backward_h, *refs):
        state, scratch = refs[:3], refs[3:]
        slots_kernel(
            False, meta, probe, amplitudes, [tile, lower], [forward_h, backward_h], None, state, None, *scratch
        )

    return pl.pallas_call(
        kernel,
        out_shape=[field, field, pltpu.VMEM((2 * modes + 1, size, size), F32)],
        in_specs=[pl.BlockSpec(memory_space=pltpu.SMEM), vmem, hbm, hbm, pl.BlockSpec(memory_space=pl.ANY), hbm, hbm],
        out_specs=[vmem] * 3,
        scratch_shapes=scratch_for(size, modes, slots),
        compiler_params=pltpu.CompilerParams(vmem_limit_bytes=28 * MIB),
        cost_estimate=SLOTS_COST,
        name="slots_inside",
    )(meta, probe, in_hbm(amplitudes), in_hbm(tile), lower, *map(in_hbm, tables))


def visit_beyond(meta, probe, amplitudes, rims, note, state):
    size, modes, slots = probe.shape[2], probe.shape[0], amplitudes.shape[0]
    rows, cols = (n - size for n in state[0].shape[1:])
    tables = [jnp.asarray(item) for item in dft_tables(size)]
    vmem = pl.BlockSpec(memory_space=pltpu.VMEM)
    hbm = pl.BlockSpec(memory_space=pltpu.HBM)
    anywhere = pl.BlockSpec(memory_space=pl.ANY)
    shapes = [
        (2, rows - size + 8, size),
        (2, size, size),
        (2, size + 8, size),
        (2, size + 8, cols),
        (2 * modes + 1, size // 2, size),
    ]

    def kernel(meta, probe, amplitudes, forward_h, backward_h, *refs):
        rims, note, refs = refs[:3], refs[3], refs[7:]
        state, outs, scratch = refs[:3], refs[3:9], refs[9:]
        slots_kernel(True, meta, probe, amplitudes, rims, [forward_h, backward_h], note, state, outs, *scratch)

    out = pl.pallas_call(
        kernel,
        out_shape=[pltpu.VMEM(item.shape, item.dtype) for item in state]
        + [pltpu.HBM((2, rows, cols), F32)]
        + [jax.ShapeDtypeStruct(shape, F32) for shape in shapes],
        in_specs=[pl.BlockSpec(memory_space=pltpu.SMEM), vmem] + [hbm] * 3 + [anywhere] * 4 + [vmem] * 3,
        out_specs=[vmem] * 3 + [hbm] + [anywhere] * 5,
        input_output_aliases={9 + i: i for i in range(3)},
        scratch_shapes=scratch_for(size, modes, slots),
        compiler_params=pltpu.CompilerParams(vmem_limit_bytes=28 * MIB),
        cost_estimate=SLOTS_COST,
        name="slots_beyond",
    )(meta, probe, *map(in_hbm, [amplitudes, *tables]), *rims, note, *state)
    return (*out[3:], out[2])


def finish_kernel(
    chosen, own, top, bottom, lower, scale, tile, out, own_s, right_s, lower_s, scale_s, tile_s, in_sems, out_sems
):
    size = right_s.shape[2]
    block = 128
    blocks = own_s.shape[1] // block

    def copies(i):
        rows = pl.ds(i * block, block)
        pairs = [
            (own.at[:, rows], own_s.at[:, rows]),
            (scale.at[rows], scale_s.at[rows]),
            (tile.at[:, rows], tile_s.at[:, rows]),
        ]
        if i < size // block:
            pairs.append((top.at[:, rows], right_s.at[:, rows]))
            pairs.append((lower.at[:, rows], lower_s.at[:, rows]))
        else:
            pairs.append((bottom.at[:, pl.ds(i * block - size, block)], right_s.at[:, rows]))
        return [pltpu.make_async_copy(a, b, in_sems.at[i, k]) for k, (a, b) in enumerate(pairs)]

    loads = {i: copies(i) for i in range(blocks) if chosen(i * block)}
    for load in loads.values():
        for copy in load:
            copy.start()
    stores = []
    for i in loads:
        for copy in loads[i]:
            copy.wait()
        rows = pl.ds(i * block, block)
        for at in range(i * block, (i + 1) * block, 32):
            part = pl.ds(at, 32)
            for c in range(2):
                near, far = own_s[c, part, :size] + right_s[c, part, :], own_s[c, part, size:]
                if i < size // block:
                    near, far = near + lower_s[c, part, :size], far + lower_s[c, part, size:]
                own_s[c, part, :size] = tile_s[c, part, :size] + near * scale_s[part, :size]
                own_s[c, part, size:] = tile_s[c, part, size:] + far * scale_s[part, size:]
        stores.append(pltpu.make_async_copy(own_s.at[:, rows], out.at[:, rows], out_sems.at[i]))
        stores[-1].start()
    for store in stores:
        store.wait()


def finish(own, top, bottom, lower, inverse_light, tile, before=None):
    rows, cols = tile.shape[1:]
    size = bottom.shape[2]
    anywhere = pl.BlockSpec(memory_space=pl.ANY)
    hbm = pl.BlockSpec(memory_space=pltpu.HBM)
    if before is None:

        def kernel(own, bottom, scale, tile, *refs):
            finish_kernel(lambda at: at >= size, own, None, bottom, None, scale, tile, *refs)

        operands = (in_hbm(own), bottom, inverse_light, in_hbm(tile))
        in_specs = [hbm, anywhere, anywhere, hbm]
        aliases = {}
    else:

        def kernel(before, own, top, lower, scale, tile, *refs):
            finish_kernel(lambda at: at < size, own, top, None, lower, scale, tile, *refs)

        operands = (in_hbm(before), in_hbm(own), top, lower, inverse_light, in_hbm(tile))
        in_specs = [hbm, hbm, anywhere, anywhere, anywhere, hbm]
        aliases = {0: 0}
    return pl.pallas_call(
        kernel,
        out_shape=pltpu.HBM(tile.shape, F32),
        in_specs=in_specs,
        out_specs=hbm,
        input_output_aliases=aliases,
        scratch_shapes=[
            pltpu.VMEM(tile.shape, F32),
            pltpu.VMEM((2, rows, size), F32),
            pltpu.VMEM((2, size, cols), F32),
            pltpu.VMEM((rows, cols), F32),
            pltpu.VMEM(tile.shape, F32),
            pltpu.SemaphoreType.DMA((rows // 128, 5)),
            pltpu.SemaphoreType.DMA((rows // 128,)),
        ],
        compiler_params=pltpu.CompilerParams(vmem_limit_bytes=12 * MIB),
        cost_estimate=pl.CostEstimate(flops=2_000_000_000, bytes_accessed=6_000_000, transcendentals=0),
        name="finish_far" if before is None else "finish_near",
    )(*operands)


def from_behind(array, axis, by):
    count = lax.axis_size(axis)
    pairs = [(i, i + by) for i in range(count) if 0 <= i + by < count]
    return lax.ppermute(array, axis, pairs)


def exchange(array, axis, bit):
    count = lax.axis_size(axis)
    return lax.ppermute(array, axis, [(i, i ^ bit) for i in range(count)])


def together(*arrays):
    return lax.optimization_barrier(arrays)


def cut(tile, regions, cost, name):
    def kernel(tile, *refs):
        sems = refs[-1]
        copies = [
            pltpu.make_async_copy(tile.at[:, pl.ds(at, height), pl.ds(0, width)], out, sems.at[i])
            for i, ((at, height, width), out) in enumerate(zip(regions, refs[:-1]))
        ]
        for copy in copies:
            copy.start()
        for copy in copies:
            copy.wait()

    return pl.pallas_call(
        kernel,
        out_shape=[jax.ShapeDtypeStruct((2, height, width), F32) for _, height, width in regions],
        in_specs=[pl.BlockSpec(memory_space=pltpu.HBM)],
        out_specs=[pl.BlockSpec(memory_space=pltpu.VMEM)] * len(regions),
        scratch_shapes=[pltpu.SemaphoreType.DMA((len(regions),))],
        compiler_params=pltpu.CompilerParams(vmem_limit_bytes=4 * MIB),
        cost_estimate=cost,
        name=name,
    )(in_hbm(tile))


def fold(places, index, mine, got, upper):
    count, half, width = got.shape
    quarter = half // 2

    def kernel(places, mine, got, send, keep):
        base = 0 if index is None else places[0, index] * half
        for k, out in ((1 - places[0, upper], send), (places[0, upper], keep)):
            for c in range(count):
                out[c] = (
                    mine[c, pl.ds(pl.multiple_of(base + k * quarter, quarter), quarter), :]
                    + got[c, pl.ds(pl.multiple_of(k * quarter, quarter), quarter), :]
                )

    vmem = pl.BlockSpec(memory_space=pltpu.VMEM)
    shape = jax.ShapeDtypeStruct((count, quarter, width), F32)
    return pl.pallas_call(
        kernel,
        out_shape=[shape, shape],
        in_specs=[pl.BlockSpec(memory_space=pltpu.SMEM), vmem, vmem],
        out_specs=[vmem, vmem],
        compiler_params=pltpu.CompilerParams(vmem_limit_bytes=6 * MIB),
        cost_estimate=SHORT,
        name="fold",
    )(places, mine, got)


def merge(top, corner):
    size = top.shape[1]

    def kernel(top, corner, out):
        for c in range(2):
            out[c] = top[c] + corner[c, :size, :]

    vmem = pl.BlockSpec(memory_space=pltpu.VMEM)
    return pl.pallas_call(
        kernel,
        out_shape=jax.ShapeDtypeStruct(top.shape, F32),
        in_specs=[vmem, vmem],
        out_specs=vmem,
        compiler_params=pltpu.CompilerParams(vmem_limit_bytes=4 * MIB),
        cost_estimate=SHORT,
        name="merge",
    )(top, corner)


def annotate(lower, bottom):
    size = bottom.shape[2]

    def kernel(lower, bottom, out, sem):
        source = bottom.at[0, pl.ds(bottom.shape[1] - 8, 8)]
        copy = pltpu.make_async_copy(source, out.at[0, pl.ds(out.shape[1] - 8, 8), pl.ds(0, size)], sem.at[0])
        copy.start()
        copy.wait()

    anywhere = pl.BlockSpec(memory_space=pl.ANY)
    return pl.pallas_call(
        kernel,
        out_shape=jax.ShapeDtypeStruct(lower.shape, F32),
        in_specs=[anywhere, anywhere],
        out_specs=anywhere,
        input_output_aliases={0: 0},
        scratch_shapes=[pltpu.SemaphoreType.DMA((1,))],
        compiler_params=pltpu.CompilerParams(vmem_limit_bytes=MIB),
        cost_estimate=SHORT,
        name="annotate",
    )(lower, bottom)


def deal(terms, parts, rows):
    count, _, width = terms[0].shape
    if rows % 8:
        return sum(terms).reshape(count, parts, rows, width).transpose(1, 0, 2, 3)

    def kernel(*refs):
        terms, out = refs[:-1], refs[-1]
        for j in range(parts):
            for c in range(count):
                out[j, c] = sum(term[c, j * rows : (j + 1) * rows, :] for term in terms)

    vmem = pl.BlockSpec(memory_space=pltpu.VMEM)
    return pl.pallas_call(
        kernel,
        out_shape=jax.ShapeDtypeStruct((parts, count, rows, width), F32),
        in_specs=[vmem] * len(terms),
        out_specs=vmem,
        compiler_params=pltpu.CompilerParams(vmem_limit_bytes=4 * MIB),
        cost_estimate=SHORT,
        name="deal",
    )(*terms)


def settle(places, start, probe, pieces):
    parts, count, rows, width = pieces.shape
    shape = (parts, count - 1, rows, width)
    if rows % 8:
        share = pieces.sum(axis=0)
        old = lax.dynamic_slice_in_dim(probe, places[0, start], rows, axis=1)
        return jnp.broadcast_to((old + share[:-1] / (share[-1:] + 1.0))[None], shape)

    def kernel(places, probe, pieces, out, old, sem):
        spot = pl.ds(pl.multiple_of(places[0, start], 8), rows)
        copy = pltpu.make_async_copy(probe.at[:, spot], old, sem.at[0])
        copy.start()
        share = sum(pieces[j] for j in range(parts))
        copy.wait()
        new = old[...] + share[:-1] / (share[-1:] + 1.0)
        for j in range(parts):
            out[j] = new

    vmem = pl.BlockSpec(memory_space=pltpu.VMEM)
    return pl.pallas_call(
        kernel,
        out_shape=jax.ShapeDtypeStruct(shape, F32),
        in_specs=[pl.BlockSpec(memory_space=pltpu.SMEM), pl.BlockSpec(memory_space=pltpu.HBM), vmem],
        out_specs=vmem,
        scratch_shapes=[pltpu.VMEM(shape[1:], F32), pltpu.SemaphoreType.DMA((1,))],
        compiler_params=pltpu.CompilerParams(vmem_limit_bytes=4 * MIB),
        cost_estimate=SHORT,
        name="settle",
    )(places, in_hbm(probe), pieces)


def collect(pieces):
    parts, count, rows, width = pieces.shape
    if rows % 8:
        return pieces.transpose(1, 0, 2, 3).reshape(count, parts * rows, width)

    def kernel(pieces, out):
        for j in range(parts):
            for c in range(count):
                out[c, j * rows : (j + 1) * rows, :] = pieces[j, c]

    vmem = pl.BlockSpec(memory_space=pltpu.VMEM)
    return pl.pallas_call(
        kernel,
        out_shape=jax.ShapeDtypeStruct((count, parts * rows, width), F32),
        in_specs=[vmem],
        out_specs=vmem,
        compiler_params=pltpu.CompilerParams(vmem_limit_bytes=4 * MIB),
        cost_estimate=LONG,
        name="collect",
    )(pieces)


def join(places, upper, mine, other):
    half = mine.shape[1]

    def kernel(places, mine, other, out, sems):
        copies = [
            pltpu.make_async_copy(source, out.at[:, pl.ds(pl.multiple_of(at * half, half), half)], sems.at[i])
            for i, (source, at) in enumerate(((mine, places[0, upper]), (other, 1 - places[0, upper])))
        ]
        for copy in copies:
            copy.start()
        for copy in copies:
            copy.wait()

    anywhere = pl.BlockSpec(memory_space=pl.ANY)
    return pl.pallas_call(
        kernel,
        out_shape=jax.ShapeDtypeStruct((mine.shape[0], 2 * half) + mine.shape[2:], F32),
        in_specs=[pl.BlockSpec(memory_space=pltpu.SMEM), anywhere, anywhere],
        out_specs=anywhere,
        scratch_shapes=[pltpu.SemaphoreType.DMA((2,))],
        compiler_params=pltpu.CompilerParams(vmem_limit_bytes=MIB),
        cost_estimate=pl.CostEstimate(flops=0, bytes_accessed=2_000_000, transcendentals=0),
        name="join",
    )(places, mine, other)


def body(object_field, probe, amplitudes, positions, counts):
    modes, _, size, _ = probe.shape
    tile_rows, tile_cols = object_field.shape[1:]
    slots = amplitudes.shape[0]
    origin = jnp.stack([lax.axis_index("row") * tile_rows, lax.axis_index("col") * tile_cols]).astype(jnp.int32)
    bits = [1 << k for k in range(lax.axis_size("row").bit_length() - 1)]
    uppers = [(lax.axis_index("row") & bit) // bit for bit in bits]

    def relative(table):
        return jnp.concatenate([table[:, : 2 * slots] - jnp.tile(origin, slots)[None], table[:, 2 * slots :]], axis=1)

    right_up, right_down = cut(
        object_field, ((0, size, size), (size, tile_rows - size, size)), SHORT, "cut_right"
    )
    right_up, right_down, after_right = together(right_up, right_down, object_field)
    right_up = from_behind(right_up, "col", -1)
    right_down = from_behind(right_down, "col", -1)
    (lower,) = cut(after_right, ((0, size, tile_cols),), LONG, "cut_lower")
    meta = jnp.concatenate([positions.reshape(1, 2 * slots), counts.reshape(1, 1)], axis=1)
    lower = from_behind(lower, "row", -1)

    parts = lax.axis_size("col")
    rows = (size >> len(bits)) // parts
    me = lax.axis_index("col")
    start = sum(upper * (size >> (k + 1)) for k, upper in enumerate(uppers)) + me * rows
    bit_at = 2 * slots + 2
    me_at = bit_at + len(bits)
    start_at, origin_at = me_at + 1, me_at + 2
    extra = [1 - uppers[0], *uppers, me, start, origin[0], origin[1]]
    mine = jnp.concatenate([relative(meta), jnp.stack([item.astype(jnp.int32) for item in extra])[None]], axis=1)
    note = jnp.pad(meta.astype(F32), ((0, 7), (0, size - meta.shape[1])))
    mine, note = together(mine, note)
    amplitudes = arrange(mine, amplitudes)
    right_up, amplitudes = together(right_up, amplitudes)
    corner = from_behind(right_up, "row", -1)
    amplitudes, lower = together(amplitudes, lower)
    state = visit_inside(mine, probe, amplitudes, object_field, lower)
    right_up, right_down, corner, *state = together(right_up, right_down, corner, *state)
    own, bottom_spill, top_spill, corner_spill, lower_spill, send, share = visit_beyond(
        mine, probe, amplitudes, [right_up, right_down, corner], note, state
    )

    index = bit_at
    for k, bit in enumerate(bits):
        got = exchange(send, "row", bit)
        if k == 0:
            bottom_spill = from_behind(bottom_spill, "col", 1)
        if k + 1 < len(bits):
            send, share = fold(mine, index, share, got, bit_at + k + 1)
            index = None
    got, bottom_spill, lower_spill = together(got, bottom_spill, lower_spill)
    lower_spill = from_behind(annotate(lower_spill, bottom_spill), "row", 1)
    pieces = lax.all_to_all(deal([share, got], parts, rows), "col", 0, 0, tiled=True)
    new = settle(mine, start_at, probe.reshape(2 * modes, size, size), pieces)
    new, lower_spill, corner_spill = together(new, lower_spill, corner_spill)
    corner_spill = from_behind(corner_spill, "row", 1)
    inverse_light = light(
        mine, slots, origin_at, probe, bottom_spill, corner_spill, lower_spill, (tile_rows, tile_cols)
    )
    new = lax.all_to_all(new, "col", 0, 0, tiled=True)
    new, corner_spill = together(new, corner_spill)
    top_spill, new = together(merge(top_spill, corner_spill), new)
    top_spill = from_behind(top_spill, "col", 1)
    new = collect(new)
    for k, bit in reversed(list(enumerate(bits))):
        if k == 0:
            new, own = together(new, own)
            new_object = finish(own, None, bottom_spill, lower_spill, inverse_light, object_field)
            new_object, top_spill = together(new_object, top_spill)
            new_object = finish(
                own, top_spill, bottom_spill, lower_spill, inverse_light, object_field, before=new_object
            )
        other = exchange(new, "row", bit)
        if k + 1 == len(bits):
            other, inverse_light = together(other, inverse_light)
        if k == 0:
            other, new_object = together(other, new_object)
        new = join(mine, bit_at + k, new, other)
    return (new_object, new.reshape(modes, 2, size, size))


def solution(mesh):
    in_specs = (
        P(None, "row", "col"),
        P(),
        P(("row", "col"), None, None),
        P(("row", "col"), None),
        P(("row", "col")),
    )
    out_specs = (P(None, "row", "col"), P())
    return jax.shard_map(body, mesh=mesh, in_specs=in_specs, out_specs=out_specs, check_vma=False)
```

```python
import functools
import math

import jax
import jax.numpy as jnp
import ml_dtypes
import numpy as np
from jax import lax
from jax.experimental import pallas as pl
from jax.experimental.pallas import tpu as pltpu
from jax.sharding import PartitionSpec as P

F32 = jnp.float32
BF16 = jnp.bfloat16
MIB = 1024 * 1024
LONG = pl.CostEstimate(flops=30_000_000_000, bytes_accessed=4_000_000, transcendentals=0)
SHORT = pl.CostEstimate(flops=0, bytes_accessed=1_000_000, transcendentals=0)
FLOOR = 0.3


def split_np(table):
    high = table.astype(ml_dtypes.bfloat16)
    low = (table - high.astype(np.float64)).astype(ml_dtypes.bfloat16)
    return high, low


def dft_tables(length):
    half = length // 2
    q = np.arange(half)[:, None]
    n = np.arange(half)[None, :]
    forward = []
    for odd in range(2):
        phase = (n * (2 * q + odd)) % length
        angle = phase * (-2.0 * math.pi / length)
        re = np.cos(angle) / math.sqrt(length)
        im = np.sin(angle) / math.sqrt(length)
        forward.append(np.stack(split_np(np.block([[re, -im], [im, re]]))))
    forward = np.stack(forward)
    return forward, np.ascontiguousarray(forward.transpose(0, 1, 3, 2))


def in_hbm(array):
    return pltpu.with_memory_space_constraint(array, pltpu.HBM)


def dot(a, b):
    return jnp.dot(a, b, preferred_element_type=F32)


def split(x):
    high = x.astype(BF16)
    return high, (x - high.astype(F32)).astype(BF16)


def roll_rows(x, shift):
    return pltpu.roll(x.reshape(x.shape[0] // 8, 8, x.shape[1]), shift, 1)


def roll_rows(x, shift):
    return pltpu.roll(x.reshape(x.shape[0] // 8, 8, x.shape[1]), shift, 1)


def roll_rows(x, shift):
    return pltpu.roll(x.reshape(x.shape[0] // 8, 8, x.shape[1]), shift, 1)


def roll_rows(x, shift):
    return pltpu.roll(x.reshape(x.shape[0] // 8, 8, x.shape[1]), shift, 1)


def split_three(x):
    high = x.astype(BF16)
    rest = x - high.astype(F32)
    middle = rest.astype(BF16)
    return high, middle, (rest - middle.astype(F32)).astype(BF16)


def add_shifted(template, grid, where_t, where_g, top, left, size):
    top_s = top & 7
    top_b = pl.multiple_of(top - top_s, 8)
    left_s = left & 127
    left_b = pl.multiple_of(left - left_s, 128)
    step = 24
    wrapped = lax.broadcasted_iota(jnp.int32, (step, 128), 1) < left_s
    wrapped_rows = lax.broadcasted_iota(jnp.int32, (step // 8, 8, 128), 1) < top_s
    zero = jnp.zeros((step, 128), F32)
    blocks = size // 128
    for at in range(0, size + 8, step):
        parts = []
        for j in range(blocks):
            x = roll_rows(template[where_t + (pl.ds(at, step + 8), pl.ds(128 * j, 128))], top_s)
            x = jnp.where(wrapped_rows, x[:-1], x[1:]).reshape(step, 128)
            parts.append(pltpu.roll(x, left_s, 1))
        for j in range(blocks + 1):
            before = parts[j - 1] if j > 0 else zero
            after = parts[j] if j < blocks else zero
            spot = where_g + (pl.ds(top_b + at, step), pl.ds(left_b + 128 * j, 128))
            grid[spot] += jnp.where(wrapped, before, after)


def take_shifted(field, where, top, left, at, step, size):
    top_s = top & 7
    top_b = pl.multiple_of(top - top_s, 8)
    left_s = left & 127
    left_b = pl.multiple_of(left - left_s, 128)
    back = (128 - left_s) & 127
    keep = lax.broadcasted_iota(jnp.int32, (step + 8, 128), 1) < 128 - left_s
    keep_rows = lax.broadcasted_iota(jnp.int32, (step // 8, 8, 128), 1) < 8 - top_s
    blocks = size // 128
    parts = [
        pltpu.roll(field[where + (pl.ds(top_b + at, step + 8), pl.ds(left_b + 128 * j, 128))], back, 1)
        for j in range(blocks + 1)
    ]
    pieces = []
    for j in range(blocks):
        x = roll_rows(jnp.where(keep, parts[j], parts[j + 1]), (8 - top_s) & 7)
        pieces.append(jnp.where(keep_rows, x[:-1], x[1:]).reshape(step, 128))
    return jnp.concatenate(pieces, axis=1)


def light_kernel(slots, origin, meta, probe_h, bottom, corner, lower, inverse_light, probe, template, grid, notes, sems):
    size = probe.shape[2]
    tile_rows, tile_cols = inverse_light.shape
    copies = [
        pltpu.make_async_copy(spill.at[0, pl.ds(spill.shape[1] - 8, 8), pl.ds(0, 128)], notes.at[i], sems.at[i])
        for i, spill in enumerate((bottom, corner, lower))
    ]
    copy = pltpu.make_async_copy(probe_h, probe, sems.at[3])
    copy.start()
    for item in copies:
        item.start()
    template[0:8, :] = jnp.zeros((8, size), F32)
    template[8 + size :, :] = jnp.zeros((8, size), F32)
    copy.wait()
    for at in range(0, size, 32):
        rows = pl.ds(at, 32)
        total = jnp.zeros((32, size), F32)
        for m in range(probe.shape[0]):
            total += probe[m, 0, rows] * probe[m, 0, rows] + probe[m, 1, rows] * probe[m, 1, rows]
        template[pl.ds(8 + at, 32), :] = total

    @pl.loop(0, tile_rows // 32)
    def _(step):
        rows = pl.ds(pl.multiple_of(size + step * 32, 32), 32)
        grid[rows, size : size + tile_cols] = jnp.zeros((32, tile_cols), F32)

    def add(top, left):
        @pl.when((top > 0) & (left > 0))
        def _():
            add_shifted(template, grid, (), (), top, left, size)

    @pl.loop(0, meta[0, 2 * slots])
    def _(slot):
        add(meta[0, 2 * slot] + size, meta[0, 2 * slot + 1] + size)

    for item in copies:
        item.wait()
    for device in range(3):

        @pl.loop(0, notes[device, 0, 2 * slots].astype(jnp.int32))
        def _(slot):
            top = notes[device, 0, 2 * slot].astype(jnp.int32) - meta[0, origin]
            left = notes[device, 0, 2 * slot + 1].astype(jnp.int32) - meta[0, origin + 1]
            add(top + size, left + size)

    @pl.loop(0, tile_rows // 32)
    def _(step):
        rows = pl.ds(pl.multiple_of(size + step * 32, 32), 32)
        out_rows = pl.ds(pl.multiple_of(step * 32, 32), 32)
        inverse_light[out_rows, :] = 1.0 / (grid[rows, size : size + tile_cols] + 1.0)


def light(meta, slots, origin, probe, bottom, corner, lower, tile_shape):
    size = probe.shape[2]
    hbm = pl.BlockSpec(memory_space=pltpu.HBM)
    anywhere = pl.BlockSpec(memory_space=pl.ANY)
    return pl.pallas_call(
        functools.partial(light_kernel, slots, origin),
        out_shape=jax.ShapeDtypeStruct(tile_shape, F32),
        in_specs=[pl.BlockSpec(memory_space=pltpu.SMEM), hbm] + [anywhere] * 3,
        out_specs=pl.BlockSpec(memory_space=pltpu.VMEM),
        scratch_shapes=[
            pltpu.VMEM(probe.shape, F32),
            pltpu.VMEM((size + 16, size), F32),
            pltpu.VMEM((tile_shape[0] + 2 * size, tile_shape[1] + 2 * size), F32),
            pltpu.SMEM((3, 8, 128), F32),
            pltpu.SemaphoreType.DMA((4,)),
        ],
        compiler_params=pltpu.CompilerParams(vmem_limit_bytes=8 * MIB),
        cost_estimate=pl.CostEstimate(flops=4_000_000_000, bytes_accessed=4_000_000, transcendentals=0),
        name="light",
    )(meta, in_hbm(probe), bottom, corner, lower)


def arrange_kernel(meta, amplitudes, out, given, moved, in_sems, out_sems):
    slots, size, _ = amplitudes.shape
    count = meta[0, 2 * slots]

    def load(slot):
        return pltpu.make_async_copy(amplitudes.at[slot], given.at[slot], in_sems.at[slot])

    def store(slot):
        return pltpu.make_async_copy(moved.at[slot], out.at[slot], out_sems.at[slot])

    @pl.loop(0, count)
    def _(slot):
        load(slot).start()

    first = lax.broadcasted_iota(jnp.int32, (size, size), 0)
    second = lax.broadcasted_iota(jnp.int32, (size, size), 1)
    half = size // 2

    def source(index):
        return jnp.where(index < half, 2 * index, 2 * index - (size - 1))

    rows = (source(first) == second).astype(F32).astype(BF16)
    cols = (source(second) == first).astype(F32).astype(BF16)
    rows = jnp.concatenate([rows, rows], axis=1)
    cols = jnp.concatenate([cols, cols], axis=0)

    def each(pair, act):
        act(2 * pair)

        @pl.when(2 * pair + 1 < count)
        def _():
            act(2 * pair + 1)

    @pl.loop(0, (count + 1) // 2)
    def _(pair):
        each(pair, lambda slot: load(slot).wait())
        x = [dot(rows, jnp.concatenate(split(given[2 * pair + k]), axis=0)) for k in range(2)]
        for k in range(2):
            moved[2 * pair + k] = dot(jnp.concatenate(split(x[k]), axis=1), cols)
        each(pair, lambda slot: store(slot).start())

    @pl.loop(0, count)
    def _(slot):
        store(slot).wait()


def arrange(meta, amplitudes):
    slots = amplitudes.shape[0]
    hbm = pl.BlockSpec(memory_space=pltpu.HBM)
    return pl.pallas_call(
        arrange_kernel,
        out_shape=pltpu.HBM(amplitudes.shape, F32),
        in_specs=[pl.BlockSpec(memory_space=pltpu.SMEM), hbm],
        out_specs=hbm,
        scratch_shapes=[
            pltpu.VMEM(amplitudes.shape, F32),
            pltpu.VMEM(amplitudes.shape, F32),
            pltpu.SemaphoreType.DMA((slots,)),
            pltpu.SemaphoreType.DMA((slots,)),
        ],
        compiler_params=pltpu.CompilerParams(vmem_limit_bytes=8 * MIB),
        cost_estimate=LONG,
        name="arrange",
    )(meta, in_hbm(amplitudes))


def three_left(table, t):
    return jnp.concatenate([table[t, 0], table[t, 0], table[t, 1]], axis=1)


def three_right(table, v):
    return jnp.concatenate([table[v, 0], table[v, 0], table[v, 1]], axis=0)


def weave(first, second):
    total = max(len(first), len(second))
    done = [0, 0]
    for i in range(1, total + 1):
        for k, pieces in enumerate((first, second)):
            while done[k] * total < i * len(pieces):
                pieces[done[k]]()
                done[k] += 1


def slots_kernel(
    needs_rim, meta, probe, amplitudes, sources, tables, note, state, outs,
    amp, forward_t, backward_t, chosen, patch_f, patch_b, x_f, y_f, z_f, g_s, x_b, z_b, back, template,
    load_sems, amp_sems, out_sems,
):
    ext, grid, probe_out = state
    size = probe.shape[2]
    half = size // 2
    modes = probe.shape[0]
    slots = amplitudes.shape[0]
    tile_rows, tile_cols = (n - size for n in ext.shape[1:])
    step = 32
    fine = 16

    body_rows, rim_rows = pl.ds(0, tile_rows), pl.ds(tile_rows, size)
    body_cols, rim_cols = pl.ds(0, tile_cols), pl.ds(tile_cols, size)
    if needs_rim:
        places = [
            ext.at[:, pl.ds(0, size), rim_cols],
            ext.at[:, pl.ds(size, tile_rows - size), rim_cols],
            ext.at[:, rim_rows, rim_cols],
        ]
    else:
        places = [ext.at[:, body_rows, body_cols], ext.at[:, rim_rows, body_cols]]
    places += [forward_t, backward_t]
    loads = [
        pltpu.make_async_copy(source, place, load_sems.at[i])
        for i, (source, place) in enumerate(zip([*sources, *tables], places))
    ]
    for load in loads:
        load.start()

    def amp_copy(slot):
        return pltpu.make_async_copy(amplitudes.at[slot], amp.at[slot], amp_sems.at[slot])

    def choose(slot, found):
        beyond = meta[0, 2 * slot + 1] + size > tile_cols
        wanted = beyond if needs_rim else jnp.logical_not(beyond)

        @pl.when(wanted)
        def _():
            chosen[found] = slot
            amp_copy(slot).start()

        return found + wanted.astype(jnp.int32)

    count = lax.fori_loop(0, meta[0, 2 * slots], choose, jnp.zeros((), jnp.int32))

    if not needs_rim:

        @pl.loop(0, (tile_rows + size) // step)
        def _(at):
            rows = pl.ds(pl.multiple_of(at * step, step), step)
            for c in range(2):
                grid[c, rows, :] = jnp.zeros((step, tile_cols + size), F32)

        @pl.loop(0, size // step)
        def _(at):
            rows = pl.ds(pl.multiple_of(at * step, step), step)
            for c in range(2 * modes + 1):
                probe_out[c, rows, :] = jnp.zeros((step, size), F32)

    for c in range(2):
        template[c, 0:8, :] = jnp.zeros((8, size), F32)
        template[c, 8 + size :, :] = jnp.zeros((8, size), F32)
    for load in loads:
        load.wait()

    def corner(slot):
        return meta[0, 2 * slot], meta[0, 2 * slot + 1]

    def forward(slot):
        top, left = corner(slot)

        def take(at):
            for c in range(2):
                patch_f[c, pl.ds(at, step), :] = take_shifted(ext, (c,), top, left, at, step, size)

        def fold_rows(m, at):
            cols = pl.ds(m * size, size)
            parts = []
            for base in (at, half + at):
                rows = pl.ds(base, fine)
                pr, pi = patch_f[0, rows, :], patch_f[1, rows, :]
                qr, qi = probe[m, 0, rows, :], probe[m, 1, rows, :]
                parts.append((qr * pr - qi * pi, qr * pi + qi * pr))
            for c in range(2):
                rows = pl.ds(c * half + at, fine)
                for t, value in enumerate((parts[0][c] + parts[1][c], parts[0][c] - parts[1][c])):
                    x_f[t, 0, rows, cols], x_f[t, 1, rows, cols] = split(value)

        def dft_rows(m, t):
            cols = pl.ds(m * size, size)
            high = x_f[t, 0, :, cols]
            u = dot(three_left(forward_t, t), jnp.concatenate([high, x_f[t, 1, :, cols], high], axis=0))
            rows = pl.ds(m * size + t * half, half)
            for v, value in enumerate((u[:, :half] + u[:, half:], u[:, :half] - u[:, half:])):
                high, low = split(value)
                for c in range(2):
                    lanes = pl.ds(c * half, half)
                    y_f[v, 0, rows, lanes] = high[c * half : (c + 1) * half]
                    y_f[v, 1, rows, lanes] = low[c * half : (c + 1) * half]

        def dft_cols(v):
            high = y_f[v, 0]
            z_f[v] = dot(jnp.concatenate([high, y_f[v, 1], high], axis=1), three_right(backward_t, v))

        def scale(v, at):
            if v == 0 and at == 0:
                amp_copy(slot).wait()
            waves = [z_f[v, pl.ds(m * size + at, fine), :] for m in range(modes)]
            total = jnp.zeros((fine, half), F32)
            for wave in waves:
                total += wave[:, :half] * wave[:, :half] + wave[:, half:] * wave[:, half:]
            measured = amp[slot, pl.ds(at, fine), pl.ds(v * half, half)]
            factor = measured * lax.rsqrt(jnp.maximum(total, FLOOR * FLOOR)) - 1.0
            factor = jnp.concatenate([factor, factor], axis=1)
            for m in range(modes):
                rows = pl.ds(m * size + at, fine)
                g_s[v, 0, rows, :], g_s[v, 1, rows, :] = split(waves[m] * factor)

        pieces = [(take, at) for at in range(0, size, step)]
        for m in range(modes):
            pieces += [(fold_rows, m, at) for at in range(0, half, fine)]
            pieces += [(dft_rows, m, t) for t in range(2)]
        pieces += [(dft_cols, v) for v in range(2)]
        pieces += [(scale, v, at) for v in range(2) for at in range(0, size, fine)]
        return [functools.partial(*piece) for piece in pieces]

    def backward(slot):
        top, left = corner(slot)

        def dft_cols(v):
            high = g_s[v, 0]
            z_b[v] = dot(jnp.concatenate([high, g_s[v, 1], high], axis=1), three_right(forward_t, v))

        def unfold_cols(m, t, at):
            rows = pl.ds(m * size + t * half + at, step)
            even, odd = z_b[0, rows, :], z_b[1, rows, :]
            for v, value in enumerate((even + odd, even - odd)):
                high, low = split(value)
                cols = pl.ds(m * size + v * half, half)
                for c in range(2):
                    spot = pl.ds(c * half + at, step)
                    x_b[t, 0, spot, cols] = high[:, c * half : (c + 1) * half]
                    x_b[t, 1, spot, cols] = low[:, c * half : (c + 1) * half]

        def dft_rows(m, t):
            cols = pl.ds(m * size, size)
            high = x_b[t, 0, :, cols]
            back[m, t] = dot(three_left(backward_t, t), jnp.concatenate([high, x_b[t, 1, :, cols], high], axis=0))

        def gradients(at):
            waves = []
            for m in range(modes):
                pair = []
                for c in range(2):
                    rows = pl.ds(c * half + at, fine)
                    even, odd = back[m, 0, rows, :], back[m, 1, rows, :]
                    pair.append((even + odd, even - odd))
                waves.append(pair)
            for h in range(2):
                rows = pl.ds(h * half + at, fine)
                pr, pi = patch_b[0, rows, :], patch_b[1, rows, :]
                grad_r = jnp.zeros((fine, size), F32)
                grad_i = jnp.zeros((fine, size), F32)
                for m in range(modes):
                    br, bi = waves[m][0][h], waves[m][1][h]
                    qr, qi = probe[m, 0, rows, :], probe[m, 1, rows, :]
                    grad_r += qr * br + qi * bi
                    grad_i += qr * bi - qi * br
                    probe_out[2 * m, rows, :] += pr * br + pi * bi
                    probe_out[2 * m + 1, rows, :] += pr * bi - pi * br
                probe_out[2 * modes, rows, :] += pr * pr + pi * pi
                spot = pl.ds(8 + h * half + at, fine)
                template[0, spot, :] = grad_r
                template[1, spot, :] = grad_i

        def add(c):
            add_shifted(template, grid, (c,), (c,), top, left, size)

        pieces = [(dft_cols, v) for v in range(2)]
        for m in range(modes):
            pieces += [(unfold_cols, m, t, at) for t in range(2) for at in range(0, half, step)]
            pieces += [(dft_rows, m, t) for t in range(2)]
        pieces += [(gradients, at) for at in range(0, half, fine)]
        pieces += [(add, c) for c in range(2)]
        return [functools.partial(*piece) for piece in pieces]

    def hand_over():
        for at in range(0, size, step):
            for c in range(2):
                patch_b[c, pl.ds(at, step), :] = patch_f[c, pl.ds(at, step), :]

    @pl.when(count > 0)
    def _():
        weave(forward(chosen[0]), [])
        hand_over()

        def visit(index, _):
            weave(backward(chosen[index]), forward(chosen[index + 1]))
            hand_over()
            return 0

        lax.fori_loop(0, count - 1, visit, 0)
        weave(backward(chosen[count - 1]), [])

    if needs_rim:
        top, bottom = pl.ds(0, size), pl.ds(size, tile_rows - size)
        parts = [
            (grid.at[:, body_rows, body_cols], outs[0]),
            (grid.at[:, bottom, rim_cols], outs[1].at[:, pl.ds(0, tile_rows - size)]),
            (note, outs[1].at[0, pl.ds(tile_rows - size, 8)]),
            (grid.at[:, top, rim_cols], outs[2]),
            (grid.at[:, rim_rows, rim_cols], outs[3].at[:, top]),
            (note, outs[3].at[0, pl.ds(size, 8)]),
            (grid.at[:, rim_rows, body_cols], outs[4].at[:, top]),
            (probe_out.at[:, pl.ds(pl.multiple_of(meta[0, 2 * slots + 1] * half, half), half)], outs[5]),
        ]
        stores = [pltpu.make_async_copy(part, out, out_sems.at[i]) for i, (part, out) in enumerate(parts)]
        for store in stores:
            store.start()
        for store in stores:
            store.wait()


def scratch_for(size, modes, slots):
    return [
        pltpu.VMEM((slots, size, size), F32),
        pltpu.VMEM((2, 2, size, size), BF16),
        pltpu.VMEM((2, 2, size, size), BF16),
        pltpu.SMEM((slots,), jnp.int32),
        pltpu.VMEM((2, size, size), F32),
        pltpu.VMEM((2, size, size), F32),
        pltpu.VMEM((2, 2, size, modes * size), BF16),
        pltpu.VMEM((2, 2, modes * size, size), BF16),
        pltpu.VMEM((2, modes * size, size), F32),
        pltpu.VMEM((2, 2, modes * size, size), BF16),
        pltpu.VMEM((2, 2, size, modes * size), BF16),
        pltpu.VMEM((2, modes * size, size), F32),
        pltpu.VMEM((modes, 2, size, size), F32),
        pltpu.VMEM((2, size + 16, size), F32),
        pltpu.SemaphoreType.DMA((5,)),
        pltpu.SemaphoreType.DMA((slots,)),
        pltpu.SemaphoreType.DMA((8,)),
    ]


SLOTS_COST = pl.CostEstimate(flops=12_000_000_000, bytes_accessed=16_000_000, transcendentals=0)


def visit_inside(meta, probe, amplitudes, tile, lower):
    size, modes, slots = probe.shape[2], probe.shape[0], amplitudes.shape[0]
    rows, cols = tile.shape[1:]
    tables = [jnp.asarray(item) for item in dft_tables(size)]
    vmem = pl.BlockSpec(memory_space=pltpu.VMEM)
    hbm = pl.BlockSpec(memory_space=pltpu.HBM)
    field = pltpu.VMEM((2, rows + size, cols + size), F32)

    def kernel(meta, probe, amplitudes, tile, lower, forward_h, backward_h, *refs):
        state, scratch = refs[:3], refs[3:]
        slots_kernel(
            False, meta, probe, amplitudes, [tile, lower], [forward_h, backward_h], None, state, None, *scratch
        )

    return pl.pallas_call(
        kernel,
        out_shape=[field, field, pltpu.VMEM((2 * modes + 1, size, size), F32)],
        in_specs=[pl.BlockSpec(memory_space=pltpu.SMEM), vmem, hbm, hbm, pl.BlockSpec(memory_space=pl.ANY), hbm, hbm],
        out_specs=[vmem] * 3,
        scratch_shapes=scratch_for(size, modes, slots),
        compiler_params=pltpu.CompilerParams(vmem_limit_bytes=28 * MIB),
        cost_estimate=SLOTS_COST,
        name="slots_inside",
    )(meta, probe, in_hbm(amplitudes), in_hbm(tile), lower, *map(in_hbm, tables))


def visit_beyond(meta, probe, amplitudes, rims, note, state):
    size, modes, slots = probe.shape[2], probe.shape[0], amplitudes.shape[0]
    rows, cols = (n - size for n in state[0].shape[1:])
    tables = [jnp.asarray(item) for item in dft_tables(size)]
    vmem = pl.BlockSpec(memory_space=pltpu.VMEM)
    hbm = pl.BlockSpec(memory_space=pltpu.HBM)
    anywhere = pl.BlockSpec(memory_space=pl.ANY)
    shapes = [
        (2, rows - size + 8, size),
        (2, size, size),
        (2, size + 8, size),
        (2, size + 8, cols),
        (2 * modes + 1, size // 2, size),
    ]

    def kernel(meta, probe, amplitudes, forward_h, backward_h, *refs):
        rims, note, refs = refs[:3], refs[3], refs[7:]
        state, outs, scratch = refs[:3], refs[3:9], refs[9:]
        slots_kernel(True, meta, probe, amplitudes, rims, [forward_h, backward_h], note, state, outs, *scratch)

    out = pl.pallas_call(
        kernel,
        out_shape=[pltpu.VMEM(item.shape, item.dtype) for item in state]
        + [pltpu.HBM((2, rows, cols), F32)]
        + [jax.ShapeDtypeStruct(shape, F32) for shape in shapes],
        in_specs=[pl.BlockSpec(memory_space=pltpu.SMEM), vmem] + [hbm] * 3 + [anywhere] * 4 + [vmem] * 3,
        out_specs=[vmem] * 3 + [hbm] + [anywhere] * 5,
        input_output_aliases={9 + i: i for i in range(3)},
        scratch_shapes=scratch_for(size, modes, slots),
        compiler_params=pltpu.CompilerParams(vmem_limit_bytes=28 * MIB),
        cost_estimate=SLOTS_COST,
        name="slots_beyond",
    )(meta, probe, *map(in_hbm, [amplitudes, *tables]), *rims, note, *state)
    return (*out[3:], out[2])


def finish_far_kernel(own, bottom, lower, scale, tile, out, own_s, right_s, lower_s, scale_s, tile_s, in_sems, out_sems):
    size = right_s.shape[2]
    block = 128
    blocks = own_s.shape[1] // block

    def copies(i):
        rows = pl.ds(i * block, block)
        pairs = [
            (own.at[:, rows], own_s.at[:, rows]),
            (scale.at[rows], scale_s.at[rows]),
            (tile.at[:, rows], tile_s.at[:, rows]),
        ]
        if i < size // block:
            pairs.append((lower.at[:, rows], lower_s.at[:, rows]))
        else:
            pairs.append((bottom.at[:, pl.ds(i * block - size, block)], right_s.at[:, pl.ds(i * block - size, block)]))
        return [pltpu.make_async_copy(a, b, in_sems.at[i, k]) for k, (a, b) in enumerate(pairs)]

    loads = [copies(i) for i in range(blocks)]
    for load in loads:
        for copy in load:
            copy.start()
    stores = []
    for i in range(blocks):
        for copy in loads[i]:
            copy.wait()
        rows = pl.ds(i * block, block)
        for at in range(i * block, (i + 1) * block, 32):
            part = pl.ds(at, 32)
            for c in range(2):
                near, far = own_s[c, part, :size], own_s[c, part, size:]
                if i < size // block:
                    near, far = near + lower_s[c, part, :size], far + lower_s[c, part, size:]
                else:
                    near = near + right_s[c, pl.ds(at - size, 32), :]
                own_s[c, part, :size] = tile_s[c, part, :size] + near * scale_s[part, :size]
                own_s[c, part, size:] = tile_s[c, part, size:] + far * scale_s[part, size:]
        stores.append(pltpu.make_async_copy(own_s.at[:, rows], out.at[:, rows], out_sems.at[i]))
        stores[-1].start()
    for store in stores:
        store.wait()


def finish_far(own, bottom, lower, inverse_light, tile):
    rows, cols = tile.shape[1:]
    size = bottom.shape[2]
    anywhere = pl.BlockSpec(memory_space=pl.ANY)
    hbm = pl.BlockSpec(memory_space=pltpu.HBM)
    return pl.pallas_call(
        finish_far_kernel,
        out_shape=pltpu.HBM(tile.shape, F32),
        in_specs=[hbm, anywhere, anywhere, anywhere, hbm],
        out_specs=hbm,
        scratch_shapes=[
            pltpu.VMEM(tile.shape, F32),
            pltpu.VMEM((2, rows - size, size), F32),
            pltpu.VMEM((2, size, cols), F32),
            pltpu.VMEM((rows, cols), F32),
            pltpu.VMEM(tile.shape, F32),
            pltpu.SemaphoreType.DMA((rows // 128, 4)),
            pltpu.SemaphoreType.DMA((rows // 128,)),
        ],
        compiler_params=pltpu.CompilerParams(vmem_limit_bytes=12 * MIB),
        cost_estimate=pl.CostEstimate(flops=2_000_000_000, bytes_accessed=4_000_000, transcendentals=0),
        name="finish_far",
    )(in_hbm(own), bottom, lower, inverse_light, in_hbm(tile))


def finish_near(before, top, inverse_light):
    size = top.shape[2]

    def kernel(before, top, scale, out, top_s, scale_s, out_s, sems, out_sems):
        corner = (pl.ds(0, size), pl.ds(0, size))
        loads = [
            pltpu.make_async_copy(before.at[(slice(None), *corner)], out_s, sems.at[0]),
            pltpu.make_async_copy(scale.at[corner], scale_s, sems.at[1]),
            pltpu.make_async_copy(top, top_s, sems.at[2]),
        ]
        for load in loads:
            load.start()
        for load in loads:
            load.wait()
        stores = []
        for c in range(2):
            out_s[c] += top_s[c] * scale_s[...]
            stores.append(pltpu.make_async_copy(out_s.at[c], out.at[(c, *corner)], out_sems.at[c]))
            stores[-1].start()
        for store in stores:
            store.wait()

    anywhere = pl.BlockSpec(memory_space=pl.ANY)
    hbm = pl.BlockSpec(memory_space=pltpu.HBM)
    return pl.pallas_call(
        kernel,
        out_shape=pltpu.HBM(before.shape, F32),
        in_specs=[hbm, anywhere, anywhere],
        out_specs=hbm,
        input_output_aliases={0: 0},
        scratch_shapes=[
            pltpu.VMEM((2, size, size), F32),
            pltpu.VMEM((size, size), F32),
            pltpu.VMEM((2, size, size), F32),
            pltpu.SemaphoreType.DMA((3,)),
            pltpu.SemaphoreType.DMA((2,)),
        ],
        compiler_params=pltpu.CompilerParams(vmem_limit_bytes=4 * MIB),
        cost_estimate=pl.CostEstimate(flops=2_000_000_000, bytes_accessed=4_000_000, transcendentals=0),
        name="finish_near",
    )(in_hbm(before), top, inverse_light)


def from_behind(array, axis, by):
    count = lax.axis_size(axis)
    pairs = [(i, i + by) for i in range(count) if 0 <= i + by < count]
    return lax.ppermute(array, axis, pairs)


def exchange(array, axis, bit):
    count = lax.axis_size(axis)
    return lax.ppermute(array, axis, [(i, i ^ bit) for i in range(count)])


def together(*arrays):
    return lax.optimization_barrier(arrays)


def cut(tile, regions, cost, name):
    def kernel(tile, *refs):
        sems = refs[-1]
        copies = [
            pltpu.make_async_copy(tile.at[:, pl.ds(at, height), pl.ds(0, width)], out, sems.at[i])
            for i, ((at, height, width), out) in enumerate(zip(regions, refs[:-1]))
        ]
        for copy in copies:
            copy.start()
        for copy in copies:
            copy.wait()

    return pl.pallas_call(
        kernel,
        out_shape=[jax.ShapeDtypeStruct((2, height, width), F32) for _, height, width in regions],
        in_specs=[pl.BlockSpec(memory_space=pltpu.HBM)],
        out_specs=[pl.BlockSpec(memory_space=pltpu.VMEM)] * len(regions),
        scratch_shapes=[pltpu.SemaphoreType.DMA((len(regions),))],
        compiler_params=pltpu.CompilerParams(vmem_limit_bytes=4 * MIB),
        cost_estimate=cost,
        name=name,
    )(in_hbm(tile))


def fold(places, index, mine, got, upper):
    count, half, width = got.shape
    quarter = half // 2

    def kernel(places, mine, got, send, keep):
        base = 0 if index is None else places[0, index] * half
        for k, out in ((1 - places[0, upper], send), (places[0, upper], keep)):
            for c in range(count):
                out[c] = (
                    mine[c, pl.ds(pl.multiple_of(base + k * quarter, quarter), quarter), :]
                    + got[c, pl.ds(pl.multiple_of(k * quarter, quarter), quarter), :]
                )

    vmem = pl.BlockSpec(memory_space=pltpu.VMEM)
    shape = jax.ShapeDtypeStruct((count, quarter, width), F32)
    return pl.pallas_call(
        kernel,
        out_shape=[shape, shape],
        in_specs=[pl.BlockSpec(memory_space=pltpu.SMEM), vmem, vmem],
        out_specs=[vmem, vmem],
        compiler_params=pltpu.CompilerParams(vmem_limit_bytes=6 * MIB),
        cost_estimate=SHORT,
        name="fold",
    )(places, mine, got)


def merge(top, corner):
    size = top.shape[1]

    def kernel(top, corner, out):
        for c in range(2):
            out[c] = top[c] + corner[c, :size, :]

    vmem = pl.BlockSpec(memory_space=pltpu.VMEM)
    return pl.pallas_call(
        kernel,
        out_shape=jax.ShapeDtypeStruct(top.shape, F32),
        in_specs=[vmem, vmem],
        out_specs=vmem,
        compiler_params=pltpu.CompilerParams(vmem_limit_bytes=4 * MIB),
        cost_estimate=SHORT,
        name="merge",
    )(top, corner)


def annotate(lower, bottom):
    size = bottom.shape[2]

    def kernel(lower, bottom, out, sem):
        source = bottom.at[0, pl.ds(bottom.shape[1] - 8, 8)]
        copy = pltpu.make_async_copy(source, out.at[0, pl.ds(out.shape[1] - 8, 8), pl.ds(0, size)], sem.at[0])
        copy.start()
        copy.wait()

    anywhere = pl.BlockSpec(memory_space=pl.ANY)
    return pl.pallas_call(
        kernel,
        out_shape=jax.ShapeDtypeStruct(lower.shape, F32),
        in_specs=[anywhere, anywhere],
        out_specs=anywhere,
        input_output_aliases={0: 0},
        scratch_shapes=[pltpu.SemaphoreType.DMA((1,))],
        compiler_params=pltpu.CompilerParams(vmem_limit_bytes=MIB),
        cost_estimate=SHORT,
        name="annotate",
    )(lower, bottom)


def deal(terms, parts, rows):
    count, _, width = terms[0].shape
    if rows % 8:
        return sum(terms).reshape(count, parts, rows, width).transpose(1, 0, 2, 3)

    def kernel(*refs):
        terms, out = refs[:-1], refs[-1]
        for j in range(parts):
            for c in range(count):
                out[j, c] = sum(term[c, j * rows : (j + 1) * rows, :] for term in terms)

    vmem = pl.BlockSpec(memory_space=pltpu.VMEM)
    return pl.pallas_call(
        kernel,
        out_shape=jax.ShapeDtypeStruct((parts, count, rows, width), F32),
        in_specs=[vmem] * len(terms),
        out_specs=vmem,
        compiler_params=pltpu.CompilerParams(vmem_limit_bytes=4 * MIB),
        cost_estimate=SHORT,
        name="deal",
    )(*terms)


def settle(places, start, probe, pieces):
    parts, count, rows, width = pieces.shape
    shape = (parts, count - 1, rows, width)
    if rows % 8:
        share = pieces.sum(axis=0)
        old = lax.dynamic_slice_in_dim(probe, places[0, start], rows, axis=1)
        return jnp.broadcast_to((old + share[:-1] / (share[-1:] + 1.0))[None], shape)

    def kernel(places, probe, pieces, out, old, sem):
        spot = pl.ds(pl.multiple_of(places[0, start], 8), rows)
        copy = pltpu.make_async_copy(probe.at[:, spot], old, sem.at[0])
        copy.start()
        share = sum(pieces[j] for j in range(parts))
        copy.wait()
        new = old[...] + share[:-1] / (share[-1:] + 1.0)
        for j in range(parts):
            out[j] = new

    vmem = pl.BlockSpec(memory_space=pltpu.VMEM)
    return pl.pallas_call(
        kernel,
        out_shape=jax.ShapeDtypeStruct(shape, F32),
        in_specs=[pl.BlockSpec(memory_space=pltpu.SMEM), pl.BlockSpec(memory_space=pltpu.HBM), vmem],
        out_specs=vmem,
        scratch_shapes=[pltpu.VMEM(shape[1:], F32), pltpu.SemaphoreType.DMA((1,))],
        compiler_params=pltpu.CompilerParams(vmem_limit_bytes=4 * MIB),
        cost_estimate=SHORT,
        name="settle",
    )(places, in_hbm(probe), pieces)


def collect(pieces):
    parts, count, rows, width = pieces.shape
    if rows % 8:
        return pieces.transpose(1, 0, 2, 3).reshape(count, parts * rows, width)

    def kernel(pieces, out):
        for j in range(parts):
            for c in range(count):
                out[c, j * rows : (j + 1) * rows, :] = pieces[j, c]

    vmem = pl.BlockSpec(memory_space=pltpu.VMEM)
    return pl.pallas_call(
        kernel,
        out_shape=jax.ShapeDtypeStruct((count, parts * rows, width), F32),
        in_specs=[vmem],
        out_specs=vmem,
        compiler_params=pltpu.CompilerParams(vmem_limit_bytes=4 * MIB),
        cost_estimate=pl.CostEstimate(flops=30_000_000_000, bytes_accessed=4_000_000, transcendentals=0),
        name="collect",
    )(pieces)


def join(places, upper, mine, other):
    half = mine.shape[1]

    def kernel(places, mine, other, out, sems):
        copies = [
            pltpu.make_async_copy(source, out.at[:, pl.ds(pl.multiple_of(at * half, half), half)], sems.at[i])
            for i, (source, at) in enumerate(((mine, places[0, upper]), (other, 1 - places[0, upper])))
        ]
        for copy in copies:
            copy.start()
        for copy in copies:
            copy.wait()

    anywhere = pl.BlockSpec(memory_space=pl.ANY)
    return pl.pallas_call(
        kernel,
        out_shape=jax.ShapeDtypeStruct((mine.shape[0], 2 * half) + mine.shape[2:], F32),
        in_specs=[pl.BlockSpec(memory_space=pltpu.SMEM), anywhere, anywhere],
        out_specs=anywhere,
        scratch_shapes=[pltpu.SemaphoreType.DMA((2,))],
        compiler_params=pltpu.CompilerParams(vmem_limit_bytes=MIB),
        cost_estimate=pl.CostEstimate(flops=0, bytes_accessed=2_000_000, transcendentals=0),
        name="join",
    )(places, mine, other)


def body(object_field, probe, amplitudes, positions, counts):
    modes, _, size, _ = probe.shape
    tile_rows, tile_cols = object_field.shape[1:]
    slots = amplitudes.shape[0]
    origin = jnp.stack([lax.axis_index("row") * tile_rows, lax.axis_index("col") * tile_cols]).astype(jnp.int32)
    bits = [1 << k for k in range(lax.axis_size("row").bit_length() - 1)]
    uppers = [(lax.axis_index("row") & bit) // bit for bit in bits]

    def relative(table):
        return jnp.concatenate([table[:, : 2 * slots] - jnp.tile(origin, slots)[None], table[:, 2 * slots :]], axis=1)

    right_up, right_down = cut(
        object_field, ((0, size, size), (size, tile_rows - size, size)), SHORT, "cut_right"
    )
    right_up, right_down, after_right = together(right_up, right_down, object_field)
    right_up = from_behind(right_up, "col", -1)
    right_down = from_behind(right_down, "col", -1)
    (lower,) = cut(after_right, ((0, size, tile_cols),), LONG, "cut_lower")
    meta = jnp.concatenate([positions.reshape(1, 2 * slots), counts.reshape(1, 1)], axis=1)
    lower = from_behind(lower, "row", -1)

    parts = lax.axis_size("col")
    rows = (size >> len(bits)) // parts
    me = lax.axis_index("col")
    start = sum(upper * (size >> (k + 1)) for k, upper in enumerate(uppers)) + me * rows
    bit_at = 2 * slots + 2
    me_at = bit_at + len(bits)
    start_at, origin_at = me_at + 1, me_at + 2
    extra = [1 - uppers[0], *uppers, me, start, origin[0], origin[1]]
    mine = jnp.concatenate([relative(meta), jnp.stack([item.astype(jnp.int32) for item in extra])[None]], axis=1)
    note = jnp.pad(meta.astype(F32), ((0, 7), (0, size - meta.shape[1])))
    mine, note = together(mine, note)
    amplitudes = arrange(mine, amplitudes)
    right_up, amplitudes = together(right_up, amplitudes)
    corner = from_behind(right_up, "row", -1)
    amplitudes, lower = together(amplitudes, lower)
    state = visit_inside(mine, probe, amplitudes, object_field, lower)
    right_up, right_down, corner, *state = together(right_up, right_down, corner, *state)
    own, bottom_spill, top_spill, corner_spill, lower_spill, send, share = visit_beyond(
        mine, probe, amplitudes, [right_up, right_down, corner], note, state
    )

    index = bit_at
    for k, bit in enumerate(bits):
        got = exchange(send, "row", bit)
        if k == 0:
            bottom_spill = from_behind(bottom_spill, "col", 1)
        if k + 1 < len(bits):
            send, share = fold(mine, index, share, got, bit_at + k + 1)
            index = None
    pieces = lax.all_to_all(deal([share, got], parts, rows), "col", 0, 0, tiled=True)
    new = settle(mine, start_at, probe.reshape(2 * modes, size, size), pieces)
    new, bottom_spill, lower_spill, corner_spill = together(new, bottom_spill, lower_spill, corner_spill)
    corner_spill = from_behind(corner_spill, "row", 1)
    lower_spill = from_behind(annotate(lower_spill, bottom_spill), "row", 1)
    new = lax.all_to_all(new, "col", 0, 0, tiled=True)
    new, corner_spill = together(new, corner_spill)
    top_spill, new = together(merge(top_spill, corner_spill), new)
    top_spill = from_behind(top_spill, "col", 1)
    new = collect(new)
    inverse_light = light(
        mine, slots, origin_at, probe, bottom_spill, corner_spill, lower_spill, (tile_rows, tile_cols)
    )
    for k, bit in reversed(list(enumerate(bits))):
        if k == 0:
            new, own = together(new, own)
            new_object = finish_far(own, bottom_spill, lower_spill, inverse_light, object_field)
        other = exchange(new, "row", bit)
        if k + 1 == len(bits):
            other, inverse_light = together(other, inverse_light)
        if k == 0:
            new_object, top_spill = together(new_object, top_spill)
            new_object = finish_near(new_object, top_spill, inverse_light)
            other, new_object = together(other, new_object)
        new = join(mine, bit_at + k, new, other)
    return (new_object, new.reshape(modes, 2, size, size))


def solution(mesh):
    in_specs = (
        P(None, "row", "col"),
        P(),
        P(("row", "col"), None, None),
        P(("row", "col"), None),
        P(("row", "col")),
    )
    out_specs = (P(None, "row", "col"), P())
    return jax.shard_map(body, mesh=mesh, in_specs=in_specs, out_specs=out_specs, check_vma=False)
```

```python
import functools
import math

import jax
import jax.numpy as jnp
import ml_dtypes
import numpy as np
from jax import lax
from jax.experimental import pallas as pl
from jax.experimental.pallas import tpu as pltpu
from jax.sharding import PartitionSpec as P

F32 = jnp.float32
BF16 = jnp.bfloat16
MIB = 1024 * 1024
LONG = pl.CostEstimate(flops=30_000_000_000, bytes_accessed=4_000_000, transcendentals=0)
SHORT = pl.CostEstimate(flops=0, bytes_accessed=1_000_000, transcendentals=0)
FLOOR = 0.3


def split_np(table):
    high = table.astype(ml_dtypes.bfloat16)
    low = (table - high.astype(np.float64)).astype(ml_dtypes.bfloat16)
    return high, low


def dft_tables(length):
    half = length // 2
    q = np.arange(half)[:, None]
    n = np.arange(half)[None, :]
    forward = []
    for odd in range(2):
        phase = (n * (2 * q + odd)) % length
        angle = phase * (-2.0 * math.pi / length)
        re = np.cos(angle) / math.sqrt(length)
        im = np.sin(angle) / math.sqrt(length)
        forward.append(np.stack(split_np(np.block([[re, -im], [im, re]]))))
    forward = np.stack(forward)
    return forward, np.ascontiguousarray(forward.transpose(0, 1, 3, 2))


def in_hbm(array):
    return pltpu.with_memory_space_constraint(array, pltpu.HBM)


def dot(a, b):
    return jnp.dot(a, b, preferred_element_type=F32)


def split(x):
    high = x.astype(BF16)
    return high, (x - high.astype(F32)).astype(BF16)


def roll_rows(x, shift):
    return pltpu.roll(x.reshape(x.shape[0] // 8, 8, x.shape[1]), shift, 1)


def roll_rows(x, shift):
    return pltpu.roll(x.reshape(x.shape[0] // 8, 8, x.shape[1]), shift, 1)


def roll_rows(x, shift):
    return pltpu.roll(x.reshape(x.shape[0] // 8, 8, x.shape[1]), shift, 1)


def roll_rows(x, shift):
    return pltpu.roll(x.reshape(x.shape[0] // 8, 8, x.shape[1]), shift, 1)


def split_three(x):
    high = x.astype(BF16)
    rest = x - high.astype(F32)
    middle = rest.astype(BF16)
    return high, middle, (rest - middle.astype(F32)).astype(BF16)


def add_shifted(template, grid, where_t, where_g, top, left, size):
    top_s = top & 7
    top_b = pl.multiple_of(top - top_s, 8)
    left_s = left & 127
    left_b = pl.multiple_of(left - left_s, 128)
    step = 24
    wrapped = lax.broadcasted_iota(jnp.int32, (step, 128), 1) < left_s
    wrapped_rows = lax.broadcasted_iota(jnp.int32, (step // 8, 8, 128), 1) < top_s
    zero = jnp.zeros((step, 128), F32)
    blocks = size // 128
    for at in range(0, size + 8, step):
        parts = []
        for j in range(blocks):
            x = roll_rows(template[where_t + (pl.ds(at, step + 8), pl.ds(128 * j, 128))], top_s)
            x = jnp.where(wrapped_rows, x[:-1], x[1:]).reshape(step, 128)
            parts.append(pltpu.roll(x, left_s, 1))
        for j in range(blocks + 1):
            before = parts[j - 1] if j > 0 else zero
            after = parts[j] if j < blocks else zero
            spot = where_g + (pl.ds(top_b + at, step), pl.ds(left_b + 128 * j, 128))
            grid[spot] += jnp.where(wrapped, before, after)


def take_shifted(field, where, top, left, at, step, size):
    top_s = top & 7
    top_b = pl.multiple_of(top - top_s, 8)
    left_s = left & 127
    left_b = pl.multiple_of(left - left_s, 128)
    back = (128 - left_s) & 127
    keep = lax.broadcasted_iota(jnp.int32, (step + 8, 128), 1) < 128 - left_s
    keep_rows = lax.broadcasted_iota(jnp.int32, (step // 8, 8, 128), 1) < 8 - top_s
    blocks = size // 128
    parts = [
        pltpu.roll(field[where + (pl.ds(top_b + at, step + 8), pl.ds(left_b + 128 * j, 128))], back, 1)
        for j in range(blocks + 1)
    ]
    pieces = []
    for j in range(blocks):
        x = roll_rows(jnp.where(keep, parts[j], parts[j + 1]), (8 - top_s) & 7)
        pieces.append(jnp.where(keep_rows, x[:-1], x[1:]).reshape(step, 128))
    return jnp.concatenate(pieces, axis=1)


def light_kernel(slots, origin, meta, probe_h, bottom, corner, lower, inverse_light, probe, template, grid, notes, sems):
    size = probe.shape[2]
    tile_rows, tile_cols = inverse_light.shape
    copies = [
        pltpu.make_async_copy(spill.at[0, pl.ds(spill.shape[1] - 8, 8), pl.ds(0, 128)], notes.at[i], sems.at[i])
        for i, spill in enumerate((bottom, corner, lower))
    ]
    copy = pltpu.make_async_copy(probe_h, probe, sems.at[3])
    copy.start()
    for item in copies:
        item.start()
    template[0:8, :] = jnp.zeros((8, size), F32)
    template[8 + size :, :] = jnp.zeros((8, size), F32)
    copy.wait()
    for at in range(0, size, 32):
        rows = pl.ds(at, 32)
        total = jnp.zeros((32, size), F32)
        for m in range(probe.shape[0]):
            total += probe[m, 0, rows] * probe[m, 0, rows] + probe[m, 1, rows] * probe[m, 1, rows]
        template[pl.ds(8 + at, 32), :] = total

    @pl.loop(0, tile_rows // 32)
    def _(step):
        rows = pl.ds(pl.multiple_of(size + step * 32, 32), 32)
        grid[rows, size : size + tile_cols] = jnp.zeros((32, tile_cols), F32)

    def add(top, left):
        @pl.when((top > 0) & (left > 0))
        def _():
            add_shifted(template, grid, (), (), top, left, size)

    @pl.loop(0, meta[0, 2 * slots])
    def _(slot):
        add(meta[0, 2 * slot] + size, meta[0, 2 * slot + 1] + size)

    for item in copies:
        item.wait()
    for device in range(3):

        @pl.loop(0, notes[device, 0, 2 * slots].astype(jnp.int32))
        def _(slot):
            top = notes[device, 0, 2 * slot].astype(jnp.int32) - meta[0, origin]
            left = notes[device, 0, 2 * slot + 1].astype(jnp.int32) - meta[0, origin + 1]
            add(top + size, left + size)

    @pl.loop(0, tile_rows // 32)
    def _(step):
        rows = pl.ds(pl.multiple_of(size + step * 32, 32), 32)
        out_rows = pl.ds(pl.multiple_of(step * 32, 32), 32)
        inverse_light[out_rows, :] = 1.0 / (grid[rows, size : size + tile_cols] + 1.0)


def light(meta, slots, origin, probe, bottom, corner, lower, tile_shape):
    size = probe.shape[2]
    hbm = pl.BlockSpec(memory_space=pltpu.HBM)
    anywhere = pl.BlockSpec(memory_space=pl.ANY)
    return pl.pallas_call(
        functools.partial(light_kernel, slots, origin),
        out_shape=jax.ShapeDtypeStruct(tile_shape, F32),
        in_specs=[pl.BlockSpec(memory_space=pltpu.SMEM), hbm] + [anywhere] * 3,
        out_specs=pl.BlockSpec(memory_space=pltpu.VMEM),
        scratch_shapes=[
            pltpu.VMEM(probe.shape, F32),
            pltpu.VMEM((size + 16, size), F32),
            pltpu.VMEM((tile_shape[0] + 2 * size, tile_shape[1] + 2 * size), F32),
            pltpu.SMEM((3, 8, 128), F32),
            pltpu.SemaphoreType.DMA((4,)),
        ],
        compiler_params=pltpu.CompilerParams(vmem_limit_bytes=8 * MIB),
        cost_estimate=pl.CostEstimate(flops=4_000_000_000, bytes_accessed=4_000_000, transcendentals=0),
        name="light",
    )(meta, in_hbm(probe), bottom, corner, lower)


def arrange_kernel(meta, amplitudes, out, given, moved, in_sems, out_sems):
    slots, size, _ = amplitudes.shape
    count = meta[0, 2 * slots]

    def load(slot):
        return pltpu.make_async_copy(amplitudes.at[slot], given.at[slot], in_sems.at[slot])

    def store(slot):
        return pltpu.make_async_copy(moved.at[slot], out.at[slot], out_sems.at[slot])

    @pl.loop(0, count)
    def _(slot):
        load(slot).start()

    first = lax.broadcasted_iota(jnp.int32, (size, size), 0)
    second = lax.broadcasted_iota(jnp.int32, (size, size), 1)
    half = size // 2

    def source(index):
        return jnp.where(index < half, 2 * index, 2 * index - (size - 1))

    rows = (source(first) == second).astype(F32).astype(BF16)
    cols = (source(second) == first).astype(F32).astype(BF16)
    rows = jnp.concatenate([rows, rows], axis=1)
    cols = jnp.concatenate([cols, cols], axis=0)

    def each(pair, act):
        act(2 * pair)

        @pl.when(2 * pair + 1 < count)
        def _():
            act(2 * pair + 1)

    @pl.loop(0, (count + 1) // 2)
    def _(pair):
        each(pair, lambda slot: load(slot).wait())
        x = [dot(rows, jnp.concatenate(split(given[2 * pair + k]), axis=0)) for k in range(2)]
        for k in range(2):
            moved[2 * pair + k] = dot(jnp.concatenate(split(x[k]), axis=1), cols)
        each(pair, lambda slot: store(slot).start())

    @pl.loop(0, count)
    def _(slot):
        store(slot).wait()


def arrange(meta, amplitudes):
    slots = amplitudes.shape[0]
    hbm = pl.BlockSpec(memory_space=pltpu.HBM)
    return pl.pallas_call(
        arrange_kernel,
        out_shape=pltpu.HBM(amplitudes.shape, F32),
        in_specs=[pl.BlockSpec(memory_space=pltpu.SMEM), hbm],
        out_specs=hbm,
        scratch_shapes=[
            pltpu.VMEM(amplitudes.shape, F32),
            pltpu.VMEM(amplitudes.shape, F32),
            pltpu.SemaphoreType.DMA((slots,)),
            pltpu.SemaphoreType.DMA((slots,)),
        ],
        compiler_params=pltpu.CompilerParams(vmem_limit_bytes=8 * MIB),
        cost_estimate=LONG,
        name="arrange",
    )(meta, in_hbm(amplitudes))


def three_left(table, t):
    return jnp.concatenate([table[t, 0], table[t, 0], table[t, 1]], axis=1)


def three_right(table, v):
    return jnp.concatenate([table[v, 0], table[v, 0], table[v, 1]], axis=0)


def weave(first, second):
    total = max(len(first), len(second))
    done = [0, 0]
    for i in range(1, total + 1):
        for k, pieces in enumerate((first, second)):
            while done[k] * total < i * len(pieces):
                pieces[done[k]]()
                done[k] += 1


def slots_kernel(
    needs_rim, meta, probe, amplitudes, sources, tables, note, state, outs,
    amp, forward_t, backward_t, chosen, patch_f, patch_b, x_f, y_f, z_f, g_s, x_b, z_b, back, template,
    load_sems, amp_sems, out_sems,
):
    ext, grid, probe_out = state
    size = probe.shape[2]
    half = size // 2
    modes = probe.shape[0]
    slots = amplitudes.shape[0]
    tile_rows, tile_cols = (n - size for n in ext.shape[1:])
    step = 32
    fine = 16

    body_rows, rim_rows = pl.ds(0, tile_rows), pl.ds(tile_rows, size)
    body_cols, rim_cols = pl.ds(0, tile_cols), pl.ds(tile_cols, size)
    if needs_rim:
        places = [
            ext.at[:, pl.ds(0, size), rim_cols],
            ext.at[:, pl.ds(size, tile_rows - size), rim_cols],
            ext.at[:, rim_rows, rim_cols],
        ]
    else:
        places = [ext.at[:, body_rows, body_cols], ext.at[:, rim_rows, body_cols]]
    places += [forward_t, backward_t]
    loads = [
        pltpu.make_async_copy(source, place, load_sems.at[i])
        for i, (source, place) in enumerate(zip([*sources, *tables], places))
    ]
    for load in loads:
        load.start()

    def amp_copy(slot):
        return pltpu.make_async_copy(amplitudes.at[slot], amp.at[slot], amp_sems.at[slot])

    def choose(slot, found):
        beyond = meta[0, 2 * slot + 1] + size > tile_cols
        wanted = beyond if needs_rim else jnp.logical_not(beyond)

        @pl.when(wanted)
        def _():
            chosen[found] = slot
            amp_copy(slot).start()

        return found + wanted.astype(jnp.int32)

    count = lax.fori_loop(0, meta[0, 2 * slots], choose, jnp.zeros((), jnp.int32))

    if not needs_rim:

        @pl.loop(0, (tile_rows + size) // step)
        def _(at):
            rows = pl.ds(pl.multiple_of(at * step, step), step)
            for c in range(2):
                grid[c, rows, :] = jnp.zeros((step, tile_cols + size), F32)

        @pl.loop(0, size // step)
        def _(at):
            rows = pl.ds(pl.multiple_of(at * step, step), step)
            for c in range(2 * modes + 1):
                probe_out[c, rows, :] = jnp.zeros((step, size), F32)

    for c in range(2):
        template[c, 0:8, :] = jnp.zeros((8, size), F32)
        template[c, 8 + size :, :] = jnp.zeros((8, size), F32)
    for load in loads:
        load.wait()

    def corner(slot):
        return meta[0, 2 * slot], meta[0, 2 * slot + 1]

    def forward(slot):
        top, left = corner(slot)

        def take(at):
            for c in range(2):
                patch_f[c, pl.ds(at, step), :] = take_shifted(ext, (c,), top, left, at, step, size)

        def fold_rows(m, at):
            cols = pl.ds(m * size, size)
            parts = []
            for base in (at, half + at):
                rows = pl.ds(base, fine)
                pr, pi = patch_f[0, rows, :], patch_f[1, rows, :]
                qr, qi = probe[m, 0, rows, :], probe[m, 1, rows, :]
                parts.append((qr * pr - qi * pi, qr * pi + qi * pr))
            for c in range(2):
                rows = pl.ds(c * half + at, fine)
                for t, value in enumerate((parts[0][c] + parts[1][c], parts[0][c] - parts[1][c])):
                    x_f[t, 0, rows, cols], x_f[t, 1, rows, cols] = split(value)

        def dft_rows(m, t):
            cols = pl.ds(m * size, size)
            high = x_f[t, 0, :, cols]
            u = dot(three_left(forward_t, t), jnp.concatenate([high, x_f[t, 1, :, cols], high], axis=0))
            rows = pl.ds(m * size + t * half, half)
            for v, value in enumerate((u[:, :half] + u[:, half:], u[:, :half] - u[:, half:])):
                high, low = split(value)
                for c in range(2):
                    lanes = pl.ds(c * half, half)
                    y_f[v, 0, rows, lanes] = high[c * half : (c + 1) * half]
                    y_f[v, 1, rows, lanes] = low[c * half : (c + 1) * half]

        def dft_cols(v):
            high = y_f[v, 0]
            z_f[v] = dot(jnp.concatenate([high, y_f[v, 1], high], axis=1), three_right(backward_t, v))

        def scale(v, at):
            if v == 0 and at == 0:
                amp_copy(slot).wait()
            waves = [z_f[v, pl.ds(m * size + at, fine), :] for m in range(modes)]
            total = jnp.zeros((fine, half), F32)
            for wave in waves:
                total += wave[:, :half] * wave[:, :half] + wave[:, half:] * wave[:, half:]
            measured = amp[slot, pl.ds(at, fine), pl.ds(v * half, half)]
            factor = measured * lax.rsqrt(jnp.maximum(total, FLOOR * FLOOR)) - 1.0
            factor = jnp.concatenate([factor, factor], axis=1)
            for m in range(modes):
                rows = pl.ds(m * size + at, fine)
                g_s[v, 0, rows, :], g_s[v, 1, rows, :] = split(waves[m] * factor)

        pieces = [(take, at) for at in range(0, size, step)]
        for m in range(modes):
            pieces += [(fold_rows, m, at) for at in range(0, half, fine)]
            pieces += [(dft_rows, m, t) for t in range(2)]
        pieces += [(dft_cols, v) for v in range(2)]
        pieces += [(scale, v, at) for v in range(2) for at in range(0, size, fine)]
        return [functools.partial(*piece) for piece in pieces]

    def backward(slot):
        top, left = corner(slot)

        def dft_cols(v):
            high = g_s[v, 0]
            z_b[v] = dot(jnp.concatenate([high, g_s[v, 1], high], axis=1), three_right(forward_t, v))

        def unfold_cols(m, t, at):
            rows = pl.ds(m * size + t * half + at, step)
            even, odd = z_b[0, rows, :], z_b[1, rows, :]
            for v, value in enumerate((even + odd, even - odd)):
                high, low = split(value)
                cols = pl.ds(m * size + v * half, half)
                for c in range(2):
                    spot = pl.ds(c * half + at, step)
                    x_b[t, 0, spot, cols] = high[:, c * half : (c + 1) * half]
                    x_b[t, 1, spot, cols] = low[:, c * half : (c + 1) * half]

        def dft_rows(m, t):
            cols = pl.ds(m * size, size)
            high = x_b[t, 0, :, cols]
            back[m, t] = dot(three_left(backward_t, t), jnp.concatenate([high, x_b[t, 1, :, cols], high], axis=0))

        def gradients(at):
            waves = []
            for m in range(modes):
                pair = []
                for c in range(2):
                    rows = pl.ds(c * half + at, fine)
                    even, odd = back[m, 0, rows, :], back[m, 1, rows, :]
                    pair.append((even + odd, even - odd))
                waves.append(pair)
            for h in range(2):
                rows = pl.ds(h * half + at, fine)
                pr, pi = patch_b[0, rows, :], patch_b[1, rows, :]
                grad_r = jnp.zeros((fine, size), F32)
                grad_i = jnp.zeros((fine, size), F32)
                for m in range(modes):
                    br, bi = waves[m][0][h], waves[m][1][h]
                    qr, qi = probe[m, 0, rows, :], probe[m, 1, rows, :]
                    grad_r += qr * br + qi * bi
                    grad_i += qr * bi - qi * br
                    probe_out[2 * m, rows, :] += pr * br + pi * bi
                    probe_out[2 * m + 1, rows, :] += pr * bi - pi * br
                probe_out[2 * modes, rows, :] += pr * pr + pi * pi
                spot = pl.ds(8 + h * half + at, fine)
                template[0, spot, :] = grad_r
                template[1, spot, :] = grad_i

        def add(c):
            add_shifted(template, grid, (c,), (c,), top, left, size)

        pieces = [(dft_cols, v) for v in range(2)]
        for m in range(modes):
            pieces += [(unfold_cols, m, t, at) for t in range(2) for at in range(0, half, step)]
            pieces += [(dft_rows, m, t) for t in range(2)]
        pieces += [(gradients, at) for at in range(0, half, fine)]
        pieces += [(add, c) for c in range(2)]
        return [functools.partial(*piece) for piece in pieces]

    def hand_over():
        for at in range(0, size, step):
            for c in range(2):
                patch_b[c, pl.ds(at, step), :] = patch_f[c, pl.ds(at, step), :]

    @pl.when(count > 0)
    def _():
        weave(forward(chosen[0]), [])
        hand_over()

        def visit(index, _):
            weave(backward(chosen[index]), forward(chosen[index + 1]))
            hand_over()
            return 0

        lax.fori_loop(0, count - 1, visit, 0)
        weave(backward(chosen[count - 1]), [])

    if needs_rim:
        top, bottom = pl.ds(0, size), pl.ds(size, tile_rows - size)
        parts = [
            (grid.at[:, body_rows, body_cols], outs[0]),
            (grid.at[:, bottom, rim_cols], outs[1].at[:, pl.ds(0, tile_rows - size)]),
            (note, outs[1].at[0, pl.ds(tile_rows - size, 8)]),
            (grid.at[:, top, rim_cols], outs[2]),
            (grid.at[:, rim_rows, rim_cols], outs[3].at[:, top]),
            (note, outs[3].at[0, pl.ds(size, 8)]),
            (grid.at[:, rim_rows, body_cols], outs[4].at[:, top]),
            (probe_out.at[:, pl.ds(pl.multiple_of(meta[0, 2 * slots + 1] * half, half), half)], outs[5]),
        ]
        stores = [pltpu.make_async_copy(part, out, out_sems.at[i]) for i, (part, out) in enumerate(parts)]
        for store in stores:
            store.start()
        for store in stores:
            store.wait()


def scratch_for(size, modes, slots):
    return [
        pltpu.VMEM((slots, size, size), F32),
        pltpu.VMEM((2, 2, size, size), BF16),
        pltpu.VMEM((2, 2, size, size), BF16),
        pltpu.SMEM((slots,), jnp.int32),
        pltpu.VMEM((2, size, size), F32),
        pltpu.VMEM((2, size, size), F32),
        pltpu.VMEM((2, 2, size, modes * size), BF16),
        pltpu.VMEM((2, 2, modes * size, size), BF16),
        pltpu.VMEM((2, modes * size, size), F32),
        pltpu.VMEM((2, 2, modes * size, size), BF16),
        pltpu.VMEM((2, 2, size, modes * size), BF16),
        pltpu.VMEM((2, modes * size, size), F32),
        pltpu.VMEM((modes, 2, size, size), F32),
        pltpu.VMEM((2, size + 16, size), F32),
        pltpu.SemaphoreType.DMA((5,)),
        pltpu.SemaphoreType.DMA((slots,)),
        pltpu.SemaphoreType.DMA((8,)),
    ]


SLOTS_COST = pl.CostEstimate(flops=12_000_000_000, bytes_accessed=16_000_000, transcendentals=0)


def visit_inside(meta, probe, amplitudes, tile, lower):
    size, modes, slots = probe.shape[2], probe.shape[0], amplitudes.shape[0]
    rows, cols = tile.shape[1:]
    tables = [jnp.asarray(item) for item in dft_tables(size)]
    vmem = pl.BlockSpec(memory_space=pltpu.VMEM)
    hbm = pl.BlockSpec(memory_space=pltpu.HBM)
    field = pltpu.VMEM((2, rows + size, cols + size), F32)

    def kernel(meta, probe, amplitudes, tile, lower, forward_h, backward_h, *refs):
        state, scratch = refs[:3], refs[3:]
        slots_kernel(
            False, meta, probe, amplitudes, [tile, lower], [forward_h, backward_h], None, state, None, *scratch
        )

    return pl.pallas_call(
        kernel,
        out_shape=[field, field, pltpu.VMEM((2 * modes + 1, size, size), F32)],
        in_specs=[pl.BlockSpec(memory_space=pltpu.SMEM), vmem, hbm, hbm, pl.BlockSpec(memory_space=pl.ANY), hbm, hbm],
        out_specs=[vmem] * 3,
        scratch_shapes=scratch_for(size, modes, slots),
        compiler_params=pltpu.CompilerParams(vmem_limit_bytes=28 * MIB),
        cost_estimate=SLOTS_COST,
        name="slots_inside",
    )(meta, probe, in_hbm(amplitudes), in_hbm(tile), lower, *map(in_hbm, tables))


def visit_beyond(meta, probe, amplitudes, rims, note, state):
    size, modes, slots = probe.shape[2], probe.shape[0], amplitudes.shape[0]
    rows, cols = (n - size for n in state[0].shape[1:])
    tables = [jnp.asarray(item) for item in dft_tables(size)]
    vmem = pl.BlockSpec(memory_space=pltpu.VMEM)
    hbm = pl.BlockSpec(memory_space=pltpu.HBM)
    anywhere = pl.BlockSpec(memory_space=pl.ANY)
    shapes = [
        (2, rows - size + 8, size),
        (2, size, size),
        (2, size + 8, size),
        (2, size + 8, cols),
        (2 * modes + 1, size // 2, size),
    ]

    def kernel(meta, probe, amplitudes, forward_h, backward_h, *refs):
        rims, note, refs = refs[:3], refs[3], refs[7:]
        state, outs, scratch = refs[:3], refs[3:9], refs[9:]
        slots_kernel(True, meta, probe, amplitudes, rims, [forward_h, backward_h], note, state, outs, *scratch)

    out = pl.pallas_call(
        kernel,
        out_shape=[pltpu.VMEM(item.shape, item.dtype) for item in state]
        + [pltpu.HBM((2, rows, cols), F32)]
        + [jax.ShapeDtypeStruct(shape, F32) for shape in shapes],
        in_specs=[pl.BlockSpec(memory_space=pltpu.SMEM), vmem] + [hbm] * 3 + [anywhere] * 4 + [vmem] * 3,
        out_specs=[vmem] * 3 + [hbm] + [anywhere] * 5,
        input_output_aliases={9 + i: i for i in range(3)},
        scratch_shapes=scratch_for(size, modes, slots),
        compiler_params=pltpu.CompilerParams(vmem_limit_bytes=28 * MIB),
        cost_estimate=SLOTS_COST,
        name="slots_beyond",
    )(meta, probe, *map(in_hbm, [amplitudes, *tables]), *rims, note, *state)
    return (*out[3:], out[2])


def finish_far_kernel(own, bottom, lower, scale, tile, out, own_s, right_s, lower_s, scale_s, tile_s, in_sems, out_sems):
    size = right_s.shape[2]
    block = 128
    blocks = own_s.shape[1] // block

    def copies(i):
        rows = pl.ds(i * block, block)
        pairs = [
            (own.at[:, rows], own_s.at[:, rows]),
            (scale.at[rows], scale_s.at[rows]),
            (tile.at[:, rows], tile_s.at[:, rows]),
        ]
        if i < size // block:
            pairs.append((lower.at[:, rows], lower_s.at[:, rows]))
        else:
            pairs.append((bottom.at[:, pl.ds(i * block - size, block)], right_s.at[:, pl.ds(i * block - size, block)]))
        return [pltpu.make_async_copy(a, b, in_sems.at[i, k]) for k, (a, b) in enumerate(pairs)]

    loads = [copies(i) for i in range(blocks)]
    for load in loads:
        for copy in load:
            copy.start()
    stores = []
    for i in range(blocks):
        for copy in loads[i]:
            copy.wait()
        rows = pl.ds(i * block, block)
        for at in range(i * block, (i + 1) * block, 32):
            part = pl.ds(at, 32)
            for c in range(2):
                near, far = own_s[c, part, :size], own_s[c, part, size:]
                if i < size // block:
                    near, far = near + lower_s[c, part, :size], far + lower_s[c, part, size:]
                else:
                    near = near + right_s[c, pl.ds(at - size, 32), :]
                own_s[c, part, :size] = tile_s[c, part, :size] + near * scale_s[part, :size]
                own_s[c, part, size:] = tile_s[c, part, size:] + far * scale_s[part, size:]
        stores.append(pltpu.make_async_copy(own_s.at[:, rows], out.at[:, rows], out_sems.at[i]))
        stores[-1].start()
    for store in stores:
        store.wait()


def finish_far(own, bottom, lower, inverse_light, tile):
    rows, cols = tile.shape[1:]
    size = bottom.shape[2]
    anywhere = pl.BlockSpec(memory_space=pl.ANY)
    hbm = pl.BlockSpec(memory_space=pltpu.HBM)
    return pl.pallas_call(
        finish_far_kernel,
        out_shape=pltpu.HBM(tile.shape, F32),
        in_specs=[hbm, anywhere, anywhere, anywhere, hbm],
        out_specs=hbm,
        scratch_shapes=[
            pltpu.VMEM(tile.shape, F32),
            pltpu.VMEM((2, rows - size, size), F32),
            pltpu.VMEM((2, size, cols), F32),
            pltpu.VMEM((rows, cols), F32),
            pltpu.VMEM(tile.shape, F32),
            pltpu.SemaphoreType.DMA((rows // 128, 4)),
            pltpu.SemaphoreType.DMA((rows // 128,)),
        ],
        compiler_params=pltpu.CompilerParams(vmem_limit_bytes=12 * MIB),
        cost_estimate=pl.CostEstimate(flops=2_000_000_000, bytes_accessed=4_000_000, transcendentals=0),
        name="finish_far",
    )(in_hbm(own), bottom, lower, inverse_light, in_hbm(tile))


def finish_near(before, top, inverse_light):
    size = top.shape[2]

    def kernel(before, top, scale, out, top_s, scale_s, out_s, sems, out_sems):
        corner = (pl.ds(0, size), pl.ds(0, size))
        loads = [
            pltpu.make_async_copy(before.at[(slice(None), *corner)], out_s, sems.at[0]),
            pltpu.make_async_copy(scale.at[corner], scale_s, sems.at[1]),
            pltpu.make_async_copy(top, top_s, sems.at[2]),
        ]
        for load in loads:
            load.start()
        for load in loads:
            load.wait()
        stores = []
        for c in range(2):
            out_s[c] += top_s[c] * scale_s[...]
            stores.append(pltpu.make_async_copy(out_s.at[c], out.at[(c, *corner)], out_sems.at[c]))
            stores[-1].start()
        for store in stores:
            store.wait()

    anywhere = pl.BlockSpec(memory_space=pl.ANY)
    hbm = pl.BlockSpec(memory_space=pltpu.HBM)
    return pl.pallas_call(
        kernel,
        out_shape=pltpu.HBM(before.shape, F32),
        in_specs=[hbm, anywhere, anywhere],
        out_specs=hbm,
        input_output_aliases={0: 0},
        scratch_shapes=[
            pltpu.VMEM((2, size, size), F32),
            pltpu.VMEM((size, size), F32),
            pltpu.VMEM((2, size, size), F32),
            pltpu.SemaphoreType.DMA((3,)),
            pltpu.SemaphoreType.DMA((2,)),
        ],
        compiler_params=pltpu.CompilerParams(vmem_limit_bytes=4 * MIB),
        cost_estimate=pl.CostEstimate(flops=2_000_000_000, bytes_accessed=4_000_000, transcendentals=0),
        name="finish_near",
    )(in_hbm(before), top, inverse_light)


def from_behind(array, axis, by):
    count = lax.axis_size(axis)
    pairs = [(i, i + by) for i in range(count) if 0 <= i + by < count]
    return lax.ppermute(array, axis, pairs)


def exchange(array, axis, bit):
    count = lax.axis_size(axis)
    return lax.ppermute(array, axis, [(i, i ^ bit) for i in range(count)])


def together(*arrays):
    return lax.optimization_barrier(arrays)


def cut(tile, regions, cost, name):
    def kernel(tile, *refs):
        sems = refs[-1]
        copies = [
            pltpu.make_async_copy(tile.at[:, pl.ds(at, height), pl.ds(0, width)], out, sems.at[i])
            for i, ((at, height, width), out) in enumerate(zip(regions, refs[:-1]))
        ]
        for copy in copies:
            copy.start()
        for copy in copies:
            copy.wait()

    return pl.pallas_call(
        kernel,
        out_shape=[jax.ShapeDtypeStruct((2, height, width), F32) for _, height, width in regions],
        in_specs=[pl.BlockSpec(memory_space=pltpu.HBM)],
        out_specs=[pl.BlockSpec(memory_space=pltpu.VMEM)] * len(regions),
        scratch_shapes=[pltpu.SemaphoreType.DMA((len(regions),))],
        compiler_params=pltpu.CompilerParams(vmem_limit_bytes=4 * MIB),
        cost_estimate=cost,
        name=name,
    )(in_hbm(tile))


def fold(places, index, mine, got, upper):
    count, half, width = got.shape
    quarter = half // 2

    def kernel(places, mine, got, send, keep):
        base = 0 if index is None else places[0, index] * half
        for k, out in ((1 - places[0, upper], send), (places[0, upper], keep)):
            for c in range(count):
                out[c] = (
                    mine[c, pl.ds(pl.multiple_of(base + k * quarter, quarter), quarter), :]
                    + got[c, pl.ds(pl.multiple_of(k * quarter, quarter), quarter), :]
                )

    vmem = pl.BlockSpec(memory_space=pltpu.VMEM)
    shape = jax.ShapeDtypeStruct((count, quarter, width), F32)
    return pl.pallas_call(
        kernel,
        out_shape=[shape, shape],
        in_specs=[pl.BlockSpec(memory_space=pltpu.SMEM), vmem, vmem],
        out_specs=[vmem, vmem],
        compiler_params=pltpu.CompilerParams(vmem_limit_bytes=6 * MIB),
        cost_estimate=SHORT,
        name="fold",
    )(places, mine, got)


def merge(top, corner):
    size = top.shape[1]

    def kernel(top, corner, out):
        for c in range(2):
            out[c] = top[c] + corner[c, :size, :]

    vmem = pl.BlockSpec(memory_space=pltpu.VMEM)
    return pl.pallas_call(
        kernel,
        out_shape=jax.ShapeDtypeStruct(top.shape, F32),
        in_specs=[vmem, vmem],
        out_specs=vmem,
        compiler_params=pltpu.CompilerParams(vmem_limit_bytes=4 * MIB),
        cost_estimate=SHORT,
        name="merge",
    )(top, corner)


def annotate(lower, bottom):
    size = bottom.shape[2]

    def kernel(lower, bottom, out, sem):
        source = bottom.at[0, pl.ds(bottom.shape[1] - 8, 8)]
        copy = pltpu.make_async_copy(source, out.at[0, pl.ds(out.shape[1] - 8, 8), pl.ds(0, size)], sem.at[0])
        copy.start()
        copy.wait()

    anywhere = pl.BlockSpec(memory_space=pl.ANY)
    return pl.pallas_call(
        kernel,
        out_shape=jax.ShapeDtypeStruct(lower.shape, F32),
        in_specs=[anywhere, anywhere],
        out_specs=anywhere,
        input_output_aliases={0: 0},
        scratch_shapes=[pltpu.SemaphoreType.DMA((1,))],
        compiler_params=pltpu.CompilerParams(vmem_limit_bytes=MIB),
        cost_estimate=SHORT,
        name="annotate",
    )(lower, bottom)


def deal(terms, parts, rows):
    count, _, width = terms[0].shape
    if rows % 8:
        return sum(terms).reshape(count, parts, rows, width).transpose(1, 0, 2, 3)

    def kernel(*refs):
        terms, out = refs[:-1], refs[-1]
        for j in range(parts):
            for c in range(count):
                out[j, c] = sum(term[c, j * rows : (j + 1) * rows, :] for term in terms)

    vmem = pl.BlockSpec(memory_space=pltpu.VMEM)
    return pl.pallas_call(
        kernel,
        out_shape=jax.ShapeDtypeStruct((parts, count, rows, width), F32),
        in_specs=[vmem] * len(terms),
        out_specs=vmem,
        compiler_params=pltpu.CompilerParams(vmem_limit_bytes=4 * MIB),
        cost_estimate=SHORT,
        name="deal",
    )(*terms)


def settle(places, start, probe, pieces):
    parts, count, rows, width = pieces.shape
    shape = (parts, count - 1, rows, width)
    if rows % 8:
        share = pieces.sum(axis=0)
        old = lax.dynamic_slice_in_dim(probe, places[0, start], rows, axis=1)
        return jnp.broadcast_to((old + share[:-1] / (share[-1:] + 1.0))[None], shape)

    def kernel(places, probe, pieces, out, old, sem):
        spot = pl.ds(pl.multiple_of(places[0, start], 8), rows)
        copy = pltpu.make_async_copy(probe.at[:, spot], old, sem.at[0])
        copy.start()
        share = sum(pieces[j] for j in range(parts))
        copy.wait()
        new = old[...] + share[:-1] / (share[-1:] + 1.0)
        for j in range(parts):
            out[j] = new

    vmem = pl.BlockSpec(memory_space=pltpu.VMEM)
    return pl.pallas_call(
        kernel,
        out_shape=jax.ShapeDtypeStruct(shape, F32),
        in_specs=[pl.BlockSpec(memory_space=pltpu.SMEM), pl.BlockSpec(memory_space=pltpu.HBM), vmem],
        out_specs=vmem,
        scratch_shapes=[pltpu.VMEM(shape[1:], F32), pltpu.SemaphoreType.DMA((1,))],
        compiler_params=pltpu.CompilerParams(vmem_limit_bytes=4 * MIB),
        cost_estimate=SHORT,
        name="settle",
    )(places, in_hbm(probe), pieces)


def collect(pieces):
    parts, count, rows, width = pieces.shape
    if rows % 8:
        return pieces.transpose(1, 0, 2, 3).reshape(count, parts * rows, width)

    def kernel(pieces, out):
        for j in range(parts):
            for c in range(count):
                out[c, j * rows : (j + 1) * rows, :] = pieces[j, c]

    vmem = pl.BlockSpec(memory_space=pltpu.VMEM)
    return pl.pallas_call(
        kernel,
        out_shape=jax.ShapeDtypeStruct((count, parts * rows, width), F32),
        in_specs=[vmem],
        out_specs=vmem,
        compiler_params=pltpu.CompilerParams(vmem_limit_bytes=4 * MIB),
        cost_estimate=pl.CostEstimate(flops=30_000_000_000, bytes_accessed=4_000_000, transcendentals=0),
        name="collect",
    )(pieces)


def join(places, upper, mine, other):
    half = mine.shape[1]

    def kernel(places, mine, other, out, sems):
        copies = [
            pltpu.make_async_copy(source, out.at[:, pl.ds(pl.multiple_of(at * half, half), half)], sems.at[i])
            for i, (source, at) in enumerate(((mine, places[0, upper]), (other, 1 - places[0, upper])))
        ]
        for copy in copies:
            copy.start()
        for copy in copies:
            copy.wait()

    anywhere = pl.BlockSpec(memory_space=pl.ANY)
    return pl.pallas_call(
        kernel,
        out_shape=jax.ShapeDtypeStruct((mine.shape[0], 2 * half) + mine.shape[2:], F32),
        in_specs=[pl.BlockSpec(memory_space=pltpu.SMEM), anywhere, anywhere],
        out_specs=anywhere,
        scratch_shapes=[pltpu.SemaphoreType.DMA((2,))],
        compiler_params=pltpu.CompilerParams(vmem_limit_bytes=MIB),
        cost_estimate=pl.CostEstimate(flops=0, bytes_accessed=2_000_000, transcendentals=0),
        name="join",
    )(places, mine, other)


def body(object_field, probe, amplitudes, positions, counts):
    modes, _, size, _ = probe.shape
    tile_rows, tile_cols = object_field.shape[1:]
    slots = amplitudes.shape[0]
    origin = jnp.stack([lax.axis_index("row") * tile_rows, lax.axis_index("col") * tile_cols]).astype(jnp.int32)
    bits = [1 << k for k in range(lax.axis_size("row").bit_length() - 1)]
    uppers = [(lax.axis_index("row") & bit) // bit for bit in bits]

    def relative(table):
        return jnp.concatenate([table[:, : 2 * slots] - jnp.tile(origin, slots)[None], table[:, 2 * slots :]], axis=1)

    right_up, right_down = cut(
        object_field, ((0, size, size), (size, tile_rows - size, size)), SHORT, "cut_right"
    )
    right_up, right_down, after_right = together(right_up, right_down, object_field)
    right_up = from_behind(right_up, "col", -1)
    right_down = from_behind(right_down, "col", -1)
    (lower,) = cut(after_right, ((0, size, tile_cols),), LONG, "cut_lower")
    meta = jnp.concatenate([positions.reshape(1, 2 * slots), counts.reshape(1, 1)], axis=1)
    lower = from_behind(lower, "row", -1)

    parts = lax.axis_size("col")
    rows = (size >> len(bits)) // parts
    me = lax.axis_index("col")
    start = sum(upper * (size >> (k + 1)) for k, upper in enumerate(uppers)) + me * rows
    bit_at = 2 * slots + 2
    me_at = bit_at + len(bits)
    start_at, origin_at = me_at + 1, me_at + 2
    extra = [1 - uppers[0], *uppers, me, start, origin[0], origin[1]]
    mine = jnp.concatenate([relative(meta), jnp.stack([item.astype(jnp.int32) for item in extra])[None]], axis=1)
    note = jnp.pad(meta.astype(F32), ((0, 7), (0, size - meta.shape[1])))
    mine, note = together(mine, note)
    amplitudes = arrange(mine, amplitudes)
    right_up, amplitudes = together(right_up, amplitudes)
    corner = from_behind(right_up, "row", -1)
    amplitudes, lower = together(amplitudes, lower)
    state = visit_inside(mine, probe, amplitudes, object_field, lower)
    right_up, right_down, corner, *state = together(right_up, right_down, corner, *state)
    own, bottom_spill, top_spill, corner_spill, lower_spill, send, share = visit_beyond(
        mine, probe, amplitudes, [right_up, right_down, corner], note, state
    )

    index = bit_at
    for k, bit in enumerate(bits):
        got = exchange(send, "row", bit)
        if k == 0:
            bottom_spill = from_behind(bottom_spill, "col", 1)
        if k + 1 < len(bits):
            send, share = fold(mine, index, share, got, bit_at + k + 1)
            index = None
    got, bottom_spill, lower_spill = together(got, bottom_spill, lower_spill)
    lower_spill = from_behind(annotate(lower_spill, bottom_spill), "row", 1)
    pieces = lax.all_to_all(deal([share, got], parts, rows), "col", 0, 0, tiled=True)
    new = settle(mine, start_at, probe.reshape(2 * modes, size, size), pieces)
    new, lower_spill, corner_spill = together(new, lower_spill, corner_spill)
    corner_spill = from_behind(corner_spill, "row", 1)
    inverse_light = light(
        mine, slots, origin_at, probe, bottom_spill, corner_spill, lower_spill, (tile_rows, tile_cols)
    )
    new = lax.all_to_all(new, "col", 0, 0, tiled=True)
    new, corner_spill = together(new, corner_spill)
    top_spill, new = together(merge(top_spill, corner_spill), new)
    top_spill = from_behind(top_spill, "col", 1)
    new = collect(new)
    for k, bit in reversed(list(enumerate(bits))):
        if k == 0:
            new, own = together(new, own)
            new_object = finish_far(own, bottom_spill, lower_spill, inverse_light, object_field)
        other = exchange(new, "row", bit)
        if k + 1 == len(bits):
            other, inverse_light = together(other, inverse_light)
        if k == 0:
            new_object, top_spill = together(new_object, top_spill)
            new_object = finish_near(new_object, top_spill, inverse_light)
            other, new_object = together(other, new_object)
        new = join(mine, bit_at + k, new, other)
    return (new_object, new.reshape(modes, 2, size, size))


def solution(mesh):
    in_specs = (
        P(None, "row", "col"),
        P(),
        P(("row", "col"), None, None),
        P(("row", "col"), None),
        P(("row", "col")),
    )
    out_specs = (P(None, "row", "col"), P())
    return jax.shard_map(body, mesh=mesh, in_specs=in_specs, out_specs=out_specs, check_vma=False)
```

```python
import functools
import math

import jax
import jax.numpy as jnp
import ml_dtypes
import numpy as np
from jax import lax
from jax.experimental import pallas as pl
from jax.experimental.pallas import tpu as pltpu
from jax.sharding import PartitionSpec as P

F32 = jnp.float32
BF16 = jnp.bfloat16
MIB = 1024 * 1024
LONG = pl.CostEstimate(flops=30_000_000_000, bytes_accessed=4_000_000, transcendentals=0)
SHORT = pl.CostEstimate(flops=0, bytes_accessed=1_000_000, transcendentals=0)
FLOOR = 0.3


def split_np(table):
    high = table.astype(ml_dtypes.bfloat16)
    low = (table - high.astype(np.float64)).astype(ml_dtypes.bfloat16)
    return high, low


def dft_tables(length):
    half = length // 2
    q = np.arange(half)[:, None]
    n = np.arange(half)[None, :]
    forward = []
    for odd in range(2):
        phase = (n * (2 * q + odd)) % length
        angle = phase * (-2.0 * math.pi / length)
        re = np.cos(angle) / math.sqrt(length)
        im = np.sin(angle) / math.sqrt(length)
        forward.append(np.stack(split_np(np.block([[re, -im], [im, re]]))))
    forward = np.stack(forward)
    return forward, np.ascontiguousarray(forward.transpose(0, 1, 3, 2))


def in_hbm(array):
    return pltpu.with_memory_space_constraint(array, pltpu.HBM)


def dot(a, b):
    return jnp.dot(a, b, preferred_element_type=F32)


def split(x):
    high = x.astype(BF16)
    return high, (x - high.astype(F32)).astype(BF16)


def roll_rows(x, shift):
    return pltpu.roll(x.reshape(x.shape[0] // 8, 8, x.shape[1]), shift, 1)


def roll_rows(x, shift):
    return pltpu.roll(x.reshape(x.shape[0] // 8, 8, x.shape[1]), shift, 1)


def roll_rows(x, shift):
    return pltpu.roll(x.reshape(x.shape[0] // 8, 8, x.shape[1]), shift, 1)


def roll_rows(x, shift):
    return pltpu.roll(x.reshape(x.shape[0] // 8, 8, x.shape[1]), shift, 1)


def split_three(x):
    high = x.astype(BF16)
    rest = x - high.astype(F32)
    middle = rest.astype(BF16)
    return high, middle, (rest - middle.astype(F32)).astype(BF16)


def add_shifted(template, grid, where_t, where_g, top, left, size):
    top_s = top & 7
    top_b = pl.multiple_of(top - top_s, 8)
    left_s = left & 127
    left_b = pl.multiple_of(left - left_s, 128)
    step = 24
    wrapped = lax.broadcasted_iota(jnp.int32, (step, 128), 1) < left_s
    wrapped_rows = lax.broadcasted_iota(jnp.int32, (step // 8, 8, 128), 1) < top_s
    zero = jnp.zeros((step, 128), F32)
    blocks = size // 128
    for at in range(0, size + 8, step):
        parts = []
        for j in range(blocks):
            x = roll_rows(template[where_t + (pl.ds(at, step + 8), pl.ds(128 * j, 128))], top_s)
            x = jnp.where(wrapped_rows, x[:-1], x[1:]).reshape(step, 128)
            parts.append(pltpu.roll(x, left_s, 1))
        for j in range(blocks + 1):
            before = parts[j - 1] if j > 0 else zero
            after = parts[j] if j < blocks else zero
            spot = where_g + (pl.ds(top_b + at, step), pl.ds(left_b + 128 * j, 128))
            grid[spot] += jnp.where(wrapped, before, after)


def take_shifted(field, where, top, left, at, step, size):
    top_s = top & 7
    top_b = pl.multiple_of(top - top_s, 8)
    left_s = left & 127
    left_b = pl.multiple_of(left - left_s, 128)
    back = (128 - left_s) & 127
    keep = lax.broadcasted_iota(jnp.int32, (step + 8, 128), 1) < 128 - left_s
    keep_rows = lax.broadcasted_iota(jnp.int32, (step // 8, 8, 128), 1) < 8 - top_s
    blocks = size // 128
    parts = [
        pltpu.roll(field[where + (pl.ds(top_b + at, step + 8), pl.ds(left_b + 128 * j, 128))], back, 1)
        for j in range(blocks + 1)
    ]
    pieces = []
    for j in range(blocks):
        x = roll_rows(jnp.where(keep, parts[j], parts[j + 1]), (8 - top_s) & 7)
        pieces.append(jnp.where(keep_rows, x[:-1], x[1:]).reshape(step, 128))
    return jnp.concatenate(pieces, axis=1)


def light_kernel(slots, origin, meta, probe_h, bottom, corner, lower, inverse_light, probe, template, grid, notes, sems):
    size = probe.shape[2]
    tile_rows, tile_cols = inverse_light.shape
    copies = [
        pltpu.make_async_copy(spill.at[0, pl.ds(spill.shape[1] - 8, 8), pl.ds(0, 128)], notes.at[i], sems.at[i])
        for i, spill in enumerate((bottom, corner, lower))
    ]
    copy = pltpu.make_async_copy(probe_h, probe, sems.at[3])
    copy.start()
    for item in copies:
        item.start()
    template[0:8, :] = jnp.zeros((8, size), F32)
    template[8 + size :, :] = jnp.zeros((8, size), F32)
    copy.wait()
    for at in range(0, size, 32):
        rows = pl.ds(at, 32)
        total = jnp.zeros((32, size), F32)
        for m in range(probe.shape[0]):
            total += probe[m, 0, rows] * probe[m, 0, rows] + probe[m, 1, rows] * probe[m, 1, rows]
        template[pl.ds(8 + at, 32), :] = total

    @pl.loop(0, tile_rows // 32)
    def _(step):
        rows = pl.ds(pl.multiple_of(size + step * 32, 32), 32)
        grid[rows, size : size + tile_cols] = jnp.zeros((32, tile_cols), F32)

    def add(top, left):
        @pl.when((top > 0) & (left > 0))
        def _():
            add_shifted(template, grid, (), (), top, left, size)

    @pl.loop(0, meta[0, 2 * slots])
    def _(slot):
        add(meta[0, 2 * slot] + size, meta[0, 2 * slot + 1] + size)

    for item in copies:
        item.wait()
    for device in range(3):

        @pl.loop(0, notes[device, 0, 2 * slots].astype(jnp.int32))
        def _(slot):
            top = notes[device, 0, 2 * slot].astype(jnp.int32) - meta[0, origin]
            left = notes[device, 0, 2 * slot + 1].astype(jnp.int32) - meta[0, origin + 1]
            add(top + size, left + size)

    @pl.loop(0, tile_rows // 32)
    def _(step):
        rows = pl.ds(pl.multiple_of(size + step * 32, 32), 32)
        out_rows = pl.ds(pl.multiple_of(step * 32, 32), 32)
        inverse_light[out_rows, :] = 1.0 / (grid[rows, size : size + tile_cols] + 1.0)


def light(meta, slots, origin, probe, bottom, corner, lower, tile_shape):
    size = probe.shape[2]
    hbm = pl.BlockSpec(memory_space=pltpu.HBM)
    anywhere = pl.BlockSpec(memory_space=pl.ANY)
    return pl.pallas_call(
        functools.partial(light_kernel, slots, origin),
        out_shape=jax.ShapeDtypeStruct(tile_shape, F32),
        in_specs=[pl.BlockSpec(memory_space=pltpu.SMEM), hbm] + [anywhere] * 3,
        out_specs=pl.BlockSpec(memory_space=pltpu.VMEM),
        scratch_shapes=[
            pltpu.VMEM(probe.shape, F32),
            pltpu.VMEM((size + 16, size), F32),
            pltpu.VMEM((tile_shape[0] + 2 * size, tile_shape[1] + 2 * size), F32),
            pltpu.SMEM((3, 8, 128), F32),
            pltpu.SemaphoreType.DMA((4,)),
        ],
        compiler_params=pltpu.CompilerParams(vmem_limit_bytes=8 * MIB),
        cost_estimate=pl.CostEstimate(flops=4_000_000_000, bytes_accessed=4_000_000, transcendentals=0),
        name="light",
    )(meta, in_hbm(probe), bottom, corner, lower)


def arrange_kernel(meta, amplitudes, out, given, moved, in_sems, out_sems):
    slots, size, _ = amplitudes.shape
    count = meta[0, 2 * slots]

    def load(slot):
        return pltpu.make_async_copy(amplitudes.at[slot], given.at[slot], in_sems.at[slot])

    def store(slot):
        return pltpu.make_async_copy(moved.at[slot], out.at[slot], out_sems.at[slot])

    @pl.loop(0, count)
    def _(slot):
        load(slot).start()

    first = lax.broadcasted_iota(jnp.int32, (size, size), 0)
    second = lax.broadcasted_iota(jnp.int32, (size, size), 1)
    half = size // 2

    def source(index):
        return jnp.where(index < half, 2 * index, 2 * index - (size - 1))

    rows = (source(first) == second).astype(F32).astype(BF16)
    cols = (source(second) == first).astype(F32).astype(BF16)
    rows = jnp.concatenate([rows, rows], axis=1)
    cols = jnp.concatenate([cols, cols], axis=0)

    def each(pair, act):
        act(2 * pair)

        @pl.when(2 * pair + 1 < count)
        def _():
            act(2 * pair + 1)

    @pl.loop(0, (count + 1) // 2)
    def _(pair):
        each(pair, lambda slot: load(slot).wait())
        x = [dot(rows, jnp.concatenate(split(given[2 * pair + k]), axis=0)) for k in range(2)]
        for k in range(2):
            moved[2 * pair + k] = dot(jnp.concatenate(split(x[k]), axis=1), cols)
        each(pair, lambda slot: store(slot).start())

    @pl.loop(0, count)
    def _(slot):
        store(slot).wait()


def arrange(meta, amplitudes):
    slots = amplitudes.shape[0]
    hbm = pl.BlockSpec(memory_space=pltpu.HBM)
    return pl.pallas_call(
        arrange_kernel,
        out_shape=pltpu.HBM(amplitudes.shape, F32),
        in_specs=[pl.BlockSpec(memory_space=pltpu.SMEM), hbm],
        out_specs=hbm,
        scratch_shapes=[
            pltpu.VMEM(amplitudes.shape, F32),
            pltpu.VMEM(amplitudes.shape, F32),
            pltpu.SemaphoreType.DMA((slots,)),
            pltpu.SemaphoreType.DMA((slots,)),
        ],
        compiler_params=pltpu.CompilerParams(vmem_limit_bytes=8 * MIB),
        cost_estimate=LONG,
        name="arrange",
    )(meta, in_hbm(amplitudes))


def three_left(table, t):
    return jnp.concatenate([table[t, 0], table[t, 0], table[t, 1]], axis=1)


def three_right(table, v):
    return jnp.concatenate([table[v, 0], table[v, 0], table[v, 1]], axis=0)


def weave(first, second):
    total = max(len(first), len(second))
    done = [0, 0]
    for i in range(1, total + 1):
        for k, pieces in enumerate((first, second)):
            while done[k] * total < i * len(pieces):
                pieces[done[k]]()
                done[k] += 1


def slots_kernel(
    needs_rim, meta, probe, amplitudes, sources, tables, note, state, outs,
    amp, forward_t, backward_t, chosen, patch_f, patch_b, x_f, y_f, z_f, g_s, x_b, z_b, back, template,
    load_sems, amp_sems, out_sems,
):
    ext, grid, probe_out = state
    size = probe.shape[2]
    half = size // 2
    modes = probe.shape[0]
    slots = amplitudes.shape[0]
    tile_rows, tile_cols = (n - size for n in ext.shape[1:])
    step = 32
    fine = 16

    body_rows, rim_rows = pl.ds(0, tile_rows), pl.ds(tile_rows, size)
    body_cols, rim_cols = pl.ds(0, tile_cols), pl.ds(tile_cols, size)
    if needs_rim:
        places = [
            ext.at[:, pl.ds(0, size), rim_cols],
            ext.at[:, pl.ds(size, tile_rows - size), rim_cols],
            ext.at[:, rim_rows, rim_cols],
        ]
    else:
        places = [ext.at[:, body_rows, body_cols], ext.at[:, rim_rows, body_cols]]
    places += [forward_t, backward_t]
    loads = [
        pltpu.make_async_copy(source, place, load_sems.at[i])
        for i, (source, place) in enumerate(zip([*sources, *tables], places))
    ]
    for load in loads:
        load.start()

    def amp_copy(slot):
        return pltpu.make_async_copy(amplitudes.at[slot], amp.at[slot], amp_sems.at[slot])

    def choose(slot, found):
        beyond = meta[0, 2 * slot + 1] + size > tile_cols
        wanted = beyond if needs_rim else jnp.logical_not(beyond)

        @pl.when(wanted)
        def _():
            chosen[found] = slot
            amp_copy(slot).start()

        return found + wanted.astype(jnp.int32)

    count = lax.fori_loop(0, meta[0, 2 * slots], choose, jnp.zeros((), jnp.int32))

    if not needs_rim:

        @pl.loop(0, (tile_rows + size) // step)
        def _(at):
            rows = pl.ds(pl.multiple_of(at * step, step), step)
            for c in range(2):
                grid[c, rows, :] = jnp.zeros((step, tile_cols + size), F32)

        @pl.loop(0, size // step)
        def _(at):
            rows = pl.ds(pl.multiple_of(at * step, step), step)
            for c in range(2 * modes + 1):
                probe_out[c, rows, :] = jnp.zeros((step, size), F32)

    for c in range(2):
        template[c, 0:8, :] = jnp.zeros((8, size), F32)
        template[c, 8 + size :, :] = jnp.zeros((8, size), F32)
    for load in loads:
        load.wait()

    def corner(slot):
        return meta[0, 2 * slot], meta[0, 2 * slot + 1]

    def forward(slot):
        top, left = corner(slot)

        def take(at):
            for c in range(2):
                patch_f[c, pl.ds(at, step), :] = take_shifted(ext, (c,), top, left, at, step, size)

        def fold_rows(m, at):
            cols = pl.ds(m * size, size)
            parts = []
            for base in (at, half + at):
                rows = pl.ds(base, fine)
                pr, pi = patch_f[0, rows, :], patch_f[1, rows, :]
                qr, qi = probe[m, 0, rows, :], probe[m, 1, rows, :]
                parts.append((qr * pr - qi * pi, qr * pi + qi * pr))
            for c in range(2):
                rows = pl.ds(c * half + at, fine)
                for t, value in enumerate((parts[0][c] + parts[1][c], parts[0][c] - parts[1][c])):
                    x_f[t, 0, rows, cols], x_f[t, 1, rows, cols] = split(value)

        def dft_rows(t):
            high = x_f[t, 0]
            both = dot(three_left(forward_t, t), jnp.concatenate([high, x_f[t, 1], high], axis=0))
            for m in range(modes):
                left, right = both[:, m * size : m * size + half], both[:, m * size + half : (m + 1) * size]
                rows = pl.ds(m * size + t * half, half)
                for v, value in enumerate((left + right, left - right)):
                    high, low = split(value)
                    for c in range(2):
                        lanes = pl.ds(c * half, half)
                        y_f[v, 0, rows, lanes] = high[c * half : (c + 1) * half]
                        y_f[v, 1, rows, lanes] = low[c * half : (c + 1) * half]

        def dft_cols(v):
            high = y_f[v, 0]
            z_f[v] = dot(jnp.concatenate([high, y_f[v, 1], high], axis=1), three_right(backward_t, v))

        def scale(v, at):
            if v == 0 and at == 0:
                amp_copy(slot).wait()
            waves = [z_f[v, pl.ds(m * size + at, fine), :] for m in range(modes)]
            total = jnp.zeros((fine, half), F32)
            for wave in waves:
                total += wave[:, :half] * wave[:, :half] + wave[:, half:] * wave[:, half:]
            measured = amp[slot, pl.ds(at, fine), pl.ds(v * half, half)]
            factor = measured * lax.rsqrt(jnp.maximum(total, FLOOR * FLOOR)) - 1.0
            factor = jnp.concatenate([factor, factor], axis=1)
            for m in range(modes):
                rows = pl.ds(m * size + at, fine)
                g_s[v, 0, rows, :], g_s[v, 1, rows, :] = split(waves[m] * factor)

        pieces = [(take, at) for at in range(0, size, step)]
        for m in range(modes):
            pieces += [(fold_rows, m, at) for at in range(0, half, fine)]
        pieces += [(dft_rows, t) for t in range(2)]
        pieces += [(dft_cols, v) for v in range(2)]
        pieces += [(scale, v, at) for v in range(2) for at in range(0, size, fine)]
        return [functools.partial(*piece) for piece in pieces]

    def backward(slot):
        top, left = corner(slot)

        def dft_cols(v):
            high = g_s[v, 0]
            z_b[v] = dot(jnp.concatenate([high, g_s[v, 1], high], axis=1), three_right(forward_t, v))

        def unfold_cols(m, t, at):
            rows = pl.ds(m * size + t * half + at, step)
            even, odd = z_b[0, rows, :], z_b[1, rows, :]
            for v, value in enumerate((even + odd, even - odd)):
                high, low = split(value)
                cols = pl.ds(m * size + v * half, half)
                for c in range(2):
                    spot = pl.ds(c * half + at, step)
                    x_b[t, 0, spot, cols] = high[:, c * half : (c + 1) * half]
                    x_b[t, 1, spot, cols] = low[:, c * half : (c + 1) * half]

        def dft_rows(t):
            high = x_b[t, 0]
            both = dot(three_left(backward_t, t), jnp.concatenate([high, x_b[t, 1], high], axis=0))
            for m in range(modes):
                back[m, t] = both[:, m * size : (m + 1) * size]

        def gradients(at):
            waves = []
            for m in range(modes):
                pair = []
                for c in range(2):
                    rows = pl.ds(c * half + at, fine)
                    even, odd = back[m, 0, rows, :], back[m, 1, rows, :]
                    pair.append((even + odd, even - odd))
                waves.append(pair)
            for h in range(2):
                rows = pl.ds(h * half + at, fine)
                pr, pi = patch_b[0, rows, :], patch_b[1, rows, :]
                grad_r = jnp.zeros((fine, size), F32)
                grad_i = jnp.zeros((fine, size), F32)
                for m in range(modes):
                    br, bi = waves[m][0][h], waves[m][1][h]
                    qr, qi = probe[m, 0, rows, :], probe[m, 1, rows, :]
                    grad_r += qr * br + qi * bi
                    grad_i += qr * bi - qi * br
                    probe_out[2 * m, rows, :] += pr * br + pi * bi
                    probe_out[2 * m + 1, rows, :] += pr * bi - pi * br
                probe_out[2 * modes, rows, :] += pr * pr + pi * pi
                spot = pl.ds(8 + h * half + at, fine)
                template[0, spot, :] = grad_r
                template[1, spot, :] = grad_i

        def add(c):
            add_shifted(template, grid, (c,), (c,), top, left, size)

        pieces = [(dft_cols, v) for v in range(2)]
        for m in range(modes):
            pieces += [(unfold_cols, m, t, at) for t in range(2) for at in range(0, half, step)]
        pieces += [(dft_rows, t) for t in range(2)]
        pieces += [(gradients, at) for at in range(0, half, fine)]
        pieces += [(add, c) for c in range(2)]
        return [functools.partial(*piece) for piece in pieces]

    def hand_over():
        for at in range(0, size, step):
            for c in range(2):
                patch_b[c, pl.ds(at, step), :] = patch_f[c, pl.ds(at, step), :]

    @pl.when(count > 0)
    def _():
        weave(forward(chosen[0]), [])
        hand_over()

        def visit(index, _):
            weave(backward(chosen[index]), forward(chosen[index + 1]))
            hand_over()
            return 0

        lax.fori_loop(0, count - 1, visit, 0)
        weave(backward(chosen[count - 1]), [])

    if needs_rim:
        top, bottom = pl.ds(0, size), pl.ds(size, tile_rows - size)
        parts = [
            (grid.at[:, body_rows, body_cols], outs[0]),
            (grid.at[:, bottom, rim_cols], outs[1].at[:, pl.ds(0, tile_rows - size)]),
            (note, outs[1].at[0, pl.ds(tile_rows - size, 8)]),
            (grid.at[:, top, rim_cols], outs[2]),
            (grid.at[:, rim_rows, rim_cols], outs[3].at[:, top]),
            (note, outs[3].at[0, pl.ds(size, 8)]),
            (grid.at[:, rim_rows, body_cols], outs[4].at[:, top]),
            (probe_out.at[:, pl.ds(pl.multiple_of(meta[0, 2 * slots + 1] * half, half), half)], outs[5]),
        ]
        stores = [pltpu.make_async_copy(part, out, out_sems.at[i]) for i, (part, out) in enumerate(parts)]
        for store in stores:
            store.start()
        for store in stores:
            store.wait()


def scratch_for(size, modes, slots):
    return [
        pltpu.VMEM((slots, size, size), F32),
        pltpu.VMEM((2, 2, size, size), BF16),
        pltpu.VMEM((2, 2, size, size), BF16),
        pltpu.SMEM((slots,), jnp.int32),
        pltpu.VMEM((2, size, size), F32),
        pltpu.VMEM((2, size, size), F32),
        pltpu.VMEM((2, 2, size, modes * size), BF16),
        pltpu.VMEM((2, 2, modes * size, size), BF16),
        pltpu.VMEM((2, modes * size, size), F32),
        pltpu.VMEM((2, 2, modes * size, size), BF16),
        pltpu.VMEM((2, 2, size, modes * size), BF16),
        pltpu.VMEM((2, modes * size, size), F32),
        pltpu.VMEM((modes, 2, size, size), F32),
        pltpu.VMEM((2, size + 16, size), F32),
        pltpu.SemaphoreType.DMA((5,)),
        pltpu.SemaphoreType.DMA((slots,)),
        pltpu.SemaphoreType.DMA((8,)),
    ]


SLOTS_COST = pl.CostEstimate(flops=12_000_000_000, bytes_accessed=16_000_000, transcendentals=0)


def visit_inside(meta, probe, amplitudes, tile, lower):
    size, modes, slots = probe.shape[2], probe.shape[0], amplitudes.shape[0]
    rows, cols = tile.shape[1:]
    tables = [jnp.asarray(item) for item in dft_tables(size)]
    vmem = pl.BlockSpec(memory_space=pltpu.VMEM)
    hbm = pl.BlockSpec(memory_space=pltpu.HBM)
    field = pltpu.VMEM((2, rows + size, cols + size), F32)

    def kernel(meta, probe, amplitudes, tile, lower, forward_h, backward_h, *refs):
        state, scratch = refs[:3], refs[3:]
        slots_kernel(
            False, meta, probe, amplitudes, [tile, lower], [forward_h, backward_h], None, state, None, *scratch
        )

    return pl.pallas_call(
        kernel,
        out_shape=[field, field, pltpu.VMEM((2 * modes + 1, size, size), F32)],
        in_specs=[pl.BlockSpec(memory_space=pltpu.SMEM), vmem, hbm, hbm, pl.BlockSpec(memory_space=pl.ANY), hbm, hbm],
        out_specs=[vmem] * 3,
        scratch_shapes=scratch_for(size, modes, slots),
        compiler_params=pltpu.CompilerParams(vmem_limit_bytes=28 * MIB),
        cost_estimate=SLOTS_COST,
        name="slots_inside",
    )(meta, probe, in_hbm(amplitudes), in_hbm(tile), lower, *map(in_hbm, tables))


def visit_beyond(meta, probe, amplitudes, rims, note, state):
    size, modes, slots = probe.shape[2], probe.shape[0], amplitudes.shape[0]
    rows, cols = (n - size for n in state[0].shape[1:])
    tables = [jnp.asarray(item) for item in dft_tables(size)]
    vmem = pl.BlockSpec(memory_space=pltpu.VMEM)
    hbm = pl.BlockSpec(memory_space=pltpu.HBM)
    anywhere = pl.BlockSpec(memory_space=pl.ANY)
    shapes = [
        (2, rows - size + 8, size),
        (2, size, size),
        (2, size + 8, size),
        (2, size + 8, cols),
        (2 * modes + 1, size // 2, size),
    ]

    def kernel(meta, probe, amplitudes, forward_h, backward_h, *refs):
        rims, note, refs = refs[:3], refs[3], refs[7:]
        state, outs, scratch = refs[:3], refs[3:9], refs[9:]
        slots_kernel(True, meta, probe, amplitudes, rims, [forward_h, backward_h], note, state, outs, *scratch)

    out = pl.pallas_call(
        kernel,
        out_shape=[pltpu.VMEM(item.shape, item.dtype) for item in state]
        + [pltpu.HBM((2, rows, cols), F32)]
        + [jax.ShapeDtypeStruct(shape, F32) for shape in shapes],
        in_specs=[pl.BlockSpec(memory_space=pltpu.SMEM), vmem] + [hbm] * 3 + [anywhere] * 4 + [vmem] * 3,
        out_specs=[vmem] * 3 + [hbm] + [anywhere] * 5,
        input_output_aliases={9 + i: i for i in range(3)},
        scratch_shapes=scratch_for(size, modes, slots),
        compiler_params=pltpu.CompilerParams(vmem_limit_bytes=28 * MIB),
        cost_estimate=SLOTS_COST,
        name="slots_beyond",
    )(meta, probe, *map(in_hbm, [amplitudes, *tables]), *rims, note, *state)
    return (*out[3:], out[2])


def finish_far_kernel(own, bottom, lower, scale, tile, out, own_s, right_s, lower_s, scale_s, tile_s, in_sems, out_sems):
    size = right_s.shape[2]
    block = 128
    blocks = own_s.shape[1] // block

    def copies(i):
        rows = pl.ds(i * block, block)
        pairs = [
            (own.at[:, rows], own_s.at[:, rows]),
            (scale.at[rows], scale_s.at[rows]),
            (tile.at[:, rows], tile_s.at[:, rows]),
        ]
        if i < size // block:
            pairs.append((lower.at[:, rows], lower_s.at[:, rows]))
        else:
            pairs.append((bottom.at[:, pl.ds(i * block - size, block)], right_s.at[:, pl.ds(i * block - size, block)]))
        return [pltpu.make_async_copy(a, b, in_sems.at[i, k]) for k, (a, b) in enumerate(pairs)]

    loads = [copies(i) for i in range(blocks)]
    for load in loads:
        for copy in load:
            copy.start()
    stores = []
    for i in range(blocks):
        for copy in loads[i]:
            copy.wait()
        rows = pl.ds(i * block, block)
        for at in range(i * block, (i + 1) * block, 32):
            part = pl.ds(at, 32)
            for c in range(2):
                near, far = own_s[c, part, :size], own_s[c, part, size:]
                if i < size // block:
                    near, far = near + lower_s[c, part, :size], far + lower_s[c, part, size:]
                else:
                    near = near + right_s[c, pl.ds(at - size, 32), :]
                own_s[c, part, :size] = tile_s[c, part, :size] + near * scale_s[part, :size]
                own_s[c, part, size:] = tile_s[c, part, size:] + far * scale_s[part, size:]
        stores.append(pltpu.make_async_copy(own_s.at[:, rows], out.at[:, rows], out_sems.at[i]))
        stores[-1].start()
    for store in stores:
        store.wait()


def finish_far(own, bottom, lower, inverse_light, tile):
    rows, cols = tile.shape[1:]
    size = bottom.shape[2]
    anywhere = pl.BlockSpec(memory_space=pl.ANY)
    hbm = pl.BlockSpec(memory_space=pltpu.HBM)
    return pl.pallas_call(
        finish_far_kernel,
        out_shape=pltpu.HBM(tile.shape, F32),
        in_specs=[hbm, anywhere, anywhere, anywhere, hbm],
        out_specs=hbm,
        scratch_shapes=[
            pltpu.VMEM(tile.shape, F32),
            pltpu.VMEM((2, rows - size, size), F32),
            pltpu.VMEM((2, size, cols), F32),
            pltpu.VMEM((rows, cols), F32),
            pltpu.VMEM(tile.shape, F32),
            pltpu.SemaphoreType.DMA((rows // 128, 4)),
            pltpu.SemaphoreType.DMA((rows // 128,)),
        ],
        compiler_params=pltpu.CompilerParams(vmem_limit_bytes=12 * MIB),
        cost_estimate=pl.CostEstimate(flops=2_000_000_000, bytes_accessed=4_000_000, transcendentals=0),
        name="finish_far",
    )(in_hbm(own), bottom, lower, inverse_light, in_hbm(tile))


def finish_near(before, top, inverse_light):
    size = top.shape[2]

    def kernel(before, top, scale, out, top_s, scale_s, out_s, sems, out_sems):
        corner = (pl.ds(0, size), pl.ds(0, size))
        loads = [
            pltpu.make_async_copy(before.at[(slice(None), *corner)], out_s, sems.at[0]),
            pltpu.make_async_copy(scale.at[corner], scale_s, sems.at[1]),
            pltpu.make_async_copy(top, top_s, sems.at[2]),
        ]
        for load in loads:
            load.start()
        for load in loads:
            load.wait()
        stores = []
        for c in range(2):
            out_s[c] += top_s[c] * scale_s[...]
            stores.append(pltpu.make_async_copy(out_s.at[c], out.at[(c, *corner)], out_sems.at[c]))
            stores[-1].start()
        for store in stores:
            store.wait()

    anywhere = pl.BlockSpec(memory_space=pl.ANY)
    hbm = pl.BlockSpec(memory_space=pltpu.HBM)
    return pl.pallas_call(
        kernel,
        out_shape=pltpu.HBM(before.shape, F32),
        in_specs=[hbm, anywhere, anywhere],
        out_specs=hbm,
        input_output_aliases={0: 0},
        scratch_shapes=[
            pltpu.VMEM((2, size, size), F32),
            pltpu.VMEM((size, size), F32),
            pltpu.VMEM((2, size, size), F32),
            pltpu.SemaphoreType.DMA((3,)),
            pltpu.SemaphoreType.DMA((2,)),
        ],
        compiler_params=pltpu.CompilerParams(vmem_limit_bytes=4 * MIB),
        cost_estimate=pl.CostEstimate(flops=2_000_000_000, bytes_accessed=4_000_000, transcendentals=0),
        name="finish_near",
    )(in_hbm(before), top, inverse_light)


def from_behind(array, axis, by):
    count = lax.axis_size(axis)
    pairs = [(i, i + by) for i in range(count) if 0 <= i + by < count]
    return lax.ppermute(array, axis, pairs)


def exchange(array, axis, bit):
    count = lax.axis_size(axis)
    return lax.ppermute(array, axis, [(i, i ^ bit) for i in range(count)])


def together(*arrays):
    return lax.optimization_barrier(arrays)


def cut(tile, regions, cost, name):
    def kernel(tile, *refs):
        sems = refs[-1]
        copies = [
            pltpu.make_async_copy(tile.at[:, pl.ds(at, height), pl.ds(0, width)], out, sems.at[i])
            for i, ((at, height, width), out) in enumerate(zip(regions, refs[:-1]))
        ]
        for copy in copies:
            copy.start()
        for copy in copies:
            copy.wait()

    return pl.pallas_call(
        kernel,
        out_shape=[jax.ShapeDtypeStruct((2, height, width), F32) for _, height, width in regions],
        in_specs=[pl.BlockSpec(memory_space=pltpu.HBM)],
        out_specs=[pl.BlockSpec(memory_space=pltpu.VMEM)] * len(regions),
        scratch_shapes=[pltpu.SemaphoreType.DMA((len(regions),))],
        compiler_params=pltpu.CompilerParams(vmem_limit_bytes=4 * MIB),
        cost_estimate=cost,
        name=name,
    )(in_hbm(tile))


def fold(places, index, mine, got, upper):
    count, half, width = got.shape
    quarter = half // 2

    def kernel(places, mine, got, send, keep):
        base = 0 if index is None else places[0, index] * half
        for k, out in ((1 - places[0, upper], send), (places[0, upper], keep)):
            for c in range(count):
                out[c] = (
                    mine[c, pl.ds(pl.multiple_of(base + k * quarter, quarter), quarter), :]
                    + got[c, pl.ds(pl.multiple_of(k * quarter, quarter), quarter), :]
                )

    vmem = pl.BlockSpec(memory_space=pltpu.VMEM)
    shape = jax.ShapeDtypeStruct((count, quarter, width), F32)
    return pl.pallas_call(
        kernel,
        out_shape=[shape, shape],
        in_specs=[pl.BlockSpec(memory_space=pltpu.SMEM), vmem, vmem],
        out_specs=[vmem, vmem],
        compiler_params=pltpu.CompilerParams(vmem_limit_bytes=6 * MIB),
        cost_estimate=SHORT,
        name="fold",
    )(places, mine, got)


def merge(top, corner):
    size = top.shape[1]

    def kernel(top, corner, out):
        for c in range(2):
            out[c] = top[c] + corner[c, :size, :]

    vmem = pl.BlockSpec(memory_space=pltpu.VMEM)
    return pl.pallas_call(
        kernel,
        out_shape=jax.ShapeDtypeStruct(top.shape, F32),
        in_specs=[vmem, vmem],
        out_specs=vmem,
        compiler_params=pltpu.CompilerParams(vmem_limit_bytes=4 * MIB),
        cost_estimate=SHORT,
        name="merge",
    )(top, corner)


def annotate(lower, bottom):
    size = bottom.shape[2]

    def kernel(lower, bottom, out, sem):
        source = bottom.at[0, pl.ds(bottom.shape[1] - 8, 8)]
        copy = pltpu.make_async_copy(source, out.at[0, pl.ds(out.shape[1] - 8, 8), pl.ds(0, size)], sem.at[0])
        copy.start()
        copy.wait()

    anywhere = pl.BlockSpec(memory_space=pl.ANY)
    return pl.pallas_call(
        kernel,
        out_shape=jax.ShapeDtypeStruct(lower.shape, F32),
        in_specs=[anywhere, anywhere],
        out_specs=anywhere,
        input_output_aliases={0: 0},
        scratch_shapes=[pltpu.SemaphoreType.DMA((1,))],
        compiler_params=pltpu.CompilerParams(vmem_limit_bytes=MIB),
        cost_estimate=SHORT,
        name="annotate",
    )(lower, bottom)


def deal(terms, parts, rows):
    count, _, width = terms[0].shape
    if rows % 8:
        return sum(terms).reshape(count, parts, rows, width).transpose(1, 0, 2, 3)

    def kernel(*refs):
        terms, out = refs[:-1], refs[-1]
        for j in range(parts):
            for c in range(count):
                out[j, c] = sum(term[c, j * rows : (j + 1) * rows, :] for term in terms)

    vmem = pl.BlockSpec(memory_space=pltpu.VMEM)
    return pl.pallas_call(
        kernel,
        out_shape=jax.ShapeDtypeStruct((parts, count, rows, width), F32),
        in_specs=[vmem] * len(terms),
        out_specs=vmem,
        compiler_params=pltpu.CompilerParams(vmem_limit_bytes=4 * MIB),
        cost_estimate=SHORT,
        name="deal",
    )(*terms)


def settle(places, start, probe, pieces):
    parts, count, rows, width = pieces.shape
    shape = (parts, count - 1, rows, width)
    if rows % 8:
        share = pieces.sum(axis=0)
        old = lax.dynamic_slice_in_dim(probe, places[0, start], rows, axis=1)
        return jnp.broadcast_to((old + share[:-1] / (share[-1:] + 1.0))[None], shape)

    def kernel(places, probe, pieces, out, old, sem):
        spot = pl.ds(pl.multiple_of(places[0, start], 8), rows)
        copy = pltpu.make_async_copy(probe.at[:, spot], old, sem.at[0])
        copy.start()
        share = sum(pieces[j] for j in range(parts))
        copy.wait()
        new = old[...] + share[:-1] / (share[-1:] + 1.0)
        for j in range(parts):
            out[j] = new

    vmem = pl.BlockSpec(memory_space=pltpu.VMEM)
    return pl.pallas_call(
        kernel,
        out_shape=jax.ShapeDtypeStruct(shape, F32),
        in_specs=[pl.BlockSpec(memory_space=pltpu.SMEM), pl.BlockSpec(memory_space=pltpu.HBM), vmem],
        out_specs=vmem,
        scratch_shapes=[pltpu.VMEM(shape[1:], F32), pltpu.SemaphoreType.DMA((1,))],
        compiler_params=pltpu.CompilerParams(vmem_limit_bytes=4 * MIB),
        cost_estimate=SHORT,
        name="settle",
    )(places, in_hbm(probe), pieces)


def collect(pieces):
    parts, count, rows, width = pieces.shape
    if rows % 8:
        return pieces.transpose(1, 0, 2, 3).reshape(count, parts * rows, width)

    def kernel(pieces, out):
        for j in range(parts):
            for c in range(count):
                out[c, j * rows : (j + 1) * rows, :] = pieces[j, c]

    vmem = pl.BlockSpec(memory_space=pltpu.VMEM)
    return pl.pallas_call(
        kernel,
        out_shape=jax.ShapeDtypeStruct((count, parts * rows, width), F32),
        in_specs=[vmem],
        out_specs=vmem,
        compiler_params=pltpu.CompilerParams(vmem_limit_bytes=4 * MIB),
        cost_estimate=pl.CostEstimate(flops=30_000_000_000, bytes_accessed=4_000_000, transcendentals=0),
        name="collect",
    )(pieces)


def join(places, upper, mine, other):
    half = mine.shape[1]

    def kernel(places, mine, other, out, sems):
        copies = [
            pltpu.make_async_copy(source, out.at[:, pl.ds(pl.multiple_of(at * half, half), half)], sems.at[i])
            for i, (source, at) in enumerate(((mine, places[0, upper]), (other, 1 - places[0, upper])))
        ]
        for copy in copies:
            copy.start()
        for copy in copies:
            copy.wait()

    anywhere = pl.BlockSpec(memory_space=pl.ANY)
    return pl.pallas_call(
        kernel,
        out_shape=jax.ShapeDtypeStruct((mine.shape[0], 2 * half) + mine.shape[2:], F32),
        in_specs=[pl.BlockSpec(memory_space=pltpu.SMEM), anywhere, anywhere],
        out_specs=anywhere,
        scratch_shapes=[pltpu.SemaphoreType.DMA((2,))],
        compiler_params=pltpu.CompilerParams(vmem_limit_bytes=MIB),
        cost_estimate=pl.CostEstimate(flops=0, bytes_accessed=2_000_000, transcendentals=0),
        name="join",
    )(places, mine, other)


def body(object_field, probe, amplitudes, positions, counts):
    modes, _, size, _ = probe.shape
    tile_rows, tile_cols = object_field.shape[1:]
    slots = amplitudes.shape[0]
    origin = jnp.stack([lax.axis_index("row") * tile_rows, lax.axis_index("col") * tile_cols]).astype(jnp.int32)
    bits = [1 << k for k in range(lax.axis_size("row").bit_length() - 1)]
    uppers = [(lax.axis_index("row") & bit) // bit for bit in bits]

    def relative(table):
        return jnp.concatenate([table[:, : 2 * slots] - jnp.tile(origin, slots)[None], table[:, 2 * slots :]], axis=1)

    right_up, right_down = cut(
        object_field, ((0, size, size), (size, tile_rows - size, size)), SHORT, "cut_right"
    )
    right_up, right_down, after_right = together(right_up, right_down, object_field)
    right_up = from_behind(right_up, "col", -1)
    right_down = from_behind(right_down, "col", -1)
    (lower,) = cut(after_right, ((0, size, tile_cols),), LONG, "cut_lower")
    meta = jnp.concatenate([positions.reshape(1, 2 * slots), counts.reshape(1, 1)], axis=1)
    lower = from_behind(lower, "row", -1)

    parts = lax.axis_size("col")
    rows = (size >> len(bits)) // parts
    me = lax.axis_index("col")
    start = sum(upper * (size >> (k + 1)) for k, upper in enumerate(uppers)) + me * rows
    bit_at = 2 * slots + 2
    me_at = bit_at + len(bits)
    start_at, origin_at = me_at + 1, me_at + 2
    extra = [1 - uppers[0], *uppers, me, start, origin[0], origin[1]]
    mine = jnp.concatenate([relative(meta), jnp.stack([item.astype(jnp.int32) for item in extra])[None]], axis=1)
    note = jnp.pad(meta.astype(F32), ((0, 7), (0, size - meta.shape[1])))
    mine, note = together(mine, note)
    amplitudes = arrange(mine, amplitudes)
    right_up, amplitudes = together(right_up, amplitudes)
    corner = from_behind(right_up, "row", -1)
    amplitudes, lower = together(amplitudes, lower)
    state = visit_inside(mine, probe, amplitudes, object_field, lower)
    right_up, right_down, corner, *state = together(right_up, right_down, corner, *state)
    own, bottom_spill, top_spill, corner_spill, lower_spill, send, share = visit_beyond(
        mine, probe, amplitudes, [right_up, right_down, corner], note, state
    )

    index = bit_at
    for k, bit in enumerate(bits):
        got = exchange(send, "row", bit)
        if k == 0:
            bottom_spill = from_behind(bottom_spill, "col", 1)
        if k + 1 < len(bits):
            send, share = fold(mine, index, share, got, bit_at + k + 1)
            index = None
    got, bottom_spill, lower_spill = together(got, bottom_spill, lower_spill)
    lower_spill = from_behind(annotate(lower_spill, bottom_spill), "row", 1)
    pieces = lax.all_to_all(deal([share, got], parts, rows), "col", 0, 0, tiled=True)
    new = settle(mine, start_at, probe.reshape(2 * modes, size, size), pieces)
    new, lower_spill, corner_spill = together(new, lower_spill, corner_spill)
    corner_spill = from_behind(corner_spill, "row", 1)
    inverse_light = light(
        mine, slots, origin_at, probe, bottom_spill, corner_spill, lower_spill, (tile_rows, tile_cols)
    )
    new = lax.all_to_all(new, "col", 0, 0, tiled=True)
    new, corner_spill = together(new, corner_spill)
    top_spill, new = together(merge(top_spill, corner_spill), new)
    top_spill = from_behind(top_spill, "col", 1)
    new = collect(new)
    for k, bit in reversed(list(enumerate(bits))):
        if k == 0:
            new, own = together(new, own)
            new_object = finish_far(own, bottom_spill, lower_spill, inverse_light, object_field)
        other = exchange(new, "row", bit)
        if k + 1 == len(bits):
            other, inverse_light = together(other, inverse_light)
        if k == 0:
            new_object, top_spill = together(new_object, top_spill)
            new_object = finish_near(new_object, top_spill, inverse_light)
            other, new_object = together(other, new_object)
        new = join(mine, bit_at + k, new, other)
    return (new_object, new.reshape(modes, 2, size, size))


def solution(mesh):
    in_specs = (
        P(None, "row", "col"),
        P(),
        P(("row", "col"), None, None),
        P(("row", "col"), None),
        P(("row", "col")),
    )
    out_specs = (P(None, "row", "col"), P())
    return jax.shard_map(body, mesh=mesh, in_specs=in_specs, out_specs=out_specs, check_vma=False)
```
